32 devices in a mesh: section: 2 (over core), row: 4 (over y, x), col: 4 (over z).
Axes of the slice: x: 2, y: 2, z: 4, core: 2. Of those that a mesh axis runs over, the one named last changes fastest.
Arguments:
- tokens: bfloat16 [3, 1536, 1024], P(None, 'col', 'row'), may hold values from -6 to 6
- cotangent: bfloat16 [3, 1536, 1024], P(None, 'col', 'row'), may hold values from -6 to 6
- block_order: int32 [3, 24], replicated, may hold values from 0 to 23, each once within a row
- lengths: int32 [3, 4], replicated, may hold values from 1 to 12, 24 in all within a row
- decay: float32 [2, 3, 24, 8], P('section', None, 'col', 'row'), may hold values from 0 to 1
- write_gate: float32 [2, 3, 1536, 8], P('section', None, 'col', 'row'), may hold values from 0.1 to 1
- gain_attn: bfloat16 [2, 1024], P('section', ('row', 'col')), may hold values from 0.5 to 1.5
- w_query: bfloat16 [2, 1024, 1024], P('section', 'col', 'row'), may hold values from -0.1875 to 0.1875
- w_key: bfloat16 [2, 1024, 1024], P('section', 'col', 'row'), may hold values from -0.1875 to 0.1875
- w_value: bfloat16 [2, 1024, 1024], P('section', 'col', 'row'), may hold values from -0.1875 to 0.1875
- persist_key: bfloat16 [2, 16, 1024], P('section', 'col', 'row'), may hold values from -6 to 6
- persist_value: bfloat16 [2, 16, 1024], P('section', 'col', 'row'), may hold values from -6 to 6
- w_output: bfloat16 [2, 1024, 1024], P('section', 'row', 'col'), may hold values from -0.75 to 0.75
- gain_ffn: bfloat16 [2, 1024], P('section', ('row', 'col')), may hold values from 0.5 to 1.5
- w_gate: bfloat16 [2, 1024, 2816], P('section', 'col', 'row'), may hold values from -0.1875 to 0.1875
- w_up: bfloat16 [2, 1024, 2816], P('section', 'col', 'row'), may hold values from -0.1875 to 0.1875
- w_down: bfloat16 [2, 2816, 1024], P('section', 'row', 'col'), may hold values from -0.21875 to 0.21875
Outputs:
- activations: bfloat16 [2, 3, 1536, 1024], P('section', None, 'col', 'row')
- input_grads: bfloat16 [2, 3, 1536, 1024], P('section', None, 'col', 'row')
- grad_gain_attn: float32 [2, 1024], P('section', ('row', 'col'))
- grad_query: float32 [2, 1024, 1024], P('section', 'col', 'row')
- grad_key: float32 [2, 1024, 1024], P('section', 'col', 'row')
- grad_value: float32 [2, 1024, 1024], P('section', 'col', 'row')
- grad_pkey: float32 [2, 16, 1024], P('section', 'col', 'row')
- grad_pvalue: float32 [2, 16, 1024], P('section', 'col', 'row')
- grad_output: float32 [2, 1024, 1024], P('section', 'row', 'col')
- grad_gain_ffn: float32 [2, 1024], P('section', ('row', 'col'))
- grad_gate: float32 [2, 1024, 2816], P('section', 'col', 'row')
- grad_up: float32 [2, 1024, 2816], P('section', 'col', 'row')
- grad_down: float32 [2, 2816, 1024], P('section', 'row', 'col')
The draws below stay inside these ranges and needn't reach their ends.
Inputs may be any that keep to these rules, and one draw needn't show every extreme that they name: Each row block_order[m] is a permutation of the 24 block numbers. lengths[m] lists, in blocks of 64 tokens, the lengths of the 4 sequences of micro-batch m laid end to end in dealt order; for each micro-batch they sum to 24, and the longest has exactly 12 blocks.
All inputs are finite; a program needn't handle non-finite values.
Results may differ from the reference program's by a relative error of at most 0.033.
Values may be sent and summed in bfloat16 or wider, within the bound.
A program may use at most 192 MiB of HBM per device.

```python
import math
from functools import partial
import jax
import jax.numpy as jnp
import numpy as np
from jax import lax

D = 1024
HEAD_TOTAL = 8
FF = 2816
P_SIZE = 16
BLOCK = 64
MICRO_BATCHES = 3
DH = 128
TOKENS = 1536
MEMORY_STEPS = 24
MAX_BLOCKS = 12
NSEQ = 4


def draw_decay(key, part):
    key = jax.random.fold_in(key, 7)
    rate_random_key, noise_random_key, spike_random_key, depth_random_key = jax.random.split(key, 4)
    lowest_rate = 0.3 / MAX_BLOCKS
    highest_rate = 2.0
    rate_logarithm = jax.random.uniform(rate_random_key, (2, 1, 1, HEAD_TOTAL), jnp.float32, jnp.log(lowest_rate), jnp.log(highest_rate))
    random_noise = jax.random.uniform(noise_random_key, (2, MICRO_BATCHES, MEMORY_STEPS, HEAD_TOTAL), jnp.float32, 0.5, 1.5)
    spike_events = jax.random.bernoulli(spike_random_key, 1.0 / MAX_BLOCKS, (2, MICRO_BATCHES, MEMORY_STEPS, HEAD_TOTAL))
    spike_depth = jax.random.uniform(depth_random_key, (2, MICRO_BATCHES, MEMORY_STEPS, HEAD_TOTAL), jnp.float32, 0.5, 0.8)
    return jnp.exp(-jnp.exp(rate_logarithm) * random_noise) * jnp.where(spike_events, spike_depth, 1.0)


def block_levels(rng, shape, shards, smallest, top_value):
    level = 1.0
    for axis_at, parts in shards:
        heights = jax.random.uniform(jax.random.fold_in(jax.random.fold_in(rng, 6), axis_at), (parts,), jnp.float32, smallest / len(shards), top_value / len(shards))
        level = level * jnp.repeat(jnp.exp(heights), shape[axis_at] // parts).reshape((-1,) + (1,) * (len(shape) - 1 - axis_at))
    return level


def profile(number_of, total, bound, slope):
    portions = [(1 << 20) // math.isqrt(standing ** slope) + 1 for standing in range(2, number_of + 1)]
    rest, holding = total - bound - (number_of - 1), [1] * (number_of - 1)
    while rest > 0:
        candidates = [i for i in range(number_of - 1) if holding[i] < bound]
        mass, left = sum([portions[i] for i in candidates]), rest
        for i in candidates:
            extra = min(bound - holding[i], max(1, left * portions[i] // mass), rest)
            holding[i] = holding[i] + extra
            rest = rest - extra
    return np.array([bound] + holding)


def uneven(rng, number_of, total, most, slope):
    if number_of == 2:
        one = jax.random.randint(rng, (), max(1, total - most), min(most, total - 1) + 1)
        return jnp.stack([one, total - one])
    tallies = jnp.asarray(profile(number_of, total, most, slope), jnp.int32)
    pairs = (number_of - 1) // 2
    donor, sink = tallies[1:1 + 2 * pairs:2], tallies[2:2 + 2 * pairs:2]
    margin = jnp.minimum(donor - 1, most - sink)
    moved = jax.random.randint(jax.random.fold_in(rng, 1), (pairs,), 0, 1 << 20) % (margin + 1)
    tallies = tallies.at[1:1 + 2 * pairs:2].set(donor - moved).at[2:2 + 2 * pairs:2].set(sink + moved)
    return tallies[jax.random.permutation(jax.random.fold_in(rng, 2), number_of)]


def gaussian(key, extent, width, limit, cuts=(), kind=jnp.bfloat16):
    values = jax.random.normal(key, extent, jnp.float32) * width
    if len(cuts) > 0:
        values = block_levels(key, extent, cuts, -0.22, 0.18) * values
    return jnp.clip(values, min=-limit, max=limit).astype(kind)


def setup_inputs(seed: int = 0) -> dict:
    keys = jax.random.split(jax.random.key(seed), 18)
    tokens = gaussian(keys[0], (MICRO_BATCHES, TOKENS, D), 1.0, 6.0, ((1, 4), (2, 4)))
    cotangent = gaussian(keys[1], (MICRO_BATCHES, TOKENS, D), 1.0, 6.0, ((1, 4), (2, 4)))
    block_order = jax.vmap(lambda own: jax.random.permutation(own, MEMORY_STEPS))(jax.random.split(keys[2], MICRO_BATCHES)).reshape((MICRO_BATCHES, MEMORY_STEPS)).astype(jnp.int32)
    lengths = jax.vmap(lambda own: uneven(own, NSEQ, MEMORY_STEPS, MAX_BLOCKS, 1))(jax.random.split(keys[3], MICRO_BATCHES)).reshape((MICRO_BATCHES, NSEQ)).astype(jnp.int32)
    decay = draw_decay(jax.random.fold_in(keys[17], 71), 0)
    write_gate = jnp.clip(0.1 + 0.9 * jax.random.uniform(keys[5], (2, MICRO_BATCHES, TOKENS, HEAD_TOTAL), jnp.float32) ** block_levels(keys[5], (2, MICRO_BATCHES, TOKENS, HEAD_TOTAL), ((0, 2), (2, 4), (3, 4)), -0.2, 0.2), 0.1, 1.0)
    gain_attn = jnp.clip(1.0 + 0.1 * jax.random.normal(keys[6], (2, D), jnp.float32), 0.5, 1.5).astype(jnp.bfloat16)
    w_query = gaussian(keys[7], (2, D, D), D ** -0.5, 0.1875, ((0, 2), (1, 4), (2, 4)))
    w_key = gaussian(keys[8], (2, D, D), D ** -0.5, 0.1875, ((0, 2), (1, 4), (2, 4)))
    w_value = gaussian(keys[9], (2, D, D), D ** -0.5, 0.1875, ((0, 2), (1, 4), (2, 4)))
    persist_key = gaussian(keys[10], (2, P_SIZE, D), 1.0, 6.0, ((0, 2), (1, 4), (2, 4)))
    persist_value = gaussian(keys[11], (2, P_SIZE, D), 1.0, 6.0, ((0, 2), (1, 4), (2, 4)))
    w_output = gaussian(keys[12], (2, D, D), (D // 16) ** -0.5, 0.75, ((0, 2), (1, 4), (2, 4)))
    gain_ffn = jnp.clip(1.0 + 0.1 * jax.random.normal(keys[13], (2, D), jnp.float32), 0.5, 1.5).astype(jnp.bfloat16)
    w_gate = gaussian(keys[14], (2, D, FF), D ** -0.5, 0.1875, ((0, 2), (1, 4), (2, 4)))
    w_up = gaussian(keys[15], (2, D, FF), D ** -0.5, 0.1875, ((0, 2), (1, 4), (2, 4)))
    w_down = gaussian(keys[16], (2, FF, D), (FF // 4) ** -0.5, 0.21875, ((0, 2), (1, 4), (2, 4)))
    return dict(tokens=tokens, cotangent=cotangent, block_order=block_order, lengths=lengths, decay=decay, write_gate=write_gate, gain_attn=gain_attn, w_query=w_query, w_key=w_key, w_value=w_value, persist_key=persist_key, persist_value=persist_value, w_output=w_output, gain_ffn=gain_ffn, w_gate=w_gate, w_up=w_up, w_down=w_down)


epsilon = 1e-06
highest = lax.Precision.HIGHEST

@jax.custom_vjp
def low(v):
    return lax.optimization_barrier(v.astype(jnp.bfloat16)).astype(jnp.float32)

@jax.custom_vjp
def low_back(v):
    return v

def low_keep(v):
    return (low(v), None)

def low_pass(kept, grad):
    return (grad,)

def back_keep(v):
    return (v, None)

def back_low(kept, grad):
    return (low(grad),)
low.defvjp(low_keep, low_pass)
low_back.defvjp(back_keep, back_low)

def matmul(left, right):
    return jnp.dot(left, right, precision=highest)

def rms_norm(values, gain):
    return values * lax.rsqrt(lax.optimization_barrier(jnp.mean(values * values, axis=-1, keepdims=True)) + epsilon) * gain

def block_keep(length_row, decay_rows):
    seq_ends = jnp.cumsum(length_row)
    starts = seq_ends - length_row
    block_ids = jnp.arange(MEMORY_STEPS, dtype=jnp.int32)
    is_start = jnp.any(block_ids[:, None] == starts[None, :], axis=1)
    return jnp.where(is_start[:, None], jnp.zeros_like(decay_rows), decay_rows)

def reorder_blocks(values, picks):
    blocks = values.reshape(MEMORY_STEPS, BLOCK, D)
    return jnp.take(blocks, picks.astype(jnp.int32), axis=0).reshape(TOKENS, D)

def memory_block(persist_keys, persist_values, memory, block_in):
    queries, keys_blk, values_blk, gate_blk, keep_blk = block_in
    score_scale = DH ** (-0.5)
    state_now = keep_blk[:, None, None] * memory
    inner_scores = low_back(jnp.einsum('ihd,jhd->hij', queries, keys_blk, precision=highest) * score_scale)
    outer_scores = low_back(jnp.einsum('ihd,phd->hip', queries, persist_keys, precision=highest) * score_scale)
    causal = jnp.arange(BLOCK)[:, None] >= jnp.arange(BLOCK)[None, :]
    inner_scores = jnp.where(causal[None], inner_scores, -1e+30)
    weights = low(jax.nn.softmax(jnp.concatenate([outer_scores, inner_scores], axis=-1), axis=-1))
    attended = jnp.einsum('hip,phd->ihd', weights[..., :P_SIZE], persist_values, precision=highest)
    attended = attended + jnp.einsum('hij,jhd->ihd', weights[..., P_SIZE:], values_blk, precision=highest)
    mem_read = jnp.einsum('ihd,hde->ihe', queries, state_now, precision=highest) * score_scale
    update = jnp.einsum('ihd,ihe->hde', keys_blk * gate_blk[..., None], values_blk, precision=highest) / BLOCK
    return (state_now + update, attended + mem_read)

def split_heads(values):
    return values.reshape(MEMORY_STEPS, BLOCK, HEAD_TOTAL, DH)

def section_layer(gate_rows, keep_rows, layer_in, params):
    gain_attn, w_query, w_key, w_value, persist_key, persist_value, w_output, gain_ffn, w_gate, w_up, w_down = params
    residual = low_back(layer_in)
    attn_in = low(rms_norm(residual, gain_attn))
    queries = low(low_back(matmul(attn_in, w_query)))
    keys_all = low(low_back(matmul(attn_in, w_key)))
    values_all = low(low_back(matmul(attn_in, w_value)))
    block_fn = jax.checkpoint(partial(memory_block, persist_key.reshape(P_SIZE, HEAD_TOTAL, DH), persist_value.reshape(P_SIZE, HEAD_TOTAL, DH)))
    _, mixed_out = lax.scan(block_fn, jnp.zeros((HEAD_TOTAL, DH, DH), jnp.float32), (split_heads(queries), split_heads(keys_all), split_heads(values_all), gate_rows.reshape(MEMORY_STEPS, BLOCK, HEAD_TOTAL), keep_rows))
    mixed_out = low(low_back(mixed_out.reshape(TOKENS, D)))
    middle = residual + low_back(matmul(mixed_out, w_output))
    ffn_in = low(rms_norm(middle, gain_ffn))
    gate_pre = low_back(matmul(ffn_in, w_gate))
    up_pre = low_back(matmul(ffn_in, w_up))
    ffn_act = low(jax.nn.silu(gate_pre) * up_pre)
    return low(middle + low_back(matmul(ffn_act, w_down)))

def reference(tokens, cotangent, block_order, lengths, decay, write_gate, gain_attn, w_query, w_key, w_value, persist_key, persist_value, w_output, gain_ffn, w_gate, w_up, w_down):
    weight_list = [gain_attn, w_query, w_key, w_value, persist_key, persist_value, w_output, gain_ffn, w_gate, w_up, w_down]
    weight_list = [member.astype(jnp.float32) for member in weight_list]
    params_first = tuple((member[0] for member in weight_list))
    params_second = tuple((member[1] for member in weight_list))
    grads_first = tuple((jnp.zeros_like(member) for member in params_first))
    grads_second = tuple((jnp.zeros_like(member) for member in params_second))
    first_outs, second_outs, first_grads, second_grads = ([], [], [], [])
    for micro_idx in range(MICRO_BATCHES):
        order = block_order[micro_idx].astype(jnp.int32)
        inverse = jnp.argsort(order).astype(jnp.int32)
        keep_first = block_keep(lengths[micro_idx], decay[0, micro_idx])
        keep_second = block_keep(lengths[micro_idx], decay[1, micro_idx])
        run_first = partial(section_layer, write_gate[0, micro_idx], keep_first)
        run_second = partial(section_layer, write_gate[1, micro_idx], keep_second)
        dealt_in = reorder_blocks(tokens[micro_idx].astype(jnp.float32), order)
        dealt_cot = reorder_blocks(cotangent[micro_idx].astype(jnp.float32), order)
        middle_act, back_first = jax.vjp(run_first, dealt_in, params_first)
        final_act, back_second = jax.vjp(run_second, middle_act, params_second)
        grad_middle, param_second = back_second(dealt_cot)
        grad_middle = low(grad_middle)
        grad_tokens, param_first = back_first(grad_middle)
        grads_first = tuple((running + fresh for running, fresh in zip(grads_first, param_first)))
        grads_second = tuple((running + fresh for running, fresh in zip(grads_second, param_second)))
        first_outs.append(reorder_blocks(middle_act, inverse))
        second_outs.append(reorder_blocks(final_act, inverse))
        first_grads.append(reorder_blocks(grad_tokens, inverse))
        second_grads.append(reorder_blocks(grad_middle, inverse))
    activations = jnp.stack([jnp.stack(first_outs), jnp.stack(second_outs)]).astype(jnp.bfloat16)
    input_grads = jnp.stack([jnp.stack(first_grads), jnp.stack(second_grads)]).astype(jnp.bfloat16)
    stacked = [jnp.stack([one_grad, two_grad]) for one_grad, two_grad in zip(grads_first, grads_second)]
    return (activations, input_grads, stacked[0], stacked[1], stacked[2], stacked[3], stacked[4], stacked[5], stacked[6], stacked[7], stacked[8], stacked[9], stacked[10])
```

```python
import functools

import jax
import jax.numpy as jnp
from jax import lax
from jax.experimental import pallas as pl
from jax.experimental.pallas import tpu as pltpu
from jax.sharding import PartitionSpec as P

BLOCK = 64
EPS = 1e-06
MESH = pl.DeviceIdType.MESH
F32 = jnp.float32
BF16 = jnp.bfloat16
VMEM_LIMIT = 56 << 20
N_AG, N_RS = 8, 7


def dot(a, b, ca=1, cb=0):
    return lax.dot_general(a, b, (((ca,), (cb,)), ((), ())), preferred_element_type=F32)


class Rows:
    def __init__(self, rows, own, width, send, recv):
        self.rows, self.own, self.width, self.half = rows, own, width, width // 2
        self.send, self.recv = send, recv
        self.s, self.r, self.c = (lax.axis_index(a) for a in ("section", "row", "col"))
        self.rx = self.r + 1 - 2 * lax.rem(self.r, 2)
        self.ry = lax.rem(self.r + 2, 4)
        self.rd = lax.rem(self.rx + 2, 4)
        self.x = (self.s, self.rx, self.c)
        self.y = (self.s, self.ry, self.c)
        self.sib = (1 - self.s, self.r, self.c)
        self.started = []

    def greet(self, others=()):
        barrier = pltpu.get_barrier_semaphore()
        peers = [self.x, self.y, self.sib] + list(others)
        for peer in peers:
            pl.semaphore_signal(barrier, inc=1, device_id=peer, device_id_type=MESH)
        pl.semaphore_wait(barrier, len(peers))

    def copy(self, src, dst, m, k, peer):
        return pltpu.make_async_remote_copy(
            src_ref=src,
            dst_ref=dst,
            send_sem=self.send.at[m, k],
            recv_sem=self.recv.at[m, k],
            device_id=peer,
            device_id_type=MESH,
        )

    def go(self, copy):
        copy.start()
        self.started.append(copy)

    def finish(self):
        for copy in self.started:
            copy.wait_send()

    def span(self, m, s, r):
        return pl.ds(pl.multiple_of(m * self.rows + (s * 4 + r) * self.own, 16), self.own)

    def ag_copy(self, full, m, k):
        left, right = pl.ds(0, self.half), pl.ds(self.half, self.half)
        mine, atx, aty, atd = (
            self.span(m, self.s, r) for r in (self.r, self.rx, self.ry, self.rd)
        )
        if k == 0:
            return self.copy(full.at[mine, :], full.at[mine, :], m, 0, self.x)
        if k == 1:
            return self.copy(full.at[mine, :], full.at[mine, :], m, 1, self.y)
        if k == 2:
            return self.copy(full.at[mine, :], full.at[mine, :], m, 2, self.sib)
        if k == 3:
            return self.copy(full.at[atx, left], full.at[atx, left], m, 3, self.y)
        if k == 4:
            return self.copy(full.at[aty, right], full.at[aty, right], m, 4, self.x)
        if k == 5:
            return self.copy(full.at[atx, :], full.at[atx, :], m, 5, self.sib)
        if k == 6:
            return self.copy(full.at[aty, :], full.at[aty, :], m, 6, self.sib)
        return self.copy(full.at[atd, :], full.at[atd, :], m, 7, self.sib)

    def ag_start(self, full, m):
        for k in (0, 1, 2):
            self.go(self.ag_copy(full, m, k))

    def ag_pass(self, full, m):
        self.ag_copy(full, m, 0).wait_recv()
        self.go(self.ag_copy(full, m, 3))
        self.go(self.ag_copy(full, m, 5))
        self.ag_copy(full, m, 1).wait_recv()
        self.go(self.ag_copy(full, m, 4))
        self.go(self.ag_copy(full, m, 6))

    def ag_diag(self, full, m):
        self.ag_copy(full, m, 3).wait_recv()
        self.ag_copy(full, m, 4).wait_recv()
        self.go(self.ag_copy(full, m, 7))

    def ag_wait(self, full, m):
        for k in (2, 5, 6, 7):
            self.ag_copy(full, m, k).wait_recv()

    def rs_copy(self, m, k):
        part, pair, both, transit, final = self.buffers
        left, right = pl.ds(0, self.half), pl.ds(self.half, self.half)
        if k == 8:
            other = pl.ds(
                pl.multiple_of(m * self.rows + (1 - self.s) * 4 * self.own, 16), 4 * self.own
            )
            return self.copy(part.at[other, :], pair.at[m], m, 8, self.sib)
        if k == 9:
            return self.copy(both.at[m, self.rd, :, left], transit.at[m, 0], m, 9, self.x)
        if k == 10:
            return self.copy(both.at[m, self.rd, :, right], transit.at[m, 1], m, 10, self.y)
        if k == 11:
            return self.copy(both.at[m, self.rx, :, left], final.at[m, 0, :, left], m, 11, self.x)
        if k == 12:
            return self.copy(both.at[m, self.ry, :, right], final.at[m, 1, :, right], m, 12, self.y)
        if k == 13:
            return self.copy(both.at[m, self.ry, :, left], final.at[m, 1, :, left], m, 13, self.y)
        return self.copy(both.at[m, self.rx, :, right], final.at[m, 0, :, right], m, 14, self.x)

    def rs_start(self, m):
        self.go(self.rs_copy(m, 8))

    def rs_pair(self, m):
        part, pair, both, _, _ = self.buffers
        self.rs_copy(m, 8).wait_recv()
        for r in range(4):
            mine = part[self.span(m, self.s, r), :].astype(F32)
            theirs = pair[m, r * self.own : (r + 1) * self.own, :].astype(F32)
            both[m, r] = (mine + theirs).astype(BF16)
        for k in (9, 10, 11, 12):
            self.go(self.rs_copy(m, k))

    def rs_transit(self, m):
        _, _, both, transit, _ = self.buffers
        left, right = pl.ds(0, self.half), pl.ds(self.half, self.half)
        self.rs_copy(m, 9).wait_recv()
        total = both[m, self.ry, :, left].astype(F32) + transit[m, 0].astype(F32)
        both[m, self.ry, :, left] = total.astype(BF16)
        self.go(self.rs_copy(m, 13))
        self.rs_copy(m, 10).wait_recv()
        total = both[m, self.rx, :, right].astype(F32) + transit[m, 1].astype(F32)
        both[m, self.rx, :, right] = total.astype(BF16)
        self.go(self.rs_copy(m, 14))

    def rs_result(self, m):
        _, _, both, _, final = self.buffers
        for k in (11, 12, 13, 14):
            self.rs_copy(m, k).wait_recv()
        return both[m, self.r].astype(F32) + final[m, 0].astype(F32) + final[m, 1].astype(F32)


def row_scratch(micros, rows, own, width):
    return [
        pltpu.VMEM((micros * rows, width), BF16),
        pltpu.VMEM((micros, 4 * own, width), BF16),
        pltpu.VMEM((micros, 4, own, width), BF16),
        pltpu.VMEM((micros, 2, own, width // 2), BF16),
        pltpu.VMEM((micros, 2, own, width), BF16),
        pltpu.SemaphoreType.DMA((micros, N_AG + N_RS)),
        pltpu.SemaphoreType.DMA((micros, N_AG + N_RS)),
    ]


class Local:
    def __init__(self, sems):
        self.sems, self.used, self.open = sems, 0, []

    def start(self, src, dst):
        copy = pltpu.make_async_copy(src, dst, self.sems.at[self.used])
        self.used += 1
        copy.start()
        self.open.append(copy)
        return copy

    def wait(self, copy):
        copy.wait()
        self.open.remove(copy)

    def finish(self):
        for copy in list(self.open):
            copy.wait()


def inv_rms(values):
    return lax.rsqrt(jnp.mean(values * values, axis=1, keepdims=True) + EPS)


def norm_to(full, gain, values, span):
    full[span, :] = (values * inv_rms(values) * gain).astype(BF16)


def norm_back(values, gain, grad):
    scale = inv_rms(values)
    weighted = grad * gain
    inner = jnp.mean(weighted * values, axis=1, keepdims=True)
    back = scale * weighted - values * (scale * scale * scale * inner)
    return back, jnp.sum(grad * values * scale, axis=0, keepdims=True)


def ffn_forward_kernel(
    micros, rows, own, mid, gain, wg_h, wu_h, wd_h, in_o, gp_o, up_o, act_o, y_o,
    full, wg, wu, wd, gp, up, act, part, pair, both, transit, final, send, recv, sems,
):
    width = mid.shape[2]
    row = Rows(rows, own, width, send, recv)
    row.buffers = (part, pair, both, transit, final)
    loc = Local(sems)
    loads = [loc.start(a, b) for a, b in ((wg_h, wg), (wu_h, wu), (wd_h, wd))]
    scale = gain[...]
    for m in range(micros):
        norm_to(full, scale, mid[m], row.span(m, row.s, row.r))
    row.greet()

    def compute(m):
        here = pl.ds(m * rows, rows)
        loc.start(full.at[here, :], in_o.at[here, :])
        gate = dot(full[here, :], wg[...])
        lift = dot(full[here, :], wu[...])
        gp[here, :] = gate.astype(BF16)
        up[here, :] = lift.astype(BF16)
        act[here, :] = (gate * jax.nn.sigmoid(gate) * lift).astype(BF16)
        part[here, :] = dot(act[here, :], wd[...]).astype(BF16)
        for a, b in ((gp, gp_o), (up, up_o), (act, act_o)):
            loc.start(a.at[here, :], b.at[here, :])

    def result(m):
        y_o[m] = (mid[m] + row.rs_result(m)).astype(BF16)

    def before(m):
        if m == 0:
            for copy in loads:
                loc.wait(copy)

    schedule(row, full, micros, before, compute, result)
    row.finish()
    loc.finish()


def schedule(row, full, micros, before, compute, result, between=None):
    row.ag_start(full, 0)
    if micros > 1:
        row.ag_start(full, 1)
    row.ag_pass(full, 0)
    for m in range(2, micros):
        row.ag_start(full, m)
    if micros > 1:
        row.ag_pass(full, 1)
    row.ag_diag(full, 0)
    for m in range(micros):
        row.ag_wait(full, m)
        before(m)
        if m >= 1:
            row.rs_pair(m - 1)
        if m >= 2:
            row.rs_transit(m - 2)
        compute(m)
        row.rs_start(m)
        if m + 2 < micros:
            row.ag_pass(full, m + 2)
        if m + 1 < micros:
            row.ag_diag(full, m + 1)
    tail(row, micros, result, between)


def tail(row, micros, result, between=None):
    more = list(between) if between else []

    def step():
        if more:
            more.pop(0)()

    step()
    if micros > 1:
        row.rs_transit(micros - 2)
    row.rs_pair(micros - 1)
    for m in range(micros - 1):
        if m < micros - 2:
            step()
            result(m)
    step()
    row.rs_transit(micros - 1)
    if micros > 1:
        result(micros - 2)
    while more:
        step()
    result(micros - 1)


def ffn_backward_kernel(
    micros, rows, own, dy, mid, gain, wg_h, wu_h, wd_h, in_h, gp_h, up_h, act_h,
    dmid_o, dgain_o, gg_o, gu_o, gd_o,
    full, wg, wu, wd, xin, gp, up, act, dg, du, gg, gu, gd,
    part, pair, both, transit, final, send, recv, sems,
):
    width = mid.shape[2]
    row = Rows(rows, own, width, send, recv)
    row.buffers = (part, pair, both, transit, final)
    loc = Local(sems)
    early = [
        loc.start(a, b)
        for a, b in ((wd_h, wd), (gp_h, gp), (up_h, up), (wg_h, wg), (wu_h, wu))
    ]
    late = [loc.start(a, b) for a, b in ((act_h, act), (in_h, xin))]
    for m in range(micros):
        full[row.span(m, row.s, row.r), :] = dy[m]
    row.greet()
    scale = gain[...]
    dgain_o[...] = jnp.zeros_like(dgain_o)

    def before(m):
        if m == 0:
            for copy in early:
                loc.wait(copy)

    def compute(m):
        here = pl.ds(m * rows, rows)
        d_act = dot(full[here, :], wd[...], 1, 1)
        gate = gp[here, :].astype(F32)
        lift = up[here, :].astype(F32)
        sig = jax.nn.sigmoid(gate)
        silu = gate * sig
        dg[here, :] = (d_act * lift * (sig + silu * (1.0 - sig))).astype(BF16)
        du[here, :] = (d_act * silu).astype(BF16)
        total = dot(dg[here, :], wg[...], 1, 1) + dot(du[here, :], wu[...], 1, 1)
        part[here, :] = total.astype(BF16)

    def result(m):
        back, gains = norm_back(mid[m], scale, row.rs_result(m))
        dmid_o[m] = dy[m].astype(F32) + back
        dgain_o[...] += gains

    def down():
        for copy in late:
            loc.wait(copy)
        tiles(width, lambda at: store(gd, at, dot(act[...], full[:, at], 0, 0), True))
        loc.start(gd, gd_o)

    def gates():
        tiles(width, lambda at: store(gg, at, dot(xin[:, at], dg[...], 0, 0), False))
        loc.start(gg, gg_o)

    def ups():
        tiles(width, lambda at: store(gu, at, dot(xin[:, at], du[...], 0, 0), False))
        loc.start(gu, gu_o)

    schedule(row, full, micros, before, compute, result, [down, gates, ups])
    row.finish()
    loc.finish()


def store(ref, at, value, columns):
    if columns:
        ref[:, at] = value.astype(ref.dtype)
    else:
        ref[at, :] = value.astype(ref.dtype)


def tiles(width, body, tile=256):
    @pl.loop(0, width // tile)
    def _(i):
        body(pl.ds(pl.multiple_of(i * tile, tile), tile))


def pair_masks(size):
    rows_at = lax.broadcasted_iota(jnp.int32, (size, size), 0)
    cols_at = lax.broadcasted_iota(jnp.int32, (size, size), 1)
    return (rows_at >= cols_at) & (rows_at // BLOCK == cols_at // BLOCK)


def pair_probs(q, k, pk, mask, scale):
    inner = jnp.where(mask, dot(q, k, 1, 1) * scale, -1e30)
    outer = dot(q, pk, 1, 1) * scale
    top = jnp.maximum(
        jnp.max(inner, axis=1, keepdims=True), jnp.max(outer, axis=1, keepdims=True)
    )
    inner = jnp.exp(inner - top)
    outer = jnp.exp(outer - top)
    norm = 1.0 / (jnp.sum(inner, axis=1, keepdims=True) + jnp.sum(outer, axis=1, keepdims=True))
    return inner * norm, outer * norm


def col_peers(row, groups):
    return [(row.s, row.r, lax.rem(row.c + k, groups)) for k in range(1, groups)]


class States:
    def __init__(self, row, groups, mine, box, send, recv):
        self.row, self.groups, self.mine, self.box = row, groups, mine, box
        self.send, self.recv = send, recv

    def copies(self, m):
        for k in range(1, self.groups):
            yield pltpu.make_async_remote_copy(
                src_ref=self.mine.at[m],
                dst_ref=self.box.at[m, k],
                send_sem=self.send.at[m, k],
                recv_sem=self.recv.at[m, k],
                device_id=(self.row.s, self.row.r, lax.rem(self.row.c + k, self.groups)),
                device_id_type=MESH,
            )

    def start(self, m):
        for copy in self.copies(m):
            self.row.go(copy)

    def wait(self, m):
        for copy in self.copies(m):
            copy.wait_recv()

    def fold(self, m, through, entering, backward):
        entering[...] = jnp.zeros_like(entering)
        for k in range(self.groups - 1, 0, -1):
            if backward:

                @pl.when(self.row.c + k < self.groups)
                def _(k=k):
                    factor = through[m, lax.rem(self.row.c + k, self.groups)]
                    entering[...] = factor * entering[...] + self.box[
                        m, self.groups - k
                    ].astype(F32)
            else:

                @pl.when(self.row.c >= k)
                def _(k=k):
                    factor = through[m, lax.rem(self.row.c - k + self.groups, self.groups)]
                    entering[...] = factor * entering[...] + self.box[m, k].astype(F32)


def attn_forward_kernel(
    micros, rows, own, groups, x, gain, pk, pv, gate, keep, through, wqkv_h, wo_h,
    in_o, qkv_o, state_o, mixed_o, mid_o,
    full, wqkv, wo, qkv, state, mixed, update, entering, leaving, box,
    ssend, srecv, part, pair, both, transit, final, send, recv, sems,
):
    width, size = x.shape[2], pk.shape[1]
    blocks = rows // BLOCK
    factor = size ** (-0.5)
    row = Rows(rows, own, width, send, recv)
    row.buffers = (part, pair, both, transit, final)
    loc = Local(sems)
    loads = [loc.start(wqkv_h, wqkv), loc.start(wo_h, wo)]
    scale = gain[...]
    for m in range(micros):
        norm_to(full, scale, x[m].astype(F32), row.span(m, row.s, row.r))
    row.greet(col_peers(row, groups))
    states = States(row, groups, leaving, box, ssend, srecv)
    qs, ks, vs = (pl.ds(i * size, size) for i in range(3))
    mask = pair_masks(2 * BLOCK)

    row.ag_start(full, 0)
    row.ag_start(full, 1)
    row.ag_pass(full, 0)
    for m in range(2, micros):
        row.ag_start(full, m)
    row.ag_pass(full, 1)
    row.ag_diag(full, 0)
    for copy in loads:
        loc.wait(copy)
    for m in range(micros):
        row.ag_wait(full, m)
        here = pl.ds(m * rows, rows)
        loc.start(full.at[here, :], in_o.at[here, :])
        qkv[here, :] = dot(full[here, :], wqkv[...]).astype(BF16)
        loc.start(qkv.at[here, :], qkv_o.at[here, :])
        total = jnp.zeros((size, size), F32)
        for b in range(blocks):
            at = pl.ds(m * rows + b * BLOCK, BLOCK)
            keys = (qkv[at, ks].astype(F32) * gate[at, :]).astype(BF16)
            fresh = dot(keys, qkv[at, vs], 0, 0)
            update[m * blocks + b] = fresh
            total = keep[m, b] * total + fresh
        leaving[m] = total.astype(BF16)
        states.start(m)
        if m + 2 < micros:
            row.ag_pass(full, m + 2)
        if m + 1 < micros:
            row.ag_diag(full, m + 1)

    def compute(m):
        here = pl.ds(m * rows, rows)
        states.wait(m)
        states.fold(m, through, entering, False)
        memory = entering[...]
        for b in range(0, blocks, 2):
            at = pl.ds(m * rows + b * BLOCK, 2 * BLOCK)
            q, k, v = qkv[at, qs], qkv[at, ks], qkv[at, vs]
            inner, outer = pair_probs(q, k, pk[...], mask, factor)
            value = dot(inner.astype(BF16), v) + dot(outer.astype(BF16), pv[...])
            reads = []
            for i in range(2):
                now = keep[m, b + i] * memory
                low = now.astype(BF16)
                state[m * blocks + b + i] = low
                reads.append(dot(q[i * BLOCK : (i + 1) * BLOCK, :], low) * factor)
                memory = now + update[m * blocks + b + i]
            mixed[at, :] = (value + jnp.concatenate(reads, axis=0)).astype(BF16)
        part[here, :] = dot(mixed[here, :], wo[...]).astype(BF16)
        loc.start(mixed.at[here, :], mixed_o.at[here, :])

    def result(m):
        mid_o[m] = x[m].astype(F32) + row.rs_result(m)

    for m in range(micros):
        compute(m)
        row.rs_start(m)
        if m >= 1:
            row.rs_pair(m - 1)
        if m >= 2:
            row.rs_transit(m - 2)
    loc.start(state, state_o)
    tail(row, micros, result)
    row.finish()
    loc.finish()


def attn_backward_kernel(
    micros, rows, own, groups, dmid, x, gain, pk, pv, gate, keep, through, wqkv_h, wo_h,
    in_h, qkv_h, state_h, mixed_h,
    dx_o, dgain_o, dpk_o, dpv_o, gqkv_o, go_o,
    full, wqkv, wo, xin, qkv, state, mixed, dmix, dqkv, update, entering, leaving, box, gqkv, go,
    ssend, srecv, part, pair, both, transit, final, send, recv, sems,
):
    width, size = x.shape[2], pk.shape[1]
    blocks = rows // BLOCK
    factor = size ** (-0.5)
    row = Rows(rows, own, width, send, recv)
    row.buffers = (part, pair, both, transit, final)
    loc = Local(sems)
    first = [loc.start(wo_h, wo), loc.start(qkv_h, qkv)]
    second = [loc.start(state_h, state), loc.start(wqkv_h, wqkv)]
    third = [loc.start(mixed_h, mixed), loc.start(in_h, xin)]
    for m in range(micros):
        full[row.span(m, row.s, row.r), :] = dmid[m].astype(BF16)
    row.greet(col_peers(row, groups))
    states = States(row, groups, leaving, box, ssend, srecv)
    qs, ks, vs = (pl.ds(i * size, size) for i in range(3))
    mask = pair_masks(2 * BLOCK)
    scale = gain[...]
    dgain_o[...] = jnp.zeros_like(dgain_o)
    dpk_o[...] = jnp.zeros_like(dpk_o)
    dpv_o[...] = jnp.zeros_like(dpv_o)

    row.ag_start(full, 0)
    row.ag_start(full, 1)
    row.ag_pass(full, 0)
    for m in range(2, micros):
        row.ag_start(full, m)
    row.ag_pass(full, 1)
    row.ag_diag(full, 0)
    for copy in first:
        loc.wait(copy)
    for m in range(micros):
        row.ag_wait(full, m)
        here = pl.ds(m * rows, rows)
        dmix[here, :] = dot(full[here, :], wo[...], 1, 1).astype(BF16)
        total = jnp.zeros((size, size), F32)
        for b in reversed(range(blocks)):
            at = pl.ds(m * rows + b * BLOCK, BLOCK)
            fresh = dot(qkv[at, qs], dmix[at, :], 0, 0) * factor
            update[m * blocks + b] = fresh
            total = keep[m, b] * (fresh + total)
        leaving[m] = total.astype(BF16)
        states.start(m)
        if m + 2 < micros:
            row.ag_pass(full, m + 2)
        if m + 1 < micros:
            row.ag_diag(full, m + 1)
    for copy in second:
        loc.wait(copy)

    def compute(m):
        here = pl.ds(m * rows, rows)
        states.wait(m)
        states.fold(m, through, entering, True)
        memory = entering[...]
        for b in reversed(range(0, blocks, 2)):
            at = pl.ds(m * rows + b * BLOCK, 2 * BLOCK)
            q, k, v, d = qkv[at, qs], qkv[at, ks], qkv[at, vs], dmix[at, :]
            inner, outer = pair_probs(q, k, pk[...], mask, factor)
            d_inner = dot(d, v, 1, 1)
            d_outer = dot(d, pv[...], 1, 1)
            centre = jnp.sum(inner * d_inner, axis=1, keepdims=True) + jnp.sum(
                outer * d_outer, axis=1, keepdims=True
            )
            d_inner = (inner * (d_inner - centre)).astype(BF16)
            d_outer = (outer * (d_outer - centre)).astype(BF16)
            inner, outer = inner.astype(BF16), outer.astype(BF16)
            dpk_o[...] += dot(d_outer, q, 0, 0) * factor
            dpv_o[...] += dot(outer, d, 0, 0)
            dq = dot(d_inner, k) + dot(d_outer, pk[...])
            dk = dot(d_inner, q, 0, 0) * factor
            dv = dot(inner, d, 0, 0)
            keys = (k.astype(F32) * gate[at, :]).astype(BF16)
            parts = [None, None]
            for i in (1, 0):
                sub = slice(i * BLOCK, (i + 1) * BLOCK)
                low = memory.astype(BF16)
                parts[i] = (
                    dot(d[sub, :], state[m * blocks + b + i], 1, 1),
                    dot(v[sub, :], low, 1, 1),
                    dot(keys[sub, :], low),
                )
                memory = keep[m, b + i] * (update[m * blocks + b + i] + memory)
            more_q, more_k, more_v = (jnp.concatenate(pieces, axis=0) for pieces in zip(*parts))
            dqkv[at, qs] = ((dq + more_q) * factor).astype(BF16)
            dqkv[at, ks] = (dk + gate[at, :] * more_k).astype(BF16)
            dqkv[at, vs] = (dv + more_v).astype(BF16)
        part[here, :] = dot(dqkv[here, :], wqkv[...], 1, 1).astype(BF16)

    def result(m):
        back, gains = norm_back(x[m].astype(F32), scale, row.rs_result(m))
        dx_o[m] = (dmid[m] + back).astype(BF16)
        dgain_o[...] += gains

    for m in range(micros):
        compute(m)
        row.rs_start(m)
        if m >= 1:
            row.rs_pair(m - 1)
        if m >= 2:
            row.rs_transit(m - 2)

    def out_grad():
        for copy in third:
            loc.wait(copy)
        tiles(width, lambda at: store(go, at, dot(mixed[...], full[:, at], 0, 0), True))
        loc.start(go, go_o)

    def qkv_grad():
        tiles(width, lambda at: store(gqkv, at, dot(xin[:, at], dqkv[...], 0, 0), False))
        loc.start(gqkv, gqkv_o)

    tail(row, micros, result, [out_grad, qkv_grad])
    row.finish()
    loc.finish()


def others():
    s, r, c = (lax.axis_index(a) for a in ("section", "row", "col"))
    for k in range(1, 8):
        ps = lax.rem(s + k // 4, 2)
        low = r + (k % 2) * (1 - 2 * lax.rem(r, 2))
        pr = lax.rem(low + 2 * ((k // 2) % 2), 4)
        yield k, (ps, pr, c)


def deal_kernel(own, features, x, o, send, recv, local):
    s, r = lax.axis_index("section"), lax.axis_index("row")
    barrier = pltpu.get_barrier_semaphore()
    for _, peer in others():
        pl.semaphore_signal(barrier, inc=1, device_id=peer, device_id_type=MESH)
    pl.semaphore_wait(barrier, 7)
    mine = pl.ds(pl.multiple_of(r * features, 128), features)

    def rows_of(ps, pr):
        return pl.ds(pl.multiple_of((ps * 4 + pr) * own, 16), own)

    keep = pltpu.make_async_copy(x.at[:, rows_of(s, r), :], o.at[s, :, :, mine], local)
    keep.start()
    copies = []
    for k, peer in others():
        copy = pltpu.make_async_remote_copy(
            src_ref=x.at[:, rows_of(peer[0], peer[1]), :],
            dst_ref=o.at[s, :, :, mine],
            send_sem=send.at[k],
            recv_sem=recv.at[k],
            device_id=peer,
            device_id_type=MESH,
        )
        copy.start()
        copies.append(copy)
    for copy in copies:
        copy.wait()
    keep.wait()


def undeal_kernel(own, features, y, o, send, recv, local):
    s, r = lax.axis_index("section"), lax.axis_index("row")
    barrier = pltpu.get_barrier_semaphore()
    for _, peer in others():
        pl.semaphore_signal(barrier, inc=1, device_id=peer, device_id_type=MESH)
    pl.semaphore_wait(barrier, 7)
    mine = pl.ds(pl.multiple_of((s * 4 + r) * own, 16), own)

    def columns(pr):
        return pl.ds(pl.multiple_of(pr * features, 128), features)

    keep = pltpu.make_async_copy(y.at[s, :, :, columns(r)], o.at[:, mine, :], local)
    keep.start()
    copies = []
    for k, peer in others():
        copy = pltpu.make_async_remote_copy(
            src_ref=y.at[peer[0], :, :, columns(peer[1])],
            dst_ref=o.at[:, mine, :],
            send_sem=send.at[k],
            recv_sem=recv.at[k],
            device_id=peer,
            device_id_type=MESH,
        )
        copy.start()
        copies.append(copy)
    for copy in copies:
        copy.wait()
    keep.wait()


def shape(dims, dtype):
    return jax.ShapeDtypeStruct(dims, dtype)


VM = pl.BlockSpec(memory_space=pltpu.VMEM)
SM = pl.BlockSpec(memory_space=pltpu.SMEM)
HB = pl.BlockSpec(memory_space=pl.ANY)


def params(collective):
    return pltpu.CompilerParams(
        collective_id=collective, has_side_effects=True, vmem_limit_bytes=VMEM_LIMIT
    )


def local(
    tokens, cotangent, block_order, lengths, decay, write_gate, gain_attn, w_query, w_key, w_value,
    persist_key, persist_value, w_output, gain_ffn, w_gate, w_up, w_down,
):
    sec, row_id, col = (lax.axis_index(a) for a in ("section", "row", "col"))
    groups = lax.axis_size("col")
    micros, rows, features = tokens.shape
    width = features * lax.axis_size("row")
    own = rows // 8
    blocks = rows // BLOCK
    all_rows = micros * rows
    size = features // 2
    ffh = w_gate.shape[2] // 2
    persist = persist_key.shape[1] * groups

    total_blocks = block_order.shape[1]
    my_blocks = col * blocks + jnp.arange(blocks, dtype=jnp.int32)
    deal_picks = lax.dynamic_slice_in_dim(block_order, col * blocks, blocks, 1)
    matches = (block_order[:, :, None] == my_blocks[None, None, :]).astype(jnp.int32)
    positions = jnp.arange(total_blocks, dtype=jnp.int32)
    back_picks = jnp.sum(matches * positions[None, :, None], axis=1)

    def pick(shard, picks):
        whole = lax.all_gather(shard, "col", axis=1, tiled=True)
        parts = whole.reshape(micros, total_blocks, BLOCK, features)
        chosen = jnp.take_along_axis(parts, picks[:, :, None, None], axis=1)
        return chosen.reshape(micros, rows, features)

    exchange_scratch = [
        pltpu.SemaphoreType.DMA((8,)),
        pltpu.SemaphoreType.DMA((8,)),
        pltpu.SemaphoreType.DMA(()),
    ]
    dealt = pick(jnp.where(sec == 0, tokens, cotangent), deal_picks)
    inputs = pl.pallas_call(
        functools.partial(deal_kernel, own, features),
        out_shape=shape((2, micros, own, width), BF16),
        in_specs=[VM],
        out_specs=VM,
        scratch_shapes=exchange_scratch,
        compiler_params=params(0),
        name="deal",
    )(dealt)

    smalls = (gain_attn[0], gain_ffn[0], persist_key[0], persist_value[0], decay[0], write_gate[0])
    packed = jnp.concatenate([a.astype(F32).reshape(-1) for a in smalls])
    spread = lax.all_gather(packed, ("section", "row", "col"))
    spread = spread.reshape(2, 4, groups, -1)
    offsets, at = [], 0
    for a in smalls:
        offsets.append((at, at + a.size))
        at += a.size
    gains_a = spread[..., offsets[0][0] : offsets[0][1]].reshape(2, 1, width)
    gains_f = spread[..., offsets[1][0] : offsets[1][1]].reshape(2, 1, width)
    line = lax.dynamic_index_in_dim(spread, row_id, 1, False)

    def head(a):
        return lax.dynamic_slice_in_dim(a, sec * (a.shape[-1] // 2), a.shape[-1] // 2, a.ndim - 1)

    def section_of(i, dims):
        return line[..., offsets[i][0] : offsets[i][1]].reshape((2, groups) + dims)

    pks = head(section_of(2, persist_key.shape[1:])).reshape(2, persist, size).astype(BF16)
    pvs = head(section_of(3, persist_value.shape[1:])).reshape(2, persist, size).astype(BF16)
    decays = head(section_of(4, decay.shape[1:]))[..., 0]
    gates = head(section_of(5, write_gate.shape[1:]))
    gates = lax.dynamic_index_in_dim(gates, col, 1, False).reshape(2, all_rows, 1) / BLOCK
    ends = jnp.cumsum(lengths, axis=1)
    is_start = jnp.any(positions[None, :, None] == (ends - lengths)[:, None, :], axis=2)
    is_start = is_start.reshape(micros, groups, blocks).transpose(1, 0, 2)
    keeps = jnp.where(is_start[None], 0.0, decays)
    through = jnp.prod(keeps, axis=3).transpose(0, 2, 1)
    keep = lax.dynamic_index_in_dim(keeps, col, 1, False)

    def halves(w, axis):
        half = w.shape[axis] // 2
        mine = lax.dynamic_slice_in_dim(w, sec * half, half, axis)
        theirs = lax.dynamic_slice_in_dim(w, (1 - sec) * half, half, axis)
        return mine, theirs

    pairs = [halves(w[0], 1) for w in (w_query, w_key, w_value)]
    stacks = [tuple(jnp.concatenate(side, axis=1) for side in zip(*pairs))]
    stacks += [halves(w_output[0], 0), halves(w_gate[0], 1), halves(w_up[0], 1)]
    stacks += [halves(w_down[0], 0)]
    swap = [(0, 1), (1, 0)]

    def layers_of(mine, theirs):
        got = lax.ppermute(theirs, "section", swap)
        return jnp.where(sec == 0, mine, got), jnp.where(sec == 0, got, mine)

    sides = [layers_of(mine, theirs) for mine, theirs in stacks]
    axes = (0, 1, 0, 0, 1)
    weights = [
        [lax.all_gather(pair[l], "col", axis=a, tiled=True) for pair, a in zip(sides, axes)]
        for l in range(2)
    ]

    row_bufs = row_scratch(micros, rows, own, width)
    full_buf = pltpu.VMEM((all_rows, width), BF16)

    def vm(dims, dtype=BF16):
        return pltpu.VMEM(dims, dtype)

    state_bufs = [
        vm((micros * blocks, size, size), F32),
        vm((size, size), F32),
        vm((micros, size, size)),
        vm((micros, groups, size, size)),
    ]
    state_sems = [pltpu.SemaphoreType.DMA((micros, groups))] * 2

    def attn_forward(x, l):
        wqkv, wo = weights[l][:2]
        return pl.pallas_call(
            functools.partial(attn_forward_kernel, micros, rows, own, groups),
            out_shape=(
                shape((all_rows, width), BF16),
                shape((all_rows, 3 * size), BF16),
                shape((micros * blocks, size, size), BF16),
                shape((all_rows, size), BF16),
                shape((micros, own, width), F32),
            ),
            in_specs=[VM, VM, VM, VM, VM, SM, SM, HB, HB],
            out_specs=(HB, HB, HB, HB, VM),
            scratch_shapes=[
                full_buf, vm((width, 3 * size)), vm((size, width)), vm((all_rows, 3 * size)),
                vm((micros * blocks, size, size)), vm((all_rows, size)), *state_bufs,
                *state_sems, *row_bufs, pltpu.SemaphoreType.DMA((16,)),
            ],
            compiler_params=params(1),
            name="attn_forward",
        )(x, gains_a[l], pks[l], pvs[l], gates[l], keep[l], through[l], wqkv, wo)

    def ffn_forward(mid, l):
        wg, wu, wd = weights[l][2:]
        return pl.pallas_call(
            functools.partial(ffn_forward_kernel, micros, rows, own),
            out_shape=(
                shape((all_rows, width), BF16),
                shape((all_rows, ffh), BF16),
                shape((all_rows, ffh), BF16),
                shape((all_rows, ffh), BF16),
                shape((micros, own, width), BF16),
            ),
            in_specs=[VM, VM, HB, HB, HB],
            out_specs=(HB, HB, HB, HB, VM),
            scratch_shapes=[
                full_buf, vm((width, ffh)), vm((width, ffh)), vm((ffh, width)),
                vm((all_rows, ffh)), vm((all_rows, ffh)), vm((all_rows, ffh)),
                *row_bufs, pltpu.SemaphoreType.DMA((16,)),
            ],
            compiler_params=params(2),
            name="ffn_forward",
        )(mid, gains_f[l], wg, wu, wd)

    def ffn_backward(dy, mid, kept, l):
        wg, wu, wd = weights[l][2:]
        return pl.pallas_call(
            functools.partial(ffn_backward_kernel, micros, rows, own),
            out_shape=(
                shape((micros, own, width), F32),
                shape((1, width), F32),
                shape((width, ffh), BF16),
                shape((width, ffh), BF16),
                shape((ffh, width), BF16),
            ),
            in_specs=[VM, VM, VM] + [HB] * 7,
            out_specs=(VM, VM, HB, HB, HB),
            scratch_shapes=[
                full_buf, vm((width, ffh)), vm((width, ffh)), vm((ffh, width)),
                full_buf, *[vm((all_rows, ffh))] * 5,
                vm((width, ffh)), vm((width, ffh)), vm((ffh, width)),
                *row_bufs, pltpu.SemaphoreType.DMA((16,)),
            ],
            compiler_params=params(3),
            name="ffn_backward",
        )(dy, mid, gains_f[l], wg, wu, wd, *kept)

    def attn_backward(dmid, x, kept, l):
        wqkv, wo = weights[l][:2]
        return pl.pallas_call(
            functools.partial(attn_backward_kernel, micros, rows, own, groups),
            out_shape=(
                shape((micros, own, width), BF16),
                shape((1, width), F32),
                shape((persist, size), F32),
                shape((persist, size), F32),
                shape((width, 3 * size), BF16),
                shape((size, width), BF16),
            ),
            in_specs=[VM] * 6 + [SM, SM] + [HB] * 6,
            out_specs=(VM, VM, VM, VM, HB, HB),
            scratch_shapes=[
                full_buf, vm((width, 3 * size)), vm((size, width)), full_buf,
                vm((all_rows, 3 * size)), vm((micros * blocks, size, size)), vm((all_rows, size)),
                vm((all_rows, size)), vm((all_rows, 3 * size)), *state_bufs,
                vm((width, 3 * size)), vm((size, width)),
                *state_sems, *row_bufs, pltpu.SemaphoreType.DMA((16,)),
            ],
            compiler_params=params(4),
            name="attn_backward",
        )(dmid, x, gains_a[l], pks[l], pvs[l], gates[l], keep[l], through[l], wqkv, wo, *kept)

    def restore(pair):
        spread_out = pl.pallas_call(
            functools.partial(undeal_kernel, own, features),
            out_shape=shape((micros, rows, features), BF16),
            in_specs=[VM],
            out_specs=VM,
            scratch_shapes=exchange_scratch,
            compiler_params=params(5),
            name="undeal",
        )(jnp.stack(pair))
        return pick(spread_out, back_picks)

    layer_in = inputs[0]
    kept = []
    outs = []
    for l in range(2):
        *attn_kept, mid = attn_forward(layer_in, l)
        *ffn_kept, layer_out = ffn_forward(mid, l)
        kept.append((layer_in, attn_kept, mid, ffn_kept))
        outs.append(layer_out)
        layer_in = layer_out
    activations = restore(outs)

    upstream = inputs[1]
    input_grads = [None, None]
    gains = [None, None]
    persists = [None, None]
    sums = [None, None]
    for l in (1, 0):
        layer_in, attn_kept, mid, ffn_kept = kept[l]
        dmid, dgain_f, gg, gu, gd = ffn_backward(upstream, mid, ffn_kept, l)
        upstream, dgain_a, dpk, dpv, gqkv, go = attn_backward(dmid, layer_in, attn_kept, l)
        input_grads[l] = upstream
        gains[l] = jnp.concatenate([dgain_a, dgain_f], axis=0)
        persists[l] = jnp.stack([dpk, dpv])
        sums[l] = [
            lax.psum_scatter(g, "col", scatter_dimension=a, tiled=True)
            for g, a in zip((gqkv, go, gg, gu, gd), axes)
        ]
    restored = restore(input_grads)

    def join(first, second, axis):
        mine = jnp.where(sec == 0, first, second)
        got = lax.ppermute(jnp.where(sec == 0, second, first), "section", swap)
        low = jnp.where(sec == 0, mine, got)
        high = jnp.where(sec == 0, got, mine)
        return jnp.concatenate([low, high], axis=axis).astype(F32)[None]

    heads = [
        join(sums[0][0][:, i * size : (i + 1) * size], sums[1][0][:, i * size : (i + 1) * size], 1)
        for i in range(3)
    ]
    grad_out = join(sums[0][1], sums[1][1], 0)
    grad_gate = join(sums[0][2], sums[1][2], 1)
    grad_up = join(sums[0][3], sums[1][3], 1)
    grad_down = join(sums[0][4], sums[1][4], 0)
    gain_sum = lax.psum(jnp.stack(gains), ("section", "row", "col"))
    share = width // (4 * groups)
    my_gain = lax.dynamic_slice_in_dim(
        lax.dynamic_index_in_dim(gain_sum, sec, 0, False), (row_id * groups + col) * share, share, 1
    )
    persist_sum = lax.psum(jnp.stack(persists), "col")
    each = persist // groups
    persist_sum = lax.dynamic_slice_in_dim(persist_sum, col * each, each, 2)
    grad_persist = join(persist_sum[0], persist_sum[1], 2)[0]
    return (
        activations[None],
        restored[None],
        my_gain[0][None],
        heads[0],
        heads[1],
        heads[2],
        grad_persist[0][None],
        grad_persist[1][None],
        grad_out,
        my_gain[1][None],
        grad_gate,
        grad_up,
        grad_down,
    )


def solution(mesh):
    weight = P("section", "col", "row")
    across = P("section", "row", "col")
    gain = P("section", ("row", "col"))
    rows = P("section", None, "col", "row")
    return jax.shard_map(
        local,
        mesh=mesh,
        in_specs=(
            P(None, "col", "row"), P(None, "col", "row"), P(), P(), rows, rows, gain, weight, weight,
            weight, weight, weight, across, gain, weight, weight, across,
        ),
        out_specs=(
            rows, rows, gain, weight, weight, weight, weight, weight, across, gain, weight, weight,
            across,
        ),
        check_vma=False,
    )
```

```python
from types import SimpleNamespace

import jax
import jax.numpy as jnp
from jax import lax
from jax.experimental import pallas as pl
from jax.experimental.pallas import tpu as pltpu
from jax.sharding import PartitionSpec as P

BLOCK = 64
EPS = 1e-06
MESH = pl.DeviceIdType.MESH
F32 = jnp.float32
BF16 = jnp.bfloat16
VMEM_LIMIT = 56 << 20
N_AG, N_RS = 8, 7


def dot(a, b, ca=1, cb=0):
    return lax.dot_general(a, b, (((ca,), (cb,)), ((), ())), preferred_element_type=F32)


class Rows:
    def __init__(self, rows, own, width, send, recv):
        self.rows, self.own, self.width, self.half = rows, own, width, width // 2
        self.send, self.recv = send, recv
        self.s, self.r, self.c = (lax.axis_index(a) for a in ("section", "row", "col"))
        self.rx = self.r + 1 - 2 * lax.rem(self.r, 2)
        self.ry = lax.rem(self.r + 2, 4)
        self.rd = lax.rem(self.rx + 2, 4)
        self.x = (self.s, self.rx, self.c)
        self.y = (self.s, self.ry, self.c)
        self.sib = (1 - self.s, self.r, self.c)
        self.started = []

    def greet(self, others=()):
        barrier = pltpu.get_barrier_semaphore()
        peers = [self.x, self.y, self.sib] + list(others)
        for peer in peers:
            pl.semaphore_signal(barrier, inc=1, device_id=peer, device_id_type=MESH)
        pl.semaphore_wait(barrier, len(peers))

    def copy(self, src, dst, m, k, peer):
        return pltpu.make_async_remote_copy(
            src_ref=src,
            dst_ref=dst,
            send_sem=self.send.at[m, k],
            recv_sem=self.recv.at[m, k],
            device_id=peer,
            device_id_type=MESH,
        )

    def go(self, copy):
        copy.start()
        self.started.append(copy)

    def finish(self):
        for copy in self.started:
            copy.wait_send()

    def span(self, m, s, r):
        return pl.ds(pl.multiple_of(m * self.rows + (s * 4 + r) * self.own, 16), self.own)

    def ag_copy(self, full, m, k):
        left, right = pl.ds(0, self.half), pl.ds(self.half, self.half)
        mine, atx, aty, atd = (
            self.span(m, self.s, r) for r in (self.r, self.rx, self.ry, self.rd)
        )
        if k == 0:
            return self.copy(full.at[mine, :], full.at[mine, :], m, 0, self.x)
        if k == 1:
            return self.copy(full.at[mine, :], full.at[mine, :], m, 1, self.y)
        if k == 2:
            return self.copy(full.at[mine, :], full.at[mine, :], m, 2, self.sib)
        if k == 3:
            return self.copy(full.at[atx, left], full.at[atx, left], m, 3, self.y)
        if k == 4:
            return self.copy(full.at[aty, right], full.at[aty, right], m, 4, self.x)
        if k == 5:
            return self.copy(full.at[atx, :], full.at[atx, :], m, 5, self.sib)
        if k == 6:
            return self.copy(full.at[aty, :], full.at[aty, :], m, 6, self.sib)
        return self.copy(full.at[atd, :], full.at[atd, :], m, 7, self.sib)

    def ag_start(self, full, m):
        for k in (0, 1, 2):
            self.go(self.ag_copy(full, m, k))

    def ag_pass(self, full, m):
        self.ag_copy(full, m, 0).wait_recv()
        self.go(self.ag_copy(full, m, 3))
        self.go(self.ag_copy(full, m, 5))
        self.ag_copy(full, m, 1).wait_recv()
        self.go(self.ag_copy(full, m, 4))
        self.go(self.ag_copy(full, m, 6))

    def ag_diag(self, full, m):
        self.ag_copy(full, m, 3).wait_recv()
        self.ag_copy(full, m, 4).wait_recv()
        self.go(self.ag_copy(full, m, 7))

    def ag_wait(self, full, m):
        for k in (2, 5, 6, 7):
            self.ag_copy(full, m, k).wait_recv()

    def rs_copy(self, m, k):
        part, pair, both, transit, final = self.buffers
        left, right = pl.ds(0, self.half), pl.ds(self.half, self.half)
        if k == 8:
            other = pl.ds(
                pl.multiple_of(m * self.rows + (1 - self.s) * 4 * self.own, 16), 4 * self.own
            )
            return self.copy(part.at[other, :], pair.at[m], m, 8, self.sib)
        if k == 9:
            return self.copy(both.at[m, self.rd, :, left], transit.at[m, 0], m, 9, self.x)
        if k == 10:
            return self.copy(both.at[m, self.rd, :, right], transit.at[m, 1], m, 10, self.y)
        if k == 11:
            return self.copy(both.at[m, self.rx, :, left], final.at[m, 0, :, left], m, 11, self.x)
        if k == 12:
            return self.copy(both.at[m, self.ry, :, right], final.at[m, 1, :, right], m, 12, self.y)
        if k == 13:
            return self.copy(both.at[m, self.ry, :, left], final.at[m, 1, :, left], m, 13, self.y)
        return self.copy(both.at[m, self.rx, :, right], final.at[m, 0, :, right], m, 14, self.x)

    def rs_start(self, m):
        self.go(self.rs_copy(m, 8))

    def rs_pair(self, m):
        part, pair, both, _, _ = self.buffers
        self.rs_copy(m, 8).wait_recv()
        for r in range(4):
            mine = part[self.span(m, self.s, r), :].astype(F32)
            theirs = pair[m, r * self.own : (r + 1) * self.own, :].astype(F32)
            both[m, r] = (mine + theirs).astype(BF16)
        for k in (9, 10, 11, 12):
            self.go(self.rs_copy(m, k))

    def rs_transit(self, m):
        _, _, both, transit, _ = self.buffers
        left, right = pl.ds(0, self.half), pl.ds(self.half, self.half)
        self.rs_copy(m, 9).wait_recv()
        total = both[m, self.ry, :, left].astype(F32) + transit[m, 0].astype(F32)
        both[m, self.ry, :, left] = total.astype(BF16)
        self.go(self.rs_copy(m, 13))
        self.rs_copy(m, 10).wait_recv()
        total = both[m, self.rx, :, right].astype(F32) + transit[m, 1].astype(F32)
        both[m, self.rx, :, right] = total.astype(BF16)
        self.go(self.rs_copy(m, 14))

    def rs_result(self, m):
        _, _, both, _, final = self.buffers
        for k in (11, 12, 13, 14):
            self.rs_copy(m, k).wait_recv()
        return both[m, self.r].astype(F32) + final[m, 0].astype(F32) + final[m, 1].astype(F32)


class Local:
    def __init__(self, sems):
        self.sems, self.used, self.open = sems, 0, []

    def start(self, src, dst):
        copy = pltpu.make_async_copy(src, dst, self.sems.at[self.used])
        self.used += 1
        copy.start()
        self.open.append(copy)
        return copy

    def wait(self, copy):
        copy.wait()
        self.open.remove(copy)

    def finish(self):
        for copy in list(self.open):
            copy.wait()


def inv_rms(values):
    return lax.rsqrt(jnp.mean(values * values, axis=1, keepdims=True) + EPS)


def norm_to(full, gain, values, span):
    full[span, :] = (values * inv_rms(values) * gain).astype(BF16)


def norm_back(values, gain, grad):
    scale = inv_rms(values)
    weighted = grad * gain
    inner = jnp.mean(weighted * values, axis=1, keepdims=True)
    back = scale * weighted - values * (scale * scale * scale * inner)
    return back, jnp.sum(grad * values * scale, axis=0, keepdims=True)


def wait_both(copies):
    for condition, copy in copies:

        @pl.when(condition)
        def _(copy=copy):
            copy.wait_send()


class Side:
    def __init__(self, tag):
        self.tag = tag

    def ref(self, name):
        return getattr(self.ns, self.tag + name)

    def bind(self, ns, row, groups):
        self.ns, self.row, self.c, self.groups = ns, row, row.c, groups
        self.sent = []

    def when(self, condition, copy):
        @pl.when(condition)
        def _():
            copy.start()

        self.sent.append((condition, copy))

    def arrived(self, condition, copy):
        @pl.when(condition)
        def _():
            copy.wait_recv()

    def remote(self, src, dst, send, recv, to):
        return pltpu.make_async_remote_copy(
            src_ref=src,
            dst_ref=dst,
            send_sem=send,
            recv_sem=recv,
            device_id=(self.row.s, self.row.r, to),
            device_id_type=MESH,
        )


def part_of(ref, at, per, axis):
    where = pl.ds(pl.multiple_of(at * per, per), per)
    return ref.at[(slice(None),) * axis + (where,)]


class Gather(Side):
    def __init__(self, tag, array, dims, groups, axis, view=None, home=None):
        super().__init__(tag)
        self.array, self.axis, self.view, self.home = array, axis, view, home
        self.per = dims[axis]
        self.dims = dims[:axis] + (dims[axis] * groups,) + dims[axis + 1 :]

    def declare(self, ins, outs, scratch, groups):
        if self.array is not None:
            ins[self.tag + "src"] = (self.array, HB)
        if self.home is None:
            outs[self.tag + "dst"] = (self.dims, BF16, HB)
        else:
            scratch[self.tag + "dst"] = pltpu.VMEM(self.dims, BF16)
        scratch[self.tag + "send"] = pltpu.SemaphoreType.DMA((2, groups))
        scratch[self.tag + "recv"] = pltpu.SemaphoreType.DMA((groups,))
        scratch[self.tag + "own"] = pltpu.SemaphoreType.DMA((1,))

    def slot(self, j):
        return part_of(self.ref("dst"), jnp.clip(j, 0, self.groups - 1), self.per, self.axis)

    def source(self):
        return self.view(self.ns, self.row) if self.view else self.ref("src")

    def move(self, j, side, src=None):
        to = jnp.clip(self.c + (1 - 2 * side), 0, self.groups - 1)
        j = jnp.clip(j, 0, self.groups - 1)
        src = self.slot(j) if src is None else src
        return self.remote(
            src, self.slot(j), self.ref("send").at[side, j], self.ref("recv").at[j], to
        )

    def start(self):
        c, n = self.c, self.groups
        self.at, self.done = 1, False
        self.own = pltpu.make_async_copy(self.source(), self.slot(c), self.ref("own").at[0])
        self.own.start()
        self.when(c + 1 < n, self.move(c, 0, self.source()))
        self.when(c >= 1, self.move(c, 1, self.source()))

    def step(self):
        c, n, k = self.c, self.groups, self.at
        if k < n:
            self.arrived(c >= k, self.move(c - k, 0))
            self.arrived(c + k < n, self.move(c + k, 1))
            if k < n - 1:
                self.when((c >= k) & (c + 1 < n), self.move(c - k, 0))
                self.when((c + k < n) & (c >= 1), self.move(c + k, 1))
        self.at += 1

    def finish(self):
        if not self.done:
            while self.at < self.groups:
                self.step()
            self.own.wait()
            self.done = True

    def drain(self):
        wait_both(self.sent)


class Total(Side):
    def __init__(self, tag, parts, groups, span=None, home=None):
        super().__init__(tag)
        self.parts, self.span, self.home = parts, span, home
        self.per = parts.shape[1] // groups
        self.count = span[1] if span else parts.shape[0]
        self.dims = (self.count, self.per, parts.shape[2])

    def declare(self, ins, outs, scratch, groups):
        if self.home is None:
            outs[self.tag + "sum"] = (self.dims, BF16, VM)
        else:
            scratch[self.tag + "sum"] = pltpu.VMEM(self.dims, BF16)
        ins[self.tag + "parts"] = (self.parts, HB)
        whole = (self.count, self.per * groups, self.dims[2])
        scratch[self.tag + "mine"] = pltpu.VMEM(whole, BF16)
        scratch[self.tag + "box"] = pltpu.VMEM((2, groups) + self.dims, BF16)
        scratch[self.tag + "send"] = pltpu.SemaphoreType.DMA((2, groups))
        scratch[self.tag + "recv"] = pltpu.SemaphoreType.DMA((2, groups))
        scratch[self.tag + "load"] = pltpu.SemaphoreType.DMA((1,))

    def clip(self, j):
        return jnp.clip(j, 0, self.groups - 1)

    def piece(self, ref, d, p=None):
        d = self.clip(d)
        where = pl.ds(pl.multiple_of(d * self.per, self.per), self.per)
        return ref.at[:, where, :] if p is None else ref[p, where, :]

    def source(self):
        parts = self.ref("parts")
        return parts.at[pl.ds(*self.span)] if self.span else parts

    def move(self, side, d, src):
        d = self.clip(d)
        to = self.clip(self.c + (1 - 2 * side))
        return self.remote(
            src,
            self.ref("box").at[side, d],
            self.ref("send").at[side, d],
            self.ref("recv").at[side, d],
            to,
        )

    def boxed(self, side, d):
        return self.ref("box").at[side, self.clip(d)]

    def start(self):
        c, n = self.c, self.groups
        self.at, self.done = 1, False
        self.load = pltpu.make_async_copy(self.source(), self.ref("mine"), self.ref("load").at[0])
        self.load.start()
        self.ends(0)

    def ends(self, t):
        c, n = self.c, self.groups
        self.when(c == 0, self.move(0, n - 1 - t, self.piece(self.source(), n - 1 - t)))
        self.when(c == n - 1, self.move(1, t, self.piece(self.source(), t)))

    def step(self):
        c, n, t = self.c, self.groups, self.at
        box, mine = self.ref("box"), self.ref("mine")
        if t == 1:
            self.load.wait()
        if t < n - 1:
            self.ends(t)
            for side, place, d in ((0, c, n - 1 - t + c), (1, n - 1 - c, t + c - (n - 1))):
                here = (place >= 1) & (place <= t)
                self.arrived(here, self.move(side, d, self.boxed(side, d)))

                @pl.when(here)
                def _(side=side, d=d):
                    for p in range(self.count):
                        total = self.piece(mine, d, p).astype(F32)
                        total = total + box[side, self.clip(d), p].astype(F32)
                        box[side, self.clip(d), p] = total.astype(BF16)

                self.when(here, self.move(side, d, self.boxed(side, d)))
        self.at += 1

    def finish(self):
        if self.done:
            return
        self.done = True
        c, n = self.c, self.groups
        while self.at < n - 1:
            self.step()
        box, mine = self.ref("box"), self.ref("mine")
        above, below = c >= 1, c + 1 < n
        self.arrived(above, self.move(0, c, self.boxed(0, c)))
        self.arrived(below, self.move(1, c, self.boxed(1, c)))
        for p in range(self.count):
            first = jnp.where(c >= 1, 0, 1)
            total = self.piece(mine, c, p).astype(F32) + box[first, c, p].astype(F32)
            self.ref("sum")[p] = total.astype(BF16)

            @pl.when(above & below)
            def _(p=p, total=total):
                self.ref("sum")[p] = (total + box[1, c, p].astype(F32)).astype(BF16)

    def drain(self):
        wait_both(self.sent)


def others(row):
    for k in range(1, 8):
        ps = lax.rem(row.s + k // 4, 2)
        low = row.rx if k % 2 else row.r
        pr = lax.rem(low + 2 * ((k // 2) % 2), 4)
        yield k, ps, pr


class Swap:
    def __init__(self, tag):
        self.tag = tag

    def declare(self, scratch):
        scratch[self.tag + "send"] = pltpu.SemaphoreType.DMA((8,))
        scratch[self.tag + "recv"] = pltpu.SemaphoreType.DMA((8,))
        scratch[self.tag + "own"] = pltpu.SemaphoreType.DMA((1,))

    def start(self, ns, row, own, lanes, src, dst, to_tokens):
        send, recv, local = (getattr(ns, self.tag + a) for a in ("send", "recv", "own"))

        def tokens_of(s, r):
            return pl.ds(pl.multiple_of((s * 4 + r) * own, 16), own)

        def lanes_of(s, r):
            return pl.ds(pl.multiple_of((r * 2 + s) * lanes, 128), lanes)

        def ends(ps, pr):
            if to_tokens:
                return src.at[:, tokens_of(ps, pr), :], dst.at[:, :, lanes_of(row.s, row.r)]
            return src.at[:, :, lanes_of(ps, pr)], dst.at[:, tokens_of(row.s, row.r), :]

        a, b = ends(row.s, row.r)
        self.mine = pltpu.make_async_copy(a, b, local.at[0])
        self.mine.start()
        self.copies = []
        for k, ps, pr in others(row):
            a, b = ends(ps, pr)
            copy = pltpu.make_async_remote_copy(
                src_ref=a,
                dst_ref=b,
                send_sem=send.at[k],
                recv_sem=recv.at[k],
                device_id=(ps, pr, row.c),
                device_id_type=MESH,
            )
            copy.start()
            self.copies.append(copy)

    def wait(self):
        for copy in self.copies:
            copy.wait_recv()
        self.mine.wait()

    def drain(self):
        for copy in self.copies:
            copy.wait_send()


def plane_peers(row):
    return [
        (ps, pr, row.c) for k, ps, pr in others(row) if k not in (1, 2, 4)
    ]


def schedule(row, full, micros, compute, result, hook, between=()):
    gather_first(row, full, micros)
    hook("gathering")
    for m in range(micros):
        row.ag_wait(full, m)
        hook(f"gathered{m}")
        if m >= 1:
            row.rs_pair(m - 1)
        if m >= 2:
            row.rs_transit(m - 2)
        compute(m)
        row.rs_start(m)
        if m + 2 < micros:
            row.ag_pass(full, m + 2)
        if m + 1 < micros:
            row.ag_diag(full, m + 1)
        hook(f"computed{m}")
    tail(row, micros, result, hook, between)


def gather_first(row, full, micros):
    row.ag_start(full, 0)
    if micros > 1:
        row.ag_start(full, 1)
    row.ag_pass(full, 0)
    for m in range(2, micros):
        row.ag_start(full, m)
    if micros > 1:
        row.ag_pass(full, 1)
    row.ag_diag(full, 0)


def tail(row, micros, result, hook, between=()):
    more = list(between)

    def step():
        if more:
            more.pop(0)()

    step()
    if micros > 1:
        row.rs_transit(micros - 2)
    row.rs_pair(micros - 1)
    for m in range(micros - 1):
        if m < micros - 2:
            step()
            result(m)
    step()
    row.rs_transit(micros - 1)
    hook("tail")
    if micros > 1:
        result(micros - 2)
    while more:
        step()
    hook("last")
    result(micros - 1)


def ffn_forward_kernel(k, row, loc, cfg, begin, hook, end):
    micros, rows = cfg.micros, cfg.rows
    loads = cfg.load_weights(k, loc)
    scale = gain_row(k, cfg, cfg.layer, 1)
    for m in range(micros):
        norm_to(k.full, scale, k.mid[m], row.span(m, row.s, row.r))
    begin()

    def compute(m):
        here = pl.ds(m * rows, rows)
        loc.start(k.full.at[here, :], k.xin_o.at[here, :])
        if m == 0:
            for copy in loads:
                loc.wait(copy)
        gate = dot(k.full[here, :], k.w[0])
        lift = dot(k.full[here, :], k.w[1])
        k.gp[here, :] = gate.astype(BF16)
        k.up[here, :] = lift.astype(BF16)
        k.act[here, :] = (gate * jax.nn.sigmoid(gate) * lift).astype(BF16)
        k.part[here, :] = dot(k.act[here, :], k.w[2], 1, 1).astype(BF16)
        for a, b in ((k.gp, k.gp_o), (k.up, k.up_o), (k.act, k.act_o)):
            loc.start(a.at[here, :], b.at[here, :])

    def result(m):
        k.y_o[m] = (k.mid[m] + row.rs_result(m)).astype(BF16)

    schedule(row, k.full, micros, compute, result, hook)
    end()


def ffn_backward_kernel(k, row, loc, cfg, begin, hook, end):
    micros, rows = cfg.micros, cfg.rows
    width = cfg.width
    early = cfg.load_weights(k, loc)
    early += [loc.start(a, b) for a, b in ((k.gp_h, k.gp), (k.up_h, k.up))]
    late = [loc.start(a, b) for a, b in ((k.act_h, k.act), (k.xin_h, k.xin))]
    for m in range(micros):
        k.full[row.span(m, row.s, row.r), :] = k.dy[m]
    begin()
    scale = gain_row(k, cfg, cfg.layer, 1)
    k.dgain_o[...] = jnp.zeros_like(k.dgain_o)

    def compute(m):
        if m == 0:
            for copy in early:
                loc.wait(copy)
        here = pl.ds(m * rows, rows)
        d_act = dot(k.full[here, :], k.w[2])
        gate = k.gp[here, :].astype(F32)
        lift = k.up[here, :].astype(F32)
        sig = jax.nn.sigmoid(gate)
        silu = gate * sig
        k.dg[here, :] = (d_act * lift * (sig + silu * (1.0 - sig))).astype(BF16)
        k.du[here, :] = (d_act * silu).astype(BF16)
        total = dot(k.dg[here, :], k.w[0], 1, 1) + dot(k.du[here, :], k.w[1], 1, 1)
        k.part[here, :] = total.astype(BF16)

    def result(m):
        back, gains = norm_back(k.mid[m], scale, row.rs_result(m))
        k.dmid_o[m] = k.dy[m].astype(F32) + back
        k.dgain_o[...] += gains

    def grad(i, left, right):
        def body():
            if i == 2:
                for copy in late:
                    loc.wait(copy)

            @pl.loop(0, width // 256)
            def _(t):
                at = pl.ds(pl.multiple_of(t * 256, 256), 256)
                k.grad[i, at, :] = dot(left[:, at], right[...], 0, 0).astype(BF16)

            loc.start(k.grad.at[i], k.grad_o.at[i])

        return body

    grads = [grad(2, k.full, k.act), grad(0, k.xin, k.dg), grad(1, k.xin, k.du)]
    schedule(row, k.full, micros, compute, result, hook, grads)
    end()


def pair_masks(size):
    rows_at = lax.broadcasted_iota(jnp.int32, (size, size), 0)
    cols_at = lax.broadcasted_iota(jnp.int32, (size, size), 1)
    return (rows_at >= cols_at) & (rows_at // BLOCK == cols_at // BLOCK)


def gate_columns(gates, columns):
    count, size = gates.shape
    rows_at = lax.broadcasted_iota(jnp.int32, (size, size), 0)
    cols_at = lax.broadcasted_iota(jnp.int32, (size, size), 1)
    for i in range(count):
        spread = jnp.where(rows_at == cols_at, gates[i : i + 1, :], 0.0)
        columns[i * size : (i + 1) * size, :] = jnp.sum(spread, axis=1, keepdims=True)


def gain_row(k, cfg, layer, kind):
    rows_each = cfg.width // 4 // 128
    pieces = [
        k.gains[layer, r, kind * rows_each + h : kind * rows_each + h + 1, :]
        for r in range(4)
        for h in range(rows_each)
    ]
    return jnp.concatenate(pieces, axis=1)


class Heads:
    def __init__(self, k, row, cfg, layer):
        self.k, self.row, self.cfg, self.layer = k, row, cfg, layer

    def persist(self):
        k, cfg = self.k, self.cfg
        out = []
        for kind in range(2):
            start = pl.multiple_of(8 + (2 * kind + self.row.s) * 8, 8)
            for j in range(cfg.groups):
                block = k.line[self.layer, j, pl.ds(start, 8), :]
                k.persist[j * cfg.per : (j + 1) * cfg.per, :] = block[: cfg.per, :]
            out.append(k.persist[...].astype(BF16))
        return out

    def keeps(self, j):
        decays = self.k.line[self.layer, j, 40:48, :] * self.k.starts[j]
        return jnp.where(self.row.s == 0, decays[0:1, :], decays[1:2, :])

    def own(self):
        keeps = self.keeps(self.row.c)
        blocks = self.cfg.blocks

        def of(m, b):
            return keeps[:, m * blocks + b : m * blocks + b + 1]

        return of

    def through(self, m, j):
        keeps = self.keeps(j)
        product = None
        for b in range(self.cfg.blocks):
            at = m * self.cfg.blocks + b
            one = keeps[:, at : at + 1]
            product = one if product is None else product * one
        return product


def pair_probs(q, k, pk, mask, scale):
    inner = jnp.where(mask, dot(q, k, 1, 1) * scale, -1e30)
    outer = dot(q, pk, 1, 1) * scale
    top = jnp.maximum(
        jnp.max(inner, axis=1, keepdims=True), jnp.max(outer, axis=1, keepdims=True)
    )
    inner = jnp.exp(inner - top)
    outer = jnp.exp(outer - top)
    norm = 1.0 / (jnp.sum(inner, axis=1, keepdims=True) + jnp.sum(outer, axis=1, keepdims=True))
    return inner * norm, outer * norm


class States:
    def __init__(self, row, groups, k, backward):
        self.backward, self.sent = backward, []
        self.row, self.groups, self.mine, self.box = row, groups, k.leaving, k.box
        self.send, self.recv, self.entering = k.ssend, k.srecv, k.entering

    def copy(self, m, k):
        n = self.groups
        to = self.row.c + (-k if self.backward else k)
        return pltpu.make_async_remote_copy(
            src_ref=self.mine.at[m],
            dst_ref=self.box.at[m, k],
            send_sem=self.send.at[m, k],
            recv_sem=self.recv.at[m, k],
            device_id=(self.row.s, self.row.r, jnp.clip(to, 0, n - 1)),
            device_id_type=MESH,
        )

    def after(self, k):
        c, n = self.row.c, self.groups
        return (c >= k) if self.backward else (c + k < n)

    def before(self, k):
        c, n = self.row.c, self.groups
        return (c + k < n) if self.backward else (c >= k)

    def start(self, m):
        for k in range(1, self.groups):

            @pl.when(self.after(k))
            def _(k=k):
                self.copy(m, k).start()

            self.sent.append((self.after(k), self.copy(m, k)))

    def wait(self, m):
        for k in range(1, self.groups):

            @pl.when(self.before(k))
            def _(k=k):
                self.copy(m, k).wait_recv()

    def drain(self):
        wait_both(self.sent)

    def fold(self, m, through):
        entering = self.entering
        entering[...] = jnp.zeros_like(entering)
        for k in range(self.groups - 1, 0, -1):

            @pl.when(self.before(k))
            def _(k=k):
                source = self.row.c + (k if self.backward else -k)
                factor = through(m, jnp.clip(source, 0, self.groups - 1))
                entering[...] = factor * entering[...] + self.box[m, k].astype(F32)


def attn_forward_kernel(k, row, loc, cfg, begin, hook, end):
    micros, rows, size = cfg.micros, cfg.rows, cfg.size
    blocks = rows // BLOCK
    factor = size ** (-0.5)
    load = loc.start(k.weights, k.w)
    scale = gain_row(k, cfg, cfg.layer, 0)
    for m in range(micros):
        norm_to(k.full, scale, k.x[m].astype(F32), row.span(m, row.s, row.r))
    begin()
    states = States(row, cfg.groups, k, False)
    qs, ks, vs = (pl.ds(i * size, size) for i in range(3))
    mask = pair_masks(2 * BLOCK)
    gather_first(row, k.full, micros)
    gate_columns(k.gates[cfg.layer, 0 : cfg.micros * cfg.rows // 128, :], k.gate)
    heads = Heads(k, row, cfg, cfg.layer)
    pk, pv = heads.persist()
    keep = heads.own()
    loc.wait(load)
    for m in range(micros):
        row.ag_wait(k.full, m)
        here = pl.ds(m * rows, rows)
        loc.start(k.full.at[here, :], k.xin_o.at[here, :])
        k.qkv[here, :] = dot(k.full[here, :], k.w[0]).astype(BF16)
        loc.start(k.qkv.at[here, :], k.qkv_o.at[here, :])
        total = jnp.zeros((size, size), F32)
        for b in range(blocks):
            at = pl.ds(m * rows + b * BLOCK, BLOCK)
            keys = (k.qkv[at, ks].astype(F32) * k.gate[at, :]).astype(BF16)
            fresh = dot(keys, k.qkv[at, vs], 0, 0)
            k.update[m * blocks + b] = fresh
            total = keep(m, b) * total + fresh
        k.leaving[m] = total.astype(BF16)
        states.start(m)
        if m + 2 < micros:
            row.ag_pass(k.full, m + 2)
        if m + 1 < micros:
            row.ag_diag(k.full, m + 1)
        hook(f"states{m}")

    def compute(m):
        here = pl.ds(m * rows, rows)
        states.wait(m)
        states.fold(m, heads.through)
        memory = k.entering[...]
        for b in range(0, blocks, 2):
            at = pl.ds(m * rows + b * BLOCK, 2 * BLOCK)
            q, ky, v = k.qkv[at, qs], k.qkv[at, ks], k.qkv[at, vs]
            inner, outer = pair_probs(q, ky, pk, mask, factor)
            value = dot(inner.astype(BF16), v) + dot(outer.astype(BF16), pv)
            reads = []
            for i in range(2):
                now = keep(m, b + i) * memory
                low = now.astype(BF16)
                k.state[m * blocks + b + i] = low
                reads.append(dot(q[i * BLOCK : (i + 1) * BLOCK, :], low) * factor)
                memory = now + k.update[m * blocks + b + i]
            k.mixed[at, :] = (value + jnp.concatenate(reads, axis=0)).astype(BF16)
        if m == 0:
            hook("out")
        k.part[here, :] = dot(k.mixed[here, :], k.wo_dst[0], 1, 1).astype(BF16)
        loc.start(k.mixed.at[here, :], k.mixed_o.at[here, :])

    def result(m):
        k.mid_o[m] = k.x[m].astype(F32) + row.rs_result(m)
        if m == 0:
            loc.start(k.wo_dst, k.wo_o)

    for m in range(micros):
        compute(m)
        row.rs_start(m)
        if m >= 1:
            row.rs_pair(m - 1)
        if m >= 2:
            row.rs_transit(m - 2)
        hook(f"computed{m}")
    loc.start(k.state, k.state_o)
    tail(row, micros, result, hook)
    states.drain()
    end()


def attn_backward_kernel(k, row, loc, cfg, begin, hook, end):
    micros, rows, size, width = cfg.micros, cfg.rows, cfg.size, cfg.width
    blocks = rows // BLOCK
    factor = size ** (-0.5)
    first = [loc.start(k.weights, k.w), loc.start(k.wo_h, k.wo), loc.start(k.qkv_h, k.qkv)]
    second = [loc.start(k.state_h, k.state)]
    third = [loc.start(k.mixed_h, k.mixed), loc.start(k.xin_h, k.xin)]
    for m in range(micros):
        k.full[row.span(m, row.s, row.r), :] = k.dmid[m].astype(BF16)
    begin()
    states = States(row, cfg.groups, k, True)
    qs, ks, vs = (pl.ds(i * size, size) for i in range(3))
    in_cols, out_cols = pl.ds(0, 3 * size), pl.ds(3 * size, size)
    mask = pair_masks(2 * BLOCK)
    scale = gain_row(k, cfg, cfg.layer, 0)
    k.dgain_o[...] = jnp.zeros_like(k.dgain_o)
    k.dpersist_o[...] = jnp.zeros_like(k.dpersist_o)
    gather_first(row, k.full, micros)
    gate_columns(k.gates[cfg.layer, 0 : cfg.micros * cfg.rows // 128, :], k.gate)
    heads = Heads(k, row, cfg, cfg.layer)
    pk, pv = heads.persist()
    keep = heads.own()
    for copy in first:
        loc.wait(copy)
    for m in range(micros):
        row.ag_wait(k.full, m)
        here = pl.ds(m * rows, rows)
        k.dmix[here, :] = dot(k.full[here, :], k.wo[0]).astype(BF16)
        total = jnp.zeros((size, size), F32)
        for b in reversed(range(blocks)):
            at = pl.ds(m * rows + b * BLOCK, BLOCK)
            fresh = dot(k.qkv[at, qs], k.dmix[at, :], 0, 0) * factor
            k.update[m * blocks + b] = fresh
            total = keep(m, b) * (fresh + total)
        k.leaving[m] = total.astype(BF16)
        states.start(m)
        if m + 2 < micros:
            row.ag_pass(k.full, m + 2)
        if m + 1 < micros:
            row.ag_diag(k.full, m + 1)
        hook(f"states{m}")
    for copy in second:
        loc.wait(copy)

    def compute(m):
        here = pl.ds(m * rows, rows)
        states.wait(m)
        states.fold(m, heads.through)
        memory = k.entering[...]
        for b in reversed(range(0, blocks, 2)):
            at = pl.ds(m * rows + b * BLOCK, 2 * BLOCK)
            q, ky, v, d = k.qkv[at, qs], k.qkv[at, ks], k.qkv[at, vs], k.dmix[at, :]
            inner, outer = pair_probs(q, ky, pk, mask, factor)
            d_inner = dot(d, v, 1, 1)
            d_outer = dot(d, pv, 1, 1)
            centre = jnp.sum(inner * d_inner, axis=1, keepdims=True) + jnp.sum(
                outer * d_outer, axis=1, keepdims=True
            )
            d_inner = (inner * (d_inner - centre)).astype(BF16)
            d_outer = (outer * (d_outer - centre)).astype(BF16)
            inner, outer = inner.astype(BF16), outer.astype(BF16)
            k.dpersist_o[0] += dot(d_outer, q, 0, 0) * factor
            k.dpersist_o[1] += dot(outer, d, 0, 0)
            dq = dot(d_inner, ky) + dot(d_outer, pk)
            dk = dot(d_inner, q, 0, 0) * factor
            dv = dot(inner, d, 0, 0)
            keys = (ky.astype(F32) * k.gate[at, :]).astype(BF16)
            parts = [None, None]
            for i in (1, 0):
                sub = slice(i * BLOCK, (i + 1) * BLOCK)
                low = memory.astype(BF16)
                parts[i] = (
                    dot(d[sub, :], k.state[m * blocks + b + i], 1, 1),
                    dot(v[sub, :], low, 1, 1),
                    dot(keys[sub, :], low),
                )
                memory = keep(m, b + i) * (k.update[m * blocks + b + i] + memory)
            more_q, more_k, more_v = (jnp.concatenate(pieces, axis=0) for pieces in zip(*parts))
            k.dqkv[at, qs] = ((dq + more_q) * factor).astype(BF16)
            k.dqkv[at, ks] = (dk + k.gate[at, :] * more_k).astype(BF16)
            k.dqkv[at, vs] = (dv + more_v).astype(BF16)
        k.part[here, :] = dot(k.dqkv[here, :], k.w[0], 1, 1).astype(BF16)

    def result(m):
        back, gains = norm_back(k.x[m].astype(F32), scale, row.rs_result(m))
        k.dx_o[m] = (k.dmid[m] + back).astype(BF16)
        k.dgain_o[...] += gains

    for m in range(micros):
        compute(m)
        row.rs_start(m)
        if m >= 1:
            row.rs_pair(m - 1)
        if m >= 2:
            row.rs_transit(m - 2)
        hook(f"computed{m}")

    def out_grad():
        for copy in third:
            loc.wait(copy)

        @pl.loop(0, width // 256)
        def _(t):
            at = pl.ds(pl.multiple_of(t * 256, 256), 256)
            k.grad[0, at, out_cols] = dot(k.full[:, at], k.mixed[...], 0, 0).astype(BF16)

    def qkv_grad():
        @pl.loop(0, width // 256)
        def _(t):
            at = pl.ds(pl.multiple_of(t * 256, 256), 256)
            k.grad[0, at, in_cols] = dot(k.xin[:, at], k.dqkv[...], 0, 0).astype(BF16)

        loc.start(k.grad, k.grad_o)

    tail(row, micros, result, hook, [out_grad, qkv_grad])
    states.drain()
    end()


VM = pl.BlockSpec(memory_space=pltpu.VMEM)
SM = pl.BlockSpec(memory_space=pltpu.SMEM)
HB = pl.BlockSpec(memory_space=pl.ANY)


def vm(dims, dtype=BF16):
    return pltpu.VMEM(dims, dtype)


def launch(name, collective, body, ins, outs, scratch):
    names = list(ins) + list(outs) + list(scratch)

    def kernel(*refs):
        body(SimpleNamespace(**dict(zip(names, refs))))

    results = pl.pallas_call(
        kernel,
        out_shape=tuple(jax.ShapeDtypeStruct(d, t) for d, t, _ in outs.values()),
        in_specs=[spec for _, spec in ins.values()],
        out_specs=tuple(spec for _, _, spec in outs.values()),
        scratch_shapes=list(scratch.values()),
        compiler_params=pltpu.CompilerParams(
            collective_id=collective, has_side_effects=True, vmem_limit_bytes=VMEM_LIMIT
        ),
        name=name,
    )(*[a for a, _ in ins.values()])
    return SimpleNamespace(**dict(zip(outs, results)))


def local(
    tokens, cotangent, block_order, lengths, decay, write_gate, gain_attn, w_query, w_key, w_value,
    persist_key, persist_value, w_output, gain_ffn, w_gate, w_up, w_down,
):
    sec, row_id, col = (lax.axis_index(a) for a in ("section", "row", "col"))
    groups = lax.axis_size("col")
    micros, rows, features = tokens.shape
    width = features * 4
    own, blocks, all_rows, size = rows // 8, rows // BLOCK, micros * rows, features // 2
    ffh = w_gate.shape[2] // 2
    per = persist_key.shape[1]
    persist = per * groups
    cfg = SimpleNamespace(
        micros=micros, rows=rows, own=own, size=size, width=width, groups=groups, blocks=blocks, per=per
    )
    total_blocks = block_order.shape[1]
    positions = jnp.arange(total_blocks, dtype=jnp.int32)
    my_blocks = col * blocks + jnp.arange(blocks, dtype=jnp.int32)
    deal_picks = lax.dynamic_slice_in_dim(block_order, col * blocks, blocks, 1)
    matches = (block_order[:, :, None] == my_blocks[None, None, :]).astype(jnp.int32)
    back_picks = jnp.sum(matches * positions[None, :, None], axis=1)

    def lanes(a):
        return jnp.pad(a, ((0, 0),) * (a.ndim - 1) + ((0, 128 - a.shape[-1]),))

    def eights(a):
        return jnp.pad(a, ((0, 0),) * (a.ndim - 2) + ((0, -a.shape[-2] % 8), (0, 0)))

    share = gain_attn.shape[1]
    own_gains = jnp.concatenate([gain_attn, gain_ffn], axis=0).astype(F32)
    placed = lax.dynamic_update_slice(
        jnp.zeros((2, features), F32), own_gains, (jnp.zeros_like(col), col * share)
    )
    packed = jnp.concatenate(
        [eights(placed.reshape(-1, 128))]
        + [
            eights(a[0].reshape(per, 2, size).transpose(1, 0, 2)).reshape(16, size).astype(F32)
            for a in (persist_key, persist_value)
        ]
        + [eights(lanes(decay[0].transpose(2, 0, 1).reshape(2, -1)))],
        axis=0,
    )
    gate_rows = eights(write_gate[0].transpose(2, 0, 1).reshape(2, -1, 128)) / BLOCK
    ends = jnp.cumsum(lengths, axis=1)
    is_start = jnp.any(positions[None, :, None] == (ends - lengths)[:, None, :], axis=2)
    starts = jnp.where(is_start, 0.0, 1.0).reshape(micros, groups, blocks).transpose(1, 0, 2)
    starts = jnp.broadcast_to(lanes(starts.reshape(groups, -1))[:, None], (groups, 8, 128))

    def cols_split(w):
        return w.reshape(w.shape[0], 2, -1).transpose(1, 0, 2)

    def rows_split(w):
        return w.reshape(2, -1, w.shape[1]).transpose(0, 2, 1)

    blocks_a = jnp.concatenate(
        [cols_split(w[0]) for w in (w_query, w_key, w_value)] + [rows_split(w_output[0])], axis=2
    )[:, None]
    blocks_b = jnp.stack(
        [cols_split(w_gate[0]), cols_split(w_up[0]), rows_split(w_down[0])], axis=1
    )

    def row_scratch():
        return {
            "part": vm((all_rows, width)),
            "pair": vm((micros, 4 * own, width)),
            "both": vm((micros, 4, own, width)),
            "transit": vm((micros, 2, own, width // 2)),
            "final": vm((micros, 2, own, width)),
            "send": pltpu.SemaphoreType.DMA((micros, N_AG + N_RS)),
            "recv": pltpu.SemaphoreType.DMA((micros, N_AG + N_RS)),
            "sems": pltpu.SemaphoreType.DMA((24,)),
            "full": vm((all_rows, width)),
        }

    def run(
        name, collective, kernel, ins, outs, scratch, sides=(), swaps=(), plan=(), layer=0,
        load_weights=None,
    ):
        ins, outs, scratch, plan = dict(ins), dict(outs), dict(scratch), dict(plan)
        ins["gains"] = (opened.gains, VM)
        own_cfg = SimpleNamespace(**vars(cfg), layer=layer, load_weights=load_weights)
        scratch.update(row_scratch())
        for side in sides:
            side.declare(ins, outs, scratch, groups)
        for swap in swaps:
            swap.declare(scratch)

        def body(k):
            row = Rows(rows, own, width, k.send, k.recv)
            row.buffers = (k.part, k.pair, k.both, k.transit, k.final)
            loc = Local(k.sems)

            def at(point):
                for action in plan.get(point, ()):
                    action(k, row)

            def begin():
                peers = [(row.s, row.r, lax.rem(row.c + i, groups)) for i in range(1, groups)]
                row.greet(peers + (plane_peers(row) if swaps else []))
                for side in sides:
                    side.bind(k, row, groups)
                at("begin")

            def end():
                for side in sides:
                    side.finish()
                at("end")
                row.finish()
                for side in sides:
                    side.drain()
                for swap in swaps:
                    swap.drain()
                loc.finish()

            kernel(k, row, loc, own_cfg, begin, at, end)

        return launch(name, collective, body, ins, outs, scratch)

    def starts_of(*sides):
        return [lambda k, row, side=side: side.start() for side in sides]

    def steps_of(*sides):
        return [lambda k, row, side=side: side.step() for side in sides]

    def ends_of(*sides):
        return [lambda k, row, side=side: side.finish() for side in sides]

    stage_dims = (micros, rows, size)
    by_block = (micros, blocks, BLOCK, size)

    def lanes_of_core(name):
        def view(k, row):
            mine = pl.ds(pl.multiple_of(row.s * size, 128), size)
            return getattr(k, name).at[:, :, :, mine]

        return view

    tokens_b = tokens.reshape(micros, blocks, BLOCK, features)
    cotangent_b = cotangent.reshape(micros, blocks, BLOCK, features)

    def chosen(k, buf, picks, stage, lead=()):
        for m in range(micros):
            for b in range(blocks):
                stage[lead + (m, pl.ds(b * BLOCK, BLOCK))] = buf[lead + (m, picks[m, b])]

    def head_body(k):
        row = Rows(rows, own, width, None, None)
        peers = [row.x, row.y, row.sib] + plane_peers(row)
        peers += [(row.s, row.r, lax.rem(row.c + i, groups)) for i in range(1, groups)]
        barrier = pltpu.get_barrier_semaphore()
        for peer in peers:
            pl.semaphore_signal(barrier, inc=1, device_id=peer, device_id_type=MESH)
        pl.semaphore_wait(barrier, len(peers))
        copies, keeps_here = [], []
        for i, (src, dst) in enumerate(((k.blocks_a, k.shards_a), (k.blocks_b, k.shards_b))):
            keep_here = pltpu.make_async_copy(src.at[row.s], dst.at[row.s], k.locals.at[i])
            copy = pltpu.make_async_remote_copy(
                src_ref=src.at[1 - row.s],
                dst_ref=dst.at[row.s],
                send_sem=k.xsend.at[i],
                recv_sem=k.xrecv.at[i],
                device_id=row.sib,
                device_id_type=MESH,
            )
            keep_here.start()
            copy.start()
            copies.append(copy)
            keeps_here.append(keep_here)
        deal.bind(k, row, groups)
        deal.start()

        def push(src, dst, i, to):
            copy = pltpu.make_async_remote_copy(
                src_ref=src,
                dst_ref=dst,
                send_sem=k.psend.at[i],
                recv_sem=k.precv.at[i],
                device_id=to,
                device_id_type=MESH,
            )
            copy.start()
            return copy

        k.line[row.s, row.c] = k.packed[...]
        k.gates[row.s] = k.gate_rows[row.s]
        small = [
            push(
                k.packed,
                k.line.at[row.s, row.c],
                i,
                (row.s, row.r, lax.rem(row.c + i, groups)),
            )
            for i in range(1, groups)
        ]
        crossing = [push(k.gate_rows.at[1 - row.s], k.gates.at[row.s], 0, row.sib)]
        copies[0].wait_recv()
        keeps_here[0].wait()
        first.bind(k, row, groups)
        first.start()
        copies[1].wait_recv()
        keeps_here[1].wait()
        down0.bind(k, row, groups)
        down0.start()
        for copy in small:
            copy.wait_recv()
        total = k.line[row.s, 0, 0:8, :]
        for j in range(1, groups):
            total = total + k.line[row.s, j, 0:8, :]
        k.gains[row.s, row.r] = total
        for i, ps, pr in others(row):
            mine = k.gains.at[row.s, row.r]
            crossing.append(push(mine, mine, groups + i, (ps, pr, row.c)))
        crossing.append(push(k.line.at[row.s], k.line.at[row.s], groups + 8, row.sib))
        deal.step()
        first.step()
        down0.step()
        deal.step()
        first.step()
        down0.step()
        deal.finish()
        chosen(k, k.deal_dst, k.picks, k.stage)
        swap.start(k, row, own, size, k.stage, k.x, True)
        first.finish()
        swap.wait()
        down0.finish()
        for copy in copies + small:
            copy.wait_send()
        for copy in crossing:
            copy.wait()
        deal.drain()
        first.drain()
        down0.drain()
        swap.drain()

    a_dims, b_dims = blocks_a.shape[1:], blocks_b.shape[1:]
    deal = Gather("deal_", tokens_b, by_block, groups, 1, lanes_of_core("deal_src"), "scratch")
    q_dims, o_dims = (1, a_dims[1], 3 * size), (1, a_dims[1], size)
    first = Gather("first_", None, q_dims, groups, 1, lambda k, row: q_of(k.shards_a, 0))

    down0 = Gather(
        "down_", None, (1,) + b_dims[1:], groups, 1, lambda k, row: k.shards_b.at[0, pl.ds(2, 1)]
    )

    def q_of(ref, layer):
        return ref.at[layer, :, :, pl.ds(0, 3 * size)]

    def o_of(ref, layer):
        return ref.at[layer, :, :, pl.ds(3 * size, size)]

    swap = Swap("swap_")
    ins = {
        "picks": (deal_picks, SM),
        "blocks_a": (blocks_a, HB),
        "blocks_b": (blocks_b, HB),
        "packed": (packed, VM),
        "gate_rows": (gate_rows, VM),
    }
    outs = {
        "x": ((micros, own, width), BF16, VM),
        "shards_a": (blocks_a.shape, BF16, HB),
        "shards_b": (blocks_b.shape, BF16, HB),
        "line": ((2, groups) + packed.shape, F32, VM),
        "gains": ((2, 4, 8, 128), F32, VM),
        "gates": ((2,) + gate_rows.shape[1:], F32, VM),
    }
    scratch = {
        "stage": vm((micros, rows, size)),
        "xsend": pltpu.SemaphoreType.DMA((2,)),
        "xrecv": pltpu.SemaphoreType.DMA((2,)),
        "locals": pltpu.SemaphoreType.DMA((2,)),
        "psend": pltpu.SemaphoreType.DMA((groups + 9,)),
        "precv": pltpu.SemaphoreType.DMA((groups + 9,)),
    }
    for side in (deal, first, down0):
        side.declare(ins, outs, scratch, groups)
    swap.declare(scratch)
    opened = launch("deal", 0, head_body, ins, outs, scratch)

    state_scratch = {
        "update": vm((micros * blocks, size, size), F32),
        "entering": vm((size, size), F32),
        "leaving": vm((micros, size, size)),
        "box": vm((micros, groups, size, size)),
        "ssend": pltpu.SemaphoreType.DMA((micros, groups)),
        "srecv": pltpu.SemaphoreType.DMA((micros, groups)),
        "gate": vm((all_rows, 1), F32),
        "persist": vm((persist, size), F32),
        "w": vm((1, width, 3 * size)),
        "qkv": vm((all_rows, 3 * size)),
        "state": vm((micros * blocks, size, size)),
        "mixed": vm((all_rows, size)),
    }
    def ffn_ins(weights):
        return {f"weights{i}": (w, HB) for i, w in enumerate(weights)}

    def ffn_loads(weights):
        def load(k, loc):
            return [
                loc.start(getattr(k, f"weights{i}"), k.w.at[pl.ds(i, 1)])
                for i in range(len(weights))
            ]

        return load

    ffn_scratch = {
        "w": vm((3, width, ffh)),
        "gp": vm((all_rows, ffh)),
        "up": vm((all_rows, ffh)),
        "act": vm((all_rows, ffh)),
    }

    def attn_ins(weights):
        return {
            "line": (opened.line, VM),
            "gates": (opened.gates, VM),
            "starts": (starts, VM),
            "weights": (weights, HB),
        }

    def attn_forward(collective, l, x, weights, more_outs=(), **more):
        outs = {
            "xin_o": ((all_rows, width), BF16, HB),
            "qkv_o": ((all_rows, 3 * size), BF16, HB),
            "state_o": ((micros * blocks, size, size), BF16, HB),
            "mixed_o": ((all_rows, size), BF16, HB),
            "mid_o": ((micros, own, width), F32, VM),
            "wo_o": ((1, width, size), BF16, HB),
            **dict(more_outs),
        }
        ins = {"x": (x, VM), **attn_ins(weights)}
        return run(
            f"attn_forward_{l}", collective, attn_forward_kernel, ins, outs, state_scratch,
            layer=l, **more,
        )

    def ffn_forward(collective, l, mid, weights, more_ins=(), more_outs=(), more_scratch=(), **more):
        outs = {
            "xin_o": ((all_rows, width), BF16, HB),
            "gp_o": ((all_rows, ffh), BF16, HB),
            "up_o": ((all_rows, ffh), BF16, HB),
            "act_o": ((all_rows, ffh), BF16, HB),
            "y_o": ((micros, own, width), BF16, VM),
            **dict(more_outs),
        }
        ins = {
            "mid": (mid, VM), **ffn_ins(weights), **dict(more_ins),
        }
        return run(
            f"ffn_forward_{l}", collective, ffn_forward_kernel, ins, outs,
            {**ffn_scratch, **dict(more_scratch)}, layer=l, load_weights=ffn_loads(weights), **more,
        )

    def ffn_backward(
        collective, l, dy, mid, kept, weights, more_ins=(), more_outs=(), more_scratch=(), **more
    ):
        outs = {
            "dmid_o": ((micros, own, width), F32, VM),
            "dgain_o": ((1, width), F32, VM),
            "grad_o": ((3, width, ffh), BF16, HB),
            **dict(more_outs),
        }
        ins = {
            "dy": (dy, VM), "mid": (mid, VM), **ffn_ins(weights), "xin_h": (kept.xin_o, HB), "gp_h": (kept.gp_o, HB),
            "up_h": (kept.up_o, HB), "act_h": (kept.act_o, HB), **dict(more_ins),
        }
        scratch = {
            **ffn_scratch, **dict(more_scratch), "xin": vm((all_rows, width)), "dg": vm((all_rows, ffh)),
            "du": vm((all_rows, ffh)), "grad": vm((3, width, ffh)),
        }
        return run(
            f"ffn_backward_{l}", collective, ffn_backward_kernel, ins, outs, scratch,
            layer=l, load_weights=ffn_loads(weights), **more,
        )

    def attn_backward(collective, l, dmid, x, kept, weights, more_ins=(), more_outs=(), **more):
        outs = {
            "dx_o": ((micros, own, width), BF16, VM),
            "dgain_o": ((1, width), F32, VM),
            "dpersist_o": ((2, persist, size), F32, VM),
            "grad_o": ((1, width, 4 * size), BF16, HB),
        }
        ins = {
            "dmid": (dmid, VM), "x": (x, VM), **attn_ins(weights), "wo_h": (kept.wo_o, HB), "xin_h": (kept.xin_o, HB),
            "qkv_h": (kept.qkv_o, HB), "state_h": (kept.state_o, HB), "mixed_h": (kept.mixed_o, HB),
        }
        scratch = {
            **state_scratch, "wo": vm((1, width, size)), "xin": vm((all_rows, width)), "dmix": vm((all_rows, size)),
            "dqkv": vm((all_rows, 3 * size)), "grad": vm((1, width, 4 * size)),
        }
        return run(
            f"attn_backward_{l}", collective, attn_backward_kernel, ins, outs, scratch,
            layer=l, **more,
        )

    def shard(name, layer, span=None):
        def view(k, row):
            ref = getattr(k, name).at[layer]
            return ref if span is None else ref.at[pl.ds(*span)]

        return view

    x0, q0 = opened.x, opened.first_dst

    def one_b(tag, layer, which, home=None):
        dims = (1,) + b_dims[1:]
        view = shard(tag + "src", layer, (which, 1))
        return Gather(tag, opened.shards_b, dims, groups, 1, view, home)

    def wo_side(layer):
        return Gather(
            "wo_", opened.shards_a, o_dims, groups, 1, lambda k, row: o_of(k.wo_src, layer), "scratch"
        )

    def attn_sides(layer):
        wo, gate, up = wo_side(layer), one_b("gate_", layer, 0), one_b("up_", layer, 1)
        plan = {
            "begin": starts_of(wo, gate, up),
            "states0": steps_of(wo, gate),
            "states1": steps_of(wo, up),
            "states2": steps_of(gate, up),
            "out": ends_of(wo),
        }
        return [wo, gate, up], plan

    def leave(swap, source, dst="stage_o"):
        return lambda k, row: swap.start(
            k, row, own, size, getattr(k, source), getattr(k, dst), False
        )

    def waited(swap):
        return lambda k, row: swap.wait()

    def staged(tag, array):
        return Gather(tag, array.reshape(by_block), by_block, groups, 1)

    sides, plan = attn_sides(0)
    fa0 = attn_forward(1, 0, x0, q0, sides=sides, plan=plan)
    b0 = [fa0.gate_dst, fa0.up_dst, opened.down_dst]
    next_down = one_b("down_", 1, 2)
    next_q = Gather("q_", opened.shards_a, q_dims, groups, 1, lambda k, row: q_of(k.q_src, 1))
    ff0 = ffn_forward(
        2, 0, fa0.mid_o, b0, sides=[next_q, next_down],
        plan={
            "begin": starts_of(next_q, next_down), "computed0": steps_of(next_q, next_down),
            "computed1": steps_of(next_q, next_down),
        },
    )
    sides, plan = attn_sides(1)
    swap_y0 = Swap("swap_")
    plan["begin"] = plan["begin"] + [leave(swap_y0, "x")]
    plan["end"] = [waited(swap_y0)]
    fa1 = attn_forward(
        3, 1, ff0.y_o, ff0.q_dst, more_outs={"stage_o": (stage_dims, BF16, HB)},
        sides=sides, swaps=[swap_y0], plan=plan,
    )
    b1 = [fa1.gate_dst, fa1.up_dst, ff0.down_dst]
    cot = Gather("cot_", cotangent_b, by_block, groups, 1, lanes_of_core("cot_src"), "scratch")
    swap_cot = Swap("swap_")

    def deal_cot(k, row):
        cot.finish()
        chosen(k, k.cot_dst, k.picks, k.stage)
        swap_cot.start(k, row, own, size, k.stage, k.dy_o, True)

    ff1 = ffn_forward(
        4, 1, fa1.mid_o, b1,
        more_ins={"picks": (deal_picks, SM)},
        more_outs={"dy_o": ((micros, own, width), BF16, VM)},
        more_scratch={"stage": vm(stage_dims)},
        sides=[cot], swaps=[swap_cot],
        plan={
            "begin": starts_of(cot), "computed0": steps_of(cot), "computed1": steps_of(cot),
            "tail": [deal_cot], "end": [waited(swap_cot)],
        },
    )

    swap_y1 = Swap("swap_")
    y0 = staged("y0_", fa1.stage_o)
    fb1 = ffn_backward(
        5, 1, ff1.dy_o, fa1.mid_o, ff1, b1,
        more_ins={"y1": (ff1.y_o, VM)}, more_outs={"stage_o": (stage_dims, BF16, HB)},
        sides=[y0], swaps=[swap_y1],
        plan={
            "begin": starts_of(y0) + [leave(swap_y1, "y1")],
            "computed0": steps_of(y0), "computed1": steps_of(y0), "end": [waited(swap_y1)],
        },
    )
    down1, gate1 = Total("td_", fb1.grad_o, groups, (2, 1)), Total("tg_", fb1.grad_o, groups, (0, 1))
    ab1 = attn_backward(
        6, 1, fb1.dmid_o, ff0.y_o, fa1, ff0.q_dst, sides=[down1, gate1],
        plan={
            "begin": starts_of(down1), "states0": steps_of(down1), "states1": steps_of(down1),
            "states2": starts_of(gate1), "computed0": steps_of(gate1), "computed1": steps_of(gate1),
        },
    )
    up1, a1 = Total("tu_", fb1.grad_o, groups, (1, 1)), Total("ta_", ab1.grad_o, groups)
    swap_g, y1 = Swap("swap_"), staged("y1_", fb1.stage_o)
    fb0 = ffn_backward(
        7, 0, ab1.dx_o, fa0.mid_o, ff0, b0, more_outs={"stage_o": (stage_dims, BF16, HB)},
        sides=[up1, a1, y1], swaps=[swap_g],
        plan={
            "begin": starts_of(y1, up1, a1) + [leave(swap_g, "dy")],
            "computed0": steps_of(y1, up1, a1), "computed1": steps_of(y1, up1, a1),
            "end": [waited(swap_g)],
        },
    )
    down0, gate0 = Total("td_", fb0.grad_o, groups, (2, 1)), Total("tg_", fb0.grad_o, groups, (0, 1))
    g1 = staged("g_", fb0.stage_o)
    ab0 = attn_backward(
        8, 0, fb0.dmid_o, x0, fa0, q0, sides=[g1, down0, gate0],
        plan={
            "begin": starts_of(g1, down0), "states2": steps_of(g1, down0) + starts_of(gate0),
            "computed1": steps_of(g1, down0, gate0), "computed2": steps_of(gate0),
        },
    )

    small_rows = 4 * width // 128 + 4 * persist
    smalls = jnp.concatenate(
        [a.reshape(-1, 128) for a in (ab0.dgain_o, fb0.dgain_o, ab1.dgain_o, fb1.dgain_o)]
        + [a.reshape(-1, 128) for a in (ab0.dpersist_o, ab1.dpersist_o)],
        axis=0,
    )
    gain_rows = 4 * width // 128
    swap_last, total_a0 = Swap("swap_"), Total("ta_", ab0.grad_o, groups, home="scratch")
    up0 = Total("tu_", fb0.grad_o, groups, (1, 1), "scratch")

    last = Gather("last_", None, by_block, groups, 1, lambda k, row: k.staged, "scratch")

    def tail_body(k):
        row = Rows(rows, own, width, None, None)
        peers = [row.x, row.y, row.sib] + plane_peers(row)
        peers += [(row.s, row.r, lax.rem(row.c + i, groups)) for i in range(1, groups)]
        barrier = pltpu.get_barrier_semaphore()
        for peer in peers:
            pl.semaphore_signal(barrier, inc=1, device_id=peer, device_id_type=MESH)
        pl.semaphore_wait(barrier, len(peers))
        swap_last.start(k, row, own, size, k.dx, k.stage, False)
        up0.bind(k, row, groups)
        up0.start()
        total_a0.bind(k, row, groups)
        total_a0.start()
        loads = []
        for i, (a, b) in enumerate(
            ((k.y0_buf, k.y_v.at[0]), (k.y1_buf, k.y_v.at[1]), (k.g_buf, k.g_v),
             (k.bg0, k.res_b.at[0, pl.ds(0, 1)]), (k.bd0, k.res_b.at[0, pl.ds(2, 1)]),
             (k.bg1, k.res_b.at[1, pl.ds(0, 1)]), (k.bu1, k.res_b.at[1, pl.ds(1, 1)]),
             (k.bd1, k.res_b.at[1, pl.ds(2, 1)]), (k.a1, k.res_a.at[1]))
        ):
            load = pltpu.make_async_copy(a, b, k.loads.at[i])
            load.start()
            loads.append(load)

        def push(src, dst, i, to):
            copy = pltpu.make_async_remote_copy(
                src_ref=src,
                dst_ref=dst,
                send_sem=k.psend.at[i],
                recv_sem=k.precv.at[i],
                device_id=to,
                device_id_type=MESH,
            )
            copy.start()
            return copy

        pushes = []
        for i in range(1, groups):
            to = (row.s, row.r, lax.rem(row.c + i, groups))
            pushes.append(push(k.smalls, k.small_box.at[i], i, to))
        swap_last.wait()
        for m in range(micros):
            for b in range(blocks):
                k.staged[m, b] = k.stage[m, b * BLOCK : (b + 1) * BLOCK, :]
        last.bind(k, row, groups)
        last.start()
        for copy in pushes:
            copy.wait_recv()
        total = k.smalls[...]
        for i in range(1, groups):
            total = total + k.small_box[i]
        k.small_sum[...] = total
        gains = []
        for i, ps, pr in others(row):
            gains.append(
                push(
                    k.small_sum.at[pl.ds(0, gain_rows), :],
                    k.gain_box.at[i],
                    groups + i,
                    (ps, pr, row.c),
                )
            )
        for load in loads:
            load.wait()
        for l in range(2):
            chosen(k, k.y_v, k.back, k.halves, (l,))
        for m in range(micros):
            for b in range(blocks):
                k.halves[3, m, pl.ds(b * BLOCK, BLOCK), :] = k.g_v[m, k.back[m, b]]
        last.step()
        up0.step()
        total_a0.step()

        mine_lanes = pl.ds(pl.multiple_of(row.s * size, 128), size)
        moved, kept_here = [], []

        def give(i, pair, out):
            base = groups + 8 + i
            copy = push(pair.at[1 - row.s], out, base, row.sib)
            moved.append(copy)
            here = pltpu.make_async_copy(pair.at[row.s], out, k.loads.at[9 + i])
            here.start()
            kept_here.append(here)

        give(0, k.halves.at[pl.ds(0, 2)], k.acts_o.at[:, :, mine_lanes])
        last.step()
        up0.step()
        total_a0.step()
        for copy in gains:
            copy.wait_recv()
        total = k.small_sum[0:gain_rows, :]
        for i in range(1, 8):
            total = total + k.gain_box[i]
        k.gain_o[...] = total
        k.persist_o[...] = k.small_sum[gain_rows:, :]
        up0.finish()
        k.res_b[0, pl.ds(1, 1)] = k.tu_sum[...]
        give(1, k.res_b, k.grad_b.at[row.s])
        total_a0.finish()
        k.res_a[0] = k.ta_sum[...]
        give(2, k.res_a, k.grad_a.at[row.s])
        last.finish()
        for m in range(micros):
            for b in range(blocks):
                k.halves[2, m, pl.ds(b * BLOCK, BLOCK), :] = k.last_dst[m, k.back[m, b]]
        give(3, k.halves.at[pl.ds(2, 2)], k.grads_o.at[:, :, mine_lanes])
        for copy in moved:
            copy.wait()
        for here in kept_here:
            here.wait()
        for copy in pushes + gains:
            copy.wait_send()
        swap_last.drain()
        total_a0.drain()
        up0.drain()
        last.drain()

    ins = {
        "dx": (ab0.dx_o, VM),
        "y0_buf": (fb1.y0_dst, HB),
        "y1_buf": (fb0.y1_dst, HB),
        "g_buf": (ab0.g_dst, HB),
        "bg0": (ab0.tg_sum, HB),
        "bd0": (ab0.td_sum, HB),
        "bg1": (ab1.tg_sum, HB),
        "bu1": (fb0.tu_sum, HB),
        "bd1": (ab1.td_sum, HB),
        "a1": (fb0.ta_sum, HB),
        "smalls": (smalls, VM),
        "back": (back_picks, SM),
    }
    outs = {
        "acts_o": ((micros, rows, features), BF16, VM),
        "grads_o": ((micros, rows, features), BF16, VM),
        "grad_a": ((2,) + total_a0.dims, BF16, VM),
        "grad_b": ((2, 3) + up0.dims[1:], BF16, VM),
        "gain_o": ((gain_rows, 128), F32, VM),
        "persist_o": ((4 * persist, 128), F32, VM),
    }
    scratch = {
        "stage": vm(stage_dims),
        "staged": vm(by_block),
        "y_v": vm((2,) + last.dims),
        "g_v": vm(last.dims),
        "halves": vm((4,) + stage_dims),
        "res_a": vm((2,) + total_a0.dims),
        "res_b": vm((2, 3) + up0.dims[1:]),
        "small_box": vm((groups, small_rows, 128), F32),
        "small_sum": vm((small_rows, 128), F32),
        "gain_box": vm((8, gain_rows, 128), F32),
        "loads": pltpu.SemaphoreType.DMA((13,)),
        "psend": pltpu.SemaphoreType.DMA((groups + 12,)),
        "precv": pltpu.SemaphoreType.DMA((groups + 12,)),
    }
    for side in (total_a0, up0, last):
        side.declare(ins, outs, scratch, groups)
    swap_last.declare(scratch)
    closed = launch("restore", 9, tail_body, ins, outs, scratch)

    def cols_join(pair):
        return jnp.concatenate([pair[0], pair[1]], axis=1).astype(F32)[None]

    def rows_join(pair):
        return jnp.concatenate([pair[0].T, pair[1].T], axis=0).astype(F32)[None]

    grad_a, grad_b = closed.grad_a[:, 0], closed.grad_b
    heads = [cols_join(grad_a[:, :, i * size : (i + 1) * size]) for i in range(3)]
    grad_out = rows_join(grad_a[:, :, 3 * size :])
    grad_gate, grad_up = cols_join(grad_b[:, 0]), cols_join(grad_b[:, 1])
    grad_down = rows_join(grad_b[:, 2])
    gain_sum = closed.gain_o.reshape(2, 2, width)
    my_gain = lax.dynamic_slice_in_dim(
        lax.dynamic_index_in_dim(gain_sum, sec, 0, False), (row_id * groups + col) * share, share, 1
    )
    persist_sum = closed.persist_o.reshape(2, 2, persist, size)
    persist_sum = lax.dynamic_slice_in_dim(persist_sum, col * per, per, 2)
    mine_p = lax.dynamic_index_in_dim(persist_sum, sec, 0, False)
    got_p = lax.ppermute(
        lax.dynamic_index_in_dim(persist_sum, 1 - sec, 0, False), "section", [(0, 1), (1, 0)]
    )
    grad_persist = jnp.concatenate(
        [jnp.where(sec == 0, mine_p, got_p), jnp.where(sec == 0, got_p, mine_p)], axis=2
    )
    return (
        closed.acts_o[None],
        closed.grads_o[None],
        my_gain[0][None],
        heads[0],
        heads[1],
        heads[2],
        grad_persist[0][None],
        grad_persist[1][None],
        grad_out,
        my_gain[1][None],
        grad_gate,
        grad_up,
        grad_down,
    )


def solution(mesh):
    weight = P("section", "col", "row")
    across = P("section", "row", "col")
    gain = P("section", ("row", "col"))
    rows = P("section", None, "col", "row")
    return jax.shard_map(
        local,
        mesh=mesh,
        in_specs=(
            P(None, "col", "row"), P(None, "col", "row"), P(), P(), rows, rows, gain, weight, weight,
            weight, weight, weight, across, gain, weight, weight, across,
        ),
        out_specs=(
            rows, rows, gain, weight, weight, weight, weight, weight, across, gain, weight, weight,
            across,
        ),
        check_vma=False,
    )
```

```python
from types import SimpleNamespace

import jax
import jax.numpy as jnp
from jax import lax
from jax.experimental import pallas as pl
from jax.experimental.pallas import tpu as pltpu
from jax.sharding import PartitionSpec as P

BLOCK = 64
EPS = 1e-06
MESH = pl.DeviceIdType.MESH
F32 = jnp.float32
BF16 = jnp.bfloat16
VMEM_LIMIT = 60 << 20
N_AG, N_RS = 8, 7


def dot(a, b, ca=1, cb=0):
    return lax.dot_general(a, b, (((ca,), (cb,)), ((), ())), preferred_element_type=F32)


class Rows:
    def __init__(self, rows, own, width, send, recv):
        self.rows, self.own, self.width, self.half = rows, own, width, width // 2
        self.send, self.recv = send, recv
        self.s, self.r, self.c = (lax.axis_index(a) for a in ("section", "row", "col"))
        self.rx = self.r + 1 - 2 * lax.rem(self.r, 2)
        self.ry = lax.rem(self.r + 2, 4)
        self.rd = lax.rem(self.rx + 2, 4)
        self.x = (self.s, self.rx, self.c)
        self.y = (self.s, self.ry, self.c)
        self.sib = (1 - self.s, self.r, self.c)
        self.started = []

    def greet(self, others=()):
        barrier = pltpu.get_barrier_semaphore()
        peers = [self.x, self.y, self.sib] + list(others)
        for peer in peers:
            pl.semaphore_signal(barrier, inc=1, device_id=peer, device_id_type=MESH)
        pl.semaphore_wait(barrier, len(peers))

    def copy(self, src, dst, m, k, peer):
        return pltpu.make_async_remote_copy(
            src_ref=src,
            dst_ref=dst,
            send_sem=self.send.at[m, k],
            recv_sem=self.recv.at[m, k],
            device_id=peer,
            device_id_type=MESH,
        )

    def go(self, copy):
        copy.start()
        self.started.append(copy)

    def finish(self):
        for copy in self.started:
            copy.wait_send()
        self.started = []

    def span(self, m, s, r):
        return pl.ds(pl.multiple_of(m * self.rows + (s * 4 + r) * self.own, 16), self.own)

    def ag_copy(self, full, m, k):
        left, right = pl.ds(0, self.half), pl.ds(self.half, self.half)
        mine, atx, aty, atd = (
            self.span(m, self.s, r) for r in (self.r, self.rx, self.ry, self.rd)
        )
        if k == 0:
            return self.copy(full.at[mine, :], full.at[mine, :], m, 0, self.x)
        if k == 1:
            return self.copy(full.at[mine, :], full.at[mine, :], m, 1, self.y)
        if k == 2:
            return self.copy(full.at[mine, :], full.at[mine, :], m, 2, self.sib)
        if k == 3:
            return self.copy(full.at[atx, left], full.at[atx, left], m, 3, self.y)
        if k == 4:
            return self.copy(full.at[aty, right], full.at[aty, right], m, 4, self.x)
        if k == 5:
            return self.copy(full.at[atx, :], full.at[atx, :], m, 5, self.sib)
        if k == 6:
            return self.copy(full.at[aty, :], full.at[aty, :], m, 6, self.sib)
        return self.copy(full.at[atd, :], full.at[atd, :], m, 7, self.sib)

    def ag_start(self, full, m):
        for k in (0, 1, 2):
            self.go(self.ag_copy(full, m, k))

    def ag_pass(self, full, m):
        self.ag_copy(full, m, 0).wait_recv()
        self.go(self.ag_copy(full, m, 3))
        self.go(self.ag_copy(full, m, 5))
        self.ag_copy(full, m, 1).wait_recv()
        self.go(self.ag_copy(full, m, 4))
        self.go(self.ag_copy(full, m, 6))

    def ag_diag(self, full, m):
        self.ag_copy(full, m, 3).wait_recv()
        self.ag_copy(full, m, 4).wait_recv()
        self.go(self.ag_copy(full, m, 7))

    def ag_wait(self, full, m):
        for k in (2, 5, 6, 7):
            self.ag_copy(full, m, k).wait_recv()

    def rs_copy(self, m, k):
        part, pair, both, transit, final = self.buffers
        left, right = pl.ds(0, self.half), pl.ds(self.half, self.half)
        if k == 8:
            other = pl.ds(
                pl.multiple_of(m * self.rows + (1 - self.s) * 4 * self.own, 16), 4 * self.own
            )
            return self.copy(part.at[other, :], pair.at[m], m, 8, self.sib)
        if k == 9:
            return self.copy(both.at[m, self.rd, :, left], transit.at[m, 0], m, 9, self.x)
        if k == 10:
            return self.copy(both.at[m, self.rd, :, right], transit.at[m, 1], m, 10, self.y)
        if k == 11:
            return self.copy(both.at[m, self.rx, :, left], final.at[m, 0, :, left], m, 11, self.x)
        if k == 12:
            return self.copy(both.at[m, self.ry, :, right], final.at[m, 1, :, right], m, 12, self.y)
        if k == 13:
            return self.copy(both.at[m, self.ry, :, left], final.at[m, 1, :, left], m, 13, self.y)
        return self.copy(both.at[m, self.rx, :, right], final.at[m, 0, :, right], m, 14, self.x)

    def rs_start(self, m):
        self.go(self.rs_copy(m, 8))

    def rs_pair(self, m):
        part, pair, both, _, _ = self.buffers
        self.rs_copy(m, 8).wait_recv()
        for r in range(4):
            mine = part[self.span(m, self.s, r), :].astype(F32)
            theirs = pair[m, r * self.own : (r + 1) * self.own, :].astype(F32)
            both[m, r] = (mine + theirs).astype(BF16)
        for k in (9, 10, 11, 12):
            self.go(self.rs_copy(m, k))

    def rs_transit(self, m):
        _, _, both, transit, _ = self.buffers
        left, right = pl.ds(0, self.half), pl.ds(self.half, self.half)
        self.rs_copy(m, 9).wait_recv()
        total = both[m, self.ry, :, left].astype(F32) + transit[m, 0].astype(F32)
        both[m, self.ry, :, left] = total.astype(BF16)
        self.go(self.rs_copy(m, 13))
        self.rs_copy(m, 10).wait_recv()
        total = both[m, self.rx, :, right].astype(F32) + transit[m, 1].astype(F32)
        both[m, self.rx, :, right] = total.astype(BF16)
        self.go(self.rs_copy(m, 14))

    def rs_result(self, m):
        _, _, both, _, final = self.buffers
        for k in (11, 12, 13, 14):
            self.rs_copy(m, k).wait_recv()
        return both[m, self.r].astype(F32) + final[m, 0].astype(F32) + final[m, 1].astype(F32)


class Local:
    def __init__(self, sems):
        self.sems, self.used, self.open = sems, 0, []

    def start(self, src, dst):
        copy = pltpu.make_async_copy(src, dst, self.sems.at[self.used])
        self.used += 1
        copy.start()
        self.open.append(copy)
        return copy

    def wait(self, copy):
        copy.wait()
        self.open = [other for other in self.open if other is not copy]

    def finish(self):
        for copy in list(self.open):
            copy.wait()


def inv_rms(values):
    return lax.rsqrt(jnp.mean(values * values, axis=1, keepdims=True) + EPS)


def norm_to(full, gain, values, span):
    full[span, :] = (values * inv_rms(values) * gain).astype(BF16)


def norm_back(values, gain, grad):
    scale = inv_rms(values)
    weighted = grad * gain
    inner = jnp.mean(weighted * values, axis=1, keepdims=True)
    back = scale * weighted - values * (scale * scale * scale * inner)
    return back, jnp.sum(grad * values * scale, axis=0, keepdims=True)


def wait_both(copies):
    for condition, copy in copies:

        @pl.when(condition)
        def _(copy=copy):
            copy.wait_send()


class Side:
    def __init__(self, tag):
        self.tag = tag

    def ref(self, name):
        return getattr(self.ns, self.tag + name)

    def bind(self, ns, row, groups):
        self.ns, self.row, self.c, self.groups = ns, row, row.c, groups
        self.sent = []

    def when(self, condition, copy):
        @pl.when(condition)
        def _():
            copy.start()

        self.sent.append((condition, copy))

    def arrived(self, condition, copy):
        @pl.when(condition)
        def _():
            copy.wait_recv()

    def remote(self, src, dst, send, recv, to):
        return pltpu.make_async_remote_copy(
            src_ref=src,
            dst_ref=dst,
            send_sem=send,
            recv_sem=recv,
            device_id=(self.row.s, self.row.r, to),
            device_id_type=MESH,
        )


def part_of(ref, at, per, axis):
    where = pl.ds(pl.multiple_of(at * per, per), per)
    return ref.at[(slice(None),) * axis + (where,)]


class Gather(Side):
    def __init__(self, tag, array, dims, groups, axis, view=None, home=None):
        super().__init__(tag)
        self.array, self.axis, self.view, self.home = array, axis, view, home
        self.per = dims[axis]
        self.dims = dims[:axis] + (dims[axis] * groups,) + dims[axis + 1 :]

    def declare(self, ins, outs, scratch, groups):
        if self.array is not None:
            ins[self.tag + "src"] = (self.array, HB)
        if self.home is None:
            outs[self.tag + "dst"] = (self.dims, BF16, HB)
        else:
            scratch[self.tag + "dst"] = pltpu.VMEM(self.dims, BF16)
        scratch[self.tag + "send"] = pltpu.SemaphoreType.DMA((2, groups))
        scratch[self.tag + "recv"] = pltpu.SemaphoreType.DMA((groups,))
        scratch[self.tag + "own"] = pltpu.SemaphoreType.DMA((1,))

    def slot(self, j):
        return part_of(self.ref("dst"), jnp.clip(j, 0, self.groups - 1), self.per, self.axis)

    def source(self):
        return self.view(self.ns, self.row) if self.view else self.ref("src")

    def move(self, j, side, src=None):
        to = jnp.clip(self.c + (1 - 2 * side), 0, self.groups - 1)
        j = jnp.clip(j, 0, self.groups - 1)
        src = self.slot(j) if src is None else src
        return self.remote(
            src, self.slot(j), self.ref("send").at[side, j], self.ref("recv").at[j], to
        )

    def start(self):
        c, n = self.c, self.groups
        self.at, self.done = 1, False
        self.own = pltpu.make_async_copy(self.source(), self.slot(c), self.ref("own").at[0])
        self.own.start()
        self.when(c + 1 < n, self.move(c, 0, self.source()))
        self.when(c >= 1, self.move(c, 1, self.source()))

    def step(self):
        c, n, k = self.c, self.groups, self.at
        if k < n:
            self.arrived(c >= k, self.move(c - k, 0))
            self.arrived(c + k < n, self.move(c + k, 1))
            if k < n - 1:
                self.when((c >= k) & (c + 1 < n), self.move(c - k, 0))
                self.when((c + k < n) & (c >= 1), self.move(c + k, 1))
        self.at += 1

    def finish(self):
        if not self.done:
            while self.at < self.groups:
                self.step()
            self.own.wait()
            self.done = True

    def drain(self):
        wait_both(self.sent)


class Total(Side):
    def __init__(self, tag, parts, dims, groups, span, view=None, home=None):
        super().__init__(tag)
        self.parts, self.span, self.view, self.home = parts, span, view, home
        self.per = dims[1] // groups
        self.count = span[1]
        self.dims = (self.count, self.per, dims[2])

    def declare(self, ins, outs, scratch, groups):
        if self.home is None:
            outs[self.tag + "sum"] = (self.dims, BF16, VM)
        else:
            scratch[self.tag + "sum"] = pltpu.VMEM(self.dims, BF16)
        if self.view is None:
            ins[self.tag + "parts"] = (self.parts, HB)
            whole = (self.count, self.per * groups, self.dims[2])
            scratch[self.tag + "mine"] = pltpu.VMEM(whole, BF16)
        scratch[self.tag + "box"] = pltpu.VMEM((2, groups) + self.dims, BF16)
        scratch[self.tag + "send"] = pltpu.SemaphoreType.DMA((2, groups))
        scratch[self.tag + "recv"] = pltpu.SemaphoreType.DMA((2, groups))
        scratch[self.tag + "load"] = pltpu.SemaphoreType.DMA((1,))

    def clip(self, j):
        return jnp.clip(j, 0, self.groups - 1)

    def piece(self, ref, d, p=None):
        d = self.clip(d)
        where = pl.ds(pl.multiple_of(d * self.per, self.per), self.per)
        if p is None:
            return ref.at[:, where, :]
        return ref[p + (self.span[0] if self.view else 0), where, :]

    def source(self):
        parts = self.view(self.ns) if self.view else self.ref("parts")
        return parts.at[pl.ds(*self.span)]

    def mine(self):
        return self.view(self.ns) if self.view else self.ref("mine")

    def move(self, side, d, src):
        d = self.clip(d)
        to = self.clip(self.c + (1 - 2 * side))
        return self.remote(
            src,
            self.ref("box").at[side, d],
            self.ref("send").at[side, d],
            self.ref("recv").at[side, d],
            to,
        )

    def boxed(self, side, d):
        return self.ref("box").at[side, self.clip(d)]

    def start(self):
        c, n = self.c, self.groups
        self.at, self.done = 1, False
        if self.view is None:
            self.load = pltpu.make_async_copy(
                self.source(), self.ref("mine"), self.ref("load").at[0]
            )
            self.load.start()
        self.ends(0)

    def ends(self, t):
        c, n = self.c, self.groups
        self.when(c == 0, self.move(0, n - 1 - t, self.piece(self.source(), n - 1 - t)))
        self.when(c == n - 1, self.move(1, t, self.piece(self.source(), t)))

    def step(self):
        c, n, t = self.c, self.groups, self.at
        box, mine = self.ref("box"), self.mine()
        if t == 1 and self.view is None:
            self.load.wait()
        if t < n - 1:
            self.ends(t)
            for side, place, d in ((0, c, n - 1 - t + c), (1, n - 1 - c, t + c - (n - 1))):
                here = (place >= 1) & (place <= t)
                self.arrived(here, self.move(side, d, self.boxed(side, d)))

                @pl.when(here)
                def _(side=side, d=d):
                    for p in range(self.count):
                        total = self.piece(mine, d, p).astype(F32)
                        total = total + box[side, self.clip(d), p].astype(F32)
                        box[side, self.clip(d), p] = total.astype(BF16)

                self.when(here, self.move(side, d, self.boxed(side, d)))
        self.at += 1

    def finish(self):
        if self.done:
            return
        self.done = True
        c, n = self.c, self.groups
        while self.at < n - 1:
            self.step()
        box, mine = self.ref("box"), self.mine()
        above, below = c >= 1, c + 1 < n
        self.arrived(above, self.move(0, c, self.boxed(0, c)))
        self.arrived(below, self.move(1, c, self.boxed(1, c)))
        for p in range(self.count):
            first = jnp.where(c >= 1, 0, 1)
            total = self.piece(mine, c, p).astype(F32) + box[first, c, p].astype(F32)
            self.ref("sum")[p] = total.astype(BF16)

            @pl.when(above & below)
            def _(p=p, total=total):
                self.ref("sum")[p] = (total + box[1, c, p].astype(F32)).astype(BF16)

    def drain(self):
        wait_both(self.sent)


def others(row):
    for k in range(1, 8):
        ps = lax.rem(row.s + k // 4, 2)
        low = row.rx if k % 2 else row.r
        pr = lax.rem(low + 2 * ((k // 2) % 2), 4)
        yield k, ps, pr


class Swap:
    def __init__(self, tag):
        self.tag = tag

    def declare(self, scratch):
        scratch[self.tag + "send"] = pltpu.SemaphoreType.DMA((8,))
        scratch[self.tag + "recv"] = pltpu.SemaphoreType.DMA((8,))
        scratch[self.tag + "own"] = pltpu.SemaphoreType.DMA((1,))

    def start(self, ns, row, own, lanes, src, dst, to_tokens):
        send, recv, local = (getattr(ns, self.tag + a) for a in ("send", "recv", "own"))

        def tokens_of(s, r):
            return pl.ds(pl.multiple_of((s * 4 + r) * own, 16), own)

        def lanes_of(s, r):
            return pl.ds(pl.multiple_of((r * 2 + s) * lanes, 128), lanes)

        def ends(ps, pr):
            if to_tokens:
                return src.at[:, tokens_of(ps, pr), :], dst.at[:, :, lanes_of(row.s, row.r)]
            return src.at[:, :, lanes_of(ps, pr)], dst.at[:, tokens_of(row.s, row.r), :]

        a, b = ends(row.s, row.r)
        self.mine = pltpu.make_async_copy(a, b, local.at[0])
        self.mine.start()
        self.copies = []
        for k, ps, pr in others(row):
            a, b = ends(ps, pr)
            copy = pltpu.make_async_remote_copy(
                src_ref=a,
                dst_ref=b,
                send_sem=send.at[k],
                recv_sem=recv.at[k],
                device_id=(ps, pr, row.c),
                device_id_type=MESH,
            )
            copy.start()
            self.copies.append(copy)

    def wait(self):
        for copy in self.copies:
            copy.wait_recv()
        self.mine.wait()

    def drain(self):
        for copy in self.copies:
            copy.wait_send()


def plane_peers(row):
    return [
        (ps, pr, row.c) for k, ps, pr in others(row) if k not in (1, 2, 4)
    ]


def gather_first(row, full, micros):
    row.ag_pass(full, 0)
    if micros > 1:
        row.ag_pass(full, 1)
    row.ag_diag(full, 0)


def gather_more(row, full, micros, m):
    if m + 2 < micros:
        row.ag_pass(full, m + 2)
    if m + 1 < micros:
        row.ag_diag(full, m + 1)


def tail(row, micros, result, hook, between=()):
    more = list(between)

    def step():
        if more:
            more.pop(0)()

    step()
    row.rs_transit(micros - 2)
    row.rs_pair(micros - 1)
    for m in range(micros - 2):
        step()
        result(m)
    hook("tail")
    step()
    row.rs_transit(micros - 1)
    result(micros - 2)
    while more:
        step()
    hook("last")
    result(micros - 1)


def ffn_forward(p, row, loc, cfg, hook, deliver):
    micros, rows, full = cfg.micros, cfg.rows, p.full
    gather_first(row, full, micros)
    for m in range(micros):
        row.ag_wait(full, m)
        hook("gathered", m)
        if m >= 1:
            row.rs_pair(m - 1)
        if m >= 2:
            row.rs_transit(m - 2)
        here = pl.ds(m * rows, rows)
        loc.start(full.at[here, :], p.xin_o.at[here, :])
        gate = dot(full[here, :], p.gate_dst[0])
        lift = dot(full[here, :], p.up_dst[0])
        p.gp[here, :] = gate.astype(BF16)
        p.up[here, :] = lift.astype(BF16)
        p.act[here, :] = (gate * jax.nn.sigmoid(gate) * lift).astype(BF16)
        hook("acted", m)
        row.part[here, :] = dot(p.act[here, :], p.down_dst[0], 1, 1).astype(BF16)
        for a, b in ((p.gp, p.gp_o), (p.up, p.up_o), (p.act, p.act_o)):
            loc.start(a.at[here, :], b.at[here, :])
        row.rs_start(m)
        gather_more(row, full, micros, m)
        hook("computed", m)
    tail(row, micros, lambda m: deliver(m, row.rs_result(m)), hook)


def ffn_backward(p, row, loc, cfg, hook, loads, late, deliver):
    micros, rows, width, full = cfg.micros, cfg.rows, cfg.width, p.full
    gather_first(row, full, micros)
    for copy in loads:
        loc.wait(copy)
    for m in range(micros):
        row.ag_wait(full, m)
        hook("gathered", m)
        if m >= 1:
            row.rs_pair(m - 1)
        if m >= 2:
            row.rs_transit(m - 2)
        here = pl.ds(m * rows, rows)
        d_act = dot(full[here, :], p.w[2])
        gate = p.gp[here, :].astype(F32)
        lift = p.up[here, :].astype(F32)
        sig = jax.nn.sigmoid(gate)
        silu = gate * sig
        p.dg[here, :] = (d_act * lift * (sig + silu * (1.0 - sig))).astype(BF16)
        p.du[here, :] = (d_act * silu).astype(BF16)
        total = dot(p.dg[here, :], p.w[0], 1, 1) + dot(p.du[here, :], p.w[1], 1, 1)
        row.part[here, :] = total.astype(BF16)
        row.rs_start(m)
        gather_more(row, full, micros, m)
        hook("computed", m)

    def grad(i, left, right):
        def body():
            if i == 2:
                for copy in late:
                    loc.wait(copy)

            @pl.loop(0, width // 256)
            def _(t):
                at = pl.ds(pl.multiple_of(t * 256, 256), 256)
                p.grad[i, at, :] = dot(left[:, at], right[...], 0, 0).astype(BF16)

            hook("grad", i)

        return body

    grads = [grad(2, full, p.act), grad(0, p.xin, p.dg), grad(1, p.xin, p.du)]
    tail(row, micros, lambda m: deliver(m, row.rs_result(m)), hook, grads)


def pair_masks(size):
    rows_at = lax.broadcasted_iota(jnp.int32, (size, size), 0)
    cols_at = lax.broadcasted_iota(jnp.int32, (size, size), 1)
    return (rows_at >= cols_at) & (rows_at // BLOCK == cols_at // BLOCK)


def gate_columns(gates, columns):
    count, size = gates.shape
    rows_at = lax.broadcasted_iota(jnp.int32, (size, size), 0)
    cols_at = lax.broadcasted_iota(jnp.int32, (size, size), 1)
    for i in range(count):
        spread = jnp.where(rows_at == cols_at, gates[i : i + 1, :], 0.0)
        columns[i * size : (i + 1) * size, :] = jnp.sum(spread, axis=1, keepdims=True)


def gain_row(k, cfg, layer, kind):
    rows_each = cfg.width // 4 // 128
    pieces = [
        k.gains[layer, r, kind * rows_each + h : kind * rows_each + h + 1, :]
        for r in range(4)
        for h in range(rows_each)
    ]
    return jnp.concatenate(pieces, axis=1)


class Heads:
    def __init__(self, k, row, cfg, layer):
        self.k, self.row, self.cfg, self.layer = k, row, cfg, layer

    def persist(self):
        k, cfg = self.k, self.cfg
        out = []
        for kind in range(2):
            start = pl.multiple_of(8 + (2 * kind + self.row.s) * 8, 8)
            for j in range(cfg.groups):
                block = k.line[self.layer, j, pl.ds(start, 8), :]
                k.persist[j * cfg.per : (j + 1) * cfg.per, :] = block[: cfg.per, :]
            out.append(k.persist[...].astype(BF16))
        return out

    def keeps(self, j):
        decays = self.k.line[self.layer, j, 40:48, :] * self.k.starts[j]
        return jnp.where(self.row.s == 0, decays[0:1, :], decays[1:2, :])

    def own(self):
        keeps = self.keeps(self.row.c)
        blocks = self.cfg.blocks

        def of(m, b):
            return keeps[:, m * blocks + b : m * blocks + b + 1]

        return of

    def through(self, m, j):
        keeps = self.keeps(j)
        product = None
        for b in range(self.cfg.blocks):
            at = m * self.cfg.blocks + b
            one = keeps[:, at : at + 1]
            product = one if product is None else product * one
        return product


def pair_probs(q, k, pk, mask, scale):
    inner = jnp.where(mask, dot(q, k, 1, 1) * scale, -1e30)
    outer = dot(q, pk, 1, 1) * scale
    top = jnp.maximum(
        jnp.max(inner, axis=1, keepdims=True), jnp.max(outer, axis=1, keepdims=True)
    )
    inner = jnp.exp(inner - top)
    outer = jnp.exp(outer - top)
    norm = 1.0 / (jnp.sum(inner, axis=1, keepdims=True) + jnp.sum(outer, axis=1, keepdims=True))
    return inner * norm, outer * norm


class States:
    def __init__(self, row, groups, k, backward):
        self.backward, self.sent = backward, []
        self.row, self.groups, self.mine, self.box = row, groups, k.leaving, k.box
        self.send, self.recv, self.entering = k.ssend, k.srecv, k.entering

    def copy(self, m, k):
        n = self.groups
        to = self.row.c + (-k if self.backward else k)
        return pltpu.make_async_remote_copy(
            src_ref=self.mine.at[m],
            dst_ref=self.box.at[m, k],
            send_sem=self.send.at[m, k],
            recv_sem=self.recv.at[m, k],
            device_id=(self.row.s, self.row.r, jnp.clip(to, 0, n - 1)),
            device_id_type=MESH,
        )

    def after(self, k):
        c, n = self.row.c, self.groups
        return (c >= k) if self.backward else (c + k < n)

    def before(self, k):
        c, n = self.row.c, self.groups
        return (c + k < n) if self.backward else (c >= k)

    def start(self, m):
        for k in range(1, self.groups):

            @pl.when(self.after(k))
            def _(k=k):
                self.copy(m, k).start()

            self.sent.append((self.after(k), self.copy(m, k)))

    def wait(self, m):
        for k in range(1, self.groups):

            @pl.when(self.before(k))
            def _(k=k):
                self.copy(m, k).wait_recv()

    def drain(self):
        wait_both(self.sent)

    def fold(self, m, through):
        entering = self.entering
        entering[...] = jnp.zeros_like(entering)
        for k in range(self.groups - 1, 0, -1):

            @pl.when(self.before(k))
            def _(k=k):
                source = self.row.c + (k if self.backward else -k)
                factor = through(m, jnp.clip(source, 0, self.groups - 1))
                entering[...] = factor * entering[...] + self.box[m, k].astype(F32)


def attn_forward(p, row, loc, cfg, hook, layer, loads, deliver):
    micros, rows, size, full = cfg.micros, cfg.rows, cfg.size, p.full
    blocks = rows // BLOCK
    factor = size ** (-0.5)
    states = States(row, cfg.groups, p, False)
    qs, ks, vs = (pl.ds(i * size, size) for i in range(3))
    mask = pair_masks(2 * BLOCK)
    gather_first(row, full, micros)
    gate_columns(p.gates[layer, 0 : micros * rows // 128, :], p.gate)
    heads = Heads(p, row, cfg, layer)
    pk, pv = heads.persist()
    keep = heads.own()
    for copy in loads:
        loc.wait(copy)
    for m in range(micros):
        row.ag_wait(full, m)
        hook("gathered", m)
        here = pl.ds(m * rows, rows)
        loc.start(full.at[here, :], p.xin_o.at[here, :])
        p.qkv[here, :] = dot(full[here, :], p.wq[0]).astype(BF16)
        loc.start(p.qkv.at[here, :], p.qkv_o.at[here, :])
        total = jnp.zeros((size, size), F32)
        for b in range(blocks):
            at = pl.ds(m * rows + b * BLOCK, BLOCK)
            keys = (p.qkv[at, ks].astype(F32) * p.gate[at, :]).astype(BF16)
            fresh = dot(keys, p.qkv[at, vs], 0, 0)
            p.update[m * blocks + b] = fresh
            total = keep(m, b) * total + fresh
        p.leaving[m] = total.astype(BF16)
        states.start(m)
        gather_more(row, full, micros, m)
        hook("states", m)
    for m in range(micros):
        here = pl.ds(m * rows, rows)
        states.wait(m)
        states.fold(m, heads.through)
        memory = p.entering[...]
        for b in range(0, blocks, 2):
            at = pl.ds(m * rows + b * BLOCK, 2 * BLOCK)
            q, ky, v = p.qkv[at, qs], p.qkv[at, ks], p.qkv[at, vs]
            inner, outer = pair_probs(q, ky, pk, mask, factor)
            value = dot(inner.astype(BF16), v) + dot(outer.astype(BF16), pv)
            reads = []
            for i in range(2):
                now = keep(m, b + i) * memory
                low = now.astype(BF16)
                p.state[m * blocks + b + i] = low
                reads.append(dot(q[i * BLOCK : (i + 1) * BLOCK, :], low) * factor)
                memory = now + p.update[m * blocks + b + i]
            p.mixed[at, :] = (value + jnp.concatenate(reads, axis=0)).astype(BF16)
        hook("mixed", m)
        row.part[here, :] = dot(p.mixed[here, :], p.wo_dst[0], 1, 1).astype(BF16)
        loc.start(p.mixed.at[here, :], p.mixed_o.at[here, :])
        row.rs_start(m)
        if m >= 1:
            row.rs_pair(m - 1)
        if m >= 2:
            row.rs_transit(m - 2)
        hook("computed", m)
    loc.start(p.state, p.state_o)
    tail(row, micros, lambda m: deliver(m, row.rs_result(m)), hook)
    states.drain()


def attn_backward(p, row, loc, cfg, hook, layer, loads, late, deliver):
    micros, rows, size, width, full = cfg.micros, cfg.rows, cfg.size, cfg.width, p.full
    blocks = rows // BLOCK
    factor = size ** (-0.5)
    states = States(row, cfg.groups, p, True)
    qs, ks, vs = (pl.ds(i * size, size) for i in range(3))
    in_cols, out_cols = pl.ds(0, 3 * size), pl.ds(3 * size, size)
    mask = pair_masks(2 * BLOCK)
    p.dpersist[...] = jnp.zeros_like(p.dpersist)
    gate_columns(p.gates[layer, 0 : micros * rows // 128, :], p.gate)
    heads = Heads(p, row, cfg, layer)
    pk, pv = heads.persist()
    keep = heads.own()
    gather_first(row, full, micros)
    for copy in loads:
        loc.wait(copy)
    for m in range(micros):
        row.ag_wait(full, m)
        hook("gathered", m)
        here = pl.ds(m * rows, rows)
        p.dmix[here, :] = dot(full[here, :], p.wo[0]).astype(BF16)
        total = jnp.zeros((size, size), F32)
        for b in reversed(range(blocks)):
            at = pl.ds(m * rows + b * BLOCK, BLOCK)
            fresh = dot(p.qkv[at, qs], p.dmix[at, :], 0, 0) * factor
            p.update[m * blocks + b] = fresh
            total = keep(m, b) * (fresh + total)
        p.leaving[m] = total.astype(BF16)
        states.start(m)
        gather_more(row, full, micros, m)
        hook("states", m)
    for m in range(micros):
        here = pl.ds(m * rows, rows)
        states.wait(m)
        states.fold(m, heads.through)
        memory = p.entering[...]
        for b in reversed(range(0, blocks, 2)):
            at = pl.ds(m * rows + b * BLOCK, 2 * BLOCK)
            q, ky, v, d = p.qkv[at, qs], p.qkv[at, ks], p.qkv[at, vs], p.dmix[at, :]
            inner, outer = pair_probs(q, ky, pk, mask, factor)
            d_inner = dot(d, v, 1, 1)
            d_outer = dot(d, pv, 1, 1)
            centre = jnp.sum(inner * d_inner, axis=1, keepdims=True) + jnp.sum(
                outer * d_outer, axis=1, keepdims=True
            )
            d_inner = (inner * (d_inner - centre)).astype(BF16)
            d_outer = (outer * (d_outer - centre)).astype(BF16)
            inner, outer = inner.astype(BF16), outer.astype(BF16)
            p.dpersist[0] += dot(d_outer, q, 0, 0) * factor
            p.dpersist[1] += dot(outer, d, 0, 0)
            dq = dot(d_inner, ky) + dot(d_outer, pk)
            dk = dot(d_inner, q, 0, 0) * factor
            dv = dot(inner, d, 0, 0)
            keys = (ky.astype(F32) * p.gate[at, :]).astype(BF16)
            parts = [None, None]
            for i in (1, 0):
                sub = slice(i * BLOCK, (i + 1) * BLOCK)
                low = memory.astype(BF16)
                parts[i] = (
                    dot(d[sub, :], p.state[m * blocks + b + i], 1, 1),
                    dot(v[sub, :], low, 1, 1),
                    dot(keys[sub, :], low),
                )
                memory = keep(m, b + i) * (p.update[m * blocks + b + i] + memory)
            more_q, more_k, more_v = (jnp.concatenate(pieces, axis=0) for pieces in zip(*parts))
            p.dqkv[at, qs] = ((dq + more_q) * factor).astype(BF16)
            p.dqkv[at, ks] = (dk + p.gate[at, :] * more_k).astype(BF16)
            p.dqkv[at, vs] = (dv + more_v).astype(BF16)
        row.part[here, :] = dot(p.dqkv[here, :], p.wq[0], 1, 1).astype(BF16)
        row.rs_start(m)
        if m >= 1:
            row.rs_pair(m - 1)
        if m >= 2:
            row.rs_transit(m - 2)
        hook("computed", m)

    def out_grad():
        for copy in late:
            loc.wait(copy)

        @pl.loop(0, width // 256)
        def _(t):
            at = pl.ds(pl.multiple_of(t * 256, 256), 256)
            p.grad[0, at, out_cols] = dot(full[:, at], p.mixed[...], 0, 0).astype(BF16)

    def qkv_grad():
        @pl.loop(0, width // 256)
        def _(t):
            at = pl.ds(pl.multiple_of(t * 256, 256), 256)
            p.grad[0, at, in_cols] = dot(p.xin[:, at], p.dqkv[...], 0, 0).astype(BF16)

        hook("grads")

    tail(row, micros, lambda m: deliver(m, row.rs_result(m)), hook, [out_grad, qkv_grad])
    states.drain()


VM = pl.BlockSpec(memory_space=pltpu.VMEM)
SM = pl.BlockSpec(memory_space=pltpu.SMEM)
HB = pl.BlockSpec(memory_space=pl.ANY)


def vm(dims, dtype=BF16):
    return pltpu.VMEM(dims, dtype)


def launch(name, collective, body, ins, outs, scratch):
    names = list(ins) + list(outs) + list(scratch)

    def kernel(*refs):
        body(SimpleNamespace(**dict(zip(names, refs))))

    results = pl.pallas_call(
        kernel,
        out_shape=tuple(jax.ShapeDtypeStruct(d, t) for d, t, _ in outs.values()),
        in_specs=[spec for _, spec in ins.values()],
        out_specs=tuple(spec for _, _, spec in outs.values()),
        scratch_shapes=list(scratch.values()),
        compiler_params=pltpu.CompilerParams(
            collective_id=collective, has_side_effects=True, vmem_limit_bytes=VMEM_LIMIT
        ),
        name=name,
    )(*[a for a, _ in ins.values()])
    return SimpleNamespace(**dict(zip(outs, results)))


def local(
    tokens, cotangent, block_order, lengths, decay, write_gate, gain_attn, w_query, w_key, w_value,
    persist_key, persist_value, w_output, gain_ffn, w_gate, w_up, w_down,
):
    sec, row_id, col = (lax.axis_index(a) for a in ("section", "row", "col"))
    groups = lax.axis_size("col")
    micros, rows, features = tokens.shape
    width = features * 4
    own, blocks, all_rows, size = rows // 8, rows // BLOCK, micros * rows, features // 2
    ffh = w_gate.shape[2] // 2
    per = persist_key.shape[1]
    persist = per * groups
    cfg = SimpleNamespace(
        micros=micros, rows=rows, own=own, size=size, width=width, groups=groups, blocks=blocks, per=per
    )
    total_blocks = block_order.shape[1]
    positions = jnp.arange(total_blocks, dtype=jnp.int32)
    my_blocks = col * blocks + jnp.arange(blocks, dtype=jnp.int32)
    deal_picks = lax.dynamic_slice_in_dim(block_order, col * blocks, blocks, 1)
    matches = (block_order[:, :, None] == my_blocks[None, None, :]).astype(jnp.int32)
    back_picks = jnp.sum(matches * positions[None, :, None], axis=1)

    def lanes(a):
        return jnp.pad(a, ((0, 0),) * (a.ndim - 1) + ((0, 128 - a.shape[-1]),))

    def eights(a):
        return jnp.pad(a, ((0, 0),) * (a.ndim - 2) + ((0, -a.shape[-2] % 8), (0, 0)))

    share = gain_attn.shape[1]
    own_gains = jnp.concatenate([gain_attn, gain_ffn], axis=0).astype(F32)
    placed = lax.dynamic_update_slice(
        jnp.zeros((2, features), F32), own_gains, (jnp.zeros_like(col), col * share)
    )
    packed = jnp.concatenate(
        [eights(placed.reshape(-1, 128))]
        + [
            eights(a[0].reshape(per, 2, size).transpose(1, 0, 2)).reshape(16, size).astype(F32)
            for a in (persist_key, persist_value)
        ]
        + [eights(lanes(decay[0].transpose(2, 0, 1).reshape(2, -1)))],
        axis=0,
    )
    gate_rows = eights(write_gate[0].transpose(2, 0, 1).reshape(2, -1, 128)) / BLOCK
    ends = jnp.cumsum(lengths, axis=1)
    is_start = jnp.any(positions[None, :, None] == (ends - lengths)[:, None, :], axis=2)
    starts = jnp.where(is_start, 0.0, 1.0).reshape(micros, groups, blocks).transpose(1, 0, 2)
    starts = jnp.broadcast_to(lanes(starts.reshape(groups, -1))[:, None], (groups, 8, 128))

    def cols_split(w):
        return w.reshape(w.shape[0], 2, -1).transpose(1, 0, 2)

    def rows_split(w):
        return w.reshape(2, -1, w.shape[1]).transpose(0, 2, 1)

    blocks_a = jnp.concatenate(
        [cols_split(w[0]) for w in (w_query, w_key, w_value)] + [rows_split(w_output[0])], axis=2
    )[:, None]
    blocks_b = jnp.stack(
        [cols_split(w_gate[0]), cols_split(w_up[0]), rows_split(w_down[0])], axis=1
    )

    a_dims, b_dims = blocks_a.shape[1:], blocks_b.shape[1:]
    q_dims, o_dims, one_dims = (1, a_dims[1], 3 * size), (1, a_dims[1], size), (1,) + b_dims[1:]
    grad_a_dims, grad_b_dims = (1, width, 4 * size), (3, width, ffh)
    stage_dims = (micros, rows, size)
    by_block = (micros, blocks, BLOCK, size)
    gain_rows = 4 * width // 128
    half_gains = width // 128
    hbm = lambda dims, dtype=BF16: (dims, dtype, HB)

    def row_scratch(prefix):
        return {
            "part": vm((all_rows, width)),
            "pair": vm((micros, 4 * own, width)),
            "both": vm((micros, 4, own, width)),
            "transit": vm((micros, 2, own, width // 2)),
            "final": vm((micros, 2, own, width)),
            prefix + "send": pltpu.SemaphoreType.DMA((micros, N_AG + N_RS)),
            prefix + "recv": pltpu.SemaphoreType.DMA((micros, N_AG + N_RS)),
            prefix + "full": vm((all_rows, width)),
        }

    def attn_scratch(prefix):
        names = dict(
            update=vm((micros * blocks, size, size), F32),
            entering=vm((size, size), F32),
            leaving=vm((micros, size, size)),
            box=vm((micros, groups, size, size)),
            ssend=pltpu.SemaphoreType.DMA((micros, groups)),
            srecv=pltpu.SemaphoreType.DMA((micros, groups)),
            gate=vm((all_rows, 1), F32),
            persist=vm((persist, size), F32),
            qkv=vm((all_rows, 3 * size)),
            state=vm((micros * blocks, size, size)),
            mixed=vm((all_rows, size)),
        )
        return {**row_scratch(prefix), **{prefix + a: b for a, b in names.items()}}

    def ffn_scratch(prefix):
        names = {a: vm((all_rows, ffh)) for a in ("gp", "up", "act")}
        return {**row_scratch(prefix), **{prefix + a: b for a, b in names.items()}}

    def view_of(k, prefix, **more):
        names = {a[len(prefix) :]: b for a, b in vars(k).items() if a.startswith(prefix)}
        return SimpleNamespace(**{**names, **more})

    def rows_of(k, prefix):
        p = view_of(k, prefix)
        row = Rows(rows, own, width, p.send, p.recv)
        row.buffers = (k.part, k.pair, k.both, k.transit, k.final)
        row.part = k.part
        return row

    def greet_all(row):
        row.greet(
            plane_peers(row)
            + [(row.s, row.r, lax.rem(row.c + i, groups)) for i in range(1, groups)]
        )

    def hooks(plan, prefix):
        def hook(point, at=""):
            for action in plan.get(prefix + point + str(at), ()):
                action()

        return hook

    def pusher(send, recv):
        def push(src, dst, i, to):
            copy = pltpu.make_async_remote_copy(
                src_ref=src,
                dst_ref=dst,
                send_sem=send.at[i],
                recv_sem=recv.at[i],
                device_id=to,
                device_id_type=MESH,
            )
            copy.start()
            return copy

        return push

    def blocks_from(buf, picks, stage, m, lead=()):
        for b in range(blocks):
            stage[lead + (m, pl.ds(b * BLOCK, BLOCK))] = buf[lead + (m, picks[m, b])]

    def forward_names(l):
        outs = dict(
            a_xin_o=hbm((all_rows, width)),
            a_qkv_o=hbm((all_rows, 3 * size)),
            a_state_o=hbm((micros * blocks, size, size)),
            a_mixed_o=hbm((all_rows, size)),
            f_xin_o=hbm((all_rows, width)),
            f_gp_o=hbm((all_rows, ffh)),
            f_up_o=hbm((all_rows, ffh)),
            f_act_o=hbm((all_rows, ffh)),
            wo_o=hbm((1, width, size)),
            w_o=hbm((3, width, ffh)),
            mid=((micros, own, width), F32, VM),
            y=((micros, own, width), BF16, VM),
        )
        return outs, {**attn_scratch("a_"), **ffn_scratch("f_")}

    def forward_layer(k, l, x, wq, loc, loads, plan, row_a, small):
        row_f = rows_of(k, "f_")
        gain_f = gain_row(small, cfg, l, 1)

        def middle(m, summed):
            k.mid[m] = x[m].astype(F32) + summed
            norm_to(k.f_full, gain_f, k.mid[m], row_f.span(m, row_f.s, row_f.r))
            row_f.ag_start(k.f_full, m)

        def leave(m, summed):
            k.y[m] = (k.mid[m] + summed).astype(BF16)

        p = view_of(k, "a_", wq=wq, wo_dst=k.wo_dst, **vars(small))
        attn_forward(p, row_a, loc, cfg, hooks(plan, "a_"), l, loads, middle)
        row_a.finish()
        loc.start(k.wo_dst, k.wo_o)
        p = view_of(k, "f_", gate_dst=k.gate_dst, up_dst=k.up_dst, down_dst=k.down_dst)
        ffn_forward(p, row_f, loc, cfg, hooks(plan, "f_"), leave)
        for i, w in enumerate((k.gate_dst, k.up_dst, k.down_dst)):
            loc.start(w, k.w_o.at[pl.ds(i, 1)])
        return row_f

    def one_b(tag, layer, which, array):
        view = None
        if array is None:
            view = lambda k, row: k.shards_b.at[layer, pl.ds(which, 1)]
        else:
            view = lambda k, row: getattr(k, tag + "src").at[layer, pl.ds(which, 1)]
        return Gather(tag, array, one_dims, groups, 1, view, "scratch")

    def q_of(ref, layer):
        return ref.at[layer, :, :, pl.ds(0, 3 * size)]

    def o_of(ref, layer):
        return ref.at[layer, :, :, pl.ds(3 * size, size)]

    def lanes_of_core(name):
        def view(k, row):
            mine = pl.ds(pl.multiple_of(row.s * size, 128), size)
            return getattr(k, name).at[:, :, :, mine]

        return view

    tokens_b = tokens.reshape(micros, blocks, BLOCK, features)
    cotangent_b = cotangent.reshape(micros, blocks, BLOCK, features)
    deal = Gather("deal_", tokens_b, by_block, groups, 1, lanes_of_core("deal_src"), "scratch")
    q0 = Gather("q0_", None, q_dims, groups, 1, lambda k, row: q_of(k.shards_a, 0), "scratch")
    wo0 = Gather("wo_", None, o_dims, groups, 1, lambda k, row: o_of(k.shards_a, 0), "scratch")
    gate0, up0, down0 = (one_b(t, 0, i, None) for i, t in enumerate(("gate_", "up_", "down_")))
    q1 = Gather("q1_", None, q_dims, groups, 1, lambda k, row: q_of(k.shards_a, 1))
    sides1 = [deal, q0, wo0, gate0, up0, down0, q1]
    swap1 = Swap("swap_")

    def first_body(k):
        row = rows_of(k, "a_")
        loc = Local(k.sems)
        greet_all(row)
        for side in sides1:
            side.bind(k, row, groups)
        push = pusher(k.psend, k.precv)
        crossing, keeps_here = [], []
        for i, (src, dst) in enumerate(((k.blocks_a, k.shards_a), (k.blocks_b, k.shards_b))):
            keeps_here.append(loc.start(src.at[row.s], dst.at[row.s]))
            crossing.append(push(src.at[1 - row.s], dst.at[row.s], groups + 9 + i, row.sib))
        deal.start()
        k.line[row.s, row.c] = k.packed[...]
        k.gates[row.s] = k.gate_rows[row.s]
        small = [
            push(
                k.packed,
                k.line.at[row.s, row.c],
                i,
                (row.s, row.r, lax.rem(row.c + i, groups)),
            )
            for i in range(1, groups)
        ]
        late = [push(k.gate_rows.at[1 - row.s], k.gates.at[row.s], 0, row.sib)]
        crossing[0].wait_recv()
        loc.wait(keeps_here[0])
        q0.start()
        deal.step()
        for copy in small:
            copy.wait_recv()
        total = k.line[row.s, 0, 0:8, :]
        for j in range(1, groups):
            total = total + k.line[row.s, j, 0:8, :]
        k.gains[row.s, row.r] = total
        for i, ps, pr in others(row):
            mine = k.gains.at[row.s, row.r]
            late.append(push(mine, mine, groups + i, (ps, pr, row.c)))
        late.append(push(k.line.at[row.s], k.line.at[row.s], groups + 8, row.sib))
        crossing[1].wait_recv()
        loc.wait(keeps_here[1])
        q0.step()
        wo0.start()
        deal.step()
        q0.step()
        gate0.start()
        up0.start()
        wo0.step()
        deal.finish()
        for m in range(micros):
            blocks_from(k.deal_dst, k.picks, k.stage, m)
        swap1.start(k, row, own, size, k.stage, k.x, True)
        q0.finish()
        wo0.step()
        for copy in late:
            copy.wait_recv()
        gain = gain_row(k, cfg, 0, 0)
        swap1.wait()
        for m in range(micros):
            norm_to(k.a_full, gain, k.x[m].astype(F32), row.span(m, row.s, row.r))
            row.ag_start(k.a_full, m)
        loc.start(k.q0_dst, k.q0_o)
        plan = dict(
            a_gathered0=[gate0.step, up0.step, down0.start],
            a_states2=[gate0.step, up0.step],
            a_mixed0=[wo0.finish],
            a_computed1=[down0.step],
            a_tail=[down0.step],
            f_gathered0=[gate0.finish, up0.finish],
            f_acted0=[down0.finish, q1.start],
            f_computed1=[q1.step],
            f_tail=[q1.step],
        )
        small_refs = SimpleNamespace(line=k.line, gains=k.gains, gates=k.gates, starts=k.starts)
        row_f = forward_layer(k, 0, k.x, k.q0_dst, loc, [], plan, row, small_refs)
        for side in sides1:
            side.finish()
        for copy in crossing + small + late:
            copy.wait_send()
        row.finish()
        row_f.finish()
        for side in sides1:
            side.drain()
        swap1.drain()
        loc.finish()

    outs, scratch = forward_names(0)
    ins = dict(
        picks=(deal_picks, SM),
        blocks_a=(blocks_a, HB),
        blocks_b=(blocks_b, HB),
        packed=(packed, VM),
        gate_rows=(gate_rows, VM),
        starts=(starts, VM),
    )
    outs.update(
        x=((micros, own, width), BF16, VM),
        shards_a=hbm(blocks_a.shape),
        shards_b=hbm(blocks_b.shape),
        line=((2, groups) + packed.shape, F32, VM),
        gains=((2, 4, 8, 128), F32, VM),
        gates=((2,) + gate_rows.shape[1:], F32, VM),
        q0_o=hbm((1, width, 3 * size)),
    )
    scratch.update(
        stage=vm(stage_dims),
        psend=pltpu.SemaphoreType.DMA((groups + 11,)),
        precv=pltpu.SemaphoreType.DMA((groups + 11,)),
        sems=pltpu.SemaphoreType.DMA((48,)),
    )
    for side in sides1:
        side.declare(ins, outs, scratch, groups)
    swap1.declare(scratch)
    f0 = launch("forward_0", 0, first_body, ins, outs, scratch)

    smalls = dict(
        line=(f0.line, VM), gains=(f0.gains, VM), gates=(f0.gates, VM),
        starts=(starts, VM),
    )

    def small_of(k):
        return SimpleNamespace(line=k.line, gains=k.gains, gates=k.gates, starts=k.starts)

    wo1 = Gather("wo_", f0.shards_a, o_dims, groups, 1, lambda k, row: o_of(k.wo_src, 1), "scratch")
    gate1, up1, down1 = (one_b(t, 1, i, f0.shards_b) for i, t in enumerate(("gate_", "up_", "down_")))
    cot = Gather("cot_", cotangent_b, by_block, groups, 1, lanes_of_core("cot_src"), "scratch")
    sides2 = [wo1, gate1, up1, down1, cot]
    swap_y, swap_c = Swap("swapy_"), Swap("swapc_")

    def second_body(k):
        row = rows_of(k, "a_")
        loc = Local(k.sems)
        loads = [loc.start(k.q_h, k.wq)]
        gain = gain_row(k, cfg, 1, 0)
        for m in range(micros):
            norm_to(k.a_full, gain, k.x[m].astype(F32), row.span(m, row.s, row.r))
        greet_all(row)
        for side in sides2:
            side.bind(k, row, groups)
        for m in range(micros):
            row.ag_start(k.a_full, m)
        for side in (wo1, gate1, up1):
            side.start()
        swap_y.start(k, row, own, size, k.x, k.stage_o, False)

        def deal_cot():
            cot.finish()
            for m in range(micros):
                blocks_from(k.cot_dst, k.picks, k.stage, m)
            swap_c.start(k, row, own, size, k.stage, k.dy, True)

        plan = dict(
            a_states0=[wo1.step, gate1.step],
            a_states1=[wo1.step],
            a_states2=[up1.step, down1.start],
            a_mixed0=[wo1.finish],
            a_computed0=[gate1.step],
            a_computed1=[up1.step, down1.step],
            a_tail=[down1.step, cot.start],
            f_gathered0=[gate1.finish, up1.finish],
            f_acted0=[down1.finish],
            f_computed0=[cot.step],
            f_computed2=[cot.step],
            f_last=[deal_cot],
        )
        row_f = forward_layer(k, 1, k.x, k.wq, loc, loads, plan, row, small_of(k))
        for side in sides2:
            side.finish()
        swap_y.wait()
        swap_c.wait()
        row.finish()
        row_f.finish()
        for side in sides2 + [swap_y, swap_c]:
            side.drain()
        loc.finish()

    outs, scratch = forward_names(1)
    ins = dict(x=(f0.y, VM), q_h=(f0.q1_dst, HB), picks=(deal_picks, SM), **smalls)
    outs.update(dy=((micros, own, width), BF16, VM), stage_o=hbm(stage_dims))
    scratch.update(
        stage=vm(stage_dims), wq=vm((1, width, 3 * size)), sems=pltpu.SemaphoreType.DMA((48,))
    )
    for side in sides2:
        side.declare(ins, outs, scratch, groups)
    swap_y.declare(scratch)
    swap_c.declare(scratch)
    f1 = launch("forward_1", 1, second_body, ins, outs, scratch)

    def backward_names(kept, dy, x, wq):
        ins = dict(
            dy=(dy, VM), mid=(kept.mid, VM), x=(x, VM), w_h=(kept.w_o, HB),
            wo_h=(kept.wo_o, HB), wq_h=(wq, HB), ax_h=(kept.a_xin_o, HB),
            qkv_h=(kept.a_qkv_o, HB), state_h=(kept.a_state_o, HB),
            mixed_h=(kept.a_mixed_o, HB), fx_h=(kept.f_xin_o, HB), gp_h=(kept.f_gp_o, HB),
            up_h=(kept.f_up_o, HB), act_h=(kept.f_act_o, HB), **smalls,
        )
        scratch = {**attn_scratch("a_"), **ffn_scratch("f_")}
        scratch.update(
            f_w=vm((3, width, ffh)), xin=vm((all_rows, width)),
            f_dg=vm((all_rows, ffh)), f_du=vm((all_rows, ffh)), f_grad=vm(grad_b_dims),
            a_wo=vm((1, width, size)), a_wq=vm((1, width, 3 * size)),
            a_dmix=vm((all_rows, size)),
            a_dqkv=vm((all_rows, 3 * size)), a_grad=vm(grad_a_dims),
            dmid=vm((micros, own, width), F32), sems=pltpu.SemaphoreType.DMA((48,)),
        )
        return ins, scratch

    def backward_layer(k, l, loc, sides, swaps_begin, plan, dx_done):
        row_f, row_a = rows_of(k, "f_"), rows_of(k, "a_")
        first = [
            loc.start(a, b) for a, b in ((k.w_h, k.f_w), (k.gp_h, k.f_gp), (k.up_h, k.f_up))
        ]
        late_f = [loc.start(a, b) for a, b in ((k.act_h, k.f_act), (k.fx_h, k.xin))]
        loads_a = [
            loc.start(a, b)
            for a, b in (
                (k.wo_h, k.a_wo), (k.qkv_h, k.a_qkv), (k.wq_h, k.a_wq), (k.state_h, k.a_state)
            )
        ]
        late_a = [loc.start(k.mixed_h, k.a_mixed)]
        for m in range(micros):
            k.f_full[row_f.span(m, row_f.s, row_f.r), :] = k.dy[m]
        greet_all(row_f)
        for side in sides:
            side.bind(k, row_f, groups)
        for m in range(micros):
            row_f.ag_start(k.f_full, m)
        swaps_begin(row_f)
        gain_a, gain_f = gain_row(k, cfg, l, 0), gain_row(k, cfg, l, 1)
        k.dgain[...] = jnp.zeros_like(k.dgain)

        def middle(m, summed):
            back, gains = norm_back(k.mid[m], gain_f, summed)
            k.dmid[m] = k.dy[m].astype(F32) + back
            k.dgain[1:2, :] += gains
            k.a_full[row_a.span(m, row_a.s, row_a.r), :] = k.dmid[m].astype(BF16)
            row_a.ag_start(k.a_full, m)

        def leave(m, summed):
            back, gains = norm_back(k.x[m].astype(F32), gain_a, summed)
            k.dx[m] = (k.dmid[m] + back).astype(BF16)
            k.dgain[0:1, :] += gains
            dx_done(m)

        ffn_backward(view_of(k, "f_", xin=k.xin), row_f, loc, cfg, hooks(plan, "f_"), first, late_f, middle)
        row_f.finish()
        late_a.append(loc.start(k.ax_h, k.xin))
        p = view_of(k, "a_", dpersist=k.dpersist, xin=k.xin, **vars(small_of(k)))
        attn_backward(p, row_a, loc, cfg, hooks(plan, "a_"), l, loads_a, late_a, leave)
        return row_f, row_a

    def staged(tag, array, home=None):
        return Gather(tag, array.reshape(by_block), by_block, groups, 1, None, home)

    def grad_of(k):
        return k.f_grad

    y0 = staged("y0_", f1.stage_o)
    y1 = Gather("y1_", None, stage_dims, groups, 1, lambda k, row: k.stage)
    td1, tg1 = (Total(t, None, grad_b_dims, groups, (i, 1), grad_of) for t, i in (("td_", 2), ("tg_", 0)))
    sides3 = [y0, y1, td1, tg1]
    swap_y1 = Swap("swap_")

    def third_body(k):
        loc = Local(k.sems)

        def begin(row):
            y0.start()
            swap_y1.start(k, row, own, size, k.y, k.stage, False)

        plan = dict(
            f_computed0=[y0.step],
            f_computed2=[y0.step, swap_y1.wait, y1.start],
            f_grad1=[td1.start],
            a_states2=[y1.step, td1.step, tg1.start],
            a_computed1=[td1.step, y1.step, tg1.step],
            a_tail=[tg1.step],
        )
        row_f, row_a = backward_layer(k, 1, loc, sides3, begin, plan, lambda m: None)
        for i in range(3):
            loc.start(k.f_grad.at[i], k.grad_b_o.at[i])
        loc.start(k.a_grad, k.grad_a_o)
        for side in sides3:
            side.finish()
        row_f.finish()
        row_a.finish()
        for side in sides3 + [swap_y1]:
            side.drain()
        loc.finish()

    ins, scratch = backward_names(f1, f1.dy, f0.y, f0.q1_dst)
    ins["y"] = (f1.y, VM)
    small_outs = dict(
        dgain=((2, width), F32, VM),
        dpersist=((2, persist, size), F32, VM),
        dx=((micros, own, width), BF16, VM),
    )
    outs = dict(grad_a_o=hbm(grad_a_dims), grad_b_o=hbm(grad_b_dims), **small_outs)
    scratch["stage"] = vm(stage_dims)
    for side in sides3:
        side.declare(ins, outs, scratch, groups)
    swap_y1.declare(scratch)
    b1 = launch("backward_1", 2, third_body, ins, outs, scratch)

    small_rows = gain_rows + 4 * persist
    tu1 = Total("tu1_", b1.grad_b_o, grad_b_dims, groups, (1, 1), None, "scratch")
    ta1 = Total("ta1_", b1.grad_a_o, grad_a_dims, groups, (0, 1), None, "scratch")
    td0, tg0, tu0 = (
        Total(t, None, grad_b_dims, groups, (i, 1), grad_of, "scratch")
        for t, i in (("td_", 2), ("tg_", 0), ("tu_", 1))
    )
    ta0 = Total("ta0_", None, grad_a_dims, groups, (0, 1), lambda k: k.a_grad, "scratch")
    g1 = Gather("g1_", None, by_block, groups, 1, lambda k, row: k.staged1)
    g0 = [
        Gather(f"g0{m}_", None, by_block[1:], groups, 0, lambda k, row, m=m: k.staged0.at[m], "scratch")
        for m in range(micros)
    ]

    def blocked(stage, staged, m):
        for b in range(blocks):
            staged[m, b] = stage[m, b * BLOCK : (b + 1) * BLOCK, :]
    sides4 = [tu1, ta1, td0, tg0, tu0, ta0, g1, *g0]
    swap_g1, swaps0 = Swap("swap_"), [Swap(f"swap{m}_") for m in range(micros)]

    def last_body(k):
        loc = Local(k.sems)
        push = pusher(k.psend, k.precv)
        load_y = loc.start(k.y0_buf, k.whole)
        loads = [
            loc.start(a, b)
            for a, b in (
                (k.bg1, k.res_b.at[1, pl.ds(0, 1)]), (k.bd1, k.res_b.at[1, pl.ds(2, 1)]),
            )
        ]

        def begin(row):
            tu1.start()
            ta1.start()
            swap_g1.start(k, row, own, size, k.dy, k.stage, False)

        def start_g1():
            swap_g1.wait()
            for m in range(micros):
                blocked(k.stage, k.staged1, m)
            g1.start()

        def dx_done(m):
            row = ta0.row
            swaps0[m].start(
                k, row, own, size, k.dx.at[pl.ds(m, 1)], k.stage0.at[pl.ds(m, 1)], False
            )

        plan = dict(
            f_gathered0=[tu1.step, ta1.step],
            f_computed0=[start_g1],
            f_computed1=[tu1.step, ta1.step],
            f_computed2=[g1.step],
            f_grad1=[td0.start],
            a_states2=[g1.step, td0.step, tg0.start, tu0.start],
            a_computed1=[td0.step, tg0.step, tu0.step],
            a_computed2=[tg0.step, tu0.step],
            a_grads=[ta0.start],
        )
        row_f, row = backward_layer(k, 0, loc, sides4, begin, plan, dx_done)
        for m in range(micros - 1):
            swaps0[m].wait()
            blocked(k.stage0, k.staged0, m)
            g0[m].start()
        for i in range(half_gains):
            lanes_here = slice(i * 128, (i + 1) * 128)
            for j, ref in enumerate((k.dgain, k.dgain1)):
                for kind in range(2):
                    at = (j * 2 + kind) * half_gains + i
                    k.smalls[at : at + 1, :] = ref[kind : kind + 1, lanes_here]
        for j, ref in enumerate((k.dpersist, k.dpersist1)):
            for kind in range(2):
                at = gain_rows + (j * 2 + kind) * persist
                k.smalls[at : at + persist, :] = ref[kind]
        swaps0[-1].wait()
        blocked(k.stage0, k.staged0, micros - 1)
        g0[-1].start()
        pushes = []
        for i in range(1, groups):
            to = (row.s, row.r, lax.rem(row.c + i, groups))
            pushes.append(push(k.smalls, k.small_box.at[i], i, to))
        for copy in loads:
            loc.wait(copy)

        def all_restored(slot):
            for m in range(micros):
                for b in range(blocks):
                    where = pl.ds(b * BLOCK, BLOCK)
                    k.halves[slot, m, where, :] = k.whole[m, k.back[m, b]]

        loc.wait(load_y)
        all_restored(0)
        loc.wait(loc.start(k.y1_buf, k.whole))
        all_restored(1)
        moved, kept_here = [], []
        mine_lanes = pl.ds(pl.multiple_of(row.s * size, 128), size)

        def give(i, pair, out):
            moved.append(push(pair.at[1 - row.s], out, groups + 8 + i, row.sib))
            kept_here.append(loc.start(pair.at[row.s], out))

        give(0, k.halves.at[pl.ds(0, 2)], k.acts_o.at[:, :, mine_lanes])

        for g in g0:
            g.step()
        ta0.step()
        g1.finish()
        loc.wait(loc.start(k.g1_dst, k.whole))
        all_restored(3)
        for g in g0:
            g.step()
        ta0.step()
        for total in (td0, tg0, tu0, tu1, ta1):
            total.finish()
        k.res_b[0, pl.ds(2, 1)] = k.td_sum[...]
        k.res_b[0, pl.ds(0, 1)] = k.tg_sum[...]
        k.res_b[0, pl.ds(1, 1)] = k.tu_sum[...]
        k.res_b[1, pl.ds(1, 1)] = k.tu1_sum[...]
        k.res_a[1] = k.ta1_sum[...]
        give(1, k.res_b, k.grad_b.at[row.s])
        for copy in pushes:
            copy.wait_recv()
        total = k.smalls[...]
        for i in range(1, groups):
            total = total + k.small_box[i]
        k.small_sum[...] = total
        gains = []
        for i, ps, pr in others(row):
            src = k.small_sum.at[pl.ds(0, gain_rows), :]
            gains.append(push(src, k.gain_box.at[i], groups + i, (ps, pr, row.c)))
        ta0.finish()
        k.res_a[0] = k.ta0_sum[...]
        give(2, k.res_a, k.grad_a.at[row.s])
        for m, g in enumerate(g0):
            g.finish()
            buf = getattr(k, f"g0{m}_dst")
            for b in range(blocks):
                k.halves[2, m, pl.ds(b * BLOCK, BLOCK), :] = buf[k.back[m, b]]
        give(3, k.halves.at[pl.ds(2, 2)], k.grads_o.at[:, :, mine_lanes])
        for copy in gains:
            copy.wait_recv()
        total = k.small_sum[0:gain_rows, :]
        for i in range(1, 8):
            total = total + k.gain_box[i]
        k.gain_o[...] = total
        k.persist_o[...] = k.small_sum[gain_rows:, :]
        for copy in moved:
            copy.wait()
        for copy in pushes + gains:
            copy.wait_send()
        for side in sides4:
            side.finish()
        row_f.finish()
        row.finish()
        for side in sides4 + [swap_g1] + swaps0:
            side.drain()
        loc.finish()

    ins, scratch = backward_names(f0, b1.dx, f0.x, f0.q0_o)
    ins.update(
        y0_buf=(b1.y0_dst, HB),
        y1_buf=(b1.y1_dst.reshape(b1.y0_dst.shape), HB),
        bg1=(b1.tg_sum, HB),
        bd1=(b1.td_sum, HB),
        dgain1=(b1.dgain, VM),
        dpersist1=(b1.dpersist, VM),
        back=(back_picks, SM),
    )
    outs = dict(
        acts_o=((micros, rows, features), BF16, VM),
        grads_o=((micros, rows, features), BF16, VM),
        grad_a=((2,) + ta0.dims, BF16, VM),
        grad_b=((2, 3) + tu0.dims[1:], BF16, VM),
        gain_o=((gain_rows, 128), F32, VM),
        persist_o=((4 * persist, 128), F32, VM),
    )
    scratch.update(
        stage=vm(stage_dims),
        stage0=vm(stage_dims),
        whole=vm((micros, total_blocks, BLOCK, size)),
        staged0=vm(by_block),
        staged1=vm(by_block),
        halves=vm((4,) + stage_dims),
        res_a=vm((2,) + ta0.dims),
        res_b=vm((2, 3) + tu0.dims[1:]),
        smalls=vm((small_rows, 128), F32),
        small_box=vm((groups, small_rows, 128), F32),
        small_sum=vm((small_rows, 128), F32),
        gain_box=vm((8, gain_rows, 128), F32),
        dgain=vm((2, width), F32),
        dpersist=vm((2, persist, size), F32),
        dx=vm((micros, own, width)),
        psend=pltpu.SemaphoreType.DMA((groups + 12,)),
        precv=pltpu.SemaphoreType.DMA((groups + 12,)),
    )
    for side in sides4:
        side.declare(ins, outs, scratch, groups)
    for swap in [swap_g1] + swaps0:
        swap.declare(scratch)
    closed = launch("backward_0", 3, last_body, ins, outs, scratch)

    def cols_join(pair):
        return jnp.concatenate([pair[0], pair[1]], axis=1).astype(F32)[None]

    def rows_join(pair):
        return jnp.concatenate([pair[0].T, pair[1].T], axis=0).astype(F32)[None]

    grad_a, grad_b = closed.grad_a[:, 0], closed.grad_b
    heads = [cols_join(grad_a[:, :, i * size : (i + 1) * size]) for i in range(3)]
    grad_out = rows_join(grad_a[:, :, 3 * size :])
    grad_gate, grad_up = cols_join(grad_b[:, 0]), cols_join(grad_b[:, 1])
    grad_down = rows_join(grad_b[:, 2])
    gain_sum = closed.gain_o.reshape(2, 2, width)
    my_gain = lax.dynamic_slice_in_dim(
        lax.dynamic_index_in_dim(gain_sum, sec, 0, False), (row_id * groups + col) * share, share, 1
    )
    persist_sum = closed.persist_o.reshape(2, 2, persist, size)
    persist_sum = lax.dynamic_slice_in_dim(persist_sum, col * per, per, 2)
    mine_p = lax.dynamic_index_in_dim(persist_sum, sec, 0, False)
    got_p = lax.ppermute(
        lax.dynamic_index_in_dim(persist_sum, 1 - sec, 0, False), "section", [(0, 1), (1, 0)]
    )
    grad_persist = jnp.concatenate(
        [jnp.where(sec == 0, mine_p, got_p), jnp.where(sec == 0, got_p, mine_p)], axis=2
    )
    return (
        closed.acts_o[None],
        closed.grads_o[None],
        my_gain[0][None],
        heads[0],
        heads[1],
        heads[2],
        grad_persist[0][None],
        grad_persist[1][None],
        grad_out,
        my_gain[1][None],
        grad_gate,
        grad_up,
        grad_down,
    )


def solution(mesh):
    weight = P("section", "col", "row")
    across = P("section", "row", "col")
    gain = P("section", ("row", "col"))
    rows = P("section", None, "col", "row")
    return jax.shard_map(
        local,
        mesh=mesh,
        in_specs=(
            P(None, "col", "row"), P(None, "col", "row"), P(), P(), rows, rows, gain, weight, weight,
            weight, weight, weight, across, gain, weight, weight, across,
        ),
        out_specs=(
            rows, rows, gain, weight, weight, weight, weight, weight, across, gain, weight, weight,
            across,
        ),
        check_vma=False,
    )
```

```python
from types import SimpleNamespace

import jax
import jax.numpy as jnp
from jax import lax
from jax.experimental import pallas as pl
from jax.experimental.pallas import tpu as pltpu
from jax.sharding import PartitionSpec as P

BLOCK = 64
EPS = 1e-06
MESH = pl.DeviceIdType.MESH
F32 = jnp.float32
BF16 = jnp.bfloat16
VMEM_LIMIT = 60 << 20
N_AG, N_RS = 8, 7

A, F = 0, 100
PLACES = dict(
    first=[
        A, A + 10, A + 30, A + 21, A + 12, A + 32, A + 41, A + 41, F + 31, F + 32,
    ],
    second=[
        A, A + 21, A + 2, A, A + 12, A + 41, A + 30, A + 32, A + 40, A + 41,
        F + 11, F + 32, F + 41,
    ],
    third=[
        F + 30, F + 32, F + 30, F + 52, F + 52, F + 50, A + 2, A + 32, A + 12, A + 31,
        A + 32,
    ],
    last=[
        F + 40, F, F, A + 31, F + 31, F + 40, F + 50, A + 10, A + 30, F + 50,
        F + 51, A + 31, A + 1, A + 2, A + 40, A + 30, A + 60,
    ],
)


def place(points, actions, fixed=()):
    plan = {}
    for point, action in list(zip(points, actions, strict=True)) + list(fixed):
        plan.setdefault(point, []).append(action)
    return plan


def dot(a, b, ca=1, cb=0):
    return lax.dot_general(a, b, (((ca,), (cb,)), ((), ())), preferred_element_type=F32)


class Rows:
    def __init__(self, rows, own, width, send, recv):
        self.rows, self.own, self.width, self.half = rows, own, width, width // 2
        self.send, self.recv = send, recv
        self.s, self.r, self.c = (lax.axis_index(a) for a in ("section", "row", "col"))
        self.rx = self.r + 1 - 2 * lax.rem(self.r, 2)
        self.ry = lax.rem(self.r + 2, 4)
        self.rd = lax.rem(self.rx + 2, 4)
        self.x = (self.s, self.rx, self.c)
        self.y = (self.s, self.ry, self.c)
        self.sib = (1 - self.s, self.r, self.c)
        self.started = []

    def greet(self, others=()):
        barrier = pltpu.get_barrier_semaphore()
        peers = [self.x, self.y, self.sib] + list(others)
        for peer in peers:
            pl.semaphore_signal(barrier, inc=1, device_id=peer, device_id_type=MESH)
        pl.semaphore_wait(barrier, len(peers))

    def copy(self, src, dst, m, k, peer):
        return pltpu.make_async_remote_copy(
            src_ref=src,
            dst_ref=dst,
            send_sem=self.send.at[m, k],
            recv_sem=self.recv.at[m, k],
            device_id=peer,
            device_id_type=MESH,
        )

    def go(self, copy):
        copy.start()
        self.started.append(copy)

    def finish(self):
        for copy in self.started:
            copy.wait_send()
        self.started = []

    def span(self, m, s, r):
        return pl.ds(pl.multiple_of(m * self.rows + (s * 4 + r) * self.own, 16), self.own)

    def ag_copy(self, full, m, k):
        left, right = pl.ds(0, self.half), pl.ds(self.half, self.half)
        mine, atx, aty, atd = (
            self.span(m, self.s, r) for r in (self.r, self.rx, self.ry, self.rd)
        )
        if k == 0:
            return self.copy(full.at[mine, :], full.at[mine, :], m, 0, self.x)
        if k == 1:
            return self.copy(full.at[mine, :], full.at[mine, :], m, 1, self.y)
        if k == 2:
            return self.copy(full.at[mine, :], full.at[mine, :], m, 2, self.sib)
        if k == 3:
            return self.copy(full.at[atx, left], full.at[atx, left], m, 3, self.y)
        if k == 4:
            return self.copy(full.at[aty, right], full.at[aty, right], m, 4, self.x)
        if k == 5:
            return self.copy(full.at[atx, :], full.at[atx, :], m, 5, self.sib)
        if k == 6:
            return self.copy(full.at[aty, :], full.at[aty, :], m, 6, self.sib)
        return self.copy(full.at[atd, :], full.at[atd, :], m, 7, self.sib)

    def ag_start(self, full, m):
        for k in (0, 1, 2):
            self.go(self.ag_copy(full, m, k))

    def ag_pass(self, full, m):
        self.ag_copy(full, m, 0).wait_recv()
        self.go(self.ag_copy(full, m, 3))
        self.go(self.ag_copy(full, m, 5))
        self.ag_copy(full, m, 1).wait_recv()
        self.go(self.ag_copy(full, m, 4))
        self.go(self.ag_copy(full, m, 6))

    def ag_diag(self, full, m):
        self.ag_copy(full, m, 3).wait_recv()
        self.ag_copy(full, m, 4).wait_recv()
        self.go(self.ag_copy(full, m, 7))

    def ag_wait(self, full, m):
        for k in (2, 5, 6, 7):
            self.ag_copy(full, m, k).wait_recv()

    def rs_copy(self, m, k):
        part, pair, both, transit, final = self.buffers
        left, right = pl.ds(0, self.half), pl.ds(self.half, self.half)
        if k == 8:
            other = pl.ds(
                pl.multiple_of(m * self.rows + (1 - self.s) * 4 * self.own, 16), 4 * self.own
            )
            return self.copy(part.at[other, :], pair.at[m], m, 8, self.sib)
        if k == 9:
            return self.copy(both.at[m, self.rd, :, left], transit.at[m, 0], m, 9, self.x)
        if k == 10:
            return self.copy(both.at[m, self.rd, :, right], transit.at[m, 1], m, 10, self.y)
        if k == 11:
            return self.copy(both.at[m, self.rx, :, left], final.at[m, 0, :, left], m, 11, self.x)
        if k == 12:
            return self.copy(both.at[m, self.ry, :, right], final.at[m, 1, :, right], m, 12, self.y)
        if k == 13:
            return self.copy(both.at[m, self.ry, :, left], final.at[m, 1, :, left], m, 13, self.y)
        return self.copy(both.at[m, self.rx, :, right], final.at[m, 0, :, right], m, 14, self.x)

    def rs_start(self, m):
        self.go(self.rs_copy(m, 8))

    def rs_pair(self, m):
        part, pair, both, _, _ = self.buffers
        self.rs_copy(m, 8).wait_recv()
        for r in range(4):
            mine = part[self.span(m, self.s, r), :].astype(F32)
            theirs = pair[m, r * self.own : (r + 1) * self.own, :].astype(F32)
            both[m, r] = (mine + theirs).astype(BF16)
        for k in (9, 10, 11, 12):
            self.go(self.rs_copy(m, k))

    def rs_transit(self, m):
        _, _, both, transit, _ = self.buffers
        left, right = pl.ds(0, self.half), pl.ds(self.half, self.half)
        self.rs_copy(m, 9).wait_recv()
        total = both[m, self.ry, :, left].astype(F32) + transit[m, 0].astype(F32)
        both[m, self.ry, :, left] = total.astype(BF16)
        self.go(self.rs_copy(m, 13))
        self.rs_copy(m, 10).wait_recv()
        total = both[m, self.rx, :, right].astype(F32) + transit[m, 1].astype(F32)
        both[m, self.rx, :, right] = total.astype(BF16)
        self.go(self.rs_copy(m, 14))

    def rs_result(self, m):
        _, _, both, _, final = self.buffers
        for k in (11, 12, 13, 14):
            self.rs_copy(m, k).wait_recv()
        return both[m, self.r].astype(F32) + final[m, 0].astype(F32) + final[m, 1].astype(F32)


class Local:
    def __init__(self, sems):
        self.sems, self.used, self.open = sems, 0, []

    def start(self, src, dst):
        copy = pltpu.make_async_copy(src, dst, self.sems.at[self.used])
        self.used += 1
        copy.start()
        self.open.append(copy)
        return copy

    def wait(self, copy):
        copy.wait()
        self.open = [other for other in self.open if other is not copy]

    def finish(self):
        for copy in list(self.open):
            copy.wait()


def inv_rms(values):
    return lax.rsqrt(jnp.mean(values * values, axis=1, keepdims=True) + EPS)


def norm_to(full, gain, values, span):
    full[span, :] = (values * inv_rms(values) * gain).astype(BF16)


def norm_back(values, gain, grad):
    scale = inv_rms(values)
    weighted = grad * gain
    inner = jnp.mean(weighted * values, axis=1, keepdims=True)
    back = scale * weighted - values * (scale * scale * scale * inner)
    return back, jnp.sum(grad * values * scale, axis=0, keepdims=True)


def wait_both(copies):
    for condition, copy in copies:

        @pl.when(condition)
        def _(copy=copy):
            copy.wait_send()


class Side:
    def __init__(self, tag):
        self.tag = tag

    def ref(self, name):
        return getattr(self.ns, self.tag + name)

    def bind(self, ns, row, groups):
        self.ns, self.row, self.c, self.groups = ns, row, row.c, groups
        self.sent = []

    def when(self, condition, copy):
        @pl.when(condition)
        def _():
            copy.start()

        self.sent.append((condition, copy))

    def arrived(self, condition, copy):
        @pl.when(condition)
        def _():
            copy.wait_recv()

    def remote(self, src, dst, send, recv, to):
        return pltpu.make_async_remote_copy(
            src_ref=src,
            dst_ref=dst,
            send_sem=send,
            recv_sem=recv,
            device_id=(self.row.s, self.row.r, to),
            device_id_type=MESH,
        )


def part_of(ref, at, per, axis):
    where = pl.ds(pl.multiple_of(at * per, per), per)
    return ref.at[(slice(None),) * axis + (where,)]


class Gather(Side):
    def __init__(self, tag, array, dims, groups, axis, view=None, home=None):
        super().__init__(tag)
        self.array, self.axis, self.view, self.home = array, axis, view, home
        self.per = dims[axis]
        self.dims = dims[:axis] + (dims[axis] * groups,) + dims[axis + 1 :]

    def declare(self, ins, outs, scratch, groups):
        if self.array is not None:
            ins[self.tag + "src"] = (self.array, HB)
        if self.home is None:
            outs[self.tag + "dst"] = (self.dims, BF16, HB)
        else:
            scratch[self.tag + "dst"] = pltpu.VMEM(self.dims, BF16)
        scratch[self.tag + "send"] = pltpu.SemaphoreType.DMA((2, groups))
        scratch[self.tag + "recv"] = pltpu.SemaphoreType.DMA((groups,))
        scratch[self.tag + "own"] = pltpu.SemaphoreType.DMA((1,))

    def slot(self, j):
        return part_of(self.ref("dst"), jnp.clip(j, 0, self.groups - 1), self.per, self.axis)

    def source(self):
        return self.view(self.ns, self.row) if self.view else self.ref("src")

    def move(self, j, side, src=None):
        to = jnp.clip(self.c + (1 - 2 * side), 0, self.groups - 1)
        j = jnp.clip(j, 0, self.groups - 1)
        src = self.slot(j) if src is None else src
        return self.remote(
            src, self.slot(j), self.ref("send").at[side, j], self.ref("recv").at[j], to
        )

    def start(self):
        c, n = self.c, self.groups
        self.at, self.done = 1, False
        self.own = pltpu.make_async_copy(self.source(), self.slot(c), self.ref("own").at[0])
        self.own.start()
        self.when(c + 1 < n, self.move(c, 0, self.source()))
        self.when(c >= 1, self.move(c, 1, self.source()))

    def step(self):
        c, n, k = self.c, self.groups, self.at
        if k < n:
            self.arrived(c >= k, self.move(c - k, 0))
            self.arrived(c + k < n, self.move(c + k, 1))
            if k < n - 1:
                self.when((c >= k) & (c + 1 < n), self.move(c - k, 0))
                self.when((c + k < n) & (c >= 1), self.move(c + k, 1))
        self.at += 1

    def finish(self):
        if not self.done:
            while self.at < self.groups:
                self.step()
            self.own.wait()
            self.done = True

    def drain(self):
        wait_both(self.sent)


class Total(Side):
    def __init__(self, tag, parts, dims, groups, span, view=None, home=None):
        super().__init__(tag)
        self.parts, self.span, self.view, self.home = parts, span, view, home
        self.per = dims[1] // groups
        self.count = span[1]
        self.dims = (self.count, self.per, dims[2])

    def declare(self, ins, outs, scratch, groups):
        if self.home is None:
            outs[self.tag + "sum"] = (self.dims, BF16, VM)
        else:
            scratch[self.tag + "sum"] = pltpu.VMEM(self.dims, BF16)
        if self.view is None:
            ins[self.tag + "parts"] = (self.parts, HB)
            whole = (self.count, self.per * groups, self.dims[2])
            scratch[self.tag + "mine"] = pltpu.VMEM(whole, BF16)
        scratch[self.tag + "box"] = pltpu.VMEM((2, groups) + self.dims, BF16)
        scratch[self.tag + "send"] = pltpu.SemaphoreType.DMA((2, groups))
        scratch[self.tag + "recv"] = pltpu.SemaphoreType.DMA((2, groups))
        scratch[self.tag + "load"] = pltpu.SemaphoreType.DMA((1,))

    def clip(self, j):
        return jnp.clip(j, 0, self.groups - 1)

    def piece(self, ref, d, p=None):
        d = self.clip(d)
        where = pl.ds(pl.multiple_of(d * self.per, self.per), self.per)
        if p is None:
            return ref.at[:, where, :]
        return ref[p + (self.span[0] if self.view else 0), where, :]

    def source(self):
        parts = self.view(self.ns) if self.view else self.ref("parts")
        return parts.at[pl.ds(*self.span)]

    def mine(self):
        return self.view(self.ns) if self.view else self.ref("mine")

    def move(self, side, d, src):
        d = self.clip(d)
        to = self.clip(self.c + (1 - 2 * side))
        return self.remote(
            src,
            self.ref("box").at[side, d],
            self.ref("send").at[side, d],
            self.ref("recv").at[side, d],
            to,
        )

    def boxed(self, side, d):
        return self.ref("box").at[side, self.clip(d)]

    def start(self):
        c, n = self.c, self.groups
        self.at, self.done = 1, False
        if self.view is None:
            self.load = pltpu.make_async_copy(
                self.source(), self.ref("mine"), self.ref("load").at[0]
            )
            self.load.start()
        self.ends(0)

    def ends(self, t):
        c, n = self.c, self.groups
        self.when(c == 0, self.move(0, n - 1 - t, self.piece(self.source(), n - 1 - t)))
        self.when(c == n - 1, self.move(1, t, self.piece(self.source(), t)))

    def step(self):
        c, n, t = self.c, self.groups, self.at
        box, mine = self.ref("box"), self.mine()
        if t == 1 and self.view is None:
            self.load.wait()
        if t < n - 1:
            self.ends(t)
            for side, place, d in ((0, c, n - 1 - t + c), (1, n - 1 - c, t + c - (n - 1))):
                here = (place >= 1) & (place <= t)
                self.arrived(here, self.move(side, d, self.boxed(side, d)))

                @pl.when(here)
                def _(side=side, d=d):
                    for p in range(self.count):
                        total = self.piece(mine, d, p).astype(F32)
                        total = total + box[side, self.clip(d), p].astype(F32)
                        box[side, self.clip(d), p] = total.astype(BF16)

                self.when(here, self.move(side, d, self.boxed(side, d)))
        self.at += 1

    def finish(self):
        if self.done:
            return
        self.done = True
        c, n = self.c, self.groups
        while self.at < n - 1:
            self.step()
        box, mine = self.ref("box"), self.mine()
        above, below = c >= 1, c + 1 < n
        self.arrived(above, self.move(0, c, self.boxed(0, c)))
        self.arrived(below, self.move(1, c, self.boxed(1, c)))
        for p in range(self.count):
            first = jnp.where(c >= 1, 0, 1)
            total = self.piece(mine, c, p).astype(F32) + box[first, c, p].astype(F32)
            self.ref("sum")[p] = total.astype(BF16)

            @pl.when(above & below)
            def _(p=p, total=total):
                self.ref("sum")[p] = (total + box[1, c, p].astype(F32)).astype(BF16)

    def drain(self):
        wait_both(self.sent)


def others(row):
    for k in range(1, 8):
        ps = lax.rem(row.s + k // 4, 2)
        low = row.rx if k % 2 else row.r
        pr = lax.rem(low + 2 * ((k // 2) % 2), 4)
        yield k, ps, pr


class Swap:
    def __init__(self, tag):
        self.tag = tag

    def declare(self, scratch):
        scratch[self.tag + "send"] = pltpu.SemaphoreType.DMA((8,))
        scratch[self.tag + "recv"] = pltpu.SemaphoreType.DMA((8,))
        scratch[self.tag + "own"] = pltpu.SemaphoreType.DMA((1,))

    def start(self, ns, row, own, lanes, src, dst, to_tokens):
        send, recv, local = (getattr(ns, self.tag + a) for a in ("send", "recv", "own"))

        def tokens_of(s, r):
            return pl.ds(pl.multiple_of((s * 4 + r) * own, 16), own)

        def lanes_of(s, r):
            return pl.ds(pl.multiple_of((r * 2 + s) * lanes, 128), lanes)

        def ends(ps, pr):
            if to_tokens:
                return src.at[:, tokens_of(ps, pr), :], dst.at[:, :, lanes_of(row.s, row.r)]
            return src.at[:, :, lanes_of(ps, pr)], dst.at[:, tokens_of(row.s, row.r), :]

        a, b = ends(row.s, row.r)
        self.mine = pltpu.make_async_copy(a, b, local.at[0])
        self.mine.start()
        self.copies = []
        for k, ps, pr in others(row):
            a, b = ends(ps, pr)
            copy = pltpu.make_async_remote_copy(
                src_ref=a,
                dst_ref=b,
                send_sem=send.at[k],
                recv_sem=recv.at[k],
                device_id=(ps, pr, row.c),
                device_id_type=MESH,
            )
            copy.start()
            self.copies.append(copy)

    def wait(self):
        for copy in self.copies:
            copy.wait_recv()
        self.mine.wait()

    def drain(self):
        for copy in self.copies:
            copy.wait_send()


def plane_peers(row):
    return [
        (ps, pr, row.c) for k, ps, pr in others(row) if k not in (1, 2, 4)
    ]


def gather_first(row, full, micros, fresh, fill=()):
    if fresh:
        row.ag_pass(full, 0)
        for m in range(2, micros):
            row.ag_start(full, m)
    for work in fill:
        work()
    row.ag_pass(full, 1)
    row.ag_diag(full, 0)


def ag_begin(row, full):
    row.ag_start(full, 0)
    row.ag_start(full, 1)


def gather_more(row, full, micros, m):
    if m + 2 < micros:
        row.ag_pass(full, m + 2)
    if m + 1 < micros:
        row.ag_diag(full, m + 1)


def tail(row, micros, result, hook, between=(), relay=None):
    more = list(between)

    def step():
        if more:
            more.pop(0)()

    row.rs_transit(micros - 2)
    for m in range(micros - 2):
        result(m)
    row.rs_pair(micros - 1)
    hook(40)
    step()
    result(micros - 2)
    row.rs_transit(micros - 1)
    if relay:
        relay()
    step()
    if relay is None:
        while more:
            step()
    hook(41)
    result(micros - 1)
    return more


def ffn_forward(p, row, loc, cfg, hook, deliver, relay=None):
    micros, rows, full = cfg.micros, cfg.rows, p.full
    gather_first(row, full, micros, False)
    for m in range(micros):
        row.ag_wait(full, m)
        hook(m)
        if m >= 1:
            row.rs_pair(m - 1)
        if m >= 2:
            row.rs_transit(m - 2)
        here = pl.ds(m * rows, rows)
        loc.start(full.at[here, :], p.xin_o.at[here, :])
        gate = dot(full[here, :], p.gate_dst[0])
        lift = dot(full[here, :], p.up_dst[0])
        p.gp[here, :] = gate.astype(BF16)
        p.up[here, :] = lift.astype(BF16)
        p.act[here, :] = (gate * jax.nn.sigmoid(gate) * lift).astype(BF16)
        hook(10 + m)
        row.part[here, :] = dot(p.act[here, :], p.down_dst[0], 1, 1).astype(BF16)
        for a, b in ((p.gp, p.gp_o), (p.up, p.up_o), (p.act, p.act_o)):
            loc.start(a.at[here, :], b.at[here, :])
        row.rs_start(m)
        gather_more(row, full, micros, m)
        hook(30 + m)
    tail(row, micros, lambda m: deliver(m, row.rs_result(m)), hook, (), relay)


def ffn_backward(p, row, loc, cfg, hook, loads, late, deliver, relay=None):
    micros, rows, width, full = cfg.micros, cfg.rows, cfg.width, p.full
    gather_first(row, full, micros, True)
    for copy in loads:
        loc.wait(copy)
    for m in range(micros):
        row.ag_wait(full, m)
        hook(m)
        if m >= 1:
            row.rs_pair(m - 1)
        if m >= 2:
            row.rs_transit(m - 2)
        here = pl.ds(m * rows, rows)
        d_act = dot(full[here, :], p.w[2])
        gate = p.gp[here, :].astype(F32)
        lift = p.up[here, :].astype(F32)
        sig = jax.nn.sigmoid(gate)
        silu = gate * sig
        p.dg[here, :] = (d_act * lift * (sig + silu * (1.0 - sig))).astype(BF16)
        p.du[here, :] = (d_act * silu).astype(BF16)
        total = dot(p.dg[here, :], p.w[0], 1, 1) + dot(p.du[here, :], p.w[1], 1, 1)
        row.part[here, :] = total.astype(BF16)
        row.rs_start(m)
        gather_more(row, full, micros, m)
        hook(30 + m)

    def grad(i, left, right):
        def body():
            if i == 2:
                for copy in late:
                    loc.wait(copy)

            @pl.loop(0, width // 256)
            def _(t):
                at = pl.ds(pl.multiple_of(t * 256, 256), 256)
                p.grad[i, at, :] = dot(left[:, at], right[...], 0, 0).astype(BF16)

            hook(50 + i)

        return body

    grads = [grad(2, full, p.act), grad(0, p.xin, p.dg), grad(1, p.xin, p.du)]
    return tail(row, micros, lambda m: deliver(m, row.rs_result(m)), hook, grads, relay)


def pair_masks(size):
    rows_at = lax.broadcasted_iota(jnp.int32, (size, size), 0)
    cols_at = lax.broadcasted_iota(jnp.int32, (size, size), 1)
    return (rows_at >= cols_at) & (rows_at // BLOCK == cols_at // BLOCK)


def gate_columns(gates, columns):
    count, size = gates.shape
    rows_at = lax.broadcasted_iota(jnp.int32, (size, size), 0)
    cols_at = lax.broadcasted_iota(jnp.int32, (size, size), 1)
    for i in range(count):
        spread = jnp.where(rows_at == cols_at, gates[i : i + 1, :], 0.0)
        columns[i * size : (i + 1) * size, :] = jnp.sum(spread, axis=1, keepdims=True)


def gain_row(k, cfg, layer, kind):
    rows_each = cfg.width // 4 // 128
    pieces = [
        k.gains[layer, r, kind * rows_each + h : kind * rows_each + h + 1, :]
        for r in range(4)
        for h in range(rows_each)
    ]
    return jnp.concatenate(pieces, axis=1)


class Heads:
    def __init__(self, k, row, cfg, layer):
        self.k, self.row, self.cfg, self.layer = k, row, cfg, layer

    def persist(self):
        k, cfg = self.k, self.cfg
        out = []
        for kind in range(2):
            start = pl.multiple_of(8 + (2 * kind + self.row.s) * 8, 8)
            for j in range(cfg.groups):
                block = k.line[self.layer, j, pl.ds(start, 8), :]
                k.persist[j * cfg.per : (j + 1) * cfg.per, :] = block[: cfg.per, :]
            out.append(k.persist[...].astype(BF16))
        return out

    def keeps(self, j):
        decays = self.k.line[self.layer, j, 40:48, :] * self.k.starts[j]
        return jnp.where(self.row.s == 0, decays[0:1, :], decays[1:2, :])

    def own(self):
        keeps = self.keeps(self.row.c)
        blocks = self.cfg.blocks

        def of(m, b):
            return keeps[:, m * blocks + b : m * blocks + b + 1]

        return of

    def through(self, m, j):
        keeps = self.keeps(j)
        product = None
        for b in range(self.cfg.blocks):
            at = m * self.cfg.blocks + b
            one = keeps[:, at : at + 1]
            product = one if product is None else product * one
        return product


def pair_probs(q, k, pk, mask, scale):
    inner = jnp.where(mask, dot(q, k, 1, 1) * scale, -1e30)
    outer = dot(q, pk, 1, 1) * scale
    top = jnp.maximum(
        jnp.max(inner, axis=1, keepdims=True), jnp.max(outer, axis=1, keepdims=True)
    )
    inner = jnp.exp(inner - top)
    outer = jnp.exp(outer - top)
    norm = 1.0 / (jnp.sum(inner, axis=1, keepdims=True) + jnp.sum(outer, axis=1, keepdims=True))
    return inner * norm, outer * norm


class States:
    def __init__(self, row, groups, k, backward):
        self.backward, self.sent = backward, []
        self.row, self.groups, self.mine, self.box = row, groups, k.leaving, k.box
        self.send, self.recv, self.entering = k.ssend, k.srecv, k.entering

    def copy(self, m, k):
        n = self.groups
        to = self.row.c + (-k if self.backward else k)
        return pltpu.make_async_remote_copy(
            src_ref=self.mine.at[m],
            dst_ref=self.box.at[m, k],
            send_sem=self.send.at[m, k],
            recv_sem=self.recv.at[m, k],
            device_id=(self.row.s, self.row.r, jnp.clip(to, 0, n - 1)),
            device_id_type=MESH,
        )

    def after(self, k):
        c, n = self.row.c, self.groups
        return (c >= k) if self.backward else (c + k < n)

    def before(self, k):
        c, n = self.row.c, self.groups
        return (c + k < n) if self.backward else (c >= k)

    def start(self, m):
        for k in range(1, self.groups):

            @pl.when(self.after(k))
            def _(k=k):
                self.copy(m, k).start()

            self.sent.append((self.after(k), self.copy(m, k)))

    def wait(self, m):
        for k in range(1, self.groups):

            @pl.when(self.before(k))
            def _(k=k):
                self.copy(m, k).wait_recv()

    def drain(self):
        wait_both(self.sent)

    def fold(self, m, through):
        entering = self.entering
        entering[...] = jnp.zeros_like(entering)
        for k in range(self.groups - 1, 0, -1):

            @pl.when(self.before(k))
            def _(k=k):
                source = self.row.c + (k if self.backward else -k)
                factor = through(m, jnp.clip(source, 0, self.groups - 1))
                entering[...] = factor * entering[...] + self.box[m, k].astype(F32)


def attn_forward(p, row, loc, cfg, hook, layer, loads, deliver, relay=None):
    micros, rows, size, full = cfg.micros, cfg.rows, cfg.size, p.full
    blocks = rows // BLOCK
    factor = size ** (-0.5)
    states = States(row, cfg.groups, p, False)
    qs, ks, vs = (pl.ds(i * size, size) for i in range(3))
    mask = pair_masks(2 * BLOCK)
    gather_first(row, full, micros, True)
    gate_columns(p.gates[layer, 0 : micros * rows // 128, :], p.gate)
    heads = Heads(p, row, cfg, layer)
    pk, pv = heads.persist()
    keep = heads.own()
    for copy in loads:
        loc.wait(copy)
    for m in range(micros):
        row.ag_wait(full, m)
        hook(m)
        here = pl.ds(m * rows, rows)
        loc.start(full.at[here, :], p.xin_o.at[here, :])
        p.qkv[here, :] = dot(full[here, :], p.wq[0]).astype(BF16)
        loc.start(p.qkv.at[here, :], p.qkv_o.at[here, :])
        total = jnp.zeros((size, size), F32)
        for b in range(blocks):
            at = pl.ds(m * rows + b * BLOCK, BLOCK)
            keys = (p.qkv[at, ks].astype(F32) * p.gate[at, :]).astype(BF16)
            fresh = dot(keys, p.qkv[at, vs], 0, 0)
            p.update[m * blocks + b] = fresh
            total = keep(m, b) * total + fresh
        p.leaving[m] = total.astype(BF16)
        states.start(m)
        gather_more(row, full, micros, m)
        hook(10 + m)
    for m in range(micros):
        here = pl.ds(m * rows, rows)
        states.wait(m)
        states.fold(m, heads.through)
        memory = p.entering[...]
        for b in range(0, blocks, 2):
            at = pl.ds(m * rows + b * BLOCK, 2 * BLOCK)
            q, ky, v = p.qkv[at, qs], p.qkv[at, ks], p.qkv[at, vs]
            inner, outer = pair_probs(q, ky, pk, mask, factor)
            value = dot(inner.astype(BF16), v) + dot(outer.astype(BF16), pv)
            reads = []
            for i in range(2):
                now = keep(m, b + i) * memory
                low = now.astype(BF16)
                p.state[m * blocks + b + i] = low
                reads.append(dot(q[i * BLOCK : (i + 1) * BLOCK, :], low) * factor)
                memory = now + p.update[m * blocks + b + i]
            p.mixed[at, :] = (value + jnp.concatenate(reads, axis=0)).astype(BF16)
        hook(20 + m)
        row.part[here, :] = dot(p.mixed[here, :], p.wo_dst[0], 1, 1).astype(BF16)
        loc.start(p.mixed.at[here, :], p.mixed_o.at[here, :])
        row.rs_start(m)
        if m >= 1:
            row.rs_pair(m - 1)
        if m >= 2:
            row.rs_transit(m - 2)
        hook(30 + m)
    loc.start(p.state, p.state_o)
    tail(row, micros, lambda m: deliver(m, row.rs_result(m)), hook, (), relay)
    states.drain()


def attn_backward(p, row, loc, cfg, hook, layer, loads, late, deliver, fill, relay=None):
    micros, rows, size, width, full = cfg.micros, cfg.rows, cfg.size, cfg.width, p.full
    blocks = rows // BLOCK
    factor = size ** (-0.5)
    states = States(row, cfg.groups, p, True)
    qs, ks, vs = (pl.ds(i * size, size) for i in range(3))
    in_cols, out_cols = pl.ds(0, 3 * size), pl.ds(3 * size, size)
    mask = pair_masks(2 * BLOCK)
    p.dpersist[...] = jnp.zeros_like(p.dpersist)
    gate_columns(p.gates[layer, 0 : micros * rows // 128, :], p.gate)
    heads = Heads(p, row, cfg, layer)
    pk, pv = heads.persist()
    keep = heads.own()
    gather_first(row, full, micros, False, fill)
    for copy in loads:
        loc.wait(copy)
    for m in range(micros):
        row.ag_wait(full, m)
        hook(m)
        here = pl.ds(m * rows, rows)
        p.dmix[here, :] = dot(full[here, :], p.wo[0]).astype(BF16)
        total = jnp.zeros((size, size), F32)
        for b in reversed(range(blocks)):
            at = pl.ds(m * rows + b * BLOCK, BLOCK)
            fresh = dot(p.qkv[at, qs], p.dmix[at, :], 0, 0) * factor
            p.update[m * blocks + b] = fresh
            total = keep(m, b) * (fresh + total)
        p.leaving[m] = total.astype(BF16)
        states.start(m)
        gather_more(row, full, micros, m)
        hook(10 + m)
    for m in range(micros):
        here = pl.ds(m * rows, rows)
        states.wait(m)
        states.fold(m, heads.through)
        memory = p.entering[...]
        for b in reversed(range(0, blocks, 2)):
            at = pl.ds(m * rows + b * BLOCK, 2 * BLOCK)
            q, ky, v, d = p.qkv[at, qs], p.qkv[at, ks], p.qkv[at, vs], p.dmix[at, :]
            inner, outer = pair_probs(q, ky, pk, mask, factor)
            d_inner = dot(d, v, 1, 1)
            d_outer = dot(d, pv, 1, 1)
            centre = jnp.sum(inner * d_inner, axis=1, keepdims=True) + jnp.sum(
                outer * d_outer, axis=1, keepdims=True
            )
            d_inner = (inner * (d_inner - centre)).astype(BF16)
            d_outer = (outer * (d_outer - centre)).astype(BF16)
            inner, outer = inner.astype(BF16), outer.astype(BF16)
            p.dpersist[0] += dot(d_outer, q, 0, 0) * factor
            p.dpersist[1] += dot(outer, d, 0, 0)
            dq = dot(d_inner, ky) + dot(d_outer, pk)
            dk = dot(d_inner, q, 0, 0) * factor
            dv = dot(inner, d, 0, 0)
            keys = (ky.astype(F32) * p.gate[at, :]).astype(BF16)
            parts = [None, None]
            for i in (1, 0):
                sub = slice(i * BLOCK, (i + 1) * BLOCK)
                low = memory.astype(BF16)
                parts[i] = (
                    dot(d[sub, :], p.state[m * blocks + b + i], 1, 1),
                    dot(v[sub, :], low, 1, 1),
                    dot(keys[sub, :], low),
                )
                memory = keep(m, b + i) * (p.update[m * blocks + b + i] + memory)
            more_q, more_k, more_v = (jnp.concatenate(pieces, axis=0) for pieces in zip(*parts))
            p.dqkv[at, qs] = ((dq + more_q) * factor).astype(BF16)
            p.dqkv[at, ks] = (dk + p.gate[at, :] * more_k).astype(BF16)
            p.dqkv[at, vs] = (dv + more_v).astype(BF16)
        row.part[here, :] = dot(p.dqkv[here, :], p.wq[0], 1, 1).astype(BF16)
        row.rs_start(m)
        if m >= 1:
            row.rs_pair(m - 1)
        if m >= 2:
            row.rs_transit(m - 2)
        hook(30 + m)

    def out_grad():
        for copy in late:
            loc.wait(copy)

        @pl.loop(0, width // 256)
        def _(t):
            at = pl.ds(pl.multiple_of(t * 256, 256), 256)
            p.grad[0, at, out_cols] = dot(full[:, at], p.mixed[...], 0, 0).astype(BF16)

    def qkv_grad():
        @pl.loop(0, width // 256)
        def _(t):
            at = pl.ds(pl.multiple_of(t * 256, 256), 256)
            p.grad[0, at, in_cols] = dot(p.xin[:, at], p.dqkv[...], 0, 0).astype(BF16)

        hook(60)

    tail(row, micros, lambda m: deliver(m, row.rs_result(m)), hook, [out_grad, qkv_grad], relay)
    states.drain()


VM = pl.BlockSpec(memory_space=pltpu.VMEM)
SM = pl.BlockSpec(memory_space=pltpu.SMEM)
HB = pl.BlockSpec(memory_space=pl.ANY)


def vm(dims, dtype=BF16):
    return pltpu.VMEM(dims, dtype)


def launch(name, collective, body, ins, outs, scratch):
    names = list(ins) + list(outs) + list(scratch)

    def kernel(*refs):
        body(SimpleNamespace(**dict(zip(names, refs))))

    results = pl.pallas_call(
        kernel,
        out_shape=tuple(jax.ShapeDtypeStruct(d, t) for d, t, _ in outs.values()),
        in_specs=[spec for _, spec in ins.values()],
        out_specs=tuple(spec for _, _, spec in outs.values()),
        scratch_shapes=list(scratch.values()),
        compiler_params=pltpu.CompilerParams(
            collective_id=collective, has_side_effects=True, vmem_limit_bytes=VMEM_LIMIT
        ),
        name=name,
    )(*[a for a, _ in ins.values()])
    return SimpleNamespace(**dict(zip(outs, results)))


def local(
    tokens, cotangent, block_order, lengths, decay, write_gate, gain_attn, w_query, w_key, w_value,
    persist_key, persist_value, w_output, gain_ffn, w_gate, w_up, w_down,
):
    sec, row_id, col = (lax.axis_index(a) for a in ("section", "row", "col"))
    groups = lax.axis_size("col")
    micros, rows, features = tokens.shape
    width = features * 4
    own, blocks, all_rows, size = rows // 8, rows // BLOCK, micros * rows, features // 2
    ffh = w_gate.shape[2] // 2
    per = persist_key.shape[1]
    persist = per * groups
    cfg = SimpleNamespace(
        micros=micros, rows=rows, own=own, size=size, width=width, groups=groups, blocks=blocks, per=per
    )
    total_blocks = block_order.shape[1]
    positions = jnp.arange(total_blocks, dtype=jnp.int32)
    my_blocks = col * blocks + jnp.arange(blocks, dtype=jnp.int32)
    deal_picks = lax.dynamic_slice_in_dim(block_order, col * blocks, blocks, 1)
    matches = (block_order[:, :, None] == my_blocks[None, None, :]).astype(jnp.int32)
    back_picks = jnp.sum(matches * positions[None, :, None], axis=1)

    def lanes(a):
        return jnp.pad(a, ((0, 0),) * (a.ndim - 1) + ((0, 128 - a.shape[-1]),))

    def eights(a):
        return jnp.pad(a, ((0, 0),) * (a.ndim - 2) + ((0, -a.shape[-2] % 8), (0, 0)))

    share = gain_attn.shape[1]
    own_gains = jnp.concatenate([gain_attn, gain_ffn], axis=0).astype(F32)
    placed = lax.dynamic_update_slice(
        jnp.zeros((2, features), F32), own_gains, (jnp.zeros_like(col), col * share)
    )
    packed = jnp.concatenate(
        [eights(placed.reshape(-1, 128))]
        + [
            eights(a[0].reshape(per, 2, size).transpose(1, 0, 2)).reshape(16, size).astype(F32)
            for a in (persist_key, persist_value)
        ]
        + [eights(lanes(decay[0].transpose(2, 0, 1).reshape(2, -1)))],
        axis=0,
    )
    gate_rows = eights(write_gate[0].transpose(2, 0, 1).reshape(2, -1, 128)) / BLOCK
    ends = jnp.cumsum(lengths, axis=1)
    is_start = jnp.any(positions[None, :, None] == (ends - lengths)[:, None, :], axis=2)
    starts = jnp.where(is_start, 0.0, 1.0).reshape(micros, groups, blocks).transpose(1, 0, 2)
    starts = jnp.broadcast_to(lanes(starts.reshape(groups, -1))[:, None], (groups, 8, 128))

    def cols_split(w):
        return w.reshape(w.shape[0], 2, -1).transpose(1, 0, 2)

    def rows_split(w):
        return w.reshape(2, -1, w.shape[1]).transpose(0, 2, 1)

    blocks_a = jnp.concatenate(
        [cols_split(w[0]) for w in (w_query, w_key, w_value)] + [rows_split(w_output[0])], axis=2
    )[:, None]
    blocks_b = jnp.stack(
        [cols_split(w_gate[0]), cols_split(w_up[0]), rows_split(w_down[0])], axis=1
    )

    a_dims, b_dims = blocks_a.shape[1:], blocks_b.shape[1:]
    q_dims, o_dims, one_dims = (1, a_dims[1], 3 * size), (1, a_dims[1], size), (1,) + b_dims[1:]
    grad_a_dims, grad_b_dims = (1, width, 4 * size), (3, width, ffh)
    stage_dims = (micros, rows, size)
    by_block = (micros, blocks, BLOCK, size)
    gain_rows = 4 * width // 128
    half_gains = width // 128
    hbm = lambda dims, dtype=BF16: (dims, dtype, HB)

    def row_scratch(prefix):
        return {
            "part": vm((all_rows, width)),
            "pair": vm((micros, 4 * own, width)),
            "both": vm((micros, 4, own, width)),
            "transit": vm((micros, 2, own, width // 2)),
            "final": vm((micros, 2, own, width)),
            prefix + "send": pltpu.SemaphoreType.DMA((micros, N_AG + N_RS)),
            prefix + "recv": pltpu.SemaphoreType.DMA((micros, N_AG + N_RS)),
            prefix + "full": vm((all_rows, width)),
        }

    def attn_scratch(prefix):
        names = dict(
            update=vm((micros * blocks, size, size), F32),
            entering=vm((size, size), F32),
            leaving=vm((micros, size, size)),
            box=vm((micros, groups, size, size)),
            ssend=pltpu.SemaphoreType.DMA((micros, groups)),
            srecv=pltpu.SemaphoreType.DMA((micros, groups)),
            gate=vm((all_rows, 1), F32),
            persist=vm((persist, size), F32),
            qkv=vm((all_rows, 3 * size)),
            state=vm((micros * blocks, size, size)),
            mixed=vm((all_rows, size)),
        )
        return {**row_scratch(prefix), **{prefix + a: b for a, b in names.items()}}

    def ffn_scratch(prefix):
        names = {a: vm((all_rows, ffh)) for a in ("gp", "up", "act")}
        return {**row_scratch(prefix), **{prefix + a: b for a, b in names.items()}}

    def view_of(k, prefix, **more):
        names = {a[len(prefix) :]: b for a, b in vars(k).items() if a.startswith(prefix)}
        return SimpleNamespace(**{**names, **more})

    def rows_of(k, prefix):
        p = view_of(k, prefix)
        row = Rows(rows, own, width, p.send, p.recv)
        row.buffers = (k.part, k.pair, k.both, k.transit, k.final)
        row.part = k.part
        return row

    def greet_all(row):
        row.greet(
            plane_peers(row)
            + [(row.s, row.r, lax.rem(row.c + i, groups)) for i in range(1, groups)]
        )

    def hooks(plan, prefix):
        def hook(point):
            for action in plan.get(prefix + point, ()):
                action()

        return hook

    def pusher(send, recv):
        def push(src, dst, i, to):
            copy = pltpu.make_async_remote_copy(
                src_ref=src,
                dst_ref=dst,
                send_sem=send.at[i],
                recv_sem=recv.at[i],
                device_id=to,
                device_id_type=MESH,
            )
            copy.start()
            return copy

        return push

    def blocks_from(buf, picks, stage, m, lead=()):
        for b in range(blocks):
            stage[lead + (m, pl.ds(b * BLOCK, BLOCK))] = buf[lead + (m, picks[m, b])]

    def forward_names(l):
        outs = dict(
            a_xin_o=hbm((all_rows, width)),
            a_qkv_o=hbm((all_rows, 3 * size)),
            a_state_o=hbm((micros * blocks, size, size)),
            a_mixed_o=hbm((all_rows, size)),
            f_xin_o=hbm((all_rows, width)),
            f_gp_o=hbm((all_rows, ffh)),
            f_up_o=hbm((all_rows, ffh)),
            f_act_o=hbm((all_rows, ffh)),
            wo_o=hbm((1, width, size)),
            w_o=hbm((3, width, ffh)),
            mid=((micros, own, width), F32, VM),
            y=((micros, own, width), BF16, VM),
        )
        return outs, {**attn_scratch("a_"), **ffn_scratch("f_")}

    def forward_layer(k, l, x, wq, loc, loads, plan, row_a, small):
        row_f = rows_of(k, "f_")
        gain_f = gain_row(small, cfg, l, 1)

        def middle(m, summed):
            k.mid[m] = x[m].astype(F32) + summed
            norm_to(k.f_full, gain_f, k.mid[m], row_f.span(m, row_f.s, row_f.r))
            row_f.ag_start(k.f_full, m)

        def leave(m, summed):
            k.y[m] = (k.mid[m] + summed).astype(BF16)

        p = view_of(k, "a_", wq=wq, wo_dst=k.wo_dst, **vars(small))
        attn_forward(
            p, row_a, loc, cfg, hooks(plan, A), l, loads, middle,
            lambda: row_f.ag_pass(k.f_full, 0),
        )
        row_a.finish()
        loc.start(k.wo_dst, k.wo_o)
        p = view_of(k, "f_", gate_dst=k.gate_dst, up_dst=k.up_dst, down_dst=k.down_dst)
        ffn_forward(p, row_f, loc, cfg, hooks(plan, F), leave)
        for i, w in enumerate((k.gate_dst, k.up_dst, k.down_dst)):
            loc.start(w, k.w_o.at[pl.ds(i, 1)])
        return row_f

    def one_b(tag, layer, which, array):
        view = None
        if array is None:
            view = lambda k, row: k.shards_b.at[layer, pl.ds(which, 1)]
        else:
            view = lambda k, row: getattr(k, tag + "src").at[layer, pl.ds(which, 1)]
        return Gather(tag, array, one_dims, groups, 1, view, "scratch")

    def q_of(ref, layer):
        return ref.at[layer, :, :, pl.ds(0, 3 * size)]

    def o_of(ref, layer):
        return ref.at[layer, :, :, pl.ds(3 * size, size)]

    def lanes_of_core(name):
        def view(k, row):
            mine = pl.ds(pl.multiple_of(row.s * size, 128), size)
            return getattr(k, name).at[:, :, :, mine]

        return view

    tokens_b = tokens.reshape(micros, blocks, BLOCK, features)
    cotangent_b = cotangent.reshape(micros, blocks, BLOCK, features)
    deal = Gather("deal_", tokens_b, by_block, groups, 1, lanes_of_core("deal_src"), "scratch")
    q0 = Gather("q0_", None, q_dims, groups, 1, lambda k, row: q_of(k.shards_a, 0), "scratch")
    wo0 = Gather("wo_", None, o_dims, groups, 1, lambda k, row: o_of(k.shards_a, 0), "scratch")
    gate0, up0, down0 = (one_b(t, 0, i, None) for i, t in enumerate(("gate_", "up_", "down_")))
    q1 = Gather("q1_", None, q_dims, groups, 1, lambda k, row: q_of(k.shards_a, 1))
    sides1 = [deal, q0, wo0, gate0, up0, down0, q1]
    swap1 = Swap("swap_")

    def first_body(k):
        row = rows_of(k, "a_")
        loc = Local(k.sems)
        greet_all(row)
        for side in sides1:
            side.bind(k, row, groups)
        push = pusher(k.psend, k.precv)
        crossing, keeps_here = [], []
        for i, (src, dst) in enumerate(((k.blocks_a, k.shards_a), (k.blocks_b, k.shards_b))):
            keeps_here.append(loc.start(src.at[row.s], dst.at[row.s]))
            crossing.append(push(src.at[1 - row.s], dst.at[row.s], groups + 9 + i, row.sib))
        deal.start()
        k.line[row.s, row.c] = k.packed[...]
        k.gates[row.s] = k.gate_rows[row.s]
        small = [
            push(
                k.packed,
                k.line.at[row.s, row.c],
                i,
                (row.s, row.r, lax.rem(row.c + i, groups)),
            )
            for i in range(1, groups)
        ]
        late = [push(k.gate_rows.at[1 - row.s], k.gates.at[row.s], 0, row.sib)]
        crossing[0].wait_recv()
        loc.wait(keeps_here[0])
        q0.start()
        deal.step()
        for copy in small:
            copy.wait_recv()
        total = k.line[row.s, 0, 0:8, :]
        for j in range(1, groups):
            total = total + k.line[row.s, j, 0:8, :]
        k.gains[row.s, row.r] = total
        for i, ps, pr in others(row):
            mine = k.gains.at[row.s, row.r]
            late.append(push(mine, mine, groups + i, (ps, pr, row.c)))
        late.append(push(k.line.at[row.s], k.line.at[row.s], groups + 8, row.sib))
        crossing[1].wait_recv()
        loc.wait(keeps_here[1])
        q0.step()
        wo0.start()
        deal.step()
        q0.step()
        gate0.start()
        up0.start()
        wo0.step()
        deal.finish()
        for m in range(micros):
            blocks_from(k.deal_dst, k.picks, k.stage, m)
        swap1.start(k, row, own, size, k.stage, k.x, True)
        q0.finish()
        wo0.step()
        for copy in late:
            copy.wait_recv()
        gain = gain_row(k, cfg, 0, 0)
        swap1.wait()
        for m in range(micros):
            norm_to(k.a_full, gain, k.x[m].astype(F32), row.span(m, row.s, row.r))
        ag_begin(row, k.a_full)
        loc.start(k.q0_dst, k.q0_o)
        plan = place(
            PLACES["first"],
            [
                gate0.step, up0.step, down0.start, gate0.step, up0.step, down0.step, down0.step,
                q1.start, q1.step, q1.step,
            ],
            [
                (A + 20, wo0.finish), (F, gate0.finish), (F, up0.finish), (F + 10, down0.finish),
            ],
        )
        small_refs = SimpleNamespace(line=k.line, gains=k.gains, gates=k.gates, starts=k.starts)
        row_f = forward_layer(k, 0, k.x, k.q0_dst, loc, [], plan, row, small_refs)
        for side in sides1:
            side.finish()
        for copy in crossing + small + late:
            copy.wait_send()
        row.finish()
        row_f.finish()
        for side in sides1:
            side.drain()
        swap1.drain()
        loc.finish()

    outs, scratch = forward_names(0)
    ins = dict(
        picks=(deal_picks, SM),
        blocks_a=(blocks_a, HB),
        blocks_b=(blocks_b, HB),
        packed=(packed, VM),
        gate_rows=(gate_rows, VM),
        starts=(starts, VM),
    )
    outs.update(
        x=((micros, own, width), BF16, VM),
        shards_a=hbm(blocks_a.shape),
        shards_b=hbm(blocks_b.shape),
        line=((2, groups) + packed.shape, F32, VM),
        gains=((2, 4, 8, 128), F32, VM),
        gates=((2,) + gate_rows.shape[1:], F32, VM),
        q0_o=hbm((1, width, 3 * size)),
    )
    scratch.update(
        stage=vm(stage_dims),
        psend=pltpu.SemaphoreType.DMA((groups + 11,)),
        precv=pltpu.SemaphoreType.DMA((groups + 11,)),
        sems=pltpu.SemaphoreType.DMA((48,)),
    )
    for side in sides1:
        side.declare(ins, outs, scratch, groups)
    swap1.declare(scratch)
    f0 = launch("forward_0", 0, first_body, ins, outs, scratch)

    smalls = dict(
        line=(f0.line, VM), gains=(f0.gains, VM), gates=(f0.gates, VM),
        starts=(starts, VM),
    )

    def small_of(k):
        return SimpleNamespace(line=k.line, gains=k.gains, gates=k.gates, starts=k.starts)

    wo1 = Gather("wo_", f0.shards_a, o_dims, groups, 1, lambda k, row: o_of(k.wo_src, 1), "scratch")
    gate1, up1, down1 = (one_b(t, 1, i, f0.shards_b) for i, t in enumerate(("gate_", "up_", "down_")))
    cot = Gather("cot_", cotangent_b, by_block, groups, 1, lanes_of_core("cot_src"), "scratch")
    sides2 = [wo1, gate1, up1, down1, cot]
    swap_y, swap_c = Swap("swapy_"), Swap("swapc_")

    def second_body(k):
        row = rows_of(k, "a_")
        loc = Local(k.sems)
        loads = [loc.start(k.q_h, k.wq)]
        gain = gain_row(k, cfg, 1, 0)
        for m in range(micros):
            norm_to(k.a_full, gain, k.x[m].astype(F32), row.span(m, row.s, row.r))
        greet_all(row)
        for side in sides2:
            side.bind(k, row, groups)
        ag_begin(row, k.a_full)
        for side in (wo1, gate1, up1):
            side.start()
        swap_y.start(k, row, own, size, k.x, k.stage_o, False)

        def deal_cot():
            cot.finish()
            for m in range(micros):
                blocks_from(k.cot_dst, k.picks, k.stage, m)
            swap_c.start(k, row, own, size, k.stage, k.dy, True)

        plan = place(
            PLACES["second"],
            [
                wo1.step, gate1.step, wo1.step, up1.step, down1.start, gate1.step, up1.step, down1.step,
                down1.step, cot.start, cot.step, cot.step, deal_cot,
            ],
            [
                (A + 20, wo1.finish), (F, gate1.finish), (F, up1.finish), (F + 10, down1.finish),
            ],
        )
        row_f = forward_layer(k, 1, k.x, k.wq, loc, loads, plan, row, small_of(k))
        for side in sides2:
            side.finish()
        swap_y.wait()
        swap_c.wait()
        row.finish()
        row_f.finish()
        for side in sides2 + [swap_y, swap_c]:
            side.drain()
        loc.finish()

    outs, scratch = forward_names(1)
    ins = dict(x=(f0.y, VM), q_h=(f0.q1_dst, HB), picks=(deal_picks, SM), **smalls)
    outs.update(dy=((micros, own, width), BF16, VM), stage_o=hbm(stage_dims))
    scratch.update(
        stage=vm(stage_dims), wq=vm((1, width, 3 * size)), sems=pltpu.SemaphoreType.DMA((48,))
    )
    for side in sides2:
        side.declare(ins, outs, scratch, groups)
    swap_y.declare(scratch)
    swap_c.declare(scratch)
    f1 = launch("forward_1", 1, second_body, ins, outs, scratch)

    def backward_names(kept, dy, x, wq):
        ins = dict(
            dy=(dy, VM), mid=(kept.mid, VM), x=(x, VM), w_h=(kept.w_o, HB),
            wo_h=(kept.wo_o, HB), wq_h=(wq, HB), ax_h=(kept.a_xin_o, HB),
            qkv_h=(kept.a_qkv_o, HB), state_h=(kept.a_state_o, HB),
            mixed_h=(kept.a_mixed_o, HB), fx_h=(kept.f_xin_o, HB), gp_h=(kept.f_gp_o, HB),
            up_h=(kept.f_up_o, HB), act_h=(kept.f_act_o, HB), **smalls,
        )
        scratch = {**attn_scratch("a_"), **ffn_scratch("f_")}
        scratch.update(
            f_w=vm((3, width, ffh)), xin=vm((all_rows, width)),
            f_dg=vm((all_rows, ffh)), f_du=vm((all_rows, ffh)), f_grad=vm(grad_b_dims),
            a_wo=vm((1, width, size)), a_wq=vm((1, width, 3 * size)),
            a_dmix=vm((all_rows, size)),
            a_dqkv=vm((all_rows, 3 * size)), a_grad=vm(grad_a_dims),
            dmid=vm((micros, own, width), F32), sems=pltpu.SemaphoreType.DMA((48,)),
        )
        return ins, scratch

    def backward_layer(k, l, loc, sides, swaps_begin, plan, dx_done):
        row_f, row_a = rows_of(k, "f_"), rows_of(k, "a_")
        first = [
            loc.start(a, b) for a, b in ((k.w_h, k.f_w), (k.gp_h, k.f_gp), (k.up_h, k.f_up))
        ]
        late_f = [loc.start(a, b) for a, b in ((k.act_h, k.f_act), (k.fx_h, k.xin))]
        loads_a = [
            loc.start(a, b)
            for a, b in (
                (k.wo_h, k.a_wo), (k.qkv_h, k.a_qkv), (k.wq_h, k.a_wq), (k.state_h, k.a_state)
            )
        ]
        late_a = [loc.start(k.mixed_h, k.a_mixed)]
        for m in range(micros):
            k.f_full[row_f.span(m, row_f.s, row_f.r), :] = k.dy[m]
        greet_all(row_f)
        for side in sides:
            side.bind(k, row_f, groups)
        ag_begin(row_f, k.f_full)
        swaps_begin(row_f)
        gain_a, gain_f = gain_row(k, cfg, l, 0), gain_row(k, cfg, l, 1)
        k.dgain[...] = jnp.zeros_like(k.dgain)

        def middle(m, summed):
            back, gains = norm_back(k.mid[m], gain_f, summed)
            k.dmid[m] = k.dy[m].astype(F32) + back
            k.dgain[1:2, :] += gains
            k.a_full[row_a.span(m, row_a.s, row_a.r), :] = k.dmid[m].astype(BF16)
            row_a.ag_start(k.a_full, m)

        def leave(m, summed):
            back, gains = norm_back(k.x[m].astype(F32), gain_a, summed)
            k.dx[m] = (k.dmid[m] + back).astype(BF16)
            k.dgain[0:1, :] += gains
            dx_done(m)

        left = ffn_backward(
            view_of(k, "f_", xin=k.xin), row_f, loc, cfg, hooks(plan, F), first, late_f, middle,
            lambda: row_a.ag_pass(k.a_full, 0),
        )
        row_f.finish()

        def load_xin():
            late_a.append(loc.start(k.ax_h, k.xin))

        left = list(left) + [load_xin]
        p = view_of(k, "a_", dpersist=k.dpersist, xin=k.xin, **vars(small_of(k)))
        attn_backward(p, row_a, loc, cfg, hooks(plan, A), l, loads_a, late_a, leave, left)
        return row_f, row_a

    def staged(tag, array, home=None):
        return Gather(tag, array.reshape(by_block), by_block, groups, 1, None, home)

    def grad_of(k):
        return k.f_grad

    y0 = staged("y0_", f1.stage_o)
    y1 = Gather("y1_", None, stage_dims, groups, 1, lambda k, row: k.stage)
    td1, tg1 = (Total(t, None, grad_b_dims, groups, (i, 1), grad_of) for t, i in (("td_", 2), ("tg_", 0)))
    sides3 = [y0, y1, td1, tg1]
    swap_y1 = Swap("swap_")

    def third_body(k):
        loc = Local(k.sems)

        def begin(row):
            y0.start()
            swap_y1.start(k, row, own, size, k.y, k.stage, False)

        def start_y1():
            swap_y1.wait()
            y1.start()

        plan = place(
            PLACES["third"],
            [
                y0.step, y0.step, start_y1, td1.start, y1.step, td1.step, tg1.start, td1.step, y1.step,
                tg1.step, tg1.step,
            ],
        )
        row_f, row_a = backward_layer(k, 1, loc, sides3, begin, plan, lambda m: None)
        for i in range(3):
            loc.start(k.f_grad.at[i], k.grad_b_o.at[i])
        loc.start(k.a_grad, k.grad_a_o)
        for side in sides3:
            side.finish()
        row_f.finish()
        row_a.finish()
        for side in sides3 + [swap_y1]:
            side.drain()
        loc.finish()

    ins, scratch = backward_names(f1, f1.dy, f0.y, f0.q1_dst)
    ins["y"] = (f1.y, VM)
    small_outs = dict(
        dgain=((2, width), F32, VM),
        dpersist=((2, persist, size), F32, VM),
        dx=((micros, own, width), BF16, VM),
    )
    outs = dict(grad_a_o=hbm(grad_a_dims), grad_b_o=hbm(grad_b_dims), **small_outs)
    scratch["stage"] = vm(stage_dims)
    for side in sides3:
        side.declare(ins, outs, scratch, groups)
    swap_y1.declare(scratch)
    b1 = launch("backward_1", 2, third_body, ins, outs, scratch)

    small_rows = gain_rows + 4 * persist
    tu1 = Total("tu1_", b1.grad_b_o, grad_b_dims, groups, (1, 1), None, "scratch")
    ta1 = Total("ta1_", b1.grad_a_o, grad_a_dims, groups, (0, 1), None, "scratch")
    td0, tg0, tu0 = (
        Total(t, None, grad_b_dims, groups, (i, 1), grad_of, "scratch")
        for t, i in (("td_", 2), ("tg_", 0), ("tu_", 1))
    )
    ta0 = Total("ta0_", None, grad_a_dims, groups, (0, 1), lambda k: k.a_grad, "scratch")
    g1 = Gather("g1_", None, by_block, groups, 1, lambda k, row: k.staged1)
    g0 = [
        Gather(f"g0{m}_", None, by_block[1:], groups, 0, lambda k, row, m=m: k.staged0.at[m], "scratch")
        for m in range(micros)
    ]

    def blocked(stage, staged, m):
        for b in range(blocks):
            staged[m, b] = stage[m, b * BLOCK : (b + 1) * BLOCK, :]
    sides4 = [tu1, ta1, td0, tg0, tu0, ta0, g1, *g0]
    swap_g1, swaps0 = Swap("swap_"), [Swap(f"swap{m}_") for m in range(micros)]

    def last_body(k):
        loc = Local(k.sems)
        push = pusher(k.psend, k.precv)
        load_y = loc.start(k.y0_buf, k.whole)
        loads = [
            loc.start(a, b)
            for a, b in (
                (k.bg1, k.res_b.at[1, pl.ds(0, 1)]), (k.bd1, k.res_b.at[1, pl.ds(2, 1)]),
            )
        ]

        def begin(row):
            tu1.start()
            ta1.start()
            swap_g1.start(k, row, own, size, k.dy, k.stage, False)

        def start_g1():
            swap_g1.wait()
            for m in range(micros):
                blocked(k.stage, k.staged1, m)
            g1.start()

        def gather_g0(m):
            swaps0[m].wait()
            blocked(k.stage0, k.staged0, m)
            g0[m].start()

        def dx_done(m):
            swaps0[m].start(
                k, ta0.row, own, size, k.dx.at[pl.ds(m, 1)], k.stage0.at[pl.ds(m, 1)], False
            )
            if m >= 1:
                gather_g0(m - 1)

        plan = place(
            PLACES["last"],
            [
                tu1.step, ta1.step, start_g1, tu1.step, ta1.step, g1.step, td0.start, g1.step, td0.step,
                tg0.start, tu0.start, td0.step, tg0.step, tu0.step, tg0.step, tu0.step, ta0.start,
            ],
        )
        row_f, row = backward_layer(k, 0, loc, sides4, begin, plan, dx_done)
        for i in range(half_gains):
            lanes_here = slice(i * 128, (i + 1) * 128)
            for j, ref in enumerate((k.dgain, k.dgain1)):
                for kind in range(2):
                    at = (j * 2 + kind) * half_gains + i
                    k.smalls[at : at + 1, :] = ref[kind : kind + 1, lanes_here]
        for j, ref in enumerate((k.dpersist, k.dpersist1)):
            for kind in range(2):
                at = gain_rows + (j * 2 + kind) * persist
                k.smalls[at : at + persist, :] = ref[kind]
        gather_g0(micros - 1)
        pushes = []
        for i in range(1, groups):
            to = (row.s, row.r, lax.rem(row.c + i, groups))
            pushes.append(push(k.smalls, k.small_box.at[i], i, to))
        for copy in loads:
            loc.wait(copy)

        def all_restored(slot):
            for m in range(micros):
                for b in range(blocks):
                    where = pl.ds(b * BLOCK, BLOCK)
                    k.halves[slot, m, where, :] = k.whole[m, k.back[m, b]]

        loc.wait(load_y)
        all_restored(0)
        loc.wait(loc.start(k.y1_buf, k.whole))
        all_restored(1)
        moved, kept_here = [], []
        mine_lanes = pl.ds(pl.multiple_of(row.s * size, 128), size)

        def give(i, pair, out):
            moved.append(push(pair.at[1 - row.s], out, groups + 8 + i, row.sib))
            kept_here.append(loc.start(pair.at[row.s], out))

        give(0, k.halves.at[pl.ds(0, 2)], k.acts_o.at[:, :, mine_lanes])

        for g in g0:
            g.step()
        ta0.step()
        g1.finish()
        loc.wait(loc.start(k.g1_dst, k.whole))
        all_restored(3)
        for g in g0:
            g.step()
        ta0.step()
        for total in (td0, tg0, tu0, tu1, ta1):
            total.finish()
        k.res_b[0, pl.ds(2, 1)] = k.td_sum[...]
        k.res_b[0, pl.ds(0, 1)] = k.tg_sum[...]
        k.res_b[0, pl.ds(1, 1)] = k.tu_sum[...]
        k.res_b[1, pl.ds(1, 1)] = k.tu1_sum[...]
        k.res_a[1] = k.ta1_sum[...]
        give(1, k.res_b, k.grad_b.at[row.s])
        for copy in pushes:
            copy.wait_recv()
        total = k.smalls[...]
        for i in range(1, groups):
            total = total + k.small_box[i]
        k.small_sum[...] = total
        gains = []
        for i, ps, pr in others(row):
            src = k.small_sum.at[pl.ds(0, gain_rows), :]
            gains.append(push(src, k.gain_box.at[i], groups + i, (ps, pr, row.c)))
        ta0.finish()
        k.res_a[0] = k.ta0_sum[...]
        give(2, k.res_a, k.grad_a.at[row.s])
        for m, g in enumerate(g0):
            g.finish()
            buf = getattr(k, f"g0{m}_dst")
            for b in range(blocks):
                k.halves[2, m, pl.ds(b * BLOCK, BLOCK), :] = buf[k.back[m, b]]
        give(3, k.halves.at[pl.ds(2, 2)], k.grads_o.at[:, :, mine_lanes])
        for copy in gains:
            copy.wait_recv()
        total = k.small_sum[0:gain_rows, :]
        for i in range(1, 8):
            total = total + k.gain_box[i]
        k.gain_o[...] = total
        k.persist_o[...] = k.small_sum[gain_rows:, :]
        for copy in moved:
            copy.wait()
        for copy in pushes + gains:
            copy.wait_send()
        for side in sides4:
            side.finish()
        row_f.finish()
        row.finish()
        for side in sides4 + [swap_g1] + swaps0:
            side.drain()
        loc.finish()

    ins, scratch = backward_names(f0, b1.dx, f0.x, f0.q0_o)
    ins.update(
        y0_buf=(b1.y0_dst, HB),
        y1_buf=(b1.y1_dst.reshape(b1.y0_dst.shape), HB),
        bg1=(b1.tg_sum, HB),
        bd1=(b1.td_sum, HB),
        dgain1=(b1.dgain, VM),
        dpersist1=(b1.dpersist, VM),
        back=(back_picks, SM),
    )
    outs = dict(
        acts_o=((micros, rows, features), BF16, VM),
        grads_o=((micros, rows, features), BF16, VM),
        grad_a=((2,) + ta0.dims, BF16, VM),
        grad_b=((2, 3) + tu0.dims[1:], BF16, VM),
        gain_o=((gain_rows, 128), F32, VM),
        persist_o=((4 * persist, 128), F32, VM),
    )
    scratch.update(
        stage=vm(stage_dims),
        stage0=vm(stage_dims),
        whole=vm((micros, total_blocks, BLOCK, size)),
        staged0=vm(by_block),
        staged1=vm(by_block),
        halves=vm((4,) + stage_dims),
        res_a=vm((2,) + ta0.dims),
        res_b=vm((2, 3) + tu0.dims[1:]),
        smalls=vm((small_rows, 128), F32),
        small_box=vm((groups, small_rows, 128), F32),
        small_sum=vm((small_rows, 128), F32),
        gain_box=vm((8, gain_rows, 128), F32),
        dgain=vm((2, width), F32),
        dpersist=vm((2, persist, size), F32),
        dx=vm((micros, own, width)),
        psend=pltpu.SemaphoreType.DMA((groups + 12,)),
        precv=pltpu.SemaphoreType.DMA((groups + 12,)),
    )
    for side in sides4:
        side.declare(ins, outs, scratch, groups)
    for swap in [swap_g1] + swaps0:
        swap.declare(scratch)
    closed = launch("backward_0", 3, last_body, ins, outs, scratch)

    def cols_join(pair):
        return jnp.concatenate([pair[0], pair[1]], axis=1).astype(F32)[None]

    def rows_join(pair):
        return jnp.concatenate([pair[0].T, pair[1].T], axis=0).astype(F32)[None]

    grad_a, grad_b = closed.grad_a[:, 0], closed.grad_b
    heads = [cols_join(grad_a[:, :, i * size : (i + 1) * size]) for i in range(3)]
    grad_out = rows_join(grad_a[:, :, 3 * size :])
    grad_gate, grad_up = cols_join(grad_b[:, 0]), cols_join(grad_b[:, 1])
    grad_down = rows_join(grad_b[:, 2])
    gain_sum = closed.gain_o.reshape(2, 2, width)
    my_gain = lax.dynamic_slice_in_dim(
        lax.dynamic_index_in_dim(gain_sum, sec, 0, False), (row_id * groups + col) * share, share, 1
    )
    persist_sum = closed.persist_o.reshape(2, 2, persist, size)
    persist_sum = lax.dynamic_slice_in_dim(persist_sum, col * per, per, 2)
    mine_p = lax.dynamic_index_in_dim(persist_sum, sec, 0, False)
    got_p = lax.ppermute(
        lax.dynamic_index_in_dim(persist_sum, 1 - sec, 0, False), "section", [(0, 1), (1, 0)]
    )
    grad_persist = jnp.concatenate(
        [jnp.where(sec == 0, mine_p, got_p), jnp.where(sec == 0, got_p, mine_p)], axis=2
    )
    return (
        closed.acts_o[None],
        closed.grads_o[None],
        my_gain[0][None],
        heads[0],
        heads[1],
        heads[2],
        grad_persist[0][None],
        grad_persist[1][None],
        grad_out,
        my_gain[1][None],
        grad_gate,
        grad_up,
        grad_down,
    )


def solution(mesh):
    weight = P("section", "col", "row")
    across = P("section", "row", "col")
    gain = P("section", ("row", "col"))
    rows = P("section", None, "col", "row")
    return jax.shard_map(
        local,
        mesh=mesh,
        in_specs=(
            P(None, "col", "row"), P(None, "col", "row"), P(), P(), rows, rows, gain, weight, weight,
            weight, weight, weight, across, gain, weight, weight, across,
        ),
        out_specs=(
            rows, rows, gain, weight, weight, weight, weight, weight, across, gain, weight, weight,
            across,
        ),
        check_vma=False,
    )
```

```python
from types import SimpleNamespace

import jax
import jax.numpy as jnp
from jax import lax
from jax.experimental import pallas as pl
from jax.experimental.pallas import tpu as pltpu
from jax.sharding import PartitionSpec as P

BLOCK = 64
EPS = 1e-06
MESH = pl.DeviceIdType.MESH
F32 = jnp.float32
BF16 = jnp.bfloat16
VMEM_LIMIT = 60 << 20
N_AG, N_RS = 8, 7

A, F, NEXT = 0, 100, 200
PLACES = dict(
    first=[
        A, A + 10, A + 30, A + 21, A + 12, A + 32, A + 41, A + 41, F + 31, F + 32,
        F + 40, NEXT, NEXT, F + 40, F + 41,
        NEXT + 12, NEXT + 2, NEXT + 12, NEXT + 41, NEXT + 30, NEXT + 32, NEXT + 40,
        NEXT + 41, NEXT + F + 11, NEXT + F + 32, NEXT + F + 41,
    ],
    third=[
        F + 30, F + 32, F + 30, F + 52, F + 52, F + 50, A + 2, A + 32, A + 12, A + 31,
        A + 32,
    ],
    last=[
        F + 40, F, F, A + 31, F + 31, F + 40, F + 50, A + 10, A + 30, F + 50,
        F + 51, A + 31, A + 1, A + 2, A + 40, A + 30, A + 60,
    ],
)


def place(points, actions, fixed=()):
    plan = {}
    for point, action in list(zip(points, actions, strict=True)) + list(fixed):
        plan.setdefault(point, []).append(action)
    return plan


def dot(a, b, ca=1, cb=0):
    return lax.dot_general(a, b, (((ca,), (cb,)), ((), ())), preferred_element_type=F32)


class Rows:
    def __init__(self, rows, own, width, send, recv):
        self.rows, self.own, self.width, self.half = rows, own, width, width // 2
        self.send, self.recv = send, recv
        self.s, self.r, self.c = (lax.axis_index(a) for a in ("section", "row", "col"))
        self.rx = self.r + 1 - 2 * lax.rem(self.r, 2)
        self.ry = lax.rem(self.r + 2, 4)
        self.rd = lax.rem(self.rx + 2, 4)
        self.x = (self.s, self.rx, self.c)
        self.y = (self.s, self.ry, self.c)
        self.sib = (1 - self.s, self.r, self.c)
        self.started = []

    def greet(self, others=()):
        barrier = pltpu.get_barrier_semaphore()
        peers = [self.x, self.y, self.sib] + list(others)
        for peer in peers:
            pl.semaphore_signal(barrier, inc=1, device_id=peer, device_id_type=MESH)
        pl.semaphore_wait(barrier, len(peers))

    def copy(self, src, dst, m, k, peer):
        return pltpu.make_async_remote_copy(
            src_ref=src,
            dst_ref=dst,
            send_sem=self.send.at[m, k],
            recv_sem=self.recv.at[m, k],
            device_id=peer,
            device_id_type=MESH,
        )

    def go(self, copy):
        copy.start()
        self.started.append(copy)

    def finish(self):
        for copy in self.started:
            copy.wait_send()
        self.started = []

    def span(self, m, s, r):
        return pl.ds(pl.multiple_of(m * self.rows + (s * 4 + r) * self.own, 16), self.own)

    def ag_copy(self, full, m, k):
        left, right = pl.ds(0, self.half), pl.ds(self.half, self.half)
        mine, atx, aty, atd = (
            self.span(m, self.s, r) for r in (self.r, self.rx, self.ry, self.rd)
        )
        if k == 0:
            return self.copy(full.at[mine, :], full.at[mine, :], m, 0, self.x)
        if k == 1:
            return self.copy(full.at[mine, :], full.at[mine, :], m, 1, self.y)
        if k == 2:
            return self.copy(full.at[mine, :], full.at[mine, :], m, 2, self.sib)
        if k == 3:
            return self.copy(full.at[atx, left], full.at[atx, left], m, 3, self.y)
        if k == 4:
            return self.copy(full.at[aty, right], full.at[aty, right], m, 4, self.x)
        if k == 5:
            return self.copy(full.at[atx, :], full.at[atx, :], m, 5, self.sib)
        if k == 6:
            return self.copy(full.at[aty, :], full.at[aty, :], m, 6, self.sib)
        return self.copy(full.at[atd, :], full.at[atd, :], m, 7, self.sib)

    def ag_start(self, full, m):
        for k in (0, 1, 2):
            self.go(self.ag_copy(full, m, k))

    def ag_pass(self, full, m):
        self.ag_copy(full, m, 0).wait_recv()
        self.go(self.ag_copy(full, m, 3))
        self.go(self.ag_copy(full, m, 5))
        self.ag_copy(full, m, 1).wait_recv()
        self.go(self.ag_copy(full, m, 4))
        self.go(self.ag_copy(full, m, 6))

    def ag_diag(self, full, m):
        self.ag_copy(full, m, 3).wait_recv()
        self.ag_copy(full, m, 4).wait_recv()
        self.go(self.ag_copy(full, m, 7))

    def ag_wait(self, full, m):
        for k in (2, 5, 6, 7):
            self.ag_copy(full, m, k).wait_recv()

    def rs_copy(self, m, k):
        part, pair, both, transit, final = self.buffers
        left, right = pl.ds(0, self.half), pl.ds(self.half, self.half)
        if k == 8:
            other = pl.ds(
                pl.multiple_of(m * self.rows + (1 - self.s) * 4 * self.own, 16), 4 * self.own
            )
            return self.copy(part.at[other, :], pair.at[m], m, 8, self.sib)
        if k == 9:
            return self.copy(both.at[m, self.rd, :, left], transit.at[m, 0], m, 9, self.x)
        if k == 10:
            return self.copy(both.at[m, self.rd, :, right], transit.at[m, 1], m, 10, self.y)
        if k == 11:
            return self.copy(both.at[m, self.rx, :, left], final.at[m, 0, :, left], m, 11, self.x)
        if k == 12:
            return self.copy(both.at[m, self.ry, :, right], final.at[m, 1, :, right], m, 12, self.y)
        if k == 13:
            return self.copy(both.at[m, self.ry, :, left], final.at[m, 1, :, left], m, 13, self.y)
        return self.copy(both.at[m, self.rx, :, right], final.at[m, 0, :, right], m, 14, self.x)

    def rs_start(self, m):
        self.go(self.rs_copy(m, 8))

    def rs_pair(self, m):
        part, pair, both, _, _ = self.buffers
        self.rs_copy(m, 8).wait_recv()
        for r in range(4):
            mine = part[self.span(m, self.s, r), :].astype(F32)
            theirs = pair[m, r * self.own : (r + 1) * self.own, :].astype(F32)
            both[m, r] = (mine + theirs).astype(BF16)
        for k in (9, 10, 11, 12):
            self.go(self.rs_copy(m, k))

    def rs_transit(self, m):
        _, _, both, transit, _ = self.buffers
        left, right = pl.ds(0, self.half), pl.ds(self.half, self.half)
        self.rs_copy(m, 9).wait_recv()
        total = both[m, self.ry, :, left].astype(F32) + transit[m, 0].astype(F32)
        both[m, self.ry, :, left] = total.astype(BF16)
        self.go(self.rs_copy(m, 13))
        self.rs_copy(m, 10).wait_recv()
        total = both[m, self.rx, :, right].astype(F32) + transit[m, 1].astype(F32)
        both[m, self.rx, :, right] = total.astype(BF16)
        self.go(self.rs_copy(m, 14))

    def rs_result(self, m):
        _, _, both, _, final = self.buffers
        for k in (11, 12, 13, 14):
            self.rs_copy(m, k).wait_recv()
        return both[m, self.r].astype(F32) + final[m, 0].astype(F32) + final[m, 1].astype(F32)


class Local:
    def __init__(self, sems):
        self.sems, self.used, self.open = sems, 0, []

    def start(self, src, dst):
        copy = pltpu.make_async_copy(src, dst, self.sems.at[self.used])
        self.used += 1
        copy.start()
        self.open.append(copy)
        return copy

    def wait(self, copy):
        copy.wait()
        self.open = [other for other in self.open if other is not copy]

    def finish(self):
        for copy in list(self.open):
            copy.wait()


def inv_rms(values):
    return lax.rsqrt(jnp.mean(values * values, axis=1, keepdims=True) + EPS)


def norm_to(full, gain, values, span):
    full[span, :] = (values * inv_rms(values) * gain).astype(BF16)


def norm_back(values, gain, grad):
    scale = inv_rms(values)
    weighted = grad * gain
    inner = jnp.mean(weighted * values, axis=1, keepdims=True)
    back = scale * weighted - values * (scale * scale * scale * inner)
    return back, jnp.sum(grad * values * scale, axis=0, keepdims=True)


def wait_both(copies):
    for condition, copy in copies:

        @pl.when(condition)
        def _(copy=copy):
            copy.wait_send()


class Side:
    def __init__(self, tag):
        self.tag = tag

    def ref(self, name):
        return getattr(self.ns, self.tag + name)

    def bind(self, ns, row, groups):
        self.ns, self.row, self.c, self.groups = ns, row, row.c, groups
        self.sent = []

    def when(self, condition, copy):
        @pl.when(condition)
        def _():
            copy.start()

        self.sent.append((condition, copy))

    def arrived(self, condition, copy):
        @pl.when(condition)
        def _():
            copy.wait_recv()

    def remote(self, src, dst, send, recv, to):
        return pltpu.make_async_remote_copy(
            src_ref=src,
            dst_ref=dst,
            send_sem=send,
            recv_sem=recv,
            device_id=(self.row.s, self.row.r, to),
            device_id_type=MESH,
        )


def part_of(ref, at, per, axis):
    where = pl.ds(pl.multiple_of(at * per, per), per)
    return ref.at[(slice(None),) * axis + (where,)]


class Gather(Side):
    def __init__(self, tag, array, dims, groups, axis, view=None, home=None):
        super().__init__(tag)
        self.array, self.axis, self.view, self.home = array, axis, view, home
        self.per = dims[axis]
        self.dims = dims[:axis] + (dims[axis] * groups,) + dims[axis + 1 :]

    def declare(self, ins, outs, scratch, groups):
        if self.array is not None:
            ins[self.tag + "src"] = (self.array, HB)
        if self.home is None:
            outs[self.tag + "dst"] = (self.dims, BF16, HB)
        else:
            scratch[self.tag + "dst"] = pltpu.VMEM(self.dims, BF16)
        scratch[self.tag + "send"] = pltpu.SemaphoreType.DMA((2, groups))
        scratch[self.tag + "recv"] = pltpu.SemaphoreType.DMA((groups,))
        scratch[self.tag + "own"] = pltpu.SemaphoreType.DMA((1,))

    def slot(self, j):
        return part_of(self.ref("dst"), jnp.clip(j, 0, self.groups - 1), self.per, self.axis)

    def source(self):
        return self.view(self.ns, self.row) if self.view else self.ref("src")

    def move(self, j, side, src=None):
        to = jnp.clip(self.c + (1 - 2 * side), 0, self.groups - 1)
        j = jnp.clip(j, 0, self.groups - 1)
        src = self.slot(j) if src is None else src
        return self.remote(
            src, self.slot(j), self.ref("send").at[side, j], self.ref("recv").at[j], to
        )

    def start(self):
        c, n = self.c, self.groups
        self.at, self.done = 1, False
        self.own = pltpu.make_async_copy(self.source(), self.slot(c), self.ref("own").at[0])
        self.own.start()
        self.when(c + 1 < n, self.move(c, 0, self.source()))
        self.when(c >= 1, self.move(c, 1, self.source()))

    def step(self):
        c, n, k = self.c, self.groups, self.at
        if k < n:
            self.arrived(c >= k, self.move(c - k, 0))
            self.arrived(c + k < n, self.move(c + k, 1))
            if k < n - 1:
                self.when((c >= k) & (c + 1 < n), self.move(c - k, 0))
                self.when((c + k < n) & (c >= 1), self.move(c + k, 1))
        self.at += 1

    def finish(self):
        if not self.done:
            while self.at < self.groups:
                self.step()
            self.own.wait()
            self.done = True

    def drain(self):
        wait_both(self.sent)


class Total(Side):
    def __init__(self, tag, parts, dims, groups, span, view=None, home=None):
        super().__init__(tag)
        self.parts, self.span, self.view, self.home = parts, span, view, home
        self.per = dims[1] // groups
        self.count = span[1]
        self.dims = (self.count, self.per, dims[2])

    def declare(self, ins, outs, scratch, groups):
        if self.home is None:
            outs[self.tag + "sum"] = (self.dims, BF16, VM)
        else:
            scratch[self.tag + "sum"] = pltpu.VMEM(self.dims, BF16)
        if self.view is None:
            ins[self.tag + "parts"] = (self.parts, HB)
            whole = (self.count, self.per * groups, self.dims[2])
            scratch[self.tag + "mine"] = pltpu.VMEM(whole, BF16)
        scratch[self.tag + "box"] = pltpu.VMEM((2, groups) + self.dims, BF16)
        scratch[self.tag + "send"] = pltpu.SemaphoreType.DMA((2, groups))
        scratch[self.tag + "recv"] = pltpu.SemaphoreType.DMA((2, groups))
        scratch[self.tag + "load"] = pltpu.SemaphoreType.DMA((1,))

    def clip(self, j):
        return jnp.clip(j, 0, self.groups - 1)

    def piece(self, ref, d, p=None):
        d = self.clip(d)
        where = pl.ds(pl.multiple_of(d * self.per, self.per), self.per)
        if p is None:
            return ref.at[:, where, :]
        return ref[p + (self.span[0] if self.view else 0), where, :]

    def source(self):
        parts = self.view(self.ns) if self.view else self.ref("parts")
        return parts.at[pl.ds(*self.span)]

    def mine(self):
        return self.view(self.ns) if self.view else self.ref("mine")

    def move(self, side, d, src):
        d = self.clip(d)
        to = self.clip(self.c + (1 - 2 * side))
        return self.remote(
            src,
            self.ref("box").at[side, d],
            self.ref("send").at[side, d],
            self.ref("recv").at[side, d],
            to,
        )

    def boxed(self, side, d):
        return self.ref("box").at[side, self.clip(d)]

    def start(self):
        c, n = self.c, self.groups
        self.at, self.done = 1, False
        if self.view is None:
            self.load = pltpu.make_async_copy(
                self.source(), self.ref("mine"), self.ref("load").at[0]
            )
            self.load.start()
        self.ends(0)

    def ends(self, t):
        c, n = self.c, self.groups
        self.when(c == 0, self.move(0, n - 1 - t, self.piece(self.source(), n - 1 - t)))
        self.when(c == n - 1, self.move(1, t, self.piece(self.source(), t)))

    def step(self):
        c, n, t = self.c, self.groups, self.at
        box, mine = self.ref("box"), self.mine()
        if t == 1 and self.view is None:
            self.load.wait()
        if t < n - 1:
            self.ends(t)
            for side, place, d in ((0, c, n - 1 - t + c), (1, n - 1 - c, t + c - (n - 1))):
                here = (place >= 1) & (place <= t)
                self.arrived(here, self.move(side, d, self.boxed(side, d)))

                @pl.when(here)
                def _(side=side, d=d):
                    for p in range(self.count):
                        total = self.piece(mine, d, p).astype(F32)
                        total = total + box[side, self.clip(d), p].astype(F32)
                        box[side, self.clip(d), p] = total.astype(BF16)

                self.when(here, self.move(side, d, self.boxed(side, d)))
        self.at += 1

    def finish(self):
        if self.done:
            return
        self.done = True
        c, n = self.c, self.groups
        while self.at < n - 1:
            self.step()
        box, mine = self.ref("box"), self.mine()
        above, below = c >= 1, c + 1 < n
        self.arrived(above, self.move(0, c, self.boxed(0, c)))
        self.arrived(below, self.move(1, c, self.boxed(1, c)))
        for p in range(self.count):
            first = jnp.where(c >= 1, 0, 1)
            total = self.piece(mine, c, p).astype(F32) + box[first, c, p].astype(F32)
            self.ref("sum")[p] = total.astype(BF16)

            @pl.when(above & below)
            def _(p=p, total=total):
                self.ref("sum")[p] = (total + box[1, c, p].astype(F32)).astype(BF16)

    def drain(self):
        wait_both(self.sent)


def others(row):
    for k in range(1, 8):
        ps = lax.rem(row.s + k // 4, 2)
        low = row.rx if k % 2 else row.r
        pr = lax.rem(low + 2 * ((k // 2) % 2), 4)
        yield k, ps, pr


class Swap:
    def __init__(self, tag):
        self.tag = tag

    def declare(self, scratch):
        scratch[self.tag + "send"] = pltpu.SemaphoreType.DMA((8,))
        scratch[self.tag + "recv"] = pltpu.SemaphoreType.DMA((8,))
        scratch[self.tag + "own"] = pltpu.SemaphoreType.DMA((1,))

    def start(self, ns, row, own, lanes, src, dst, to_tokens):
        send, recv, local = (getattr(ns, self.tag + a) for a in ("send", "recv", "own"))

        def tokens_of(s, r):
            return pl.ds(pl.multiple_of((s * 4 + r) * own, 16), own)

        def lanes_of(s, r):
            return pl.ds(pl.multiple_of((r * 2 + s) * lanes, 128), lanes)

        def ends(ps, pr):
            if to_tokens:
                return src.at[:, tokens_of(ps, pr), :], dst.at[:, :, lanes_of(row.s, row.r)]
            return src.at[:, :, lanes_of(ps, pr)], dst.at[:, tokens_of(row.s, row.r), :]

        a, b = ends(row.s, row.r)
        self.mine = pltpu.make_async_copy(a, b, local.at[0])
        self.mine.start()
        self.copies = []
        for k, ps, pr in others(row):
            a, b = ends(ps, pr)
            copy = pltpu.make_async_remote_copy(
                src_ref=a,
                dst_ref=b,
                send_sem=send.at[k],
                recv_sem=recv.at[k],
                device_id=(ps, pr, row.c),
                device_id_type=MESH,
            )
            copy.start()
            self.copies.append(copy)

    def wait(self):
        for copy in self.copies:
            copy.wait_recv()
        self.mine.wait()

    def drain(self):
        for copy in self.copies:
            copy.wait_send()


def plane_peers(row):
    return [
        (ps, pr, row.c) for k, ps, pr in others(row) if k not in (1, 2, 4)
    ]


def gather_first(row, full, micros, fresh, fill=()):
    if fresh:
        row.ag_pass(full, 0)
        for m in range(2, micros):
            row.ag_start(full, m)
    for work in fill:
        work()
    row.ag_pass(full, 1)
    row.ag_diag(full, 0)


def ag_begin(row, full):
    row.ag_start(full, 0)
    row.ag_start(full, 1)


def gather_more(row, full, micros, m):
    if m + 2 < micros:
        row.ag_pass(full, m + 2)
    if m + 1 < micros:
        row.ag_diag(full, m + 1)


def tail(row, micros, result, hook, between=(), relay=None):
    more = list(between)

    def step():
        if more:
            more.pop(0)()

    row.rs_transit(micros - 2)
    for m in range(micros - 2):
        result(m)
    row.rs_pair(micros - 1)
    hook(40)
    step()
    result(micros - 2)
    row.rs_transit(micros - 1)
    if relay:
        relay()
    step()
    if relay is None:
        while more:
            step()
    hook(41)
    result(micros - 1)
    return more


def ffn_forward(p, row, loc, cfg, hook, deliver, relay=None):
    micros, rows, full = cfg.micros, cfg.rows, p.full
    gather_first(row, full, micros, False)
    for m in range(micros):
        row.ag_wait(full, m)
        hook(m)
        if m >= 1:
            row.rs_pair(m - 1)
        if m >= 2:
            row.rs_transit(m - 2)
        here = pl.ds(m * rows, rows)
        loc.start(full.at[here, :], p.xin_o.at[here, :])
        gate = dot(full[here, :], p.gate_dst[0])
        lift = dot(full[here, :], p.up_dst[0])
        p.gp[here, :] = gate.astype(BF16)
        p.up[here, :] = lift.astype(BF16)
        p.act[here, :] = (gate * jax.nn.sigmoid(gate) * lift).astype(BF16)
        hook(10 + m)
        row.part[here, :] = dot(p.act[here, :], p.down_dst[0], 1, 1).astype(BF16)
        for a, b in ((p.gp, p.gp_o), (p.up, p.up_o), (p.act, p.act_o)):
            loc.start(a.at[here, :], b.at[here, :])
        row.rs_start(m)
        gather_more(row, full, micros, m)
        hook(30 + m)
    tail(row, micros, lambda m: deliver(m, row.rs_result(m)), hook, (), relay)


def ffn_backward(p, row, loc, cfg, hook, loads, late, deliver, relay=None):
    micros, rows, width, full = cfg.micros, cfg.rows, cfg.width, p.full
    gather_first(row, full, micros, True)
    for copy in loads:
        loc.wait(copy)
    for m in range(micros):
        row.ag_wait(full, m)
        hook(m)
        if m >= 1:
            row.rs_pair(m - 1)
        if m >= 2:
            row.rs_transit(m - 2)
        here = pl.ds(m * rows, rows)
        d_act = dot(full[here, :], p.w[2])
        gate = p.gp[here, :].astype(F32)
        lift = p.up[here, :].astype(F32)
        sig = jax.nn.sigmoid(gate)
        silu = gate * sig
        p.dg[here, :] = (d_act * lift * (sig + silu * (1.0 - sig))).astype(BF16)
        p.du[here, :] = (d_act * silu).astype(BF16)
        total = dot(p.dg[here, :], p.w[0], 1, 1) + dot(p.du[here, :], p.w[1], 1, 1)
        row.part[here, :] = total.astype(BF16)
        row.rs_start(m)
        gather_more(row, full, micros, m)
        hook(30 + m)

    def grad(i, left, right):
        def body():
            if i == 2:
                for copy in late:
                    loc.wait(copy)

            @pl.loop(0, width // 256)
            def _(t):
                at = pl.ds(pl.multiple_of(t * 256, 256), 256)
                p.grad[i, at, :] = dot(left[:, at], right[...], 0, 0).astype(BF16)

            hook(50 + i)

        return body

    grads = [grad(2, full, p.act), grad(0, p.xin, p.dg), grad(1, p.xin, p.du)]
    return tail(row, micros, lambda m: deliver(m, row.rs_result(m)), hook, grads, relay)


def pair_masks(size):
    rows_at = lax.broadcasted_iota(jnp.int32, (size, size), 0)
    cols_at = lax.broadcasted_iota(jnp.int32, (size, size), 1)
    return (rows_at >= cols_at) & (rows_at // BLOCK == cols_at // BLOCK)


def gate_columns(gates, columns):
    count, size = gates.shape
    rows_at = lax.broadcasted_iota(jnp.int32, (size, size), 0)
    cols_at = lax.broadcasted_iota(jnp.int32, (size, size), 1)
    for i in range(count):
        spread = jnp.where(rows_at == cols_at, gates[i : i + 1, :], 0.0)
        columns[i * size : (i + 1) * size, :] = jnp.sum(spread, axis=1, keepdims=True)


def gain_row(k, cfg, layer, kind):
    rows_each = cfg.width // 4 // 128
    pieces = [
        k.gains[layer, r, kind * rows_each + h : kind * rows_each + h + 1, :]
        for r in range(4)
        for h in range(rows_each)
    ]
    return jnp.concatenate(pieces, axis=1)


class Heads:
    def __init__(self, k, row, cfg, layer):
        self.k, self.row, self.cfg, self.layer = k, row, cfg, layer

    def persist(self):
        k, cfg = self.k, self.cfg
        out = []
        for kind in range(2):
            start = pl.multiple_of(8 + (2 * kind + self.row.s) * 8, 8)
            for j in range(cfg.groups):
                block = k.line[self.layer, j, pl.ds(start, 8), :]
                k.persist[j * cfg.per : (j + 1) * cfg.per, :] = block[: cfg.per, :]
            out.append(k.persist[...].astype(BF16))
        return out

    def keeps(self, j):
        decays = self.k.line[self.layer, j, 40:48, :] * self.k.starts[j]
        return jnp.where(self.row.s == 0, decays[0:1, :], decays[1:2, :])

    def own(self):
        keeps = self.keeps(self.row.c)
        blocks = self.cfg.blocks

        def of(m, b):
            return keeps[:, m * blocks + b : m * blocks + b + 1]

        return of

    def through(self, m, j):
        keeps = self.keeps(j)
        product = None
        for b in range(self.cfg.blocks):
            at = m * self.cfg.blocks + b
            one = keeps[:, at : at + 1]
            product = one if product is None else product * one
        return product


def pair_probs(q, k, pk, mask, scale):
    inner = jnp.where(mask, dot(q, k, 1, 1) * scale, -1e30)
    outer = dot(q, pk, 1, 1) * scale
    top = jnp.maximum(
        jnp.max(inner, axis=1, keepdims=True), jnp.max(outer, axis=1, keepdims=True)
    )
    inner = jnp.exp(inner - top)
    outer = jnp.exp(outer - top)
    norm = 1.0 / (jnp.sum(inner, axis=1, keepdims=True) + jnp.sum(outer, axis=1, keepdims=True))
    return inner * norm, outer * norm


class States:
    def __init__(self, row, groups, k, backward):
        self.backward, self.sent = backward, []
        self.row, self.groups, self.mine, self.box = row, groups, k.leaving, k.box
        self.send, self.recv, self.entering = k.ssend, k.srecv, k.entering

    def copy(self, m, k):
        n = self.groups
        to = self.row.c + (-k if self.backward else k)
        return pltpu.make_async_remote_copy(
            src_ref=self.mine.at[m],
            dst_ref=self.box.at[m, k],
            send_sem=self.send.at[m, k],
            recv_sem=self.recv.at[m, k],
            device_id=(self.row.s, self.row.r, jnp.clip(to, 0, n - 1)),
            device_id_type=MESH,
        )

    def after(self, k):
        c, n = self.row.c, self.groups
        return (c >= k) if self.backward else (c + k < n)

    def before(self, k):
        c, n = self.row.c, self.groups
        return (c + k < n) if self.backward else (c >= k)

    def start(self, m):
        for k in range(1, self.groups):

            @pl.when(self.after(k))
            def _(k=k):
                self.copy(m, k).start()

            self.sent.append((self.after(k), self.copy(m, k)))

    def wait(self, m):
        for k in range(1, self.groups):

            @pl.when(self.before(k))
            def _(k=k):
                self.copy(m, k).wait_recv()

    def drain(self):
        wait_both(self.sent)

    def fold(self, m, through):
        entering = self.entering
        entering[...] = jnp.zeros_like(entering)
        for k in range(self.groups - 1, 0, -1):

            @pl.when(self.before(k))
            def _(k=k):
                source = self.row.c + (k if self.backward else -k)
                factor = through(m, jnp.clip(source, 0, self.groups - 1))
                entering[...] = factor * entering[...] + self.box[m, k].astype(F32)


def attn_forward(p, row, loc, cfg, hook, layer, fresh, deliver, relay=None):
    micros, rows, size, full = cfg.micros, cfg.rows, cfg.size, p.full
    blocks = rows // BLOCK
    factor = size ** (-0.5)
    states = States(row, cfg.groups, p, False)
    qs, ks, vs = (pl.ds(i * size, size) for i in range(3))
    mask = pair_masks(2 * BLOCK)
    gather_first(row, full, micros, fresh)
    gate_columns(p.gates[layer, 0 : micros * rows // 128, :], p.gate)
    heads = Heads(p, row, cfg, layer)
    pk, pv = heads.persist()
    keep = heads.own()
    for m in range(micros):
        row.ag_wait(full, m)
        hook(m)
        here = pl.ds(m * rows, rows)
        loc.start(full.at[here, :], p.xin_o.at[here, :])
        p.qkv[here, :] = dot(full[here, :], p.wq[0]).astype(BF16)
        loc.start(p.qkv.at[here, :], p.qkv_o.at[here, :])
        total = jnp.zeros((size, size), F32)
        for b in range(blocks):
            at = pl.ds(m * rows + b * BLOCK, BLOCK)
            keys = (p.qkv[at, ks].astype(F32) * p.gate[at, :]).astype(BF16)
            fresh = dot(keys, p.qkv[at, vs], 0, 0)
            p.update[m * blocks + b] = fresh
            total = keep(m, b) * total + fresh
        p.leaving[m] = total.astype(BF16)
        states.start(m)
        gather_more(row, full, micros, m)
        hook(10 + m)
    for m in range(micros):
        here = pl.ds(m * rows, rows)
        states.wait(m)
        states.fold(m, heads.through)
        memory = p.entering[...]
        for b in range(0, blocks, 2):
            at = pl.ds(m * rows + b * BLOCK, 2 * BLOCK)
            q, ky, v = p.qkv[at, qs], p.qkv[at, ks], p.qkv[at, vs]
            inner, outer = pair_probs(q, ky, pk, mask, factor)
            value = dot(inner.astype(BF16), v) + dot(outer.astype(BF16), pv)
            reads = []
            for i in range(2):
                now = keep(m, b + i) * memory
                low = now.astype(BF16)
                p.state[m * blocks + b + i] = low
                reads.append(dot(q[i * BLOCK : (i + 1) * BLOCK, :], low) * factor)
                memory = now + p.update[m * blocks + b + i]
            p.mixed[at, :] = (value + jnp.concatenate(reads, axis=0)).astype(BF16)
        hook(20 + m)
        row.part[here, :] = dot(p.mixed[here, :], p.wo_dst[0], 1, 1).astype(BF16)
        loc.start(p.mixed.at[here, :], p.mixed_o.at[here, :])
        row.rs_start(m)
        if m >= 1:
            row.rs_pair(m - 1)
        if m >= 2:
            row.rs_transit(m - 2)
        hook(30 + m)
    loc.start(p.state, p.state_o)
    tail(row, micros, lambda m: deliver(m, row.rs_result(m)), hook, (), relay)
    states.drain()


def attn_backward(p, row, loc, cfg, hook, layer, loads, late, deliver, fill, relay=None):
    micros, rows, size, width, full = cfg.micros, cfg.rows, cfg.size, cfg.width, p.full
    blocks = rows // BLOCK
    factor = size ** (-0.5)
    states = States(row, cfg.groups, p, True)
    qs, ks, vs = (pl.ds(i * size, size) for i in range(3))
    in_cols, out_cols = pl.ds(0, 3 * size), pl.ds(3 * size, size)
    mask = pair_masks(2 * BLOCK)
    p.dpersist[...] = jnp.zeros_like(p.dpersist)
    gate_columns(p.gates[layer, 0 : micros * rows // 128, :], p.gate)
    heads = Heads(p, row, cfg, layer)
    pk, pv = heads.persist()
    keep = heads.own()
    gather_first(row, full, micros, False, fill)
    for copy in loads:
        loc.wait(copy)
    for m in range(micros):
        row.ag_wait(full, m)
        hook(m)
        here = pl.ds(m * rows, rows)
        p.dmix[here, :] = dot(full[here, :], p.wo[0]).astype(BF16)
        total = jnp.zeros((size, size), F32)
        for b in reversed(range(blocks)):
            at = pl.ds(m * rows + b * BLOCK, BLOCK)
            fresh = dot(p.qkv[at, qs], p.dmix[at, :], 0, 0) * factor
            p.update[m * blocks + b] = fresh
            total = keep(m, b) * (fresh + total)
        p.leaving[m] = total.astype(BF16)
        states.start(m)
        gather_more(row, full, micros, m)
        hook(10 + m)
    for m in range(micros):
        here = pl.ds(m * rows, rows)
        states.wait(m)
        states.fold(m, heads.through)
        memory = p.entering[...]
        for b in reversed(range(0, blocks, 2)):
            at = pl.ds(m * rows + b * BLOCK, 2 * BLOCK)
            q, ky, v, d = p.qkv[at, qs], p.qkv[at, ks], p.qkv[at, vs], p.dmix[at, :]
            inner, outer = pair_probs(q, ky, pk, mask, factor)
            d_inner = dot(d, v, 1, 1)
            d_outer = dot(d, pv, 1, 1)
            centre = jnp.sum(inner * d_inner, axis=1, keepdims=True) + jnp.sum(
                outer * d_outer, axis=1, keepdims=True
            )
            d_inner = (inner * (d_inner - centre)).astype(BF16)
            d_outer = (outer * (d_outer - centre)).astype(BF16)
            inner, outer = inner.astype(BF16), outer.astype(BF16)
            p.dpersist[0] += dot(d_outer, q, 0, 0) * factor
            p.dpersist[1] += dot(outer, d, 0, 0)
            dq = dot(d_inner, ky) + dot(d_outer, pk)
            dk = dot(d_inner, q, 0, 0) * factor
            dv = dot(inner, d, 0, 0)
            keys = (ky.astype(F32) * p.gate[at, :]).astype(BF16)
            parts = [None, None]
            for i in (1, 0):
                sub = slice(i * BLOCK, (i + 1) * BLOCK)
                low = memory.astype(BF16)
                parts[i] = (
                    dot(d[sub, :], p.state[m * blocks + b + i], 1, 1),
                    dot(v[sub, :], low, 1, 1),
                    dot(keys[sub, :], low),
                )
                memory = keep(m, b + i) * (p.update[m * blocks + b + i] + memory)
            more_q, more_k, more_v = (jnp.concatenate(pieces, axis=0) for pieces in zip(*parts))
            p.dqkv[at, qs] = ((dq + more_q) * factor).astype(BF16)
            p.dqkv[at, ks] = (dk + p.gate[at, :] * more_k).astype(BF16)
            p.dqkv[at, vs] = (dv + more_v).astype(BF16)
        row.part[here, :] = dot(p.dqkv[here, :], p.wq[0], 1, 1).astype(BF16)
        row.rs_start(m)
        if m >= 1:
            row.rs_pair(m - 1)
        if m >= 2:
            row.rs_transit(m - 2)
        hook(30 + m)

    def out_grad():
        for copy in late:
            loc.wait(copy)

        @pl.loop(0, width // 256)
        def _(t):
            at = pl.ds(pl.multiple_of(t * 256, 256), 256)
            p.grad[0, at, out_cols] = dot(full[:, at], p.mixed[...], 0, 0).astype(BF16)

    def qkv_grad():
        @pl.loop(0, width // 256)
        def _(t):
            at = pl.ds(pl.multiple_of(t * 256, 256), 256)
            p.grad[0, at, in_cols] = dot(p.xin[:, at], p.dqkv[...], 0, 0).astype(BF16)

        hook(60)

    tail(row, micros, lambda m: deliver(m, row.rs_result(m)), hook, [out_grad, qkv_grad], relay)
    states.drain()


VM = pl.BlockSpec(memory_space=pltpu.VMEM)
SM = pl.BlockSpec(memory_space=pltpu.SMEM)
HB = pl.BlockSpec(memory_space=pl.ANY)


def vm(dims, dtype=BF16):
    return pltpu.VMEM(dims, dtype)


def launch(name, collective, body, ins, outs, scratch):
    names = list(ins) + list(outs) + list(scratch)

    def kernel(*refs):
        body(SimpleNamespace(**dict(zip(names, refs))))

    results = pl.pallas_call(
        kernel,
        out_shape=tuple(jax.ShapeDtypeStruct(d, t) for d, t, _ in outs.values()),
        in_specs=[spec for _, spec in ins.values()],
        out_specs=tuple(spec for _, _, spec in outs.values()),
        scratch_shapes=list(scratch.values()),
        compiler_params=pltpu.CompilerParams(
            collective_id=collective, has_side_effects=True, vmem_limit_bytes=VMEM_LIMIT
        ),
        name=name,
    )(*[a for a, _ in ins.values()])
    return SimpleNamespace(**dict(zip(outs, results)))


def local(
    tokens, cotangent, block_order, lengths, decay, write_gate, gain_attn, w_query, w_key, w_value,
    persist_key, persist_value, w_output, gain_ffn, w_gate, w_up, w_down,
):
    sec, row_id, col = (lax.axis_index(a) for a in ("section", "row", "col"))
    groups = lax.axis_size("col")
    micros, rows, features = tokens.shape
    width = features * 4
    own, blocks, all_rows, size = rows // 8, rows // BLOCK, micros * rows, features // 2
    ffh = w_gate.shape[2] // 2
    per = persist_key.shape[1]
    persist = per * groups
    cfg = SimpleNamespace(
        micros=micros, rows=rows, own=own, size=size, width=width, groups=groups, blocks=blocks, per=per
    )
    total_blocks = block_order.shape[1]
    positions = jnp.arange(total_blocks, dtype=jnp.int32)
    my_blocks = col * blocks + jnp.arange(blocks, dtype=jnp.int32)
    deal_picks = lax.dynamic_slice_in_dim(block_order, col * blocks, blocks, 1)
    matches = (block_order[:, :, None] == my_blocks[None, None, :]).astype(jnp.int32)
    back_picks = jnp.sum(matches * positions[None, :, None], axis=1)

    def lanes(a):
        return jnp.pad(a, ((0, 0),) * (a.ndim - 1) + ((0, 128 - a.shape[-1]),))

    def eights(a):
        return jnp.pad(a, ((0, 0),) * (a.ndim - 2) + ((0, -a.shape[-2] % 8), (0, 0)))

    share = gain_attn.shape[1]
    own_gains = jnp.concatenate([gain_attn, gain_ffn], axis=0).astype(F32)
    placed = lax.dynamic_update_slice(
        jnp.zeros((2, features), F32), own_gains, (jnp.zeros_like(col), col * share)
    )
    packed = jnp.concatenate(
        [eights(placed.reshape(-1, 128))]
        + [
            eights(a[0].reshape(per, 2, size).transpose(1, 0, 2)).reshape(16, size).astype(F32)
            for a in (persist_key, persist_value)
        ]
        + [eights(lanes(decay[0].transpose(2, 0, 1).reshape(2, -1)))],
        axis=0,
    )
    gate_rows = eights(write_gate[0].transpose(2, 0, 1).reshape(2, -1, 128)) / BLOCK
    ends = jnp.cumsum(lengths, axis=1)
    is_start = jnp.any(positions[None, :, None] == (ends - lengths)[:, None, :], axis=2)
    starts = jnp.where(is_start, 0.0, 1.0).reshape(micros, groups, blocks).transpose(1, 0, 2)
    starts = jnp.broadcast_to(lanes(starts.reshape(groups, -1))[:, None], (groups, 8, 128))

    def cols_split(w):
        return w.reshape(w.shape[0], 2, -1).transpose(1, 0, 2)

    def rows_split(w):
        return w.reshape(2, -1, w.shape[1]).transpose(0, 2, 1)

    blocks_a = jnp.concatenate(
        [cols_split(w[0]) for w in (w_query, w_key, w_value)] + [rows_split(w_output[0])], axis=2
    )[:, None]
    blocks_b = jnp.stack(
        [cols_split(w_gate[0]), cols_split(w_up[0]), rows_split(w_down[0])], axis=1
    )

    a_dims, b_dims = blocks_a.shape[1:], blocks_b.shape[1:]
    q_dims, o_dims, one_dims = (1, a_dims[1], 3 * size), (1, a_dims[1], size), (1,) + b_dims[1:]
    grad_a_dims, grad_b_dims = (1, width, 4 * size), (3, width, ffh)
    stage_dims = (micros, rows, size)
    by_block = (micros, blocks, BLOCK, size)
    gain_rows = 4 * width // 128
    half_gains = width // 128
    hbm = lambda dims, dtype=BF16: (dims, dtype, HB)

    def row_scratch(prefix):
        return {
            "part": vm((all_rows, width)),
            "pair": vm((micros, 4 * own, width)),
            "both": vm((micros, 4, own, width)),
            "transit": vm((micros, 2, own, width // 2)),
            "final": vm((micros, 2, own, width)),
            prefix + "send": pltpu.SemaphoreType.DMA((micros, N_AG + N_RS)),
            prefix + "recv": pltpu.SemaphoreType.DMA((micros, N_AG + N_RS)),
            prefix + "full": vm((all_rows, width)),
        }

    shared_rows = ("part", "pair", "both", "transit", "final")

    def attn_scratch(prefix):
        names = dict(
            update=vm((micros * blocks, size, size), F32),
            entering=vm((size, size), F32),
            leaving=vm((micros, size, size)),
            box=vm((micros, groups, size, size)),
            ssend=pltpu.SemaphoreType.DMA((micros, groups)),
            srecv=pltpu.SemaphoreType.DMA((micros, groups)),
            gate=vm((all_rows, 1), F32),
            persist=vm((persist, size), F32),
            qkv=vm((all_rows, 3 * size)),
            state=vm((micros * blocks, size, size)),
            mixed=vm((all_rows, size)),
        )
        return {**row_scratch(prefix), **{prefix + a: b for a, b in names.items()}}

    def ffn_scratch(prefix):
        names = {a: vm((all_rows, ffh)) for a in ("gp", "up", "act")}
        return {**row_scratch(prefix), **{prefix + a: b for a, b in names.items()}}

    def view_of(k, prefix, **more):
        names = {a[len(prefix) :]: b for a, b in vars(k).items() if a.startswith(prefix)}
        return SimpleNamespace(**{**names, **more})

    def rows_of(k, prefix):
        p = view_of(k, prefix)
        row = Rows(rows, own, width, p.send, p.recv)
        row.buffers = (k.part, k.pair, k.both, k.transit, k.final)
        row.part = k.part
        return row

    def greet_all(row):
        row.greet(
            plane_peers(row)
            + [(row.s, row.r, lax.rem(row.c + i, groups)) for i in range(1, groups)]
        )

    def hooks(plan, prefix):
        def hook(point):
            for action in plan.get(prefix + point, ()):
                action()

        return hook

    def pusher(send, recv):
        def push(src, dst, i, to):
            copy = pltpu.make_async_remote_copy(
                src_ref=src,
                dst_ref=dst,
                send_sem=send.at[i],
                recv_sem=recv.at[i],
                device_id=to,
                device_id_type=MESH,
            )
            copy.start()
            return copy

        return push

    def blocks_from(buf, picks, stage, m, lead=()):
        for b in range(blocks):
            stage[lead + (m, pl.ds(b * BLOCK, BLOCK))] = buf[lead + (m, picks[m, b])]

    def forward_names(l):
        outs = dict(
            a_xin_o=hbm((all_rows, width)),
            a_qkv_o=hbm((all_rows, 3 * size)),
            a_state_o=hbm((micros * blocks, size, size)),
            a_mixed_o=hbm((all_rows, size)),
            f_xin_o=hbm((all_rows, width)),
            f_gp_o=hbm((all_rows, ffh)),
            f_up_o=hbm((all_rows, ffh)),
            f_act_o=hbm((all_rows, ffh)),
            wo_o=hbm((1, width, size)),
            w_o=hbm((3, width, ffh)),
            mid=((micros, own, width), F32, VM),
            y=((micros, own, width), BF16, VM),
        )
        return outs, {**attn_scratch("a_"), **ffn_scratch("f_")}

    def forward_layer(k, l, x, wq, loc, plan, base, row_a, small, fresh, leave, relay):
        row_f = rows_of(k, "f_")
        gain_f = gain_row(small, cfg, l, 1)

        def middle(m, summed):
            k.mid[m] = x[m].astype(F32) + summed
            norm_to(k.f_full, gain_f, k.mid[m], row_f.span(m, row_f.s, row_f.r))
            row_f.ag_start(k.f_full, m)

        def leave_y(m, summed):
            k.y[m] = (k.mid[m] + summed).astype(BF16)
            leave(m)

        p = view_of(k, "a_", wq=wq, wo_dst=k.wo_dst, **vars(small))
        attn_forward(
            p, row_a, loc, cfg, hooks(plan, base), l, fresh, middle,
            lambda: row_f.ag_pass(k.f_full, 0),
        )
        row_a.finish()
        loc.start(k.wo_dst, k.wo_o)
        p = view_of(k, "f_", gate_dst=k.gate_dst, up_dst=k.up_dst, down_dst=k.down_dst)
        ffn_forward(p, row_f, loc, cfg, hooks(plan, base + F), leave_y, relay)
        row_f.finish()
        for i, w in enumerate((k.gate_dst, k.up_dst, k.down_dst)):
            loc.start(w, k.w_o.at[pl.ds(i, 1)])

    def one_b(tag, layer, which):
        view = lambda k, row: k.shards_b.at[layer, pl.ds(which, 1)]
        return Gather(tag, None, one_dims, groups, 1, view, "scratch")

    def q_of(ref, layer):
        return ref.at[layer, :, :, pl.ds(0, 3 * size)]

    def o_of(ref, layer):
        return ref.at[layer, :, :, pl.ds(3 * size, size)]

    def lanes_of_core(name):
        def view(k, row):
            mine = pl.ds(pl.multiple_of(row.s * size, 128), size)
            return getattr(k, name).at[:, :, :, mine]

        return view

    tokens_b = tokens.reshape(micros, blocks, BLOCK, features)
    cotangent_b = cotangent.reshape(micros, blocks, BLOCK, features)
    deal = Gather("deal_", tokens_b, by_block, groups, 1, lanes_of_core("deal_src"), "scratch")
    q0 = Gather("q0_", None, q_dims, groups, 1, lambda k, row: q_of(k.shards_a, 0), "scratch")
    wo0 = Gather("wo_", None, o_dims, groups, 1, lambda k, row: o_of(k.shards_a, 0), "scratch")
    gate0, up0, down0 = (one_b(t, 0, i) for i, t in enumerate(("gate_", "up_", "down_")))
    q1 = Gather("q1_", None, q_dims, groups, 1, lambda k, row: q_of(k.shards_a, 1), "scratch")
    wo1 = Gather("L1_wo_", None, o_dims, groups, 1, lambda k, row: o_of(k.shards_a, 1), "scratch")
    gate1, up1, down1 = (
        one_b(t, 1, i) for i, t in enumerate(("L1_gate_", "L1_up_", "L1_down_"))
    )
    cot = Gather("cot_", cotangent_b, by_block, groups, 1, lanes_of_core("cot_src"), "scratch")
    sides1 = [deal, q0, wo0, gate0, up0, down0, q1, wo1, gate1, up1, down1, cot]
    swap1, swap_y, swap_c = Swap("swap_"), Swap("swapy_"), Swap("swapc_")

    def first_body(k):
        row = rows_of(k, "a_")
        loc = Local(k.sems)
        greet_all(row)
        for side in sides1:
            side.bind(k, row, groups)
        push = pusher(k.psend, k.precv)
        crossing, keeps_here = [], []
        for i, (src, dst) in enumerate(((k.blocks_a, k.shards_a), (k.blocks_b, k.shards_b))):
            keeps_here.append(loc.start(src.at[row.s], dst.at[row.s]))
            crossing.append(push(src.at[1 - row.s], dst.at[row.s], groups + 9 + i, row.sib))
        deal.start()
        k.line[row.s, row.c] = k.packed[...]
        k.gates[row.s] = k.gate_rows[row.s]
        small = [
            push(
                k.packed,
                k.line.at[row.s, row.c],
                i,
                (row.s, row.r, lax.rem(row.c + i, groups)),
            )
            for i in range(1, groups)
        ]
        late = [push(k.gate_rows.at[1 - row.s], k.gates.at[row.s], 0, row.sib)]
        crossing[0].wait_recv()
        loc.wait(keeps_here[0])
        q0.start()
        deal.step()
        for copy in small:
            copy.wait_recv()
        total = k.line[row.s, 0, 0:8, :]
        for j in range(1, groups):
            total = total + k.line[row.s, j, 0:8, :]
        k.gains[row.s, row.r] = total
        for i, ps, pr in others(row):
            mine = k.gains.at[row.s, row.r]
            late.append(push(mine, mine, groups + i, (ps, pr, row.c)))
        late.append(push(k.line.at[row.s], k.line.at[row.s], groups + 8, row.sib))
        crossing[1].wait_recv()
        loc.wait(keeps_here[1])
        q0.step()
        wo0.start()
        deal.step()
        q0.step()
        gate0.start()
        up0.start()
        wo0.step()
        deal.finish()
        for m in range(micros):
            blocks_from(k.deal_dst, k.picks, k.stage, m)
        swap1.start(k, row, own, size, k.stage, k.x, True)
        q0.finish()
        wo0.step()
        for copy in late:
            copy.wait_recv()
        gain = gain_row(k, cfg, 0, 0)
        swap1.wait()
        for m in range(micros):
            norm_to(k.a_full, gain, k.x[m].astype(F32), row.span(m, row.s, row.r))
        ag_begin(row, k.a_full)
        loc.start(k.q0_dst, k.q0_o)
        def deal_cot():
            cot.finish()
            for m in range(micros):
                blocks_from(k.cot_dst, k.picks, k.stage_c, m)
            swap_c.start(k, row, own, size, k.stage_c, k.dy, True)

        plan = place(
            PLACES["first"],
            [
                gate0.step, up0.step, down0.start, gate0.step, up0.step, down0.step, down0.step,
                q1.start, q1.step, q1.step, wo1.start, wo1.step, wo1.step, gate1.start, up1.start,
                down1.start, gate1.step, up1.step, down1.step, gate1.step, up1.step, down1.step,
                cot.start, cot.step, cot.step, deal_cot,
            ],
            [
                (A + 20, wo0.finish), (F, gate0.finish), (F, up0.finish), (F + 10, down0.finish),
                (NEXT, q1.finish), (NEXT + 20, wo1.finish), (NEXT + F, gate1.finish),
                (NEXT + F, up1.finish), (NEXT + F + 10, down1.finish),
            ],
        )
        small_refs = SimpleNamespace(line=k.line, gains=k.gains, gates=k.gates, starts=k.starts)
        second = SimpleNamespace(**{**vars(k), **vars(view_of(k, "L1_"))})
        row_next = rows_of(second, "a_")
        gain_next = gain_row(small_refs, cfg, 1, 0)

        def begin_next(m):
            rows_here = row_next.span(m, row_next.s, row_next.r)
            norm_to(second.a_full, gain_next, k.y[m].astype(F32), rows_here)
            row_next.ag_start(second.a_full, m)

        forward_layer(
            k, 0, k.x, k.q0_dst, loc, plan, A, row, small_refs, True, begin_next,
            lambda: row_next.ag_pass(second.a_full, 0),
        )
        swap_y.start(k, row, own, size, k.y, k.stage_o, False)
        forward_layer(
            second, 1, k.y, k.q1_dst, loc, plan, NEXT, row_next, small_refs, False, lambda m: None,
            None,
        )
        loc.start(k.q1_dst, k.q1_o)
        for side in sides1:
            side.finish()
        swap_y.wait()
        swap_c.wait()
        for copy in crossing + small + late:
            copy.wait_send()
        for side in sides1 + [swap1, swap_y, swap_c]:
            side.drain()
        loc.finish()

    outs, scratch = forward_names(0)
    for names, into in zip(forward_names(1), (outs, scratch)):
        into.update({"L1_" + a: b for a, b in names.items() if a not in shared_rows})
    ins = dict(
        picks=(deal_picks, SM),
        blocks_a=(blocks_a, HB),
        blocks_b=(blocks_b, HB),
        packed=(packed, VM),
        gate_rows=(gate_rows, VM),
        starts=(starts, VM),
    )
    outs.update(
        x=((micros, own, width), BF16, VM),
        shards_a=hbm(blocks_a.shape),
        shards_b=hbm(blocks_b.shape),
        line=((2, groups) + packed.shape, F32, VM),
        gains=((2, 4, 8, 128), F32, VM),
        gates=((2,) + gate_rows.shape[1:], F32, VM),
        q0_o=hbm((1, width, 3 * size)),
        q1_o=hbm((1, width, 3 * size)),
        dy=((micros, own, width), BF16, VM),
        stage_o=hbm(stage_dims),
    )
    scratch.update(
        stage=vm(stage_dims),
        stage_c=vm(stage_dims),
        psend=pltpu.SemaphoreType.DMA((groups + 11,)),
        precv=pltpu.SemaphoreType.DMA((groups + 11,)),
        sems=pltpu.SemaphoreType.DMA((80,)),
    )
    for side in sides1:
        side.declare(ins, outs, scratch, groups)
    for swap in (swap1, swap_y, swap_c):
        swap.declare(scratch)
    f0 = launch("forward", 0, first_body, ins, outs, scratch)
    f1 = SimpleNamespace(**{**vars(f0), **vars(view_of(f0, "L1_"))})

    smalls = dict(
        line=(f0.line, VM), gains=(f0.gains, VM), gates=(f0.gates, VM),
        starts=(starts, VM),
    )

    def small_of(k):
        return SimpleNamespace(line=k.line, gains=k.gains, gates=k.gates, starts=k.starts)

    def backward_names(kept, dy, x, wq):
        ins = dict(
            dy=(dy, VM), mid=(kept.mid, VM), x=(x, VM), w_h=(kept.w_o, HB),
            wo_h=(kept.wo_o, HB), wq_h=(wq, HB), ax_h=(kept.a_xin_o, HB),
            qkv_h=(kept.a_qkv_o, HB), state_h=(kept.a_state_o, HB),
            mixed_h=(kept.a_mixed_o, HB), fx_h=(kept.f_xin_o, HB), gp_h=(kept.f_gp_o, HB),
            up_h=(kept.f_up_o, HB), act_h=(kept.f_act_o, HB), **smalls,
        )
        scratch = {**attn_scratch("a_"), **ffn_scratch("f_")}
        scratch.update(
            f_w=vm((3, width, ffh)), xin=vm((all_rows, width)),
            f_dg=vm((all_rows, ffh)), f_du=vm((all_rows, ffh)), f_grad=vm(grad_b_dims),
            a_wo=vm((1, width, size)), a_wq=vm((1, width, 3 * size)),
            a_dmix=vm((all_rows, size)),
            a_dqkv=vm((all_rows, 3 * size)), a_grad=vm(grad_a_dims),
            dmid=vm((micros, own, width), F32), sems=pltpu.SemaphoreType.DMA((48,)),
        )
        return ins, scratch

    def backward_layer(k, l, loc, sides, swaps_begin, plan, dx_done):
        row_f, row_a = rows_of(k, "f_"), rows_of(k, "a_")
        first = [
            loc.start(a, b) for a, b in ((k.w_h, k.f_w), (k.gp_h, k.f_gp), (k.up_h, k.f_up))
        ]
        late_f = [loc.start(a, b) for a, b in ((k.act_h, k.f_act), (k.fx_h, k.xin))]
        loads_a = [
            loc.start(a, b)
            for a, b in (
                (k.wo_h, k.a_wo), (k.qkv_h, k.a_qkv), (k.wq_h, k.a_wq), (k.state_h, k.a_state)
            )
        ]
        late_a = [loc.start(k.mixed_h, k.a_mixed)]
        for m in range(micros):
            k.f_full[row_f.span(m, row_f.s, row_f.r), :] = k.dy[m]
        greet_all(row_f)
        for side in sides:
            side.bind(k, row_f, groups)
        ag_begin(row_f, k.f_full)
        swaps_begin(row_f)
        gain_a, gain_f = gain_row(k, cfg, l, 0), gain_row(k, cfg, l, 1)
        k.dgain[...] = jnp.zeros_like(k.dgain)

        def middle(m, summed):
            back, gains = norm_back(k.mid[m], gain_f, summed)
            k.dmid[m] = k.dy[m].astype(F32) + back
            k.dgain[1:2, :] += gains
            k.a_full[row_a.span(m, row_a.s, row_a.r), :] = k.dmid[m].astype(BF16)
            row_a.ag_start(k.a_full, m)

        def leave(m, summed):
            back, gains = norm_back(k.x[m].astype(F32), gain_a, summed)
            k.dx[m] = (k.dmid[m] + back).astype(BF16)
            k.dgain[0:1, :] += gains
            dx_done(m)

        left = ffn_backward(
            view_of(k, "f_", xin=k.xin), row_f, loc, cfg, hooks(plan, F), first, late_f, middle,
            lambda: row_a.ag_pass(k.a_full, 0),
        )
        row_f.finish()

        def load_xin():
            late_a.append(loc.start(k.ax_h, k.xin))

        left = list(left) + [load_xin]
        p = view_of(k, "a_", dpersist=k.dpersist, xin=k.xin, **vars(small_of(k)))
        attn_backward(p, row_a, loc, cfg, hooks(plan, A), l, loads_a, late_a, leave, left)
        return row_f, row_a

    def staged(tag, array, home=None):
        return Gather(tag, array.reshape(by_block), by_block, groups, 1, None, home)

    def grad_of(k):
        return k.f_grad

    y0 = staged("y0_", f1.stage_o)
    y1 = Gather("y1_", None, stage_dims, groups, 1, lambda k, row: k.stage)
    td1, tg1 = (Total(t, None, grad_b_dims, groups, (i, 1), grad_of) for t, i in (("td_", 2), ("tg_", 0)))
    sides3 = [y0, y1, td1, tg1]
    swap_y1 = Swap("swap_")

    def third_body(k):
        loc = Local(k.sems)

        def begin(row):
            y0.start()
            swap_y1.start(k, row, own, size, k.y, k.stage, False)

        def start_y1():
            swap_y1.wait()
            y1.start()

        plan = place(
            PLACES["third"],
            [
                y0.step, y0.step, start_y1, td1.start, y1.step, td1.step, tg1.start, td1.step, y1.step,
                tg1.step, tg1.step,
            ],
        )
        row_f, row_a = backward_layer(k, 1, loc, sides3, begin, plan, lambda m: None)
        for i in range(3):
            loc.start(k.f_grad.at[i], k.grad_b_o.at[i])
        loc.start(k.a_grad, k.grad_a_o)
        for side in sides3:
            side.finish()
        row_f.finish()
        row_a.finish()
        for side in sides3 + [swap_y1]:
            side.drain()
        loc.finish()

    ins, scratch = backward_names(f1, f1.dy, f0.y, f0.q1_o)
    ins["y"] = (f1.y, VM)
    small_outs = dict(
        dgain=((2, width), F32, VM),
        dpersist=((2, persist, size), F32, VM),
        dx=((micros, own, width), BF16, VM),
    )
    outs = dict(grad_a_o=hbm(grad_a_dims), grad_b_o=hbm(grad_b_dims), **small_outs)
    scratch["stage"] = vm(stage_dims)
    for side in sides3:
        side.declare(ins, outs, scratch, groups)
    swap_y1.declare(scratch)
    b1 = launch("backward_1", 2, third_body, ins, outs, scratch)

    small_rows = gain_rows + 4 * persist
    tu1 = Total("tu1_", b1.grad_b_o, grad_b_dims, groups, (1, 1), None, "scratch")
    ta1 = Total("ta1_", b1.grad_a_o, grad_a_dims, groups, (0, 1), None, "scratch")
    td0, tg0, tu0 = (
        Total(t, None, grad_b_dims, groups, (i, 1), grad_of, "scratch")
        for t, i in (("td_", 2), ("tg_", 0), ("tu_", 1))
    )
    ta0 = Total("ta0_", None, grad_a_dims, groups, (0, 1), lambda k: k.a_grad, "scratch")
    g1 = Gather("g1_", None, by_block, groups, 1, lambda k, row: k.staged1)
    g0 = [
        Gather(f"g0{m}_", None, by_block[1:], groups, 0, lambda k, row, m=m: k.staged0.at[m], "scratch")
        for m in range(micros)
    ]

    def blocked(stage, staged, m):
        for b in range(blocks):
            staged[m, b] = stage[m, b * BLOCK : (b + 1) * BLOCK, :]
    sides4 = [tu1, ta1, td0, tg0, tu0, ta0, g1, *g0]
    swap_g1, swaps0 = Swap("swap_"), [Swap(f"swap{m}_") for m in range(micros)]

    def last_body(k):
        loc = Local(k.sems)
        push = pusher(k.psend, k.precv)
        load_y = loc.start(k.y0_buf, k.whole)
        loads = [
            loc.start(a, b)
            for a, b in (
                (k.bg1, k.res_b.at[1, pl.ds(0, 1)]), (k.bd1, k.res_b.at[1, pl.ds(2, 1)]),
            )
        ]

        def begin(row):
            tu1.start()
            ta1.start()
            swap_g1.start(k, row, own, size, k.dy, k.stage, False)

        def start_g1():
            swap_g1.wait()
            for m in range(micros):
                blocked(k.stage, k.staged1, m)
            g1.start()

        def gather_g0(m):
            swaps0[m].wait()
            blocked(k.stage0, k.staged0, m)
            g0[m].start()

        def dx_done(m):
            swaps0[m].start(
                k, ta0.row, own, size, k.dx.at[pl.ds(m, 1)], k.stage0.at[pl.ds(m, 1)], False
            )
            if m >= 1:
                gather_g0(m - 1)

        plan = place(
            PLACES["last"],
            [
                tu1.step, ta1.step, start_g1, tu1.step, ta1.step, g1.step, td0.start, g1.step, td0.step,
                tg0.start, tu0.start, td0.step, tg0.step, tu0.step, tg0.step, tu0.step, ta0.start,
            ],
        )
        row_f, row = backward_layer(k, 0, loc, sides4, begin, plan, dx_done)
        for i in range(half_gains):
            lanes_here = slice(i * 128, (i + 1) * 128)
            for j, ref in enumerate((k.dgain, k.dgain1)):
                for kind in range(2):
                    at = (j * 2 + kind) * half_gains + i
                    k.smalls[at : at + 1, :] = ref[kind : kind + 1, lanes_here]
        for j, ref in enumerate((k.dpersist, k.dpersist1)):
            for kind in range(2):
                at = gain_rows + (j * 2 + kind) * persist
                k.smalls[at : at + persist, :] = ref[kind]
        gather_g0(micros - 1)
        pushes = []
        for i in range(1, groups):
            to = (row.s, row.r, lax.rem(row.c + i, groups))
            pushes.append(push(k.smalls, k.small_box.at[i], i, to))
        for copy in loads:
            loc.wait(copy)

        def all_restored(slot):
            for m in range(micros):
                for b in range(blocks):
                    where = pl.ds(b * BLOCK, BLOCK)
                    k.halves[slot, m, where, :] = k.whole[m, k.back[m, b]]

        loc.wait(load_y)
        all_restored(0)
        loc.wait(loc.start(k.y1_buf, k.whole))
        all_restored(1)
        moved, kept_here = [], []
        mine_lanes = pl.ds(pl.multiple_of(row.s * size, 128), size)

        def give(i, pair, out):
            moved.append(push(pair.at[1 - row.s], out, groups + 8 + i, row.sib))
            kept_here.append(loc.start(pair.at[row.s], out))

        give(0, k.halves.at[pl.ds(0, 2)], k.acts_o.at[:, :, mine_lanes])

        for g in g0:
            g.step()
        ta0.step()
        g1.finish()
        loc.wait(loc.start(k.g1_dst, k.whole))
        all_restored(3)
        for g in g0:
            g.step()
        ta0.step()
        for total in (td0, tg0, tu0, tu1, ta1):
            total.finish()
        k.res_b[0, pl.ds(2, 1)] = k.td_sum[...]
        k.res_b[0, pl.ds(0, 1)] = k.tg_sum[...]
        k.res_b[0, pl.ds(1, 1)] = k.tu_sum[...]
        k.res_b[1, pl.ds(1, 1)] = k.tu1_sum[...]
        k.res_a[1] = k.ta1_sum[...]
        give(1, k.res_b, k.grad_b.at[row.s])
        for copy in pushes:
            copy.wait_recv()
        total = k.smalls[...]
        for i in range(1, groups):
            total = total + k.small_box[i]
        k.small_sum[...] = total
        gains = []
        for i, ps, pr in others(row):
            src = k.small_sum.at[pl.ds(0, gain_rows), :]
            gains.append(push(src, k.gain_box.at[i], groups + i, (ps, pr, row.c)))
        ta0.finish()
        k.res_a[0] = k.ta0_sum[...]
        give(2, k.res_a, k.grad_a.at[row.s])
        for m, g in enumerate(g0):
            g.finish()
            buf = getattr(k, f"g0{m}_dst")
            for b in range(blocks):
                k.halves[2, m, pl.ds(b * BLOCK, BLOCK), :] = buf[k.back[m, b]]
        give(3, k.halves.at[pl.ds(2, 2)], k.grads_o.at[:, :, mine_lanes])
        for copy in gains:
            copy.wait_recv()
        total = k.small_sum[0:gain_rows, :]
        for i in range(1, 8):
            total = total + k.gain_box[i]
        k.gain_o[...] = total
        k.persist_o[...] = k.small_sum[gain_rows:, :]
        for copy in moved:
            copy.wait()
        for copy in pushes + gains:
            copy.wait_send()
        for side in sides4:
            side.finish()
        row_f.finish()
        row.finish()
        for side in sides4 + [swap_g1] + swaps0:
            side.drain()
        loc.finish()

    ins, scratch = backward_names(f0, b1.dx, f0.x, f0.q0_o)
    ins.update(
        y0_buf=(b1.y0_dst, HB),
        y1_buf=(b1.y1_dst.reshape(b1.y0_dst.shape), HB),
        bg1=(b1.tg_sum, HB),
        bd1=(b1.td_sum, HB),
        dgain1=(b1.dgain, VM),
        dpersist1=(b1.dpersist, VM),
        back=(back_picks, SM),
    )
    outs = dict(
        acts_o=((micros, rows, features), BF16, VM),
        grads_o=((micros, rows, features), BF16, VM),
        grad_a=((2,) + ta0.dims, BF16, VM),
        grad_b=((2, 3) + tu0.dims[1:], BF16, VM),
        gain_o=((gain_rows, 128), F32, VM),
        persist_o=((4 * persist, 128), F32, VM),
    )
    scratch.update(
        stage=vm(stage_dims),
        stage0=vm(stage_dims),
        whole=vm((micros, total_blocks, BLOCK, size)),
        staged0=vm(by_block),
        staged1=vm(by_block),
        halves=vm((4,) + stage_dims),
        res_a=vm((2,) + ta0.dims),
        res_b=vm((2, 3) + tu0.dims[1:]),
        smalls=vm((small_rows, 128), F32),
        small_box=vm((groups, small_rows, 128), F32),
        small_sum=vm((small_rows, 128), F32),
        gain_box=vm((8, gain_rows, 128), F32),
        dgain=vm((2, width), F32),
        dpersist=vm((2, persist, size), F32),
        dx=vm((micros, own, width)),
        psend=pltpu.SemaphoreType.DMA((groups + 12,)),
        precv=pltpu.SemaphoreType.DMA((groups + 12,)),
    )
    for side in sides4:
        side.declare(ins, outs, scratch, groups)
    for swap in [swap_g1] + swaps0:
        swap.declare(scratch)
    closed = launch("backward_0", 3, last_body, ins, outs, scratch)

    def cols_join(pair):
        return jnp.concatenate([pair[0], pair[1]], axis=1).astype(F32)[None]

    def rows_join(pair):
        return jnp.concatenate([pair[0].T, pair[1].T], axis=0).astype(F32)[None]

    grad_a, grad_b = closed.grad_a[:, 0], closed.grad_b
    heads = [cols_join(grad_a[:, :, i * size : (i + 1) * size]) for i in range(3)]
    grad_out = rows_join(grad_a[:, :, 3 * size :])
    grad_gate, grad_up = cols_join(grad_b[:, 0]), cols_join(grad_b[:, 1])
    grad_down = rows_join(grad_b[:, 2])
    gain_sum = closed.gain_o.reshape(2, 2, width)
    my_gain = lax.dynamic_slice_in_dim(
        lax.dynamic_index_in_dim(gain_sum, sec, 0, False), (row_id * groups + col) * share, share, 1
    )
    persist_sum = closed.persist_o.reshape(2, 2, persist, size)
    persist_sum = lax.dynamic_slice_in_dim(persist_sum, col * per, per, 2)
    mine_p = lax.dynamic_index_in_dim(persist_sum, sec, 0, False)
    got_p = lax.ppermute(
        lax.dynamic_index_in_dim(persist_sum, 1 - sec, 0, False), "section", [(0, 1), (1, 0)]
    )
    grad_persist = jnp.concatenate(
        [jnp.where(sec == 0, mine_p, got_p), jnp.where(sec == 0, got_p, mine_p)], axis=2
    )
    return (
        closed.acts_o[None],
        closed.grads_o[None],
        my_gain[0][None],
        heads[0],
        heads[1],
        heads[2],
        grad_persist[0][None],
        grad_persist[1][None],
        grad_out,
        my_gain[1][None],
        grad_gate,
        grad_up,
        grad_down,
    )


def solution(mesh):
    weight = P("section", "col", "row")
    across = P("section", "row", "col")
    gain = P("section", ("row", "col"))
    rows = P("section", None, "col", "row")
    return jax.shard_map(
        local,
        mesh=mesh,
        in_specs=(
            P(None, "col", "row"), P(None, "col", "row"), P(), P(), rows, rows, gain, weight, weight,
            weight, weight, weight, across, gain, weight, weight, across,
        ),
        out_specs=(
            rows, rows, gain, weight, weight, weight, weight, weight, across, gain, weight, weight,
            across,
        ),
        check_vma=False,
    )
```

```python
from types import SimpleNamespace

import jax
import jax.numpy as jnp
from jax import lax
from jax.experimental import pallas as pl
from jax.experimental.pallas import tpu as pltpu
from jax.sharding import PartitionSpec as P

BLOCK = 64
EPS = 1e-06
MESH = pl.DeviceIdType.MESH
F32 = jnp.float32
BF16 = jnp.bfloat16
VMEM_LIMIT = 60 << 20
N_AG, N_RS = 8, 7

A, F, NEXT = 0, 100, 200
PLACES = dict(
    first=[
        A, A + 10, A + 30, A + 21, A + 12, A + 32, A + 41, A + 41, F + 31, F + 32,
        F + 40, NEXT, NEXT, F + 40, F + 41,
        NEXT + 12, NEXT + 2, NEXT + 12, NEXT + 41, NEXT + 30, NEXT + 32, NEXT + 40,
        NEXT + 41, NEXT + F + 11, NEXT + F + 32, NEXT + F + 41,
    ],
    third=[
        F + 30, F + 32, F + 30, F + 52, F + 52, F + 50, A + 2, A + 32, A + 12, A + 31,
        A + 32,
    ],
    last=[
        F + 40, F, F, A + 31, F + 31, F + 40, F + 50, A + 10, A + 30, F + 50,
        F + 51, A + 31, A + 1, A + 2, A + 40, A + 30, A + 60,
    ],
)


def place(points, actions, fixed=()):
    plan = {}
    for point, action in list(zip(points, actions, strict=True)) + list(fixed):
        plan.setdefault(point, []).append(action)
    return plan


def dot(a, b, ca=1, cb=0):
    return lax.dot_general(a, b, (((ca,), (cb,)), ((), ())), preferred_element_type=F32)


class Rows:
    def __init__(self, rows, own, width, send, recv):
        self.rows, self.own, self.width, self.half = rows, own, width, width // 2
        self.send, self.recv = send, recv
        self.s, self.r, self.c = (lax.axis_index(a) for a in ("section", "row", "col"))
        self.rx = self.r + 1 - 2 * lax.rem(self.r, 2)
        self.ry = lax.rem(self.r + 2, 4)
        self.rd = lax.rem(self.rx + 2, 4)
        self.x = (self.s, self.rx, self.c)
        self.y = (self.s, self.ry, self.c)
        self.sib = (1 - self.s, self.r, self.c)
        self.started = []

    def greet(self, others=()):
        barrier = pltpu.get_barrier_semaphore()
        peers = [self.x, self.y, self.sib] + list(others)
        for peer in peers:
            pl.semaphore_signal(barrier, inc=1, device_id=peer, device_id_type=MESH)
        pl.semaphore_wait(barrier, len(peers))

    def copy(self, src, dst, m, k, peer):
        return pltpu.make_async_remote_copy(
            src_ref=src,
            dst_ref=dst,
            send_sem=self.send.at[m, k],
            recv_sem=self.recv.at[m, k],
            device_id=peer,
            device_id_type=MESH,
        )

    def go(self, copy):
        copy.start()
        self.started.append(copy)

    def finish(self):
        for copy in self.started:
            copy.wait_send()
        self.started = []

    def span(self, m, s, r):
        return pl.ds(pl.multiple_of(m * self.rows + (s * 4 + r) * self.own, 16), self.own)

    def ag_copy(self, full, m, k):
        left, right = pl.ds(0, self.half), pl.ds(self.half, self.half)
        mine, atx, aty, atd = (
            self.span(m, self.s, r) for r in (self.r, self.rx, self.ry, self.rd)
        )
        if k == 0:
            return self.copy(full.at[mine, :], full.at[mine, :], m, 0, self.x)
        if k == 1:
            return self.copy(full.at[mine, :], full.at[mine, :], m, 1, self.y)
        if k == 2:
            return self.copy(full.at[mine, :], full.at[mine, :], m, 2, self.sib)
        if k == 3:
            return self.copy(full.at[atx, left], full.at[atx, left], m, 3, self.y)
        if k == 4:
            return self.copy(full.at[aty, right], full.at[aty, right], m, 4, self.x)
        if k == 5:
            return self.copy(full.at[atx, :], full.at[atx, :], m, 5, self.sib)
        if k == 6:
            return self.copy(full.at[aty, :], full.at[aty, :], m, 6, self.sib)
        return self.copy(full.at[atd, :], full.at[atd, :], m, 7, self.sib)

    def ag_start(self, full, m):
        for k in (0, 1, 2):
            self.go(self.ag_copy(full, m, k))

    def ag_pass(self, full, m):
        self.ag_copy(full, m, 0).wait_recv()
        self.go(self.ag_copy(full, m, 3))
        self.go(self.ag_copy(full, m, 5))
        self.ag_copy(full, m, 1).wait_recv()
        self.go(self.ag_copy(full, m, 4))
        self.go(self.ag_copy(full, m, 6))

    def ag_diag(self, full, m):
        self.ag_copy(full, m, 3).wait_recv()
        self.ag_copy(full, m, 4).wait_recv()
        self.go(self.ag_copy(full, m, 7))

    def ag_wait(self, full, m):
        for k in (2, 5, 6, 7):
            self.ag_copy(full, m, k).wait_recv()

    def rs_copy(self, m, k):
        part, pair, both, transit, final = self.buffers
        left, right = pl.ds(0, self.half), pl.ds(self.half, self.half)
        if k == 8:
            other = pl.ds(
                pl.multiple_of(m * self.rows + (1 - self.s) * 4 * self.own, 16), 4 * self.own
            )
            return self.copy(part.at[other, :], pair.at[m], m, 8, self.sib)
        if k == 9:
            return self.copy(both.at[m, self.rd, :, left], transit.at[m, 0], m, 9, self.x)
        if k == 10:
            return self.copy(both.at[m, self.rd, :, right], transit.at[m, 1], m, 10, self.y)
        if k == 11:
            return self.copy(both.at[m, self.rx, :, left], final.at[m, 0, :, left], m, 11, self.x)
        if k == 12:
            return self.copy(both.at[m, self.ry, :, right], final.at[m, 1, :, right], m, 12, self.y)
        if k == 13:
            return self.copy(both.at[m, self.ry, :, left], final.at[m, 1, :, left], m, 13, self.y)
        return self.copy(both.at[m, self.rx, :, right], final.at[m, 0, :, right], m, 14, self.x)

    def rs_start(self, m):
        self.go(self.rs_copy(m, 8))

    def rs_pair(self, m):
        part, pair, both, _, _ = self.buffers
        self.rs_copy(m, 8).wait_recv()
        for r in range(4):
            mine = part[self.span(m, self.s, r), :].astype(F32)
            theirs = pair[m, r * self.own : (r + 1) * self.own, :].astype(F32)
            both[m, r] = (mine + theirs).astype(BF16)
        for k in (9, 10, 11, 12):
            self.go(self.rs_copy(m, k))

    def rs_transit(self, m):
        _, _, both, transit, _ = self.buffers
        left, right = pl.ds(0, self.half), pl.ds(self.half, self.half)
        self.rs_copy(m, 9).wait_recv()
        total = both[m, self.ry, :, left].astype(F32) + transit[m, 0].astype(F32)
        both[m, self.ry, :, left] = total.astype(BF16)
        self.go(self.rs_copy(m, 13))
        self.rs_copy(m, 10).wait_recv()
        total = both[m, self.rx, :, right].astype(F32) + transit[m, 1].astype(F32)
        both[m, self.rx, :, right] = total.astype(BF16)
        self.go(self.rs_copy(m, 14))

    def rs_result(self, m):
        _, _, both, _, final = self.buffers
        for k in (11, 12, 13, 14):
            self.rs_copy(m, k).wait_recv()
        return both[m, self.r].astype(F32) + final[m, 0].astype(F32) + final[m, 1].astype(F32)


class Local:
    def __init__(self, sems):
        self.sems, self.used, self.open = sems, 0, []

    def start(self, src, dst):
        copy = pltpu.make_async_copy(src, dst, self.sems.at[self.used])
        self.used += 1
        copy.start()
        self.open.append(copy)
        return copy

    def wait(self, copy):
        copy.wait()
        self.open = [other for other in self.open if other is not copy]

    def finish(self):
        for copy in list(self.open):
            copy.wait()


def inv_rms(values):
    return lax.rsqrt(jnp.mean(values * values, axis=1, keepdims=True) + EPS)


def norm_to(full, gain, values, span):
    full[span, :] = (values * inv_rms(values) * gain).astype(BF16)


def norm_back(values, gain, grad):
    scale = inv_rms(values)
    weighted = grad * gain
    inner = jnp.mean(weighted * values, axis=1, keepdims=True)
    back = scale * weighted - values * (scale * scale * scale * inner)
    return back, jnp.sum(grad * values * scale, axis=0, keepdims=True)


def wait_both(copies):
    for condition, copy in copies:

        @pl.when(condition)
        def _(copy=copy):
            copy.wait_send()


class Side:
    def __init__(self, tag):
        self.tag = tag

    def ref(self, name):
        return getattr(self.ns, self.tag + name)

    def bind(self, ns, row, groups):
        self.ns, self.row, self.c, self.groups = ns, row, row.c, groups
        self.sent = []

    def when(self, condition, copy):
        @pl.when(condition)
        def _():
            copy.start()

        self.sent.append((condition, copy))

    def arrived(self, condition, copy):
        @pl.when(condition)
        def _():
            copy.wait_recv()

    def remote(self, src, dst, send, recv, to):
        return pltpu.make_async_remote_copy(
            src_ref=src,
            dst_ref=dst,
            send_sem=send,
            recv_sem=recv,
            device_id=(self.row.s, self.row.r, to),
            device_id_type=MESH,
        )


def part_of(ref, at, per, axis):
    where = pl.ds(pl.multiple_of(at * per, per), per)
    return ref.at[(slice(None),) * axis + (where,)]


class Gather(Side):
    def __init__(self, tag, array, dims, groups, axis, view=None, home=None):
        super().__init__(tag)
        self.array, self.axis, self.view, self.home = array, axis, view, home
        self.per = dims[axis]
        self.dims = dims[:axis] + (dims[axis] * groups,) + dims[axis + 1 :]

    def declare(self, ins, outs, scratch, groups):
        if self.array is not None:
            ins[self.tag + "src"] = (self.array, HB)
        if self.home is None:
            outs[self.tag + "dst"] = (self.dims, BF16, HB)
        else:
            scratch[self.tag + "dst"] = pltpu.VMEM(self.dims, BF16)
        scratch[self.tag + "send"] = pltpu.SemaphoreType.DMA((2, groups))
        scratch[self.tag + "recv"] = pltpu.SemaphoreType.DMA((groups,))
        scratch[self.tag + "own"] = pltpu.SemaphoreType.DMA((1,))

    def slot(self, j):
        return part_of(self.ref("dst"), jnp.clip(j, 0, self.groups - 1), self.per, self.axis)

    def source(self):
        return self.view(self.ns, self.row) if self.view else self.ref("src")

    def move(self, j, side, src=None):
        to = jnp.clip(self.c + (1 - 2 * side), 0, self.groups - 1)
        j = jnp.clip(j, 0, self.groups - 1)
        src = self.slot(j) if src is None else src
        return self.remote(
            src, self.slot(j), self.ref("send").at[side, j], self.ref("recv").at[j], to
        )

    def start(self):
        c, n = self.c, self.groups
        self.at, self.done = 1, False
        self.own = pltpu.make_async_copy(self.source(), self.slot(c), self.ref("own").at[0])
        self.own.start()
        self.when(c + 1 < n, self.move(c, 0, self.source()))
        self.when(c >= 1, self.move(c, 1, self.source()))

    def step(self):
        c, n, k = self.c, self.groups, self.at
        if k < n:
            self.arrived(c >= k, self.move(c - k, 0))
            self.arrived(c + k < n, self.move(c + k, 1))
            if k < n - 1:
                self.when((c >= k) & (c + 1 < n), self.move(c - k, 0))
                self.when((c + k < n) & (c >= 1), self.move(c + k, 1))
        self.at += 1

    def finish(self):
        if not self.done:
            while self.at < self.groups:
                self.step()
            self.own.wait()
            self.done = True

    def drain(self):
        wait_both(self.sent)


class Total(Side):
    def __init__(self, tag, parts, dims, groups, span, view=None, home=None):
        super().__init__(tag)
        self.parts, self.span, self.view, self.home = parts, span, view, home
        self.per = dims[1] // groups
        self.count = span[1]
        self.dims = (self.count, self.per, dims[2])

    def declare(self, ins, outs, scratch, groups):
        if self.home is None:
            outs[self.tag + "sum"] = (self.dims, BF16, VM)
        else:
            scratch[self.tag + "sum"] = pltpu.VMEM(self.dims, BF16)
        if self.view is None:
            ins[self.tag + "parts"] = (self.parts, HB)
            whole = (self.count, self.per * groups, self.dims[2])
            scratch[self.tag + "mine"] = pltpu.VMEM(whole, BF16)
        scratch[self.tag + "box"] = pltpu.VMEM((2, groups) + self.dims, BF16)
        scratch[self.tag + "send"] = pltpu.SemaphoreType.DMA((2, groups))
        scratch[self.tag + "recv"] = pltpu.SemaphoreType.DMA((2, groups))
        scratch[self.tag + "load"] = pltpu.SemaphoreType.DMA((1,))

    def clip(self, j):
        return jnp.clip(j, 0, self.groups - 1)

    def piece(self, ref, d, p=None):
        d = self.clip(d)
        where = pl.ds(pl.multiple_of(d * self.per, self.per), self.per)
        if p is None:
            return ref.at[:, where, :]
        return ref[p + (self.span[0] if self.view else 0), where, :]

    def source(self):
        parts = self.view(self.ns) if self.view else self.ref("parts")
        return parts.at[pl.ds(*self.span)]

    def mine(self):
        return self.view(self.ns) if self.view else self.ref("mine")

    def move(self, side, d, src):
        d = self.clip(d)
        to = self.clip(self.c + (1 - 2 * side))
        return self.remote(
            src,
            self.ref("box").at[side, d],
            self.ref("send").at[side, d],
            self.ref("recv").at[side, d],
            to,
        )

    def boxed(self, side, d):
        return self.ref("box").at[side, self.clip(d)]

    def start(self):
        c, n = self.c, self.groups
        self.at, self.done = 1, False
        if self.view is None:
            self.load = pltpu.make_async_copy(
                self.source(), self.ref("mine"), self.ref("load").at[0]
            )
            self.load.start()
        self.ends(0)

    def ends(self, t):
        c, n = self.c, self.groups
        self.when(c == 0, self.move(0, n - 1 - t, self.piece(self.source(), n - 1 - t)))
        self.when(c == n - 1, self.move(1, t, self.piece(self.source(), t)))

    def step(self):
        c, n, t = self.c, self.groups, self.at
        box, mine = self.ref("box"), self.mine()
        if t == 1 and self.view is None:
            self.load.wait()
        if t < n - 1:
            self.ends(t)
            for side, place, d in ((0, c, n - 1 - t + c), (1, n - 1 - c, t + c - (n - 1))):
                here = (place >= 1) & (place <= t)
                self.arrived(here, self.move(side, d, self.boxed(side, d)))

                @pl.when(here)
                def _(side=side, d=d):
                    for p in range(self.count):
                        total = self.piece(mine, d, p).astype(F32)
                        total = total + box[side, self.clip(d), p].astype(F32)
                        box[side, self.clip(d), p] = total.astype(BF16)

                self.when(here, self.move(side, d, self.boxed(side, d)))
        self.at += 1

    def finish(self):
        if self.done:
            return
        self.done = True
        c, n = self.c, self.groups
        while self.at < n - 1:
            self.step()
        box, mine = self.ref("box"), self.mine()
        above, below = c >= 1, c + 1 < n
        self.arrived(above, self.move(0, c, self.boxed(0, c)))
        self.arrived(below, self.move(1, c, self.boxed(1, c)))
        for p in range(self.count):
            first = jnp.where(c >= 1, 0, 1)
            total = self.piece(mine, c, p).astype(F32) + box[first, c, p].astype(F32)
            self.ref("sum")[p] = total.astype(BF16)

            @pl.when(above & below)
            def _(p=p, total=total):
                self.ref("sum")[p] = (total + box[1, c, p].astype(F32)).astype(BF16)

    def drain(self):
        wait_both(self.sent)


def others(row):
    for k in range(1, 8):
        ps = lax.rem(row.s + k // 4, 2)
        low = row.rx if k % 2 else row.r
        pr = lax.rem(low + 2 * ((k // 2) % 2), 4)
        yield k, ps, pr


class Swap:
    def __init__(self, tag):
        self.tag = tag

    def declare(self, scratch):
        scratch[self.tag + "send"] = pltpu.SemaphoreType.DMA((8,))
        scratch[self.tag + "recv"] = pltpu.SemaphoreType.DMA((8,))
        scratch[self.tag + "own"] = pltpu.SemaphoreType.DMA((1,))

    def start(self, ns, row, own, lanes, src, dst, to_tokens):
        send, recv, local = (getattr(ns, self.tag + a) for a in ("send", "recv", "own"))

        def tokens_of(s, r):
            return pl.ds(pl.multiple_of((s * 4 + r) * own, 16), own)

        def lanes_of(s, r):
            return pl.ds(pl.multiple_of((r * 2 + s) * lanes, 128), lanes)

        def ends(ps, pr):
            if to_tokens:
                return src.at[:, tokens_of(ps, pr), :], dst.at[:, :, lanes_of(row.s, row.r)]
            return src.at[:, :, lanes_of(ps, pr)], dst.at[:, tokens_of(row.s, row.r), :]

        a, b = ends(row.s, row.r)
        self.mine = pltpu.make_async_copy(a, b, local.at[0])
        self.mine.start()
        self.copies = []
        for k, ps, pr in others(row):
            a, b = ends(ps, pr)
            copy = pltpu.make_async_remote_copy(
                src_ref=a,
                dst_ref=b,
                send_sem=send.at[k],
                recv_sem=recv.at[k],
                device_id=(ps, pr, row.c),
                device_id_type=MESH,
            )
            copy.start()
            self.copies.append(copy)

    def wait(self):
        for copy in self.copies:
            copy.wait_recv()
        self.mine.wait()

    def drain(self):
        for copy in self.copies:
            copy.wait_send()


def plane_peers(row):
    return [
        (ps, pr, row.c) for k, ps, pr in others(row) if k not in (1, 2, 4)
    ]


def gather_first(row, full, micros, fresh, fill=()):
    if fresh:
        row.ag_pass(full, 0)
        for m in range(2, micros):
            row.ag_start(full, m)
    for work in fill:
        work()
    row.ag_pass(full, 1)
    row.ag_diag(full, 0)


def ag_begin(row, full):
    row.ag_start(full, 0)
    row.ag_start(full, 1)


def gather_more(row, full, micros, m):
    if m + 2 < micros:
        row.ag_pass(full, m + 2)
    if m + 1 < micros:
        row.ag_diag(full, m + 1)


def tail(row, micros, result, hook, between=(), relay=None):
    more = list(between)

    def step():
        if more:
            more.pop(0)()

    row.rs_transit(micros - 2)
    for m in range(micros - 2):
        result(m)
    row.rs_pair(micros - 1)
    hook(40)
    step()
    result(micros - 2)
    row.rs_transit(micros - 1)
    if relay:
        relay()
    step()
    if relay is None:
        while more:
            step()
    hook(41)
    result(micros - 1)
    return more


def ffn_forward(p, row, loc, cfg, hook, deliver, relay=None):
    micros, rows, full = cfg.micros, cfg.rows, p.full
    gather_first(row, full, micros, False)
    for m in range(micros):
        row.ag_wait(full, m)
        hook(m)
        if m >= 1:
            row.rs_pair(m - 1)
        if m >= 2:
            row.rs_transit(m - 2)
        here = pl.ds(m * rows, rows)
        loc.start(full.at[here, :], p.xin_o.at[here, :])
        gate = dot(full[here, :], p.gate_dst[0])
        lift = dot(full[here, :], p.up_dst[0])
        p.gp[here, :] = gate.astype(BF16)
        p.up[here, :] = lift.astype(BF16)
        p.act[here, :] = (gate * jax.nn.sigmoid(gate) * lift).astype(BF16)
        hook(10 + m)
        row.part[here, :] = dot(p.act[here, :], p.down_dst[0], 1, 1).astype(BF16)
        for a, b in ((p.gp, p.gp_o), (p.up, p.up_o), (p.act, p.act_o)):
            loc.start(a.at[here, :], b.at[here, :])
        row.rs_start(m)
        gather_more(row, full, micros, m)
        hook(30 + m)
    tail(row, micros, lambda m: deliver(m, row.rs_result(m)), hook, (), relay)


def ffn_backward(p, row, loc, cfg, hook, loads, late, deliver, relay=None):
    micros, rows, width, full = cfg.micros, cfg.rows, cfg.width, p.full
    gather_first(row, full, micros, True)
    for copy in loads:
        loc.wait(copy)
    for m in range(micros):
        row.ag_wait(full, m)
        hook(m)
        if m >= 1:
            row.rs_pair(m - 1)
        if m >= 2:
            row.rs_transit(m - 2)
        here = pl.ds(m * rows, rows)
        d_act = dot(full[here, :], p.w[2])
        gate = p.gp[here, :].astype(F32)
        lift = p.up[here, :].astype(F32)
        sig = jax.nn.sigmoid(gate)
        silu = gate * sig
        p.dg[here, :] = (d_act * lift * (sig + silu * (1.0 - sig))).astype(BF16)
        p.du[here, :] = (d_act * silu).astype(BF16)
        total = dot(p.dg[here, :], p.w[0], 1, 1) + dot(p.du[here, :], p.w[1], 1, 1)
        row.part[here, :] = total.astype(BF16)
        row.rs_start(m)
        gather_more(row, full, micros, m)
        hook(30 + m)

    def grad(i, left, right):
        def body():
            if i == 2:
                for copy in late:
                    loc.wait(copy)

            @pl.loop(0, width // 256)
            def _(t):
                at = pl.ds(pl.multiple_of(t * 256, 256), 256)
                p.grad[i, at, :] = dot(left[:, at], right[...], 0, 0).astype(BF16)

            hook(50 + i)

        return body

    grads = [grad(2, full, p.act), grad(0, p.xin, p.dg), grad(1, p.xin, p.du)]
    return tail(row, micros, lambda m: deliver(m, row.rs_result(m)), hook, grads, relay)


def pair_masks(size):
    rows_at = lax.broadcasted_iota(jnp.int32, (size, size), 0)
    cols_at = lax.broadcasted_iota(jnp.int32, (size, size), 1)
    return (rows_at >= cols_at) & (rows_at // BLOCK == cols_at // BLOCK)


def gate_columns(gates, columns):
    count, size = gates.shape
    rows_at = lax.broadcasted_iota(jnp.int32, (size, size), 0)
    cols_at = lax.broadcasted_iota(jnp.int32, (size, size), 1)
    for i in range(count):
        spread = jnp.where(rows_at == cols_at, gates[i : i + 1, :], 0.0)
        columns[i * size : (i + 1) * size, :] = jnp.sum(spread, axis=1, keepdims=True)


def gain_row(k, cfg, layer, kind):
    rows_each = cfg.width // 4 // 128
    pieces = [
        k.gains[layer, r, kind * rows_each + h : kind * rows_each + h + 1, :]
        for r in range(4)
        for h in range(rows_each)
    ]
    return jnp.concatenate(pieces, axis=1)


class Heads:
    def __init__(self, k, row, cfg, layer):
        self.k, self.row, self.cfg, self.layer = k, row, cfg, layer

    def persist(self):
        k, cfg = self.k, self.cfg
        out = []
        for kind in range(2):
            start = pl.multiple_of(8 + (2 * kind + self.row.s) * 8, 8)
            for j in range(cfg.groups):
                block = k.line[self.layer, j, pl.ds(start, 8), :]
                k.persist[j * cfg.per : (j + 1) * cfg.per, :] = block[: cfg.per, :]
            out.append(k.persist[...].astype(BF16))
        return out

    def keeps(self, j):
        decays = self.k.line[self.layer, j, 40:48, :] * self.k.starts[j]
        return jnp.where(self.row.s == 0, decays[0:1, :], decays[1:2, :])

    def own(self):
        keeps = self.keeps(self.row.c)
        blocks = self.cfg.blocks

        def of(m, b):
            return keeps[:, m * blocks + b : m * blocks + b + 1]

        return of

    def through(self, m, j):
        keeps = self.keeps(j)
        product = None
        for b in range(self.cfg.blocks):
            at = m * self.cfg.blocks + b
            one = keeps[:, at : at + 1]
            product = one if product is None else product * one
        return product


def pair_probs(q, k, pk, mask, scale):
    inner = jnp.where(mask, dot(q, k, 1, 1) * scale, -1e30)
    outer = dot(q, pk, 1, 1) * scale
    top = jnp.maximum(
        jnp.max(inner, axis=1, keepdims=True), jnp.max(outer, axis=1, keepdims=True)
    )
    inner = jnp.exp(inner - top)
    outer = jnp.exp(outer - top)
    norm = 1.0 / (jnp.sum(inner, axis=1, keepdims=True) + jnp.sum(outer, axis=1, keepdims=True))
    return inner * norm, outer * norm


class States:
    def __init__(self, row, groups, k, backward):
        self.backward, self.sent = backward, []
        self.row, self.groups, self.mine, self.box = row, groups, k.leaving, k.box
        self.send, self.recv, self.entering = k.ssend, k.srecv, k.entering

    def copy(self, m, k):
        n = self.groups
        to = self.row.c + (-k if self.backward else k)
        return pltpu.make_async_remote_copy(
            src_ref=self.mine.at[m],
            dst_ref=self.box.at[m, k],
            send_sem=self.send.at[m, k],
            recv_sem=self.recv.at[m, k],
            device_id=(self.row.s, self.row.r, jnp.clip(to, 0, n - 1)),
            device_id_type=MESH,
        )

    def after(self, k):
        c, n = self.row.c, self.groups
        return (c >= k) if self.backward else (c + k < n)

    def before(self, k):
        c, n = self.row.c, self.groups
        return (c + k < n) if self.backward else (c >= k)

    def start(self, m):
        for k in range(1, self.groups):

            @pl.when(self.after(k))
            def _(k=k):
                self.copy(m, k).start()

            self.sent.append((self.after(k), self.copy(m, k)))

    def wait(self, m):
        for k in range(1, self.groups):

            @pl.when(self.before(k))
            def _(k=k):
                self.copy(m, k).wait_recv()

    def drain(self):
        wait_both(self.sent)

    def fold(self, m, through):
        entering = self.entering
        entering[...] = jnp.zeros_like(entering)
        for k in range(self.groups - 1, 0, -1):

            @pl.when(self.before(k))
            def _(k=k):
                source = self.row.c + (k if self.backward else -k)
                factor = through(m, jnp.clip(source, 0, self.groups - 1))
                entering[...] = factor * entering[...] + self.box[m, k].astype(F32)


def attn_forward(p, row, loc, cfg, hook, layer, fresh, deliver, relay=None):
    micros, rows, size, full = cfg.micros, cfg.rows, cfg.size, p.full
    blocks = rows // BLOCK
    factor = size ** (-0.5)
    states = States(row, cfg.groups, p, False)
    qs, ks, vs = (pl.ds(i * size, size) for i in range(3))
    mask = pair_masks(2 * BLOCK)
    gather_first(row, full, micros, fresh)
    gate_columns(p.gates[layer, 0 : micros * rows // 128, :], p.gate)
    heads = Heads(p, row, cfg, layer)
    pk, pv = heads.persist()
    keep = heads.own()
    for m in range(micros):
        row.ag_wait(full, m)
        hook(m)
        here = pl.ds(m * rows, rows)
        loc.start(full.at[here, :], p.xin_o.at[here, :])
        p.qkv[here, :] = dot(full[here, :], p.wq[0]).astype(BF16)
        loc.start(p.qkv.at[here, :], p.qkv_o.at[here, :])
        total = jnp.zeros((size, size), F32)
        for b in range(blocks):
            at = pl.ds(m * rows + b * BLOCK, BLOCK)
            keys = (p.qkv[at, ks].astype(F32) * p.gate[at, :]).astype(BF16)
            fresh = dot(keys, p.qkv[at, vs], 0, 0)
            p.update[m * blocks + b] = fresh
            total = keep(m, b) * total + fresh
        p.leaving[m] = total.astype(BF16)
        states.start(m)
        gather_more(row, full, micros, m)
        hook(10 + m)
    for m in range(micros):
        here = pl.ds(m * rows, rows)
        states.wait(m)
        states.fold(m, heads.through)
        memory = p.entering[...]
        for b in range(0, blocks, 2):
            at = pl.ds(m * rows + b * BLOCK, 2 * BLOCK)
            q, ky, v = p.qkv[at, qs], p.qkv[at, ks], p.qkv[at, vs]
            inner, outer = pair_probs(q, ky, pk, mask, factor)
            value = dot(inner.astype(BF16), v) + dot(outer.astype(BF16), pv)
            reads = []
            for i in range(2):
                now = keep(m, b + i) * memory
                low = now.astype(BF16)
                p.state[m * blocks + b + i] = low
                reads.append(dot(q[i * BLOCK : (i + 1) * BLOCK, :], low) * factor)
                memory = now + p.update[m * blocks + b + i]
            p.mixed[at, :] = (value + jnp.concatenate(reads, axis=0)).astype(BF16)
        hook(20 + m)
        row.part[here, :] = dot(p.mixed[here, :], p.wo_dst[0], 1, 1).astype(BF16)
        loc.start(p.mixed.at[here, :], p.mixed_o.at[here, :])
        row.rs_start(m)
        if m >= 1:
            row.rs_pair(m - 1)
        if m >= 2:
            row.rs_transit(m - 2)
        hook(30 + m)
    loc.start(p.state, p.state_o)
    tail(row, micros, lambda m: deliver(m, row.rs_result(m)), hook, (), relay)
    states.drain()


def attn_backward(p, row, loc, cfg, hook, layer, loads, late, deliver, fill, relay=None):
    micros, rows, size, width, full = cfg.micros, cfg.rows, cfg.size, cfg.width, p.full
    blocks = rows // BLOCK
    factor = size ** (-0.5)
    states = States(row, cfg.groups, p, True)
    qs, ks, vs = (pl.ds(i * size, size) for i in range(3))
    in_cols, out_cols = pl.ds(0, 3 * size), pl.ds(3 * size, size)
    mask = pair_masks(2 * BLOCK)
    p.dpersist[...] = jnp.zeros_like(p.dpersist)
    gate_columns(p.gates[layer, 0 : micros * rows // 128, :], p.gate)
    heads = Heads(p, row, cfg, layer)
    pk, pv = heads.persist()
    keep = heads.own()
    gather_first(row, full, micros, False, fill)
    for copy in loads:
        loc.wait(copy)
    for m in range(micros):
        row.ag_wait(full, m)
        hook(m)
        here = pl.ds(m * rows, rows)
        p.dmix[here, :] = dot(full[here, :], p.wo[0]).astype(BF16)
        total = jnp.zeros((size, size), F32)
        for b in reversed(range(blocks)):
            at = pl.ds(m * rows + b * BLOCK, BLOCK)
            fresh = dot(p.qkv[at, qs], p.dmix[at, :], 0, 0) * factor
            p.update[m * blocks + b] = fresh
            total = keep(m, b) * (fresh + total)
        p.leaving[m] = total.astype(BF16)
        states.start(m)
        gather_more(row, full, micros, m)
        hook(10 + m)
    for m in range(micros):
        here = pl.ds(m * rows, rows)
        states.wait(m)
        states.fold(m, heads.through)
        memory = p.entering[...]
        for b in reversed(range(0, blocks, 2)):
            at = pl.ds(m * rows + b * BLOCK, 2 * BLOCK)
            q, ky, v, d = p.qkv[at, qs], p.qkv[at, ks], p.qkv[at, vs], p.dmix[at, :]
            inner, outer = pair_probs(q, ky, pk, mask, factor)
            d_inner = dot(d, v, 1, 1)
            d_outer = dot(d, pv, 1, 1)
            centre = jnp.sum(inner * d_inner, axis=1, keepdims=True) + jnp.sum(
                outer * d_outer, axis=1, keepdims=True
            )
            d_inner = (inner * (d_inner - centre)).astype(BF16)
            d_outer = (outer * (d_outer - centre)).astype(BF16)
            inner, outer = inner.astype(BF16), outer.astype(BF16)
            p.dpersist[0] += dot(d_outer, q, 0, 0) * factor
            p.dpersist[1] += dot(outer, d, 0, 0)
            dq = dot(d_inner, ky) + dot(d_outer, pk)
            dk = dot(d_inner, q, 0, 0) * factor
            dv = dot(inner, d, 0, 0)
            keys = (ky.astype(F32) * p.gate[at, :]).astype(BF16)
            parts = [None, None]
            for i in (1, 0):
                sub = slice(i * BLOCK, (i + 1) * BLOCK)
                low = memory.astype(BF16)
                parts[i] = (
                    dot(d[sub, :], p.state[m * blocks + b + i], 1, 1),
                    dot(v[sub, :], low, 1, 1),
                    dot(keys[sub, :], low),
                )
                memory = keep(m, b + i) * (p.update[m * blocks + b + i] + memory)
            more_q, more_k, more_v = (jnp.concatenate(pieces, axis=0) for pieces in zip(*parts))
            p.dqkv[at, qs] = ((dq + more_q) * factor).astype(BF16)
            p.dqkv[at, ks] = (dk + p.gate[at, :] * more_k).astype(BF16)
            p.dqkv[at, vs] = (dv + more_v).astype(BF16)
        row.part[here, :] = dot(p.dqkv[here, :], p.wq[0], 1, 1).astype(BF16)
        row.rs_start(m)
        if m >= 1:
            row.rs_pair(m - 1)
        if m >= 2:
            row.rs_transit(m - 2)
        hook(30 + m)

    def out_grad():
        for copy in late:
            loc.wait(copy)

        @pl.loop(0, width // 256)
        def _(t):
            at = pl.ds(pl.multiple_of(t * 256, 256), 256)
            p.grad[0, at, out_cols] = dot(full[:, at], p.mixed[...], 0, 0).astype(BF16)

    def qkv_grad():
        @pl.loop(0, width // 256)
        def _(t):
            at = pl.ds(pl.multiple_of(t * 256, 256), 256)
            p.grad[0, at, in_cols] = dot(p.xin[:, at], p.dqkv[...], 0, 0).astype(BF16)

        hook(60)

    tail(row, micros, lambda m: deliver(m, row.rs_result(m)), hook, [out_grad, qkv_grad], relay)
    states.drain()


VM = pl.BlockSpec(memory_space=pltpu.VMEM)
SM = pl.BlockSpec(memory_space=pltpu.SMEM)
HB = pl.BlockSpec(memory_space=pl.ANY)


def vm(dims, dtype=BF16):
    return pltpu.VMEM(dims, dtype)


def launch(name, collective, body, ins, outs, scratch):
    names = list(ins) + list(outs) + list(scratch)

    def kernel(*refs):
        body(SimpleNamespace(**dict(zip(names, refs))))

    results = pl.pallas_call(
        kernel,
        out_shape=tuple(jax.ShapeDtypeStruct(d, t) for d, t, _ in outs.values()),
        in_specs=[spec for _, spec in ins.values()],
        out_specs=tuple(spec for _, _, spec in outs.values()),
        scratch_shapes=list(scratch.values()),
        compiler_params=pltpu.CompilerParams(
            collective_id=collective, has_side_effects=True, vmem_limit_bytes=VMEM_LIMIT
        ),
        name=name,
    )(*[a for a, _ in ins.values()])
    return SimpleNamespace(**dict(zip(outs, results)))


def local(
    tokens, cotangent, block_order, lengths, decay, write_gate, gain_attn, w_query, w_key, w_value,
    persist_key, persist_value, w_output, gain_ffn, w_gate, w_up, w_down,
):
    sec, row_id, col = (lax.axis_index(a) for a in ("section", "row", "col"))
    groups = lax.axis_size("col")
    micros, rows, features = tokens.shape
    width = features * 4
    own, blocks, all_rows, size = rows // 8, rows // BLOCK, micros * rows, features // 2
    ffh = w_gate.shape[2] // 2
    per = persist_key.shape[1]
    persist = per * groups
    cfg = SimpleNamespace(
        micros=micros, rows=rows, own=own, size=size, width=width, groups=groups, blocks=blocks, per=per
    )
    total_blocks = block_order.shape[1]
    positions = jnp.arange(total_blocks, dtype=jnp.int32)
    my_blocks = col * blocks + jnp.arange(blocks, dtype=jnp.int32)
    matches = (block_order[:, :, None] == my_blocks[None, None, :]).astype(jnp.int32)
    back_picks = jnp.sum(matches * positions[None, :, None], axis=1)

    def lanes(a):
        return jnp.pad(a, ((0, 0),) * (a.ndim - 1) + ((0, 128 - a.shape[-1]),))

    def eights(a):
        return jnp.pad(a, ((0, 0),) * (a.ndim - 2) + ((0, -a.shape[-2] % 8), (0, 0)))

    share = gain_attn.shape[1]
    own_gains = jnp.concatenate([gain_attn, gain_ffn], axis=0).astype(F32)
    placed = lax.dynamic_update_slice(
        jnp.zeros((2, features), F32), own_gains, (jnp.zeros_like(col), col * share)
    )
    packed = jnp.concatenate(
        [eights(placed.reshape(-1, 128))]
        + [
            eights(a[0].reshape(per, 2, size).transpose(1, 0, 2)).reshape(16, size).astype(F32)
            for a in (persist_key, persist_value)
        ]
        + [eights(lanes(decay[0].transpose(2, 0, 1).reshape(2, -1)))],
        axis=0,
    )
    gate_rows = eights(write_gate[0].transpose(2, 0, 1).reshape(2, -1, 128)) / BLOCK
    sequences = jnp.arange(lengths.shape[1])
    earlier = sequences[None, :] < sequences[:, None]
    firsts = jnp.sum(jnp.where(earlier[None], lengths[:, None, :], 0), axis=2)
    is_start = jnp.any(positions[None, :, None] == firsts[:, None, :], axis=2)
    starts = jnp.where(is_start, 0.0, 1.0).reshape(micros, groups, blocks).transpose(1, 0, 2)
    starts = jnp.broadcast_to(lanes(starts.reshape(groups, -1))[:, None], (groups, 8, 128))

    def cols_split(w):
        return w.reshape(w.shape[0], 2, -1).transpose(1, 0, 2)

    def rows_split(w):
        return w.reshape(2, -1, w.shape[1]).transpose(0, 2, 1)

    blocks_a = jnp.concatenate(
        [cols_split(w[0]) for w in (w_query, w_key, w_value)] + [rows_split(w_output[0])], axis=2
    )[:, None]
    blocks_b = jnp.stack(
        [cols_split(w_gate[0]), cols_split(w_up[0]), rows_split(w_down[0])], axis=1
    )

    a_dims, b_dims = blocks_a.shape[1:], blocks_b.shape[1:]
    q_dims, o_dims, one_dims = (1, a_dims[1], 3 * size), (1, a_dims[1], size), (1,) + b_dims[1:]
    grad_a_dims, grad_b_dims = (1, width, 4 * size), (3, width, ffh)
    stage_dims = (micros, rows, size)
    by_block = (micros, blocks, BLOCK, size)
    gain_rows = 4 * width // 128
    half_gains = width // 128
    hbm = lambda dims, dtype=BF16: (dims, dtype, HB)

    def row_scratch(prefix):
        return {
            "part": vm((all_rows, width)),
            "pair": vm((micros, 4 * own, width)),
            "both": vm((micros, 4, own, width)),
            "transit": vm((micros, 2, own, width // 2)),
            "final": vm((micros, 2, own, width)),
            prefix + "send": pltpu.SemaphoreType.DMA((micros, N_AG + N_RS)),
            prefix + "recv": pltpu.SemaphoreType.DMA((micros, N_AG + N_RS)),
            prefix + "full": vm((all_rows, width)),
        }

    shared_rows = ("part", "pair", "both", "transit", "final")

    def attn_scratch(prefix):
        names = dict(
            update=vm((micros * blocks, size, size), F32),
            entering=vm((size, size), F32),
            leaving=vm((micros, size, size)),
            box=vm((micros, groups, size, size)),
            ssend=pltpu.SemaphoreType.DMA((micros, groups)),
            srecv=pltpu.SemaphoreType.DMA((micros, groups)),
            gate=vm((all_rows, 1), F32),
            persist=vm((persist, size), F32),
            qkv=vm((all_rows, 3 * size)),
            state=vm((micros * blocks, size, size)),
            mixed=vm((all_rows, size)),
        )
        return {**row_scratch(prefix), **{prefix + a: b for a, b in names.items()}}

    def ffn_scratch(prefix):
        names = {a: vm((all_rows, ffh)) for a in ("gp", "up", "act")}
        return {**row_scratch(prefix), **{prefix + a: b for a, b in names.items()}}

    def view_of(k, prefix, **more):
        names = {a[len(prefix) :]: b for a, b in vars(k).items() if a.startswith(prefix)}
        return SimpleNamespace(**{**names, **more})

    def rows_of(k, prefix):
        p = view_of(k, prefix)
        row = Rows(rows, own, width, p.send, p.recv)
        row.buffers = (k.part, k.pair, k.both, k.transit, k.final)
        row.part = k.part
        return row

    def greet_all(row):
        row.greet(
            plane_peers(row)
            + [(row.s, row.r, lax.rem(row.c + i, groups)) for i in range(1, groups)]
        )

    def hooks(plan, prefix):
        def hook(point):
            for action in plan.get(prefix + point, ()):
                action()

        return hook

    def pusher(send, recv):
        def push(src, dst, i, to):
            copy = pltpu.make_async_remote_copy(
                src_ref=src,
                dst_ref=dst,
                send_sem=send.at[i],
                recv_sem=recv.at[i],
                device_id=to,
                device_id_type=MESH,
            )
            copy.start()
            return copy

        return push

    def blocks_from(buf, picks, stage, m, group):
        for b in range(blocks):
            stage[m, pl.ds(b * BLOCK, BLOCK), :] = buf[m, picks[m, group * blocks + b]]

    def forward_names(l):
        outs = dict(
            a_xin_o=hbm((all_rows, width)),
            a_qkv_o=hbm((all_rows, 3 * size)),
            a_state_o=hbm((micros * blocks, size, size)),
            a_mixed_o=hbm((all_rows, size)),
            f_xin_o=hbm((all_rows, width)),
            f_gp_o=hbm((all_rows, ffh)),
            f_up_o=hbm((all_rows, ffh)),
            f_act_o=hbm((all_rows, ffh)),
            wo_o=hbm((1, width, size)),
            w_o=hbm((3, width, ffh)),
            mid=((micros, own, width), F32, VM),
            y=((micros, own, width), BF16, VM),
        )
        return outs, {**attn_scratch("a_"), **ffn_scratch("f_")}

    def forward_layer(k, l, x, wq, loc, plan, base, row_a, small, fresh, leave, relay):
        row_f = rows_of(k, "f_")
        gain_f = gain_row(small, cfg, l, 1)

        def middle(m, summed):
            k.mid[m] = x[m].astype(F32) + summed
            norm_to(k.f_full, gain_f, k.mid[m], row_f.span(m, row_f.s, row_f.r))
            row_f.ag_start(k.f_full, m)

        def leave_y(m, summed):
            k.y[m] = (k.mid[m] + summed).astype(BF16)
            leave(m)

        p = view_of(k, "a_", wq=wq, wo_dst=k.wo_dst, **vars(small))
        attn_forward(
            p, row_a, loc, cfg, hooks(plan, base), l, fresh, middle,
            lambda: row_f.ag_pass(k.f_full, 0),
        )
        row_a.finish()
        loc.start(k.wo_dst, k.wo_o)
        p = view_of(k, "f_", gate_dst=k.gate_dst, up_dst=k.up_dst, down_dst=k.down_dst)
        ffn_forward(p, row_f, loc, cfg, hooks(plan, base + F), leave_y, relay)
        row_f.finish()
        for i, w in enumerate((k.gate_dst, k.up_dst, k.down_dst)):
            loc.start(w, k.w_o.at[pl.ds(i, 1)])

    def one_b(tag, layer, which):
        view = lambda k, row: k.shards_b.at[layer, pl.ds(which, 1)]
        return Gather(tag, None, one_dims, groups, 1, view, "scratch")

    def q_of(ref, layer):
        return ref.at[layer, :, :, pl.ds(0, 3 * size)]

    def o_of(ref, layer):
        return ref.at[layer, :, :, pl.ds(3 * size, size)]

    def lanes_of_core(name):
        def view(k, row):
            mine = pl.ds(pl.multiple_of(row.s * size, 128), size)
            return getattr(k, name).at[:, :, :, mine]

        return view

    tokens_b = tokens.reshape(micros, blocks, BLOCK, features)
    cotangent_b = cotangent.reshape(micros, blocks, BLOCK, features)
    deal = Gather("deal_", tokens_b, by_block, groups, 1, lanes_of_core("deal_src"), "scratch")
    q0 = Gather("q0_", None, q_dims, groups, 1, lambda k, row: q_of(k.shards_a, 0), "scratch")
    wo0 = Gather("wo_", None, o_dims, groups, 1, lambda k, row: o_of(k.shards_a, 0), "scratch")
    gate0, up0, down0 = (one_b(t, 0, i) for i, t in enumerate(("gate_", "up_", "down_")))
    q1 = Gather("q1_", None, q_dims, groups, 1, lambda k, row: q_of(k.shards_a, 1), "scratch")
    wo1 = Gather("L1_wo_", None, o_dims, groups, 1, lambda k, row: o_of(k.shards_a, 1), "scratch")
    gate1, up1, down1 = (
        one_b(t, 1, i) for i, t in enumerate(("L1_gate_", "L1_up_", "L1_down_"))
    )
    cot = Gather("cot_", cotangent_b, by_block, groups, 1, lanes_of_core("cot_src"), "scratch")
    sides1 = [deal, q0, wo0, gate0, up0, down0, q1, wo1, gate1, up1, down1, cot]
    swap1, swap_y, swap_c = Swap("swap_"), Swap("swapy_"), Swap("swapc_")

    def first_body(k):
        row = rows_of(k, "a_")
        loc = Local(k.sems)
        greet_all(row)
        for side in sides1:
            side.bind(k, row, groups)
        push = pusher(k.psend, k.precv)
        crossing, keeps_here = [], []
        for i, (src, dst) in enumerate(((k.blocks_a, k.shards_a), (k.blocks_b, k.shards_b))):
            keeps_here.append(loc.start(src.at[row.s], dst.at[row.s]))
            crossing.append(push(src.at[1 - row.s], dst.at[row.s], groups + 9 + i, row.sib))
        deal.start()
        k.line[row.s, row.c] = k.packed[...]
        k.gates[row.s] = k.gate_rows[row.s]
        small = [
            push(
                k.packed,
                k.line.at[row.s, row.c],
                i,
                (row.s, row.r, lax.rem(row.c + i, groups)),
            )
            for i in range(1, groups)
        ]
        late = [push(k.gate_rows.at[1 - row.s], k.gates.at[row.s], 0, row.sib)]
        crossing[0].wait_recv()
        loc.wait(keeps_here[0])
        q0.start()
        deal.step()
        for copy in small:
            copy.wait_recv()
        total = k.line[row.s, 0, 0:8, :]
        for j in range(1, groups):
            total = total + k.line[row.s, j, 0:8, :]
        k.gains[row.s, row.r] = total
        for i, ps, pr in others(row):
            mine = k.gains.at[row.s, row.r]
            late.append(push(mine, mine, groups + i, (ps, pr, row.c)))
        late.append(push(k.line.at[row.s], k.line.at[row.s], groups + 8, row.sib))
        crossing[1].wait_recv()
        loc.wait(keeps_here[1])
        q0.step()
        wo0.start()
        deal.step()
        q0.step()
        gate0.start()
        up0.start()
        wo0.step()
        deal.finish()
        for m in range(micros):
            blocks_from(k.deal_dst, k.picks, k.stage, m, row.c)
        swap1.start(k, row, own, size, k.stage, k.x, True)
        q0.finish()
        wo0.step()
        for copy in late:
            copy.wait_recv()
        gain = gain_row(k, cfg, 0, 0)
        swap1.wait()
        for m in range(micros):
            norm_to(k.a_full, gain, k.x[m].astype(F32), row.span(m, row.s, row.r))
        ag_begin(row, k.a_full)
        loc.start(k.q0_dst, k.q0_o)
        def deal_cot():
            cot.finish()
            for m in range(micros):
                blocks_from(k.cot_dst, k.picks, k.stage_c, m, row.c)
            swap_c.start(k, row, own, size, k.stage_c, k.dy, True)

        plan = place(
            PLACES["first"],
            [
                gate0.step, up0.step, down0.start, gate0.step, up0.step, down0.step, down0.step,
                q1.start, q1.step, q1.step, wo1.start, wo1.step, wo1.step, gate1.start, up1.start,
                down1.start, gate1.step, up1.step, down1.step, gate1.step, up1.step, down1.step,
                cot.start, cot.step, cot.step, deal_cot,
            ],
            [
                (A + 20, wo0.finish), (F, gate0.finish), (F, up0.finish), (F + 10, down0.finish),
                (NEXT, q1.finish), (NEXT + 20, wo1.finish), (NEXT + F, gate1.finish),
                (NEXT + F, up1.finish), (NEXT + F + 10, down1.finish),
            ],
        )
        small_refs = SimpleNamespace(line=k.line, gains=k.gains, gates=k.gates, starts=k.starts)
        second = SimpleNamespace(**{**vars(k), **vars(view_of(k, "L1_"))})
        row_next = rows_of(second, "a_")
        gain_next = gain_row(small_refs, cfg, 1, 0)

        def begin_next(m):
            rows_here = row_next.span(m, row_next.s, row_next.r)
            norm_to(second.a_full, gain_next, k.y[m].astype(F32), rows_here)
            row_next.ag_start(second.a_full, m)

        forward_layer(
            k, 0, k.x, k.q0_dst, loc, plan, A, row, small_refs, True, begin_next,
            lambda: row_next.ag_pass(second.a_full, 0),
        )
        swap_y.start(k, row, own, size, k.y, k.stage_o, False)
        forward_layer(
            second, 1, k.y, k.q1_dst, loc, plan, NEXT, row_next, small_refs, False, lambda m: None,
            None,
        )
        loc.start(k.q1_dst, k.q1_o)
        for side in sides1:
            side.finish()
        swap_y.wait()
        swap_c.wait()
        for copy in crossing + small + late:
            copy.wait_send()
        for side in sides1 + [swap1, swap_y, swap_c]:
            side.drain()
        loc.finish()

    outs, scratch = forward_names(0)
    for names, into in zip(forward_names(1), (outs, scratch)):
        into.update({"L1_" + a: b for a, b in names.items() if a not in shared_rows})
    ins = dict(
        picks=(block_order, SM),
        blocks_a=(blocks_a, HB),
        blocks_b=(blocks_b, HB),
        packed=(packed, VM),
        gate_rows=(gate_rows, VM),
        starts=(starts, VM),
    )
    outs.update(
        x=((micros, own, width), BF16, VM),
        shards_a=hbm(blocks_a.shape),
        shards_b=hbm(blocks_b.shape),
        line=((2, groups) + packed.shape, F32, VM),
        gains=((2, 4, 8, 128), F32, VM),
        gates=((2,) + gate_rows.shape[1:], F32, VM),
        q0_o=hbm((1, width, 3 * size)),
        q1_o=hbm((1, width, 3 * size)),
        dy=((micros, own, width), BF16, VM),
        stage_o=hbm(stage_dims),
    )
    scratch.update(
        stage=vm(stage_dims),
        stage_c=vm(stage_dims),
        psend=pltpu.SemaphoreType.DMA((groups + 11,)),
        precv=pltpu.SemaphoreType.DMA((groups + 11,)),
        sems=pltpu.SemaphoreType.DMA((80,)),
    )
    for side in sides1:
        side.declare(ins, outs, scratch, groups)
    for swap in (swap1, swap_y, swap_c):
        swap.declare(scratch)
    f0 = launch("forward", 0, first_body, ins, outs, scratch)
    f1 = SimpleNamespace(**{**vars(f0), **vars(view_of(f0, "L1_"))})

    smalls = dict(
        line=(f0.line, VM), gains=(f0.gains, VM), gates=(f0.gates, VM),
        starts=(starts, VM),
    )

    def small_of(k):
        return SimpleNamespace(line=k.line, gains=k.gains, gates=k.gates, starts=k.starts)

    def backward_names(kept, dy, x, wq):
        ins = dict(
            dy=(dy, VM), mid=(kept.mid, VM), x=(x, VM), w_h=(kept.w_o, HB),
            wo_h=(kept.wo_o, HB), wq_h=(wq, HB), ax_h=(kept.a_xin_o, HB),
            qkv_h=(kept.a_qkv_o, HB), state_h=(kept.a_state_o, HB),
            mixed_h=(kept.a_mixed_o, HB), fx_h=(kept.f_xin_o, HB), gp_h=(kept.f_gp_o, HB),
            up_h=(kept.f_up_o, HB), act_h=(kept.f_act_o, HB), **smalls,
        )
        scratch = {**attn_scratch("a_"), **ffn_scratch("f_")}
        scratch.update(
            f_w=vm((3, width, ffh)), xin=vm((all_rows, width)),
            f_dg=vm((all_rows, ffh)), f_du=vm((all_rows, ffh)), f_grad=vm(grad_b_dims),
            a_wo=vm((1, width, size)), a_wq=vm((1, width, 3 * size)),
            a_dmix=vm((all_rows, size)),
            a_dqkv=vm((all_rows, 3 * size)), a_grad=vm(grad_a_dims),
            dmid=vm((micros, own, width), F32), sems=pltpu.SemaphoreType.DMA((48,)),
        )
        return ins, scratch

    def backward_layer(k, l, loc, sides, swaps_begin, plan, dx_done):
        row_f, row_a = rows_of(k, "f_"), rows_of(k, "a_")
        first = [
            loc.start(a, b) for a, b in ((k.w_h, k.f_w), (k.gp_h, k.f_gp), (k.up_h, k.f_up))
        ]
        late_f = [loc.start(a, b) for a, b in ((k.act_h, k.f_act), (k.fx_h, k.xin))]
        loads_a = [
            loc.start(a, b)
            for a, b in (
                (k.wo_h, k.a_wo), (k.qkv_h, k.a_qkv), (k.wq_h, k.a_wq), (k.state_h, k.a_state)
            )
        ]
        late_a = [loc.start(k.mixed_h, k.a_mixed)]
        for m in range(micros):
            k.f_full[row_f.span(m, row_f.s, row_f.r), :] = k.dy[m]
        greet_all(row_f)
        for side in sides:
            side.bind(k, row_f, groups)
        ag_begin(row_f, k.f_full)
        swaps_begin(row_f)
        gain_a, gain_f = gain_row(k, cfg, l, 0), gain_row(k, cfg, l, 1)
        k.dgain[...] = jnp.zeros_like(k.dgain)

        def middle(m, summed):
            back, gains = norm_back(k.mid[m], gain_f, summed)
            k.dmid[m] = k.dy[m].astype(F32) + back
            k.dgain[1:2, :] += gains
            k.a_full[row_a.span(m, row_a.s, row_a.r), :] = k.dmid[m].astype(BF16)
            row_a.ag_start(k.a_full, m)

        def leave(m, summed):
            back, gains = norm_back(k.x[m].astype(F32), gain_a, summed)
            k.dx[m] = (k.dmid[m] + back).astype(BF16)
            k.dgain[0:1, :] += gains
            dx_done(m)

        left = ffn_backward(
            view_of(k, "f_", xin=k.xin), row_f, loc, cfg, hooks(plan, F), first, late_f, middle,
            lambda: row_a.ag_pass(k.a_full, 0),
        )
        row_f.finish()

        def load_xin():
            late_a.append(loc.start(k.ax_h, k.xin))

        left = list(left) + [load_xin]
        p = view_of(k, "a_", dpersist=k.dpersist, xin=k.xin, **vars(small_of(k)))
        attn_backward(p, row_a, loc, cfg, hooks(plan, A), l, loads_a, late_a, leave, left)
        return row_f, row_a

    def staged(tag, array, home=None):
        return Gather(tag, array.reshape(by_block), by_block, groups, 1, None, home)

    def grad_of(k):
        return k.f_grad

    y0 = staged("y0_", f1.stage_o)
    y1 = Gather("y1_", None, stage_dims, groups, 1, lambda k, row: k.stage)
    td1, tg1 = (Total(t, None, grad_b_dims, groups, (i, 1), grad_of) for t, i in (("td_", 2), ("tg_", 0)))
    sides3 = [y0, y1, td1, tg1]
    swap_y1 = Swap("swap_")

    def third_body(k):
        loc = Local(k.sems)

        def begin(row):
            y0.start()
            swap_y1.start(k, row, own, size, k.y, k.stage, False)

        def start_y1():
            swap_y1.wait()
            y1.start()

        plan = place(
            PLACES["third"],
            [
                y0.step, y0.step, start_y1, td1.start, y1.step, td1.step, tg1.start, td1.step, y1.step,
                tg1.step, tg1.step,
            ],
        )
        row_f, row_a = backward_layer(k, 1, loc, sides3, begin, plan, lambda m: None)
        for i in range(3):
            loc.start(k.f_grad.at[i], k.grad_b_o.at[i])
        loc.start(k.a_grad, k.grad_a_o)
        for side in sides3:
            side.finish()
        row_f.finish()
        row_a.finish()
        for side in sides3 + [swap_y1]:
            side.drain()
        loc.finish()

    ins, scratch = backward_names(f1, f1.dy, f0.y, f0.q1_o)
    ins["y"] = (f1.y, VM)
    small_outs = dict(
        dgain=((2, width), F32, VM),
        dpersist=((2, persist, size), F32, VM),
        dx=((micros, own, width), BF16, VM),
    )
    outs = dict(grad_a_o=hbm(grad_a_dims), grad_b_o=hbm(grad_b_dims), **small_outs)
    scratch["stage"] = vm(stage_dims)
    for side in sides3:
        side.declare(ins, outs, scratch, groups)
    swap_y1.declare(scratch)
    b1 = launch("backward_1", 2, third_body, ins, outs, scratch)

    small_rows = gain_rows + 4 * persist
    tu1 = Total("tu1_", b1.grad_b_o, grad_b_dims, groups, (1, 1), None, "scratch")
    ta1 = Total("ta1_", b1.grad_a_o, grad_a_dims, groups, (0, 1), None, "scratch")
    td0, tg0, tu0 = (
        Total(t, None, grad_b_dims, groups, (i, 1), grad_of, "scratch")
        for t, i in (("td_", 2), ("tg_", 0), ("tu_", 1))
    )
    ta0 = Total("ta0_", None, grad_a_dims, groups, (0, 1), lambda k: k.a_grad, "scratch")
    g1 = Gather("g1_", None, by_block, groups, 1, lambda k, row: k.staged1)
    g0 = [
        Gather(f"g0{m}_", None, by_block[1:], groups, 0, lambda k, row, m=m: k.staged0.at[m], "scratch")
        for m in range(micros)
    ]

    def blocked(stage, staged, m):
        for b in range(blocks):
            staged[m, b] = stage[m, b * BLOCK : (b + 1) * BLOCK, :]
    sides4 = [tu1, ta1, td0, tg0, tu0, ta0, g1, *g0]
    swap_g1, swaps0 = Swap("swap_"), [Swap(f"swap{m}_") for m in range(micros)]

    def last_body(k):
        loc = Local(k.sems)
        push = pusher(k.psend, k.precv)
        load_y = loc.start(k.y0_buf, k.whole)
        loads = [
            loc.start(a, b)
            for a, b in (
                (k.bg1, k.res_b.at[1, pl.ds(0, 1)]), (k.bd1, k.res_b.at[1, pl.ds(2, 1)]),
            )
        ]

        def begin(row):
            tu1.start()
            ta1.start()
            swap_g1.start(k, row, own, size, k.dy, k.stage, False)

        def start_g1():
            swap_g1.wait()
            for m in range(micros):
                blocked(k.stage, k.staged1, m)
            g1.start()

        def gather_g0(m):
            swaps0[m].wait()
            blocked(k.stage0, k.staged0, m)
            g0[m].start()

        def dx_done(m):
            swaps0[m].start(
                k, ta0.row, own, size, k.dx.at[pl.ds(m, 1)], k.stage0.at[pl.ds(m, 1)], False
            )
            if m >= 1:
                gather_g0(m - 1)

        plan = place(
            PLACES["last"],
            [
                tu1.step, ta1.step, start_g1, tu1.step, ta1.step, g1.step, td0.start, g1.step, td0.step,
                tg0.start, tu0.start, td0.step, tg0.step, tu0.step, tg0.step, tu0.step, ta0.start,
            ],
        )
        row_f, row = backward_layer(k, 0, loc, sides4, begin, plan, dx_done)
        for i in range(half_gains):
            lanes_here = slice(i * 128, (i + 1) * 128)
            for j, ref in enumerate((k.dgain, k.dgain1)):
                for kind in range(2):
                    at = (j * 2 + kind) * half_gains + i
                    k.smalls[at : at + 1, :] = ref[kind : kind + 1, lanes_here]
        for j, ref in enumerate((k.dpersist, k.dpersist1)):
            for kind in range(2):
                at = gain_rows + (j * 2 + kind) * persist
                k.smalls[at : at + persist, :] = ref[kind]
        gather_g0(micros - 1)
        pushes = []
        for i in range(1, groups):
            to = (row.s, row.r, lax.rem(row.c + i, groups))
            pushes.append(push(k.smalls, k.small_box.at[i], i, to))
        for copy in loads:
            loc.wait(copy)

        def all_restored(slot):
            for m in range(micros):
                for b in range(blocks):
                    where = pl.ds(b * BLOCK, BLOCK)
                    k.halves[slot, m, where, :] = k.whole[m, k.back[m, b]]

        loc.wait(load_y)
        all_restored(0)
        loc.wait(loc.start(k.y1_buf, k.whole))
        all_restored(1)
        moved, kept_here = [], []
        mine_lanes = pl.ds(pl.multiple_of(row.s * size, 128), size)

        def give(i, pair, out):
            moved.append(push(pair.at[1 - row.s], out, groups + 8 + i, row.sib))
            kept_here.append(loc.start(pair.at[row.s], out))

        give(0, k.halves.at[pl.ds(0, 2)], k.acts_o.at[:, :, mine_lanes])

        for g in g0:
            g.step()
        ta0.step()
        g1.finish()
        loc.wait(loc.start(k.g1_dst, k.whole))
        all_restored(3)
        for g in g0:
            g.step()
        ta0.step()
        for total in (td0, tg0, tu0, tu1, ta1):
            total.finish()
        k.res_b[0, pl.ds(2, 1)] = k.td_sum[...]
        k.res_b[0, pl.ds(0, 1)] = k.tg_sum[...]
        k.res_b[0, pl.ds(1, 1)] = k.tu_sum[...]
        k.res_b[1, pl.ds(1, 1)] = k.tu1_sum[...]
        k.res_a[1] = k.ta1_sum[...]
        give(1, k.res_b, k.grad_b.at[row.s])
        for copy in pushes:
            copy.wait_recv()
        total = k.smalls[...]
        for i in range(1, groups):
            total = total + k.small_box[i]
        k.small_sum[...] = total

        def persist_rows(layer):
            at = pl.multiple_of(gain_rows + layer * 2 * persist, 8)
            return k.small_sum.at[pl.ds(at, 2 * persist), :]

        out = k.persist_o.at[row.s]
        moved.append(push(persist_rows(1 - row.s), out, groups + 12, row.sib))
        kept_here.append(loc.start(persist_rows(row.s), out))
        gains = []
        for i, ps, pr in others(row):
            src = k.small_sum.at[pl.ds(0, gain_rows), :]
            gains.append(push(src, k.gain_box.at[i], groups + i, (ps, pr, row.c)))
        ta0.finish()
        k.res_a[0] = k.ta0_sum[...]
        give(2, k.res_a, k.grad_a.at[row.s])
        for m, g in enumerate(g0):
            g.finish()
            buf = getattr(k, f"g0{m}_dst")
            for b in range(blocks):
                k.halves[2, m, pl.ds(b * BLOCK, BLOCK), :] = buf[k.back[m, b]]
        give(3, k.halves.at[pl.ds(2, 2)], k.grads_o.at[:, :, mine_lanes])
        for copy in gains:
            copy.wait_recv()
        total = k.small_sum[0:gain_rows, :]
        for i in range(1, 8):
            total = total + k.gain_box[i]
        k.gain_o[...] = total
        for copy in moved:
            copy.wait()
        for copy in pushes + gains:
            copy.wait_send()
        for side in sides4:
            side.finish()
        row_f.finish()
        row.finish()
        for side in sides4 + [swap_g1] + swaps0:
            side.drain()
        loc.finish()

    ins, scratch = backward_names(f0, b1.dx, f0.x, f0.q0_o)
    ins.update(
        y0_buf=(b1.y0_dst, HB),
        y1_buf=(b1.y1_dst.reshape(b1.y0_dst.shape), HB),
        bg1=(b1.tg_sum, HB),
        bd1=(b1.td_sum, HB),
        dgain1=(b1.dgain, VM),
        dpersist1=(b1.dpersist, VM),
        back=(back_picks, SM),
    )
    outs = dict(
        acts_o=((micros, rows, features), BF16, VM),
        grads_o=((micros, rows, features), BF16, VM),
        grad_a=((2,) + ta0.dims, BF16, VM),
        grad_b=((2, 3) + tu0.dims[1:], BF16, VM),
        gain_o=((gain_rows, 128), F32, VM),
        persist_o=((2, 2 * persist, 128), F32, VM),
    )
    scratch.update(
        stage=vm(stage_dims),
        stage0=vm(stage_dims),
        whole=vm((micros, total_blocks, BLOCK, size)),
        staged0=vm(by_block),
        staged1=vm(by_block),
        halves=vm((4,) + stage_dims),
        res_a=vm((2,) + ta0.dims),
        res_b=vm((2, 3) + tu0.dims[1:]),
        smalls=vm((small_rows, 128), F32),
        small_box=vm((groups, small_rows, 128), F32),
        small_sum=vm((small_rows, 128), F32),
        gain_box=vm((8, gain_rows, 128), F32),
        dgain=vm((2, width), F32),
        dpersist=vm((2, persist, size), F32),
        dx=vm((micros, own, width)),
        psend=pltpu.SemaphoreType.DMA((groups + 13,)),
        precv=pltpu.SemaphoreType.DMA((groups + 13,)),
    )
    for side in sides4:
        side.declare(ins, outs, scratch, groups)
    for swap in [swap_g1] + swaps0:
        swap.declare(scratch)
    closed = launch("backward_0", 3, last_body, ins, outs, scratch)

    def cols_join(pair):
        return jnp.concatenate([pair[0], pair[1]], axis=1).astype(F32)[None]

    def rows_join(pair):
        return jnp.concatenate([pair[0].T, pair[1].T], axis=0).astype(F32)[None]

    grad_a, grad_b = closed.grad_a[:, 0], closed.grad_b
    heads = [cols_join(grad_a[:, :, i * size : (i + 1) * size]) for i in range(3)]
    grad_out = rows_join(grad_a[:, :, 3 * size :])
    grad_gate, grad_up = cols_join(grad_b[:, 0]), cols_join(grad_b[:, 1])
    grad_down = rows_join(grad_b[:, 2])
    gain_sum = closed.gain_o.reshape(2, 2, width)
    my_gain = lax.dynamic_slice_in_dim(
        lax.dynamic_index_in_dim(gain_sum, sec, 0, False), (row_id * groups + col) * share, share, 1
    )
    persist_sum = closed.persist_o.reshape(2, 2, persist, size)
    persist_sum = lax.dynamic_slice_in_dim(persist_sum, col * per, per, 2)
    grad_persist = jnp.concatenate([persist_sum[0], persist_sum[1]], axis=2)
    return (
        closed.acts_o[None],
        closed.grads_o[None],
        my_gain[0][None],
        heads[0],
        heads[1],
        heads[2],
        grad_persist[0][None],
        grad_persist[1][None],
        grad_out,
        my_gain[1][None],
        grad_gate,
        grad_up,
        grad_down,
    )


def solution(mesh):
    weight = P("section", "col", "row")
    across = P("section", "row", "col")
    gain = P("section", ("row", "col"))
    rows = P("section", None, "col", "row")
    return jax.shard_map(
        local,
        mesh=mesh,
        in_specs=(
            P(None, "col", "row"), P(None, "col", "row"), P(), P(), rows, rows, gain, weight, weight,
            weight, weight, weight, across, gain, weight, weight, across,
        ),
        out_specs=(
            rows, rows, gain, weight, weight, weight, weight, weight, across, gain, weight, weight,
            across,
        ),
        check_vma=False,
    )
```

```python
from types import SimpleNamespace

import jax
import jax.numpy as jnp
from jax import lax
from jax.experimental import pallas as pl
from jax.experimental.pallas import tpu as pltpu
from jax.sharding import PartitionSpec as P

BLOCK = 64
EPS = 1e-06
MESH = pl.DeviceIdType.MESH
F32 = jnp.float32
BF16 = jnp.bfloat16
VMEM_LIMIT = 60 << 20
N_AG, N_RS = 8, 7

A, F, NEXT = 0, 100, 200
PLACES = dict(
    first=[
        A, A + 10, A + 30, A + 21, A + 12, A + 32, A + 41, A + 41, F + 31, F + 32,
        F + 40, NEXT, NEXT, F + 40, F + 41,
        NEXT + 12, NEXT + 2, NEXT + 12, NEXT + 41, NEXT + 30, NEXT + 32, NEXT + 40,
        NEXT + 41, NEXT + F + 11, NEXT + F + 32, NEXT + F + 41,
    ],
    third=[
        F + 30, F + 32, F + 30, F + 52, F + 52, F + 50, A + 2, A + 32, A + 12, A + 31,
        A + 32,
    ],
    last=[
        F + 40, F, F, A + 31, F + 31, F + 40, F + 50, A + 10, A + 30, F + 50,
        F + 51, A + 31, A + 1, A + 2, A + 40, A + 30, A + 60,
    ],
)


def place(points, actions, fixed=()):
    plan = {}
    for point, action in list(zip(points, actions, strict=True)) + list(fixed):
        plan.setdefault(point, []).append(action)
    return plan


def dot(a, b, ca=1, cb=0):
    return lax.dot_general(a, b, (((ca,), (cb,)), ((), ())), preferred_element_type=F32)


class Rows:
    def __init__(self, rows, own, width, send, recv):
        self.rows, self.own, self.width, self.half = rows, own, width, width // 2
        self.send, self.recv = send, recv
        self.s, self.r, self.c = (lax.axis_index(a) for a in ("section", "row", "col"))
        self.rx = self.r + 1 - 2 * lax.rem(self.r, 2)
        self.ry = lax.rem(self.r + 2, 4)
        self.rd = lax.rem(self.rx + 2, 4)
        self.x = (self.s, self.rx, self.c)
        self.y = (self.s, self.ry, self.c)
        self.sib = (1 - self.s, self.r, self.c)
        self.started = []

    def greet(self, others=()):
        barrier = pltpu.get_barrier_semaphore()
        peers = [self.x, self.y, self.sib] + list(others)
        for peer in peers:
            pl.semaphore_signal(barrier, inc=1, device_id=peer, device_id_type=MESH)
        pl.semaphore_wait(barrier, len(peers))

    def copy(self, src, dst, m, k, peer):
        return pltpu.make_async_remote_copy(
            src_ref=src,
            dst_ref=dst,
            send_sem=self.send.at[m, k],
            recv_sem=self.recv.at[m, k],
            device_id=peer,
            device_id_type=MESH,
        )

    def go(self, copy):
        copy.start()
        self.started.append(copy)

    def finish(self):
        for copy in self.started:
            copy.wait_send()
        self.started = []

    def span(self, m, s, r):
        return pl.ds(pl.multiple_of(m * self.rows + (s * 4 + r) * self.own, 16), self.own)

    def ag_copy(self, full, m, k):
        left, right = pl.ds(0, self.half), pl.ds(self.half, self.half)
        mine, atx, aty, atd = (
            self.span(m, self.s, r) for r in (self.r, self.rx, self.ry, self.rd)
        )
        if k == 0:
            return self.copy(full.at[mine, :], full.at[mine, :], m, 0, self.x)
        if k == 1:
            return self.copy(full.at[mine, :], full.at[mine, :], m, 1, self.y)
        if k == 2:
            return self.copy(full.at[mine, :], full.at[mine, :], m, 2, self.sib)
        if k == 3:
            return self.copy(full.at[atx, left], full.at[atx, left], m, 3, self.y)
        if k == 4:
            return self.copy(full.at[aty, right], full.at[aty, right], m, 4, self.x)
        if k == 5:
            return self.copy(full.at[atx, :], full.at[atx, :], m, 5, self.sib)
        if k == 6:
            return self.copy(full.at[aty, :], full.at[aty, :], m, 6, self.sib)
        return self.copy(full.at[atd, :], full.at[atd, :], m, 7, self.sib)

    def ag_start(self, full, m):
        for k in (0, 1, 2):
            self.go(self.ag_copy(full, m, k))

    def ag_pass(self, full, m):
        self.ag_copy(full, m, 0).wait_recv()
        self.go(self.ag_copy(full, m, 3))
        self.go(self.ag_copy(full, m, 5))
        self.ag_copy(full, m, 1).wait_recv()
        self.go(self.ag_copy(full, m, 4))
        self.go(self.ag_copy(full, m, 6))

    def ag_diag(self, full, m):
        self.ag_copy(full, m, 3).wait_recv()
        self.ag_copy(full, m, 4).wait_recv()
        self.go(self.ag_copy(full, m, 7))

    def ag_wait(self, full, m):
        for k in (2, 5, 6, 7):
            self.ag_copy(full, m, k).wait_recv()

    def rs_copy(self, m, k):
        part, pair, both, transit, final = self.buffers
        left, right = pl.ds(0, self.half), pl.ds(self.half, self.half)
        if k == 8:
            other = pl.ds(
                pl.multiple_of(m * self.rows + (1 - self.s) * 4 * self.own, 16), 4 * self.own
            )
            return self.copy(part.at[other, :], pair.at[m], m, 8, self.sib)
        if k == 9:
            return self.copy(both.at[m, self.rd, :, left], transit.at[m, 0], m, 9, self.x)
        if k == 10:
            return self.copy(both.at[m, self.rd, :, right], transit.at[m, 1], m, 10, self.y)
        if k == 11:
            return self.copy(both.at[m, self.rx, :, left], final.at[m, 0, :, left], m, 11, self.x)
        if k == 12:
            return self.copy(both.at[m, self.ry, :, right], final.at[m, 1, :, right], m, 12, self.y)
        if k == 13:
            return self.copy(both.at[m, self.ry, :, left], final.at[m, 1, :, left], m, 13, self.y)
        return self.copy(both.at[m, self.rx, :, right], final.at[m, 0, :, right], m, 14, self.x)

    def rs_start(self, m):
        self.go(self.rs_copy(m, 8))

    def rs_pair(self, m):
        part, pair, both, _, _ = self.buffers
        self.rs_copy(m, 8).wait_recv()
        for r in range(4):
            mine = part[self.span(m, self.s, r), :].astype(F32)
            theirs = pair[m, r * self.own : (r + 1) * self.own, :].astype(F32)
            both[m, r] = (mine + theirs).astype(BF16)
        for k in (9, 10, 11, 12):
            self.go(self.rs_copy(m, k))

    def rs_transit(self, m):
        _, _, both, transit, _ = self.buffers
        left, right = pl.ds(0, self.half), pl.ds(self.half, self.half)
        self.rs_copy(m, 9).wait_recv()
        total = both[m, self.ry, :, left].astype(F32) + transit[m, 0].astype(F32)
        both[m, self.ry, :, left] = total.astype(BF16)
        self.go(self.rs_copy(m, 13))
        self.rs_copy(m, 10).wait_recv()
        total = both[m, self.rx, :, right].astype(F32) + transit[m, 1].astype(F32)
        both[m, self.rx, :, right] = total.astype(BF16)
        self.go(self.rs_copy(m, 14))

    def rs_result(self, m):
        _, _, both, _, final = self.buffers
        for k in (11, 12, 13, 14):
            self.rs_copy(m, k).wait_recv()
        return both[m, self.r].astype(F32) + final[m, 0].astype(F32) + final[m, 1].astype(F32)


class Local:
    def __init__(self, sems):
        self.sems, self.used, self.open = sems, 0, []

    def start(self, src, dst):
        copy = pltpu.make_async_copy(src, dst, self.sems.at[self.used])
        self.used += 1
        copy.start()
        self.open.append(copy)
        return copy

    def wait(self, copy):
        copy.wait()
        self.open = [other for other in self.open if other is not copy]

    def finish(self):
        for copy in list(self.open):
            copy.wait()


def inv_rms(values):
    return lax.rsqrt(jnp.mean(values * values, axis=1, keepdims=True) + EPS)


def norm_to(full, gain, values, span):
    full[span, :] = (values * inv_rms(values) * gain).astype(BF16)


def norm_back(values, gain, grad):
    scale = inv_rms(values)
    weighted = grad * gain
    inner = jnp.mean(weighted * values, axis=1, keepdims=True)
    back = scale * weighted - values * (scale * scale * scale * inner)
    return back, jnp.sum(grad * values * scale, axis=0, keepdims=True)


def wait_both(copies):
    for condition, copy in copies:

        @pl.when(condition)
        def _(copy=copy):
            copy.wait_send()


class Side:
    def __init__(self, tag):
        self.tag = tag

    def ref(self, name):
        return getattr(self.ns, self.tag + name)

    def bind(self, ns, row, groups):
        self.ns, self.row, self.c, self.groups = ns, row, row.c, groups
        self.sent = []

    def when(self, condition, copy):
        @pl.when(condition)
        def _():
            copy.start()

        self.sent.append((condition, copy))

    def arrived(self, condition, copy):
        @pl.when(condition)
        def _():
            copy.wait_recv()

    def remote(self, src, dst, send, recv, to):
        return pltpu.make_async_remote_copy(
            src_ref=src,
            dst_ref=dst,
            send_sem=send,
            recv_sem=recv,
            device_id=(self.row.s, self.row.r, to),
            device_id_type=MESH,
        )


def part_of(ref, at, per, axis):
    where = pl.ds(pl.multiple_of(at * per, per), per)
    return ref.at[(slice(None),) * axis + (where,)]


class Gather(Side):
    def __init__(self, tag, array, dims, groups, axis, view=None, home=None):
        super().__init__(tag)
        self.array, self.axis, self.view, self.home = array, axis, view, home
        self.per = dims[axis]
        self.dims = dims[:axis] + (dims[axis] * groups,) + dims[axis + 1 :]

    def declare(self, ins, outs, scratch, groups):
        if self.array is not None:
            ins[self.tag + "src"] = (self.array, HB)
        if self.home is None:
            outs[self.tag + "dst"] = (self.dims, BF16, HB)
        else:
            scratch[self.tag + "dst"] = pltpu.VMEM(self.dims, BF16)
        scratch[self.tag + "send"] = pltpu.SemaphoreType.DMA((2, groups))
        scratch[self.tag + "recv"] = pltpu.SemaphoreType.DMA((groups,))
        scratch[self.tag + "own"] = pltpu.SemaphoreType.DMA((1,))

    def slot(self, j):
        return part_of(self.ref("dst"), jnp.clip(j, 0, self.groups - 1), self.per, self.axis)

    def source(self):
        return self.view(self.ns, self.row) if self.view else self.ref("src")

    def move(self, j, side, src=None):
        to = jnp.clip(self.c + (1 - 2 * side), 0, self.groups - 1)
        j = jnp.clip(j, 0, self.groups - 1)
        src = self.slot(j) if src is None else src
        return self.remote(
            src, self.slot(j), self.ref("send").at[side, j], self.ref("recv").at[j], to
        )

    def start(self):
        c, n = self.c, self.groups
        self.at, self.done = 1, False
        self.own = pltpu.make_async_copy(self.source(), self.slot(c), self.ref("own").at[0])
        self.own.start()
        self.when(c + 1 < n, self.move(c, 0, self.source()))
        self.when(c >= 1, self.move(c, 1, self.source()))

    def step(self):
        c, n, k = self.c, self.groups, self.at
        if k < n:
            self.arrived(c >= k, self.move(c - k, 0))
            self.arrived(c + k < n, self.move(c + k, 1))
            if k < n - 1:
                self.when((c >= k) & (c + 1 < n), self.move(c - k, 0))
                self.when((c + k < n) & (c >= 1), self.move(c + k, 1))
        self.at += 1

    def finish(self):
        if not self.done:
            while self.at < self.groups:
                self.step()
            self.own.wait()
            self.done = True

    def drain(self):
        wait_both(self.sent)


class Total(Side):
    def __init__(self, tag, parts, dims, groups, span, view=None, home=None):
        super().__init__(tag)
        self.parts, self.span, self.view, self.home = parts, span, view, home
        self.per = dims[1] // groups
        self.count = span[1]
        self.dims = (self.count, self.per, dims[2])

    def declare(self, ins, outs, scratch, groups):
        if self.home is None:
            outs[self.tag + "sum"] = (self.dims, BF16, VM)
        else:
            scratch[self.tag + "sum"] = pltpu.VMEM(self.dims, BF16)
        if self.view is None:
            ins[self.tag + "parts"] = (self.parts, HB)
            whole = (self.count, self.per * groups, self.dims[2])
            scratch[self.tag + "mine"] = pltpu.VMEM(whole, BF16)
        scratch[self.tag + "box"] = pltpu.VMEM((2, groups) + self.dims, BF16)
        scratch[self.tag + "send"] = pltpu.SemaphoreType.DMA((2, groups))
        scratch[self.tag + "recv"] = pltpu.SemaphoreType.DMA((2, groups))
        scratch[self.tag + "load"] = pltpu.SemaphoreType.DMA((1,))

    def clip(self, j):
        return jnp.clip(j, 0, self.groups - 1)

    def piece(self, ref, d, p=None):
        d = self.clip(d)
        where = pl.ds(pl.multiple_of(d * self.per, self.per), self.per)
        if p is None:
            return ref.at[:, where, :]
        return ref[p + (self.span[0] if self.view else 0), where, :]

    def source(self):
        parts = self.view(self.ns) if self.view else self.ref("parts")
        return parts.at[pl.ds(*self.span)]

    def mine(self):
        return self.view(self.ns) if self.view else self.ref("mine")

    def move(self, side, d, src):
        d = self.clip(d)
        to = self.clip(self.c + (1 - 2 * side))
        return self.remote(
            src,
            self.ref("box").at[side, d],
            self.ref("send").at[side, d],
            self.ref("recv").at[side, d],
            to,
        )

    def boxed(self, side, d):
        return self.ref("box").at[side, self.clip(d)]

    def start(self):
        c, n = self.c, self.groups
        self.at, self.done = 1, False
        if self.view is None:
            self.load = pltpu.make_async_copy(
                self.source(), self.ref("mine"), self.ref("load").at[0]
            )
            self.load.start()
        self.ends(0)

    def ends(self, t):
        c, n = self.c, self.groups
        self.when(c == 0, self.move(0, n - 1 - t, self.piece(self.source(), n - 1 - t)))
        self.when(c == n - 1, self.move(1, t, self.piece(self.source(), t)))

    def step(self):
        c, n, t = self.c, self.groups, self.at
        box, mine = self.ref("box"), self.mine()
        if t == 1 and self.view is None:
            self.load.wait()
        if t < n - 1:
            self.ends(t)
            for side, place, d in ((0, c, n - 1 - t + c), (1, n - 1 - c, t + c - (n - 1))):
                here = (place >= 1) & (place <= t)
                self.arrived(here, self.move(side, d, self.boxed(side, d)))

                @pl.when(here)
                def _(side=side, d=d):
                    for p in range(self.count):
                        total = self.piece(mine, d, p).astype(F32)
                        total = total + box[side, self.clip(d), p].astype(F32)
                        box[side, self.clip(d), p] = total.astype(BF16)

                self.when(here, self.move(side, d, self.boxed(side, d)))
        self.at += 1

    def finish(self):
        if self.done:
            return
        self.done = True
        c, n = self.c, self.groups
        while self.at < n - 1:
            self.step()
        box, mine = self.ref("box"), self.mine()
        above, below = c >= 1, c + 1 < n
        self.arrived(above, self.move(0, c, self.boxed(0, c)))
        self.arrived(below, self.move(1, c, self.boxed(1, c)))
        for p in range(self.count):
            first = jnp.where(c >= 1, 0, 1)
            total = self.piece(mine, c, p).astype(F32) + box[first, c, p].astype(F32)
            self.ref("sum")[p] = total.astype(BF16)

            @pl.when(above & below)
            def _(p=p, total=total):
                self.ref("sum")[p] = (total + box[1, c, p].astype(F32)).astype(BF16)

    def drain(self):
        wait_both(self.sent)


def others(row):
    for k in range(1, 8):
        ps = lax.rem(row.s + k // 4, 2)
        low = row.rx if k % 2 else row.r
        pr = lax.rem(low + 2 * ((k // 2) % 2), 4)
        yield k, ps, pr


class Swap:
    def __init__(self, tag):
        self.tag = tag

    def declare(self, scratch):
        scratch[self.tag + "send"] = pltpu.SemaphoreType.DMA((8,))
        scratch[self.tag + "recv"] = pltpu.SemaphoreType.DMA((8,))
        scratch[self.tag + "own"] = pltpu.SemaphoreType.DMA((1,))

    def start(self, ns, row, own, lanes, src, dst, to_tokens):
        send, recv, local = (getattr(ns, self.tag + a) for a in ("send", "recv", "own"))

        def tokens_of(s, r):
            return pl.ds(pl.multiple_of((s * 4 + r) * own, 16), own)

        def lanes_of(s, r):
            return pl.ds(pl.multiple_of((r * 2 + s) * lanes, 128), lanes)

        def ends(ps, pr):
            if to_tokens:
                return src.at[:, tokens_of(ps, pr), :], dst.at[:, :, lanes_of(row.s, row.r)]
            return src.at[:, :, lanes_of(ps, pr)], dst.at[:, tokens_of(row.s, row.r), :]

        a, b = ends(row.s, row.r)
        self.mine = pltpu.make_async_copy(a, b, local.at[0])
        self.mine.start()
        self.copies = []
        for k, ps, pr in others(row):
            a, b = ends(ps, pr)
            copy = pltpu.make_async_remote_copy(
                src_ref=a,
                dst_ref=b,
                send_sem=send.at[k],
                recv_sem=recv.at[k],
                device_id=(ps, pr, row.c),
                device_id_type=MESH,
            )
            copy.start()
            self.copies.append(copy)

    def wait(self):
        for copy in self.copies:
            copy.wait_recv()
        self.mine.wait()

    def drain(self):
        for copy in self.copies:
            copy.wait_send()


def plane_peers(row):
    return [
        (ps, pr, row.c) for k, ps, pr in others(row) if k not in (1, 2, 4)
    ]


def gather_first(row, full, micros, fresh, fill=()):
    if fresh:
        row.ag_pass(full, 0)
        for m in range(2, micros):
            row.ag_start(full, m)
    for work in fill:
        work()
    row.ag_pass(full, 1)
    row.ag_diag(full, 0)


def ag_begin(row, full):
    row.ag_start(full, 0)
    row.ag_start(full, 1)


def gather_more(row, full, micros, m):
    if m + 2 < micros:
        row.ag_pass(full, m + 2)
    if m + 1 < micros:
        row.ag_diag(full, m + 1)


def tail(row, micros, result, hook, between=(), relay=None):
    more = list(between)

    def step():
        if more:
            more.pop(0)()

    row.rs_transit(micros - 2)
    for m in range(micros - 2):
        result(m)
    row.rs_pair(micros - 1)
    hook(40)
    step()
    result(micros - 2)
    row.rs_transit(micros - 1)
    if relay:
        relay()
    step()
    if relay is None:
        while more:
            step()
    hook(41)
    result(micros - 1)
    return more


def ffn_forward(p, row, loc, cfg, hook, deliver, relay=None):
    micros, rows, full = cfg.micros, cfg.rows, p.full
    gather_first(row, full, micros, False)
    for m in range(micros):
        row.ag_wait(full, m)
        hook(m)
        if m >= 1:
            row.rs_pair(m - 1)
        if m >= 2:
            row.rs_transit(m - 2)
        here = pl.ds(m * rows, rows)
        loc.start(full.at[here, :], p.xin_o.at[here, :])
        gate = dot(full[here, :], p.gate_dst[0])
        lift = dot(full[here, :], p.up_dst[0])
        p.gp[here, :] = gate.astype(BF16)
        p.up[here, :] = lift.astype(BF16)
        p.act[here, :] = (gate * jax.nn.sigmoid(gate) * lift).astype(BF16)
        hook(10 + m)
        row.part[here, :] = dot(p.act[here, :], p.down_dst[0], 1, 1).astype(BF16)
        for a, b in ((p.gp, p.gp_o), (p.up, p.up_o), (p.act, p.act_o)):
            loc.start(a.at[here, :], b.at[here, :])
        row.rs_start(m)
        gather_more(row, full, micros, m)
        hook(30 + m)
    tail(row, micros, lambda m: deliver(m, row.rs_result(m)), hook, (), relay)


def ffn_backward(p, row, loc, cfg, hook, loads, late, deliver, relay=None):
    micros, rows, width, full = cfg.micros, cfg.rows, cfg.width, p.full
    gather_first(row, full, micros, True)
    for copy in loads:
        loc.wait(copy)
    for m in range(micros):
        row.ag_wait(full, m)
        hook(m)
        if m >= 1:
            row.rs_pair(m - 1)
        if m >= 2:
            row.rs_transit(m - 2)
        here = pl.ds(m * rows, rows)
        d_act = dot(full[here, :], p.w[2])
        gate = p.gp[here, :].astype(F32)
        lift = p.up[here, :].astype(F32)
        sig = jax.nn.sigmoid(gate)
        silu = gate * sig
        p.dg[here, :] = (d_act * lift * (sig + silu * (1.0 - sig))).astype(BF16)
        p.du[here, :] = (d_act * silu).astype(BF16)
        total = dot(p.dg[here, :], p.w[0], 1, 1) + dot(p.du[here, :], p.w[1], 1, 1)
        row.part[here, :] = total.astype(BF16)
        row.rs_start(m)
        gather_more(row, full, micros, m)
        hook(30 + m)

    def grad(i, left, right):
        def body():
            if i == 2:
                for copy in late:
                    loc.wait(copy)

            @pl.loop(0, width // 256)
            def _(t):
                at = pl.ds(pl.multiple_of(t * 256, 256), 256)
                p.grad[i, at, :] = dot(left[:, at], right[...], 0, 0).astype(BF16)

            hook(50 + i)

        return body

    grads = [grad(2, full, p.act), grad(0, p.xin, p.dg), grad(1, p.xin, p.du)]
    return tail(row, micros, lambda m: deliver(m, row.rs_result(m)), hook, grads, relay)


def pair_masks(size):
    rows_at = lax.broadcasted_iota(jnp.int32, (size, size), 0)
    cols_at = lax.broadcasted_iota(jnp.int32, (size, size), 1)
    return (rows_at >= cols_at) & (rows_at // BLOCK == cols_at // BLOCK)


def gate_columns(gates, columns):
    count, size = gates.shape
    rows_at = lax.broadcasted_iota(jnp.int32, (size, size), 0)
    cols_at = lax.broadcasted_iota(jnp.int32, (size, size), 1)
    for i in range(count):
        spread = jnp.where(rows_at == cols_at, gates[i : i + 1, :], 0.0)
        columns[i * size : (i + 1) * size, :] = jnp.sum(spread, axis=1, keepdims=True)


def gain_row(k, cfg, layer, kind):
    rows_each = cfg.width // 4 // 128
    pieces = [
        k.gains[layer, r, kind * rows_each + h : kind * rows_each + h + 1, :]
        for r in range(4)
        for h in range(rows_each)
    ]
    return jnp.concatenate(pieces, axis=1)


class Heads:
    def __init__(self, k, row, cfg, layer):
        self.k, self.row, self.cfg, self.layer = k, row, cfg, layer

    def persist(self):
        k, cfg = self.k, self.cfg
        out = []
        for kind in range(2):
            start = pl.multiple_of(8 + (2 * kind + self.row.s) * 8, 8)
            for j in range(cfg.groups):
                block = k.line[self.layer, j, pl.ds(start, 8), :]
                k.persist[j * cfg.per : (j + 1) * cfg.per, :] = block[: cfg.per, :]
            out.append(k.persist[...].astype(BF16))
        return out

    def keeps(self, j):
        decays = self.k.line[self.layer, j, 40:48, :] * self.k.starts[j]
        return jnp.where(self.row.s == 0, decays[0:1, :], decays[1:2, :])

    def own(self):
        keeps = self.keeps(self.row.c)
        blocks = self.cfg.blocks

        def of(m, b):
            return keeps[:, m * blocks + b : m * blocks + b + 1]

        return of

    def through(self, m, j):
        keeps = self.keeps(j)
        product = None
        for b in range(self.cfg.blocks):
            at = m * self.cfg.blocks + b
            one = keeps[:, at : at + 1]
            product = one if product is None else product * one
        return product


def pair_probs(q, k, pk, mask, scale):
    inner = jnp.where(mask, dot(q, k, 1, 1) * scale, -1e30)
    outer = dot(q, pk, 1, 1) * scale
    top = jnp.maximum(
        jnp.max(inner, axis=1, keepdims=True), jnp.max(outer, axis=1, keepdims=True)
    )
    inner = jnp.exp(inner - top)
    outer = jnp.exp(outer - top)
    norm = 1.0 / (jnp.sum(inner, axis=1, keepdims=True) + jnp.sum(outer, axis=1, keepdims=True))
    return inner * norm, outer * norm


class States:
    def __init__(self, row, groups, k, backward):
        self.backward, self.sent = backward, []
        self.row, self.groups, self.mine, self.box = row, groups, k.leaving, k.box
        self.send, self.recv, self.entering = k.ssend, k.srecv, k.entering

    def copy(self, m, k):
        n = self.groups
        to = self.row.c + (-k if self.backward else k)
        return pltpu.make_async_remote_copy(
            src_ref=self.mine.at[m],
            dst_ref=self.box.at[m, k],
            send_sem=self.send.at[m, k],
            recv_sem=self.recv.at[m, k],
            device_id=(self.row.s, self.row.r, jnp.clip(to, 0, n - 1)),
            device_id_type=MESH,
        )

    def after(self, k):
        c, n = self.row.c, self.groups
        return (c >= k) if self.backward else (c + k < n)

    def before(self, k):
        c, n = self.row.c, self.groups
        return (c + k < n) if self.backward else (c >= k)

    def start(self, m):
        for k in range(1, self.groups):

            @pl.when(self.after(k))
            def _(k=k):
                self.copy(m, k).start()

            self.sent.append((self.after(k), self.copy(m, k)))

    def wait(self, m):
        for k in range(1, self.groups):

            @pl.when(self.before(k))
            def _(k=k):
                self.copy(m, k).wait_recv()

    def drain(self):
        wait_both(self.sent)

    def fold(self, m, through):
        entering = self.entering
        entering[...] = jnp.zeros_like(entering)
        for k in range(self.groups - 1, 0, -1):

            @pl.when(self.before(k))
            def _(k=k):
                source = self.row.c + (k if self.backward else -k)
                factor = through(m, jnp.clip(source, 0, self.groups - 1))
                entering[...] = factor * entering[...] + self.box[m, k].astype(F32)


def attn_forward(p, row, loc, cfg, hook, layer, fresh, deliver, relay=None):
    micros, rows, size, full = cfg.micros, cfg.rows, cfg.size, p.full
    blocks = rows // BLOCK
    factor = size ** (-0.5)
    states = States(row, cfg.groups, p, False)
    qs, ks, vs = (pl.ds(i * size, size) for i in range(3))
    mask = pair_masks(2 * BLOCK)
    gather_first(row, full, micros, fresh)
    gate_columns(p.gates[layer, 0 : micros * rows // 128, :], p.gate)
    heads = Heads(p, row, cfg, layer)
    pk, pv = heads.persist()
    keep = heads.own()
    for m in range(micros):
        row.ag_wait(full, m)
        hook(m)
        here = pl.ds(m * rows, rows)
        loc.start(full.at[here, :], p.xin_o.at[here, :])
        p.qkv[here, :] = dot(full[here, :], p.wq[0]).astype(BF16)
        loc.start(p.qkv.at[here, :], p.qkv_o.at[here, :])
        total = jnp.zeros((size, size), F32)
        for b in range(blocks):
            at = pl.ds(m * rows + b * BLOCK, BLOCK)
            keys = (p.qkv[at, ks].astype(F32) * p.gate[at, :]).astype(BF16)
            fresh = dot(keys, p.qkv[at, vs], 0, 0)
            p.update[m * blocks + b] = fresh
            total = keep(m, b) * total + fresh
        p.leaving[m] = total.astype(BF16)
        states.start(m)
        gather_more(row, full, micros, m)
        hook(10 + m)
    for m in range(micros):
        here = pl.ds(m * rows, rows)
        states.wait(m)
        states.fold(m, heads.through)
        memory = p.entering[...]
        for b in range(0, blocks, 2):
            at = pl.ds(m * rows + b * BLOCK, 2 * BLOCK)
            q, ky, v = p.qkv[at, qs], p.qkv[at, ks], p.qkv[at, vs]
            inner, outer = pair_probs(q, ky, pk, mask, factor)
            value = dot(inner.astype(BF16), v) + dot(outer.astype(BF16), pv)
            reads = []
            for i in range(2):
                now = keep(m, b + i) * memory
                low = now.astype(BF16)
                p.state[m * blocks + b + i] = low
                reads.append(dot(q[i * BLOCK : (i + 1) * BLOCK, :], low) * factor)
                memory = now + p.update[m * blocks + b + i]
            p.mixed[at, :] = (value + jnp.concatenate(reads, axis=0)).astype(BF16)
        hook(20 + m)
        row.part[here, :] = dot(p.mixed[here, :], p.wo_dst[0], 1, 1).astype(BF16)
        loc.start(p.mixed.at[here, :], p.mixed_o.at[here, :])
        row.rs_start(m)
        if m >= 1:
            row.rs_pair(m - 1)
        if m >= 2:
            row.rs_transit(m - 2)
        hook(30 + m)
    loc.start(p.state, p.state_o)
    tail(row, micros, lambda m: deliver(m, row.rs_result(m)), hook, (), relay)
    states.drain()


def attn_backward(p, row, loc, cfg, hook, layer, loads, late, deliver, fill, relay=None):
    micros, rows, size, width, full = cfg.micros, cfg.rows, cfg.size, cfg.width, p.full
    blocks = rows // BLOCK
    factor = size ** (-0.5)
    states = States(row, cfg.groups, p, True)
    qs, ks, vs = (pl.ds(i * size, size) for i in range(3))
    in_cols, out_cols = pl.ds(0, 3 * size), pl.ds(3 * size, size)
    mask = pair_masks(2 * BLOCK)
    p.dpersist[...] = jnp.zeros_like(p.dpersist)
    gate_columns(p.gates[layer, 0 : micros * rows // 128, :], p.gate)
    heads = Heads(p, row, cfg, layer)
    pk, pv = heads.persist()
    keep = heads.own()
    gather_first(row, full, micros, False, fill)
    for copy in loads:
        loc.wait(copy)
    for m in range(micros):
        row.ag_wait(full, m)
        hook(m)
        here = pl.ds(m * rows, rows)
        p.dmix[here, :] = dot(full[here, :], p.wo[0]).astype(BF16)
        total = jnp.zeros((size, size), F32)
        for b in reversed(range(blocks)):
            at = pl.ds(m * rows + b * BLOCK, BLOCK)
            fresh = dot(p.qkv[at, qs], p.dmix[at, :], 0, 0) * factor
            p.update[m * blocks + b] = fresh
            total = keep(m, b) * (fresh + total)
        p.leaving[m] = total.astype(BF16)
        states.start(m)
        gather_more(row, full, micros, m)
        hook(10 + m)
    for m in range(micros):
        here = pl.ds(m * rows, rows)
        states.wait(m)
        states.fold(m, heads.through)
        memory = p.entering[...]
        for b in reversed(range(0, blocks, 2)):
            at = pl.ds(m * rows + b * BLOCK, 2 * BLOCK)
            q, ky, v, d = p.qkv[at, qs], p.qkv[at, ks], p.qkv[at, vs], p.dmix[at, :]
            inner, outer = pair_probs(q, ky, pk, mask, factor)
            d_inner = dot(d, v, 1, 1)
            d_outer = dot(d, pv, 1, 1)
            centre = jnp.sum(inner * d_inner, axis=1, keepdims=True) + jnp.sum(
                outer * d_outer, axis=1, keepdims=True
            )
            d_inner = (inner * (d_inner - centre)).astype(BF16)
            d_outer = (outer * (d_outer - centre)).astype(BF16)
            inner, outer = inner.astype(BF16), outer.astype(BF16)
            p.dpersist[0] += dot(d_outer, q, 0, 0) * factor
            p.dpersist[1] += dot(outer, d, 0, 0)
            dq = dot(d_inner, ky) + dot(d_outer, pk)
            dk = dot(d_inner, q, 0, 0) * factor
            dv = dot(inner, d, 0, 0)
            keys = (ky.astype(F32) * p.gate[at, :]).astype(BF16)
            parts = [None, None]
            for i in (1, 0):
                sub = slice(i * BLOCK, (i + 1) * BLOCK)
                low = memory.astype(BF16)
                parts[i] = (
                    dot(d[sub, :], p.state[m * blocks + b + i], 1, 1),
                    dot(v[sub, :], low, 1, 1),
                    dot(keys[sub, :], low),
                )
                memory = keep(m, b + i) * (p.update[m * blocks + b + i] + memory)
            more_q, more_k, more_v = (jnp.concatenate(pieces, axis=0) for pieces in zip(*parts))
            p.dqkv[at, qs] = ((dq + more_q) * factor).astype(BF16)
            p.dqkv[at, ks] = (dk + p.gate[at, :] * more_k).astype(BF16)
            p.dqkv[at, vs] = (dv + more_v).astype(BF16)
        row.part[here, :] = dot(p.dqkv[here, :], p.wq[0], 1, 1).astype(BF16)
        row.rs_start(m)
        if m >= 1:
            row.rs_pair(m - 1)
        if m >= 2:
            row.rs_transit(m - 2)
        hook(30 + m)

    def out_grad():
        for copy in late:
            loc.wait(copy)

        @pl.loop(0, width // 256)
        def _(t):
            at = pl.ds(pl.multiple_of(t * 256, 256), 256)
            p.grad[0, at, out_cols] = dot(full[:, at], p.mixed[...], 0, 0).astype(BF16)

    def qkv_grad():
        @pl.loop(0, width // 256)
        def _(t):
            at = pl.ds(pl.multiple_of(t * 256, 256), 256)
            p.grad[0, at, in_cols] = dot(p.xin[:, at], p.dqkv[...], 0, 0).astype(BF16)

        hook(60)

    tail(row, micros, lambda m: deliver(m, row.rs_result(m)), hook, [out_grad, qkv_grad], relay)
    states.drain()


VM = pl.BlockSpec(memory_space=pltpu.VMEM)
SM = pl.BlockSpec(memory_space=pltpu.SMEM)
HB = pl.BlockSpec(memory_space=pl.ANY)


def vm(dims, dtype=BF16):
    return pltpu.VMEM(dims, dtype)


def launch(name, collective, body, ins, outs, scratch):
    names = list(ins) + list(outs) + list(scratch)

    def kernel(*refs):
        body(SimpleNamespace(**dict(zip(names, refs))))

    results = pl.pallas_call(
        kernel,
        out_shape=tuple(jax.ShapeDtypeStruct(d, t) for d, t, _ in outs.values()),
        in_specs=[spec for _, spec in ins.values()],
        out_specs=tuple(spec for _, _, spec in outs.values()),
        scratch_shapes=list(scratch.values()),
        compiler_params=pltpu.CompilerParams(
            collective_id=collective, has_side_effects=True, vmem_limit_bytes=VMEM_LIMIT
        ),
        name=name,
    )(*[a for a, _ in ins.values()])
    return SimpleNamespace(**dict(zip(outs, results)))


def local(
    tokens, cotangent, block_order, lengths, decay, write_gate, gain_attn, w_query, w_key, w_value,
    persist_key, persist_value, w_output, gain_ffn, w_gate, w_up, w_down,
):
    sec, row_id, col = (lax.axis_index(a) for a in ("section", "row", "col"))
    groups = lax.axis_size("col")
    micros, rows, features = tokens.shape
    width = features * 4
    own, blocks, all_rows, size = rows // 8, rows // BLOCK, micros * rows, features // 2
    ffh = w_gate.shape[2] // 2
    per = persist_key.shape[1]
    persist = per * groups
    cfg = SimpleNamespace(
        micros=micros, rows=rows, own=own, size=size, width=width, groups=groups, blocks=blocks, per=per
    )
    total_blocks = block_order.shape[1]
    positions = jnp.arange(total_blocks, dtype=jnp.int32)
    my_blocks = col * blocks + jnp.arange(blocks, dtype=jnp.int32)
    matches = (block_order[:, :, None] == my_blocks[None, None, :]).astype(jnp.int32)
    back_picks = jnp.sum(matches * positions[None, :, None], axis=1)

    def lanes(a):
        return jnp.pad(a, ((0, 0),) * (a.ndim - 1) + ((0, 128 - a.shape[-1]),))

    def eights(a):
        return jnp.pad(a, ((0, 0),) * (a.ndim - 2) + ((0, -a.shape[-2] % 8), (0, 0)))

    share = gain_attn.shape[1]
    own_gains = jnp.concatenate([gain_attn, gain_ffn], axis=0).astype(F32)
    placed = lax.dynamic_update_slice(
        jnp.zeros((2, features), F32), own_gains, (jnp.zeros_like(col), col * share)
    )
    packed = jnp.concatenate(
        [eights(placed.reshape(-1, 128))]
        + [
            eights(a[0].reshape(per, 2, size).transpose(1, 0, 2)).reshape(16, size).astype(F32)
            for a in (persist_key, persist_value)
        ]
        + [eights(lanes(decay[0].transpose(2, 0, 1).reshape(2, -1)))],
        axis=0,
    )
    gate_rows = eights(write_gate[0].transpose(2, 0, 1).reshape(2, -1, 128)) / BLOCK
    sequences = jnp.arange(lengths.shape[1])
    earlier = sequences[None, :] < sequences[:, None]
    firsts = jnp.sum(jnp.where(earlier[None], lengths[:, None, :], 0), axis=2)
    is_start = jnp.any(positions[None, :, None] == firsts[:, None, :], axis=2)
    starts = jnp.where(is_start, 0.0, 1.0).reshape(micros, groups, blocks).transpose(1, 0, 2)
    starts = jnp.broadcast_to(lanes(starts.reshape(groups, -1))[:, None], (groups, 8, 128))

    def cols_split(w):
        return w.reshape(w.shape[0], 2, -1).transpose(1, 0, 2)

    def rows_split(w):
        return w.reshape(2, -1, w.shape[1]).transpose(0, 2, 1)

    blocks_a = jnp.concatenate(
        [cols_split(w[0]) for w in (w_query, w_key, w_value)] + [rows_split(w_output[0])], axis=2
    )[:, None]
    blocks_b = jnp.stack(
        [cols_split(w_gate[0]), cols_split(w_up[0]), rows_split(w_down[0])], axis=1
    )

    a_dims, b_dims = blocks_a.shape[1:], blocks_b.shape[1:]
    q_dims, o_dims, one_dims = (1, a_dims[1], 3 * size), (1, a_dims[1], size), (1,) + b_dims[1:]
    grad_a_dims, grad_b_dims = (1, width, 4 * size), (3, width, ffh)
    stage_dims = (micros, rows, size)
    by_block = (micros, blocks, BLOCK, size)
    gain_rows = 4 * width // 128
    half_gains = width // 128
    hbm = lambda dims, dtype=BF16: (dims, dtype, HB)

    def row_scratch(prefix):
        return {
            "part": vm((all_rows, width)),
            "pair": vm((micros, 4 * own, width)),
            "both": vm((micros, 4, own, width)),
            "transit": vm((micros, 2, own, width // 2)),
            "final": vm((micros, 2, own, width)),
            prefix + "send": pltpu.SemaphoreType.DMA((micros, N_AG + N_RS)),
            prefix + "recv": pltpu.SemaphoreType.DMA((micros, N_AG + N_RS)),
            prefix + "full": vm((all_rows, width)),
        }

    shared_rows = ("part", "pair", "both", "transit", "final")

    def attn_scratch(prefix):
        names = dict(
            update=vm((micros * blocks, size, size), F32),
            entering=vm((size, size), F32),
            leaving=vm((micros, size, size)),
            box=vm((micros, groups, size, size)),
            ssend=pltpu.SemaphoreType.DMA((micros, groups)),
            srecv=pltpu.SemaphoreType.DMA((micros, groups)),
            gate=vm((all_rows, 1), F32),
            persist=vm((persist, size), F32),
            qkv=vm((all_rows, 3 * size)),
            state=vm((micros * blocks, size, size)),
            mixed=vm((all_rows, size)),
        )
        return {**row_scratch(prefix), **{prefix + a: b for a, b in names.items()}}

    def ffn_scratch(prefix):
        names = {a: vm((all_rows, ffh)) for a in ("gp", "up", "act")}
        return {**row_scratch(prefix), **{prefix + a: b for a, b in names.items()}}

    def view_of(k, prefix, **more):
        names = {a[len(prefix) :]: b for a, b in vars(k).items() if a.startswith(prefix)}
        return SimpleNamespace(**{**names, **more})

    def rows_of(k, prefix):
        p = view_of(k, prefix)
        row = Rows(rows, own, width, p.send, p.recv)
        row.buffers = (k.part, k.pair, k.both, k.transit, k.final)
        row.part = k.part
        return row

    def greet_all(row):
        row.greet(
            plane_peers(row)
            + [(row.s, row.r, lax.rem(row.c + i, groups)) for i in range(1, groups)]
        )

    def hooks(plan, prefix):
        def hook(point):
            for action in plan.get(prefix + point, ()):
                action()

        return hook

    def pusher(send, recv):
        def push(src, dst, i, to):
            copy = pltpu.make_async_remote_copy(
                src_ref=src,
                dst_ref=dst,
                send_sem=send.at[i],
                recv_sem=recv.at[i],
                device_id=to,
                device_id_type=MESH,
            )
            copy.start()
            return copy

        return push

    def blocks_from(buf, picks, stage, m, group):
        for b in range(blocks):
            stage[m, pl.ds(b * BLOCK, BLOCK), :] = buf[m, picks[m, group * blocks + b]]

    def forward_names(l):
        outs = dict(
            a_xin_o=hbm((all_rows, width)),
            a_qkv_o=hbm((all_rows, 3 * size)),
            a_state_o=hbm((micros * blocks, size, size)),
            a_mixed_o=hbm((all_rows, size)),
            f_xin_o=hbm((all_rows, width)),
            f_gp_o=hbm((all_rows, ffh)),
            f_up_o=hbm((all_rows, ffh)),
            f_act_o=hbm((all_rows, ffh)),
            wo_o=hbm((1, width, size)),
            w_o=hbm((3, width, ffh)),
            mid=((micros, own, width), F32, VM),
            y=((micros, own, width), BF16, VM),
        )
        return outs, {**attn_scratch("a_"), **ffn_scratch("f_")}

    def forward_layer(k, l, x, wq, loc, plan, base, row_a, small, fresh, leave, relay):
        row_f = rows_of(k, "f_")
        gain_f = gain_row(small, cfg, l, 1)

        def middle(m, summed):
            k.mid[m] = x[m].astype(F32) + summed
            norm_to(k.f_full, gain_f, k.mid[m], row_f.span(m, row_f.s, row_f.r))
            row_f.ag_start(k.f_full, m)

        def leave_y(m, summed):
            k.y[m] = (k.mid[m] + summed).astype(BF16)
            leave(m)

        p = view_of(k, "a_", wq=wq, wo_dst=k.wo_dst, **vars(small))
        attn_forward(
            p, row_a, loc, cfg, hooks(plan, base), l, fresh, middle,
            lambda: row_f.ag_pass(k.f_full, 0),
        )
        row_a.finish()
        loc.start(k.wo_dst, k.wo_o)
        p = view_of(k, "f_", gate_dst=k.gate_dst, up_dst=k.up_dst, down_dst=k.down_dst)
        ffn_forward(p, row_f, loc, cfg, hooks(plan, base + F), leave_y, relay)
        row_f.finish()
        for i, w in enumerate((k.gate_dst, k.up_dst, k.down_dst)):
            loc.start(w, k.w_o.at[pl.ds(i, 1)])

    def one_b(tag, layer, which):
        view = lambda k, row: k.shards_b.at[layer, pl.ds(which, 1)]
        return Gather(tag, None, one_dims, groups, 1, view, "scratch")

    def q_of(ref, layer):
        return ref.at[layer, :, :, pl.ds(0, 3 * size)]

    def o_of(ref, layer):
        return ref.at[layer, :, :, pl.ds(3 * size, size)]

    def lanes_of_core(name):
        def view(k, row):
            mine = pl.ds(pl.multiple_of(row.s * size, 128), size)
            return getattr(k, name).at[:, :, :, mine]

        return view

    tokens_b = tokens.reshape(micros, blocks, BLOCK, features)
    cotangent_b = cotangent.reshape(micros, blocks, BLOCK, features)

    def tokens_of(m):
        def view(k, row):
            mine = pl.ds(pl.multiple_of(row.s * size, 128), size)
            return k.deal0_src.at[m, :, :, mine]

        return view

    deals = [
        Gather(
            f"deal{m}_", tokens_b if m == 0 else None, by_block[1:], groups, 0, tokens_of(m), "scratch"
        )
        for m in range(micros)
    ]
    q0 = Gather("q0_", None, q_dims, groups, 1, lambda k, row: q_of(k.shards_a, 0), "scratch")
    wo0 = Gather("wo_", None, o_dims, groups, 1, lambda k, row: o_of(k.shards_a, 0), "scratch")
    gate0, up0, down0 = (one_b(t, 0, i) for i, t in enumerate(("gate_", "up_", "down_")))
    q1 = Gather("q1_", None, q_dims, groups, 1, lambda k, row: q_of(k.shards_a, 1), "scratch")
    wo1 = Gather("L1_wo_", None, o_dims, groups, 1, lambda k, row: o_of(k.shards_a, 1), "scratch")
    gate1, up1, down1 = (
        one_b(t, 1, i) for i, t in enumerate(("L1_gate_", "L1_up_", "L1_down_"))
    )
    cot = Gather("cot_", cotangent_b, by_block, groups, 1, lanes_of_core("cot_src"), "scratch")
    sides1 = [*deals, q0, wo0, gate0, up0, down0, q1, wo1, gate1, up1, down1, cot]
    swaps1 = [Swap(f"swap{m}_") for m in range(micros)]
    swap_y, swap_c = Swap("swapy_"), Swap("swapc_")

    def first_body(k):
        row = rows_of(k, "a_")
        loc = Local(k.sems)
        greet_all(row)
        for side in sides1:
            side.bind(k, row, groups)
        push = pusher(k.psend, k.precv)
        crossing, keeps_here = [], []
        for i, (src, dst) in enumerate(((k.blocks_a, k.shards_a), (k.blocks_b, k.shards_b))):
            keeps_here.append(loc.start(src.at[row.s], dst.at[row.s]))
            crossing.append(push(src.at[1 - row.s], dst.at[row.s], groups + 9 + i, row.sib))
        for side in deals[:2]:
            side.start()
        k.line[row.s, row.c] = k.packed[...]
        k.gates[row.s] = k.gate_rows[row.s]
        small = [
            push(
                k.packed,
                k.line.at[row.s, row.c],
                i,
                (row.s, row.r, lax.rem(row.c + i, groups)),
            )
            for i in range(1, groups)
        ]
        late = [push(k.gate_rows.at[1 - row.s], k.gates.at[row.s], 0, row.sib)]
        crossing[0].wait_recv()
        loc.wait(keeps_here[0])
        q0.start()
        for side in deals[2:]:
            side.start()
        for side in deals[:2]:
            side.step()
        for copy in small:
            copy.wait_recv()
        total = k.line[row.s, 0, 0:8, :]
        for j in range(1, groups):
            total = total + k.line[row.s, j, 0:8, :]
        k.gains[row.s, row.r] = total
        for i, ps, pr in others(row):
            mine = k.gains.at[row.s, row.r]
            late.append(push(mine, mine, groups + i, (ps, pr, row.c)))
        late.append(push(k.line.at[row.s], k.line.at[row.s], groups + 8, row.sib))
        crossing[1].wait_recv()
        loc.wait(keeps_here[1])
        q0.step()
        for side in deals[2:] + deals[:2]:
            side.step()
        q0.step()
        for side in deals[2:]:
            side.step()
        wo0.start()
        gate0.start()
        up0.start()
        for m in range(micros):
            deals[m].finish()
            buf = getattr(k, f"deal{m}_dst")
            for b in range(blocks):
                where = pl.ds(b * BLOCK, BLOCK)
                k.stage[m, where, :] = buf[k.picks[m, row.c * blocks + b]]
            one = pl.ds(m, 1)
            swaps1[m].start(k, row, own, size, k.stage.at[one], k.x.at[one], True)
        for copy in late:
            copy.wait_recv()
        gain = gain_row(k, cfg, 0, 0)
        for m in range(micros):
            swaps1[m].wait()
            norm_to(k.a_full, gain, k.x[m].astype(F32), row.span(m, row.s, row.r))
            if m < 2:
                row.ag_start(k.a_full, m)
        wo0.step()
        wo0.step()
        q0.finish()
        loc.start(k.q0_dst, k.q0_o)
        def deal_cot():
            cot.finish()
            for m in range(micros):
                blocks_from(k.cot_dst, k.picks, k.stage_c, m, row.c)
            swap_c.start(k, row, own, size, k.stage_c, k.dy, True)

        plan = place(
            PLACES["first"],
            [
                gate0.step, up0.step, down0.start, gate0.step, up0.step, down0.step, down0.step,
                q1.start, q1.step, q1.step, wo1.start, wo1.step, wo1.step, gate1.start, up1.start,
                down1.start, gate1.step, up1.step, down1.step, gate1.step, up1.step, down1.step,
                cot.start, cot.step, cot.step, deal_cot,
            ],
            [
                (A + 20, wo0.finish), (F, gate0.finish), (F, up0.finish), (F + 10, down0.finish),
                (NEXT, q1.finish), (NEXT + 20, wo1.finish), (NEXT + F, gate1.finish),
                (NEXT + F, up1.finish), (NEXT + F + 10, down1.finish),
            ],
        )
        small_refs = SimpleNamespace(line=k.line, gains=k.gains, gates=k.gates, starts=k.starts)
        second = SimpleNamespace(**{**vars(k), **vars(view_of(k, "L1_"))})
        row_next = rows_of(second, "a_")
        gain_next = gain_row(small_refs, cfg, 1, 0)

        def begin_next(m):
            rows_here = row_next.span(m, row_next.s, row_next.r)
            norm_to(second.a_full, gain_next, k.y[m].astype(F32), rows_here)
            row_next.ag_start(second.a_full, m)

        forward_layer(
            k, 0, k.x, k.q0_dst, loc, plan, A, row, small_refs, True, begin_next,
            lambda: row_next.ag_pass(second.a_full, 0),
        )
        swap_y.start(k, row, own, size, k.y, k.stage_o, False)
        forward_layer(
            second, 1, k.y, k.q1_dst, loc, plan, NEXT, row_next, small_refs, False, lambda m: None,
            None,
        )
        loc.start(k.q1_dst, k.q1_o)
        for side in sides1:
            side.finish()
        swap_y.wait()
        swap_c.wait()
        for copy in crossing + small + late:
            copy.wait_send()
        for side in sides1 + swaps1 + [swap_y, swap_c]:
            side.drain()
        loc.finish()

    outs, scratch = forward_names(0)
    for names, into in zip(forward_names(1), (outs, scratch)):
        into.update({"L1_" + a: b for a, b in names.items() if a not in shared_rows})
    ins = dict(
        picks=(block_order, SM),
        blocks_a=(blocks_a, HB),
        blocks_b=(blocks_b, HB),
        packed=(packed, VM),
        gate_rows=(gate_rows, VM),
        starts=(starts, VM),
    )
    outs.update(
        x=((micros, own, width), BF16, VM),
        shards_a=hbm(blocks_a.shape),
        shards_b=hbm(blocks_b.shape),
        line=((2, groups) + packed.shape, F32, VM),
        gains=((2, 4, 8, 128), F32, VM),
        gates=((2,) + gate_rows.shape[1:], F32, VM),
        q0_o=hbm((1, width, 3 * size)),
        q1_o=hbm((1, width, 3 * size)),
        dy=((micros, own, width), BF16, VM),
        stage_o=hbm(stage_dims),
    )
    scratch.update(
        stage=vm(stage_dims),
        stage_c=vm(stage_dims),
        psend=pltpu.SemaphoreType.DMA((groups + 11,)),
        precv=pltpu.SemaphoreType.DMA((groups + 11,)),
        sems=pltpu.SemaphoreType.DMA((80,)),
    )
    for side in sides1:
        side.declare(ins, outs, scratch, groups)
    for swap in (*swaps1, swap_y, swap_c):
        swap.declare(scratch)
    f0 = launch("forward", 0, first_body, ins, outs, scratch)
    f1 = SimpleNamespace(**{**vars(f0), **vars(view_of(f0, "L1_"))})

    smalls = dict(
        line=(f0.line, VM), gains=(f0.gains, VM), gates=(f0.gates, VM),
        starts=(starts, VM),
    )

    def small_of(k):
        return SimpleNamespace(line=k.line, gains=k.gains, gates=k.gates, starts=k.starts)

    def backward_names(kept, dy, x, wq):
        ins = dict(
            dy=(dy, VM), mid=(kept.mid, VM), x=(x, VM), w_h=(kept.w_o, HB),
            wo_h=(kept.wo_o, HB), wq_h=(wq, HB), ax_h=(kept.a_xin_o, HB),
            qkv_h=(kept.a_qkv_o, HB), state_h=(kept.a_state_o, HB),
            mixed_h=(kept.a_mixed_o, HB), fx_h=(kept.f_xin_o, HB), gp_h=(kept.f_gp_o, HB),
            up_h=(kept.f_up_o, HB), act_h=(kept.f_act_o, HB), **smalls,
        )
        scratch = {**attn_scratch("a_"), **ffn_scratch("f_")}
        scratch.update(
            f_w=vm((3, width, ffh)), xin=vm((all_rows, width)),
            f_dg=vm((all_rows, ffh)), f_du=vm((all_rows, ffh)), f_grad=vm(grad_b_dims),
            a_wo=vm((1, width, size)), a_wq=vm((1, width, 3 * size)),
            a_dmix=vm((all_rows, size)),
            a_dqkv=vm((all_rows, 3 * size)), a_grad=vm(grad_a_dims),
            dmid=vm((micros, own, width), F32), sems=pltpu.SemaphoreType.DMA((48,)),
        )
        return ins, scratch

    def backward_layer(k, l, loc, sides, swaps_begin, plan, dx_done):
        row_f, row_a = rows_of(k, "f_"), rows_of(k, "a_")
        first = [
            loc.start(a, b) for a, b in ((k.w_h, k.f_w), (k.gp_h, k.f_gp), (k.up_h, k.f_up))
        ]
        late_f = [loc.start(a, b) for a, b in ((k.act_h, k.f_act), (k.fx_h, k.xin))]
        loads_a = [
            loc.start(a, b)
            for a, b in (
                (k.wo_h, k.a_wo), (k.qkv_h, k.a_qkv), (k.wq_h, k.a_wq), (k.state_h, k.a_state)
            )
        ]
        late_a = [loc.start(k.mixed_h, k.a_mixed)]
        for m in range(micros):
            k.f_full[row_f.span(m, row_f.s, row_f.r), :] = k.dy[m]
        greet_all(row_f)
        for side in sides:
            side.bind(k, row_f, groups)
        ag_begin(row_f, k.f_full)
        swaps_begin(row_f)
        gain_a, gain_f = gain_row(k, cfg, l, 0), gain_row(k, cfg, l, 1)
        k.dgain[...] = jnp.zeros_like(k.dgain)

        def middle(m, summed):
            back, gains = norm_back(k.mid[m], gain_f, summed)
            k.dmid[m] = k.dy[m].astype(F32) + back
            k.dgain[1:2, :] += gains
            k.a_full[row_a.span(m, row_a.s, row_a.r), :] = k.dmid[m].astype(BF16)
            row_a.ag_start(k.a_full, m)

        def leave(m, summed):
            back, gains = norm_back(k.x[m].astype(F32), gain_a, summed)
            k.dx[m] = (k.dmid[m] + back).astype(BF16)
            k.dgain[0:1, :] += gains
            dx_done(m)

        left = ffn_backward(
            view_of(k, "f_", xin=k.xin), row_f, loc, cfg, hooks(plan, F), first, late_f, middle,
            lambda: row_a.ag_pass(k.a_full, 0),
        )
        row_f.finish()

        def load_xin():
            late_a.append(loc.start(k.ax_h, k.xin))

        left = list(left) + [load_xin]
        p = view_of(k, "a_", dpersist=k.dpersist, xin=k.xin, **vars(small_of(k)))
        attn_backward(p, row_a, loc, cfg, hooks(plan, A), l, loads_a, late_a, leave, left)
        return row_f, row_a

    def staged(tag, array, home=None):
        return Gather(tag, array.reshape(by_block), by_block, groups, 1, None, home)

    def grad_of(k):
        return k.f_grad

    y0 = staged("y0_", f1.stage_o)
    y1 = Gather("y1_", None, stage_dims, groups, 1, lambda k, row: k.stage)
    td1, tg1 = (Total(t, None, grad_b_dims, groups, (i, 1), grad_of) for t, i in (("td_", 2), ("tg_", 0)))
    sides3 = [y0, y1, td1, tg1]
    swap_y1 = Swap("swap_")

    def third_body(k):
        loc = Local(k.sems)

        def begin(row):
            y0.start()
            swap_y1.start(k, row, own, size, k.y, k.stage, False)

        def start_y1():
            swap_y1.wait()
            y1.start()

        plan = place(
            PLACES["third"],
            [
                y0.step, y0.step, start_y1, td1.start, y1.step, td1.step, tg1.start, td1.step, y1.step,
                tg1.step, tg1.step,
            ],
        )
        row_f, row_a = backward_layer(k, 1, loc, sides3, begin, plan, lambda m: None)
        for i in range(3):
            loc.start(k.f_grad.at[i], k.grad_b_o.at[i])
        loc.start(k.a_grad, k.grad_a_o)
        for side in sides3:
            side.finish()
        row_f.finish()
        row_a.finish()
        for side in sides3 + [swap_y1]:
            side.drain()
        loc.finish()

    ins, scratch = backward_names(f1, f1.dy, f0.y, f0.q1_o)
    ins["y"] = (f1.y, VM)
    small_outs = dict(
        dgain=((2, width), F32, VM),
        dpersist=((2, persist, size), F32, VM),
        dx=((micros, own, width), BF16, VM),
    )
    outs = dict(grad_a_o=hbm(grad_a_dims), grad_b_o=hbm(grad_b_dims), **small_outs)
    scratch["stage"] = vm(stage_dims)
    for side in sides3:
        side.declare(ins, outs, scratch, groups)
    swap_y1.declare(scratch)
    b1 = launch("backward_1", 2, third_body, ins, outs, scratch)

    small_rows = gain_rows + 4 * persist
    tu1 = Total("tu1_", b1.grad_b_o, grad_b_dims, groups, (1, 1), None, "scratch")
    ta1 = Total("ta1_", b1.grad_a_o, grad_a_dims, groups, (0, 1), None, "scratch")
    td0, tg0, tu0 = (
        Total(t, None, grad_b_dims, groups, (i, 1), grad_of, "scratch")
        for t, i in (("td_", 2), ("tg_", 0), ("tu_", 1))
    )
    ta0 = Total("ta0_", None, grad_a_dims, groups, (0, 1), lambda k: k.a_grad, "scratch")
    g1 = Gather("g1_", None, by_block, groups, 1, lambda k, row: k.staged1)
    g0 = [
        Gather(f"g0{m}_", None, by_block[1:], groups, 0, lambda k, row, m=m: k.staged0.at[m], "scratch")
        for m in range(micros)
    ]

    def blocked(stage, staged, m):
        for b in range(blocks):
            staged[m, b] = stage[m, b * BLOCK : (b + 1) * BLOCK, :]
    sides4 = [tu1, ta1, td0, tg0, tu0, ta0, g1, *g0]
    swap_g1, swaps0 = Swap("swap_"), [Swap(f"swap{m}_") for m in range(micros)]

    def last_body(k):
        loc = Local(k.sems)
        push = pusher(k.psend, k.precv)
        load_y = loc.start(k.y0_buf, k.whole)
        loads = [
            loc.start(a, b)
            for a, b in (
                (k.bg1, k.res_b.at[1, pl.ds(0, 1)]), (k.bd1, k.res_b.at[1, pl.ds(2, 1)]),
            )
        ]

        def begin(row):
            tu1.start()
            ta1.start()
            swap_g1.start(k, row, own, size, k.dy, k.stage, False)

        def start_g1():
            swap_g1.wait()
            for m in range(micros):
                blocked(k.stage, k.staged1, m)
            g1.start()

        def gather_g0(m):
            swaps0[m].wait()
            blocked(k.stage0, k.staged0, m)
            g0[m].start()

        def dx_done(m):
            swaps0[m].start(
                k, ta0.row, own, size, k.dx.at[pl.ds(m, 1)], k.stage0.at[pl.ds(m, 1)], False
            )
            if m >= 1:
                gather_g0(m - 1)

        plan = place(
            PLACES["last"],
            [
                tu1.step, ta1.step, start_g1, tu1.step, ta1.step, g1.step, td0.start, g1.step, td0.step,
                tg0.start, tu0.start, td0.step, tg0.step, tu0.step, tg0.step, tu0.step, ta0.start,
            ],
        )
        row_f, row = backward_layer(k, 0, loc, sides4, begin, plan, dx_done)
        for i in range(half_gains):
            lanes_here = slice(i * 128, (i + 1) * 128)
            for j, ref in enumerate((k.dgain, k.dgain1)):
                for kind in range(2):
                    at = (j * 2 + kind) * half_gains + i
                    k.smalls[at : at + 1, :] = ref[kind : kind + 1, lanes_here]
        for j, ref in enumerate((k.dpersist, k.dpersist1)):
            for kind in range(2):
                at = gain_rows + (j * 2 + kind) * persist
                k.smalls[at : at + persist, :] = ref[kind]
        gather_g0(micros - 1)
        pushes = []
        for i in range(1, groups):
            to = (row.s, row.r, lax.rem(row.c + i, groups))
            pushes.append(push(k.smalls, k.small_box.at[i], i, to))
        for copy in loads:
            loc.wait(copy)

        def all_restored(slot):
            for m in range(micros):
                for b in range(blocks):
                    where = pl.ds(b * BLOCK, BLOCK)
                    k.halves[slot, m, where, :] = k.whole[m, k.back[m, b]]

        loc.wait(load_y)
        all_restored(0)
        loc.wait(loc.start(k.y1_buf, k.whole))
        all_restored(1)
        moved, kept_here = [], []
        mine_lanes = pl.ds(pl.multiple_of(row.s * size, 128), size)

        def give(i, pair, out):
            moved.append(push(pair.at[1 - row.s], out, groups + 8 + i, row.sib))
            kept_here.append(loc.start(pair.at[row.s], out))

        give(0, k.halves.at[pl.ds(0, 2)], k.acts_o.at[:, :, mine_lanes])

        for g in g0:
            g.step()
        ta0.step()
        g1.finish()
        loc.wait(loc.start(k.g1_dst, k.whole))
        all_restored(3)
        for g in g0:
            g.step()
        ta0.step()
        for total in (td0, tg0, tu0, tu1, ta1):
            total.finish()
        k.res_b[0, pl.ds(2, 1)] = k.td_sum[...]
        k.res_b[0, pl.ds(0, 1)] = k.tg_sum[...]
        k.res_b[0, pl.ds(1, 1)] = k.tu_sum[...]
        k.res_b[1, pl.ds(1, 1)] = k.tu1_sum[...]
        k.res_a[1] = k.ta1_sum[...]
        give(1, k.res_b, k.grad_b.at[row.s])
        for copy in pushes:
            copy.wait_recv()
        total = k.smalls[...]
        for i in range(1, groups):
            total = total + k.small_box[i]
        k.small_sum[...] = total

        def persist_rows(layer):
            at = pl.multiple_of(gain_rows + layer * 2 * persist, 8)
            return k.small_sum.at[pl.ds(at, 2 * persist), :]

        out = k.persist_o.at[row.s]
        moved.append(push(persist_rows(1 - row.s), out, groups + 12, row.sib))
        kept_here.append(loc.start(persist_rows(row.s), out))
        gains = []
        for i, ps, pr in others(row):
            src = k.small_sum.at[pl.ds(0, gain_rows), :]
            gains.append(push(src, k.gain_box.at[i], groups + i, (ps, pr, row.c)))
        ta0.finish()
        k.res_a[0] = k.ta0_sum[...]
        give(2, k.res_a, k.grad_a.at[row.s])
        for m, g in enumerate(g0):
            g.finish()
            buf = getattr(k, f"g0{m}_dst")
            for b in range(blocks):
                k.halves[2, m, pl.ds(b * BLOCK, BLOCK), :] = buf[k.back[m, b]]
        give(3, k.halves.at[pl.ds(2, 2)], k.grads_o.at[:, :, mine_lanes])
        for copy in gains:
            copy.wait_recv()
        total = k.small_sum[0:gain_rows, :]
        for i in range(1, 8):
            total = total + k.gain_box[i]
        k.gain_o[...] = total
        for copy in moved:
            copy.wait()
        for copy in pushes + gains:
            copy.wait_send()
        for side in sides4:
            side.finish()
        row_f.finish()
        row.finish()
        for side in sides4 + [swap_g1] + swaps0:
            side.drain()
        loc.finish()

    ins, scratch = backward_names(f0, b1.dx, f0.x, f0.q0_o)
    ins.update(
        y0_buf=(b1.y0_dst, HB),
        y1_buf=(b1.y1_dst.reshape(b1.y0_dst.shape), HB),
        bg1=(b1.tg_sum, HB),
        bd1=(b1.td_sum, HB),
        dgain1=(b1.dgain, VM),
        dpersist1=(b1.dpersist, VM),
        back=(back_picks, SM),
    )
    outs = dict(
        acts_o=((micros, rows, features), BF16, VM),
        grads_o=((micros, rows, features), BF16, VM),
        grad_a=((2,) + ta0.dims, BF16, VM),
        grad_b=((2, 3) + tu0.dims[1:], BF16, VM),
        gain_o=((gain_rows, 128), F32, VM),
        persist_o=((2, 2 * persist, 128), F32, VM),
    )
    scratch.update(
        stage=vm(stage_dims),
        stage0=vm(stage_dims),
        whole=vm((micros, total_blocks, BLOCK, size)),
        staged0=vm(by_block),
        staged1=vm(by_block),
        halves=vm((4,) + stage_dims),
        res_a=vm((2,) + ta0.dims),
        res_b=vm((2, 3) + tu0.dims[1:]),
        smalls=vm((small_rows, 128), F32),
        small_box=vm((groups, small_rows, 128), F32),
        small_sum=vm((small_rows, 128), F32),
        gain_box=vm((8, gain_rows, 128), F32),
        dgain=vm((2, width), F32),
        dpersist=vm((2, persist, size), F32),
        dx=vm((micros, own, width)),
        psend=pltpu.SemaphoreType.DMA((groups + 13,)),
        precv=pltpu.SemaphoreType.DMA((groups + 13,)),
    )
    for side in sides4:
        side.declare(ins, outs, scratch, groups)
    for swap in [swap_g1] + swaps0:
        swap.declare(scratch)
    closed = launch("backward_0", 3, last_body, ins, outs, scratch)

    def cols_join(pair):
        return jnp.concatenate([pair[0], pair[1]], axis=1).astype(F32)[None]

    def rows_join(pair):
        return jnp.concatenate([pair[0].T, pair[1].T], axis=0).astype(F32)[None]

    grad_a, grad_b = closed.grad_a[:, 0], closed.grad_b
    heads = [cols_join(grad_a[:, :, i * size : (i + 1) * size]) for i in range(3)]
    grad_out = rows_join(grad_a[:, :, 3 * size :])
    grad_gate, grad_up = cols_join(grad_b[:, 0]), cols_join(grad_b[:, 1])
    grad_down = rows_join(grad_b[:, 2])
    gain_sum = closed.gain_o.reshape(2, 2, width)
    my_gain = lax.dynamic_slice_in_dim(
        lax.dynamic_index_in_dim(gain_sum, sec, 0, False), (row_id * groups + col) * share, share, 1
    )
    persist_sum = closed.persist_o.reshape(2, 2, persist, size)
    persist_sum = lax.dynamic_slice_in_dim(persist_sum, col * per, per, 2)
    grad_persist = jnp.concatenate([persist_sum[0], persist_sum[1]], axis=2)
    return (
        closed.acts_o[None],
        closed.grads_o[None],
        my_gain[0][None],
        heads[0],
        heads[1],
        heads[2],
        grad_persist[0][None],
        grad_persist[1][None],
        grad_out,
        my_gain[1][None],
        grad_gate,
        grad_up,
        grad_down,
    )


def solution(mesh):
    weight = P("section", "col", "row")
    across = P("section", "row", "col")
    gain = P("section", ("row", "col"))
    rows = P("section", None, "col", "row")
    return jax.shard_map(
        local,
        mesh=mesh,
        in_specs=(
            P(None, "col", "row"), P(None, "col", "row"), P(), P(), rows, rows, gain, weight, weight,
            weight, weight, weight, across, gain, weight, weight, across,
        ),
        out_specs=(
            rows, rows, gain, weight, weight, weight, weight, weight, across, gain, weight, weight,
            across,
        ),
        check_vma=False,
    )
```
